32 devices in a mesh: section: 2 (over core), seq: 4 (over z), head: 4 (over y, x).
Axes of the slice: x: 2, y: 2, z: 4, core: 2. Of those that a mesh axis runs over, the one named last changes fastest.
Arguments:
- inputs: bfloat16 [2, 1024, 1792], P(None, 'seq'), may hold values from -6 to 6
- out_grad: bfloat16 [2, 1024, 1792], P(None, 'seq'), may hold values from -6 to 6
- lengths: int32 [2, 2], replicated, may hold values from 0 to 1024, as said below
- norm_attn: float32 [2, 1792], P('section'), may hold values from 0.5 to 1.5
- norm_ffn: float32 [2, 1792], P('section'), may hold values from 0.5 to 1.5
- w_query: bfloat16 [2, 1792, 256], P('section', None, 'head'), may hold values from -0.125 to 0.125
- w_key: bfloat16 [2, 1792, 256], P('section', None, 'head'), may hold values from -0.125 to 0.125
- w_value: bfloat16 [2, 1792, 1792], P('section', None, 'head'), may hold values from -0.125 to 0.125
- w_output_gate: bfloat16 [2, 1792, 1792], P('section', None, 'head'), may hold values from -0.125 to 0.125
- conv_kernel: float32 [2, 3, 1792], P('section', None, 'head'), may hold values from -3.5 to 3.5
- w_out: bfloat16 [2, 1792, 1792], P('section', 'head'), may hold values from -1 to 1
- w_gate: bfloat16 [2, 1792, 4864], P('section', None, 'head'), may hold values from -0.125 to 0.125
- w_up: bfloat16 [2, 1792, 4864], P('section', None, 'head'), may hold values from -0.125 to 0.125
- w_down: bfloat16 [2, 4864, 1792], P('section', 'head'), may hold values from -0.078125 to 0.078125
Outputs:
- section_out: bfloat16 [2, 2, 1024, 1792], P('section', None, 'seq')
- input_grad: bfloat16 [2, 2, 1024, 1792], P('section', None, 'seq')
- grad_norm_attn: float32 [2, 1792], P('section')
- grad_norm_ffn: float32 [2, 1792], P('section')
- grad_w_query: float32 [2, 1792, 256], P('section', 'seq', 'head')
- grad_w_key: float32 [2, 1792, 256], P('section', 'seq', 'head')
- grad_w_value: float32 [2, 1792, 1792], P('section', 'seq', 'head')
- grad_w_output_gate: float32 [2, 1792, 1792], P('section', 'seq', 'head')
- grad_conv_kernel: float32 [2, 3, 1792], P('section', None, 'head')
- grad_w_out: float32 [2, 1792, 1792], P('section', 'head', 'seq')
- grad_w_gate: float32 [2, 1792, 4864], P('section', 'seq', 'head')
- grad_w_up: float32 [2, 1792, 4864], P('section', 'seq', 'head')
- grad_w_down: float32 [2, 4864, 1792], P('section', 'head', 'seq')
The draws below stay inside these ranges and needn't reach their ends.
Inputs may be any that keep to these rules, and one draw needn't show every extreme that they name: In each micro-batch the two lengths sum to 1024 or less and to 896 or more; the first is at least the smaller of 1024 and that sum; slots after both sequences are padding. In one micro-batch the first sequence fills all 1024 slots.
All inputs are finite; a program needn't handle non-finite values.
Results may differ from the reference program's by a relative error of at most 0.029.
Values may be sent and summed in bfloat16 or wider, within the bound.
A program may use at most 256 MiB of HBM per device.

```python
import math
import jax
import jax.numpy as jnp
from jax import lax

D = 1792
HEADS = 16
HD = 112
FEAT = 16
FF = 4864
KW = 3
MICRO = 2
MINLEN = 1024
TOK_DEV = 256
MBTOK = 1024
N_SECTION = 2
N_HEAD = 4


def draw_lengths(key, part):
    key = jax.random.fold_in(key, 7)
    key_pad, key_pick, key_cut = jax.random.split(key, 3)
    padding = jax.random.randint(key_pad, (MICRO,), 0, TOK_DEV // 2 + 1)
    chosen = jax.random.randint(key_pick, (), 0, MICRO)
    picked = jnp.arange(MICRO) == chosen
    used_slots = jnp.where(picked, MBTOK, MBTOK - padding)
    lower_len = jnp.minimum(MINLEN, used_slots)
    first_len = jax.random.randint(key_cut, (MICRO,), lower_len, used_slots + 1)
    first_len = jnp.where(picked, MBTOK, first_len)
    return jnp.stack([first_len, used_slots - first_len], axis=1).astype(jnp.int32)


def raised(array, key, source, target, shards_of, factor):
    owner, partner = [(jnp.arange(array.shape[dim]) // (array.shape[dim] // shards_of)).reshape([-1 if axis == dim else 1 for axis in range(array.ndim)]) for dim in (source, target)]
    chosen = jax.random.permutation(key, shards_of)[partner]
    strong = (owner == chosen) | (owner == (partner + shards_of // 2) % shards_of)
    return jnp.where(strong, factor * array, array)


def block_levels(rng, shape, cuts, low, top_value):
    gain = 1.0
    for dim, blocks in cuts:
        heights = jax.random.uniform(jax.random.fold_in(jax.random.fold_in(rng, 6), dim), (blocks,), jnp.float32, low / len(cuts), top_value / len(cuts))
        gain = gain * jnp.repeat(jnp.exp(heights), shape[dim] // blocks).reshape((-1,) + (1,) * (len(shape) - 1 - dim))
    return gain


def gaussian(rng, extent, scale, limit, shards=(), kind=jnp.bfloat16):
    entries = scale * jax.random.normal(rng, extent, jnp.float32)
    if shards:
        entries = entries * block_levels(rng, extent, shards, -0.22, 0.18)
    return jnp.clip(entries, -limit, limit).astype(kind)


def gaussian_with(own_key, shape, spread, limit, cuts, heavy, kind=jnp.bfloat16):
    values = spread * jax.random.normal(own_key, shape, jnp.float32)
    if cuts:
        values = values * block_levels(own_key, shape, cuts, -0.22, 0.18)
    return jnp.clip(raised(values, jax.random.fold_in(own_key, 3), *heavy), -limit, limit).astype(kind)


def setup_inputs(seed: int = 0) -> dict:
    streams_of = jax.random.split(jax.random.key(seed), 15)
    inputs = gaussian_with(streams_of[0], (MICRO, MBTOK, D), 1.0, 6.0, ((1, 4),), (1, 2, 4, 2.0))
    out_grad = gaussian(streams_of[1], (MICRO, MBTOK, D), 1.0, 6.0, ((1, 4),))
    lengths = draw_lengths(jax.random.fold_in(streams_of[14], 71), 0)
    norm_attn = jnp.clip(1.0 + 0.1 * jax.random.normal(streams_of[3], (N_SECTION, D), jnp.float32), 0.5, 1.5)
    norm_ffn = jnp.clip(1.0 + 0.1 * jax.random.normal(streams_of[4], (N_SECTION, D), jnp.float32), 0.5, 1.5)
    w_query = gaussian(streams_of[5], (N_SECTION, D, HEADS * FEAT), D ** -0.5, 0.125, ((0, 2), (2, 4)))
    w_key = gaussian(streams_of[6], (N_SECTION, D, HEADS * FEAT), D ** -0.5, 0.125, ((0, 2), (2, 4)))
    w_value = gaussian(streams_of[7], (N_SECTION, D, D), D ** -0.5, 0.125, ((0, 2), (2, 4)))
    w_output_gate = gaussian(streams_of[8], (N_SECTION, D, D), D ** -0.5, 0.125, ((0, 2), (2, 4)))
    conv_kernel = gaussian(streams_of[9], (N_SECTION, KW, D), KW ** -0.5, 3.5, ((0, 2), (2, 4)), jnp.float32)
    w_out = gaussian(streams_of[10], (N_SECTION, D, D), (max(1, 16 * D // MBTOK)) ** -0.5, 1.0, ((0, 2), (1, 4)))
    w_gate = gaussian(streams_of[11], (N_SECTION, D, FF), D ** -0.5, 0.125, ((0, 2), (2, 4)))
    w_up = gaussian(streams_of[12], (N_SECTION, D, FF), D ** -0.5, 0.125, ((0, 2), (2, 4)))
    w_down = gaussian(streams_of[13], (N_SECTION, FF, D), FF ** -0.5, 0.078125, ((0, 2), (1, 4)))
    return dict(inputs=inputs, out_grad=out_grad, lengths=lengths, norm_attn=norm_attn, norm_ffn=norm_ffn, w_query=w_query, w_key=w_key, w_value=w_value, w_output_gate=w_output_gate, conv_kernel=conv_kernel, w_out=w_out, w_gate=w_gate, w_up=w_up, w_down=w_down)


epsilon = 1e-05
highest = lax.Precision.HIGHEST

@jax.custom_vjp
def low(v):
    return lax.optimization_barrier(v.astype(jnp.bfloat16)).astype(jnp.float32)

@jax.custom_vjp
def low_back(v):
    return v

def low_keep(v):
    return (low(v), None)

def low_pass(kept, grad):
    return (grad,)

def back_keep(v):
    return (v, None)

def back_low(kept, grad):
    return (low(grad),)
low.defvjp(low_keep, low_pass)
low_back.defvjp(back_keep, back_low)

def matmul(left_arr, right_arr):
    return jnp.dot(left_arr, right_arr, precision=highest)

def normalize(values, gain_vec):
    inverse = lax.rsqrt(lax.optimization_barrier(jnp.mean(values * values, axis=-1, keepdims=True)) + epsilon)
    return values * inverse * gain_vec

def segment_of(position, first_len, second_len):
    inside = (position >= first_len).astype(jnp.int32) + (position >= first_len + second_len).astype(jnp.int32)
    return jnp.where(position >= 0, inside, -1)

def segment_start(segment, first_len, second_len):
    return jnp.where(segment <= 0, 0, jnp.where(segment == 1, first_len, first_len + second_len))

def taylor(values):
    row_count, head_count, feat_dim = values.shape
    outer_prod = (values[:, :, :, None] * values[:, :, None, :]).reshape(row_count, head_count, feat_dim * feat_dim)
    unit_col = jnp.ones((row_count, head_count, 1), jnp.float32)
    return jnp.concatenate([unit_col, values, outer_prod * 0.5 ** 0.5], axis=2)

def attend(queries, key_rows, value_rows, state_in, norm_in, segment, applies):
    row_count = queries.shape[0]
    scores = jnp.einsum('ihf,jhf->hij', queries, key_rows, precision=highest)
    kernel = 1.0 + scores + 0.5 * scores * scores
    order_ids = jnp.arange(row_count, dtype=jnp.int32)
    allowed = (order_ids[None, :] <= order_ids[:, None]) & (segment[None, :] == segment[:, None])
    kernel = jnp.where(allowed[None], kernel, 0.0)
    numerator = jnp.einsum('hij,jhe->ihe', kernel, value_rows, precision=highest)
    denominator = lax.optimization_barrier(jnp.sum(kernel, axis=2)).T
    lifted = taylor(queries) * applies[:, None, None]
    numerator = numerator + jnp.einsum('ihf,hfe->ihe', lifted, state_in, precision=highest)
    denominator = denominator + jnp.einsum('ihf,hf->ih', lifted, norm_in, precision=highest)
    return numerator / denominator[:, :, None]

def tail_state(key_rows, value_rows, tail_mask):
    lifted = taylor(key_rows) * tail_mask[:, None, None]
    return (jnp.einsum('ihf,ihe->hfe', lifted, value_rows, precision=highest), lax.optimization_barrier(jnp.sum(lifted, axis=0)))

def short_conv(extended, kernel, seg_ext, segment):
    kernel_width = kernel.shape[0]
    row_count = segment.shape[0]
    summed = jnp.zeros((row_count, extended.shape[1]), jnp.float32)
    for lag_step in range(kernel_width):
        begin_row = kernel_width - 1 - lag_step
        shifted = extended[begin_row:begin_row + row_count]
        same_doc = (seg_ext[begin_row:begin_row + row_count] == segment)[:, None]
        summed = summed + jnp.where(same_doc, shifted * kernel[lag_step][None, :], 0.0)
    return summed

def attention_whole(queries, key_rows, value_rows, segment, first_len, second_len):
    row_count = queries.shape[0]
    block_rows = math.gcd(row_count, 512)
    block_count = row_count // block_rows
    lifted_dim = 1 + FEAT + FEAT * FEAT

    def block_step(carry, block):
        state_prev, norm_prev = carry
        query_blk, key_blk, value_blk, seg_blk, begin_row = block
        prior_seg = segment_of(begin_row - 1, first_len, second_len)
        applies = (seg_blk == prior_seg).astype(jnp.float32)
        tail_mask = (seg_blk == seg_blk[block_rows - 1]).astype(jnp.float32)
        reset_flag = (segment_start(seg_blk[block_rows - 1], first_len, second_len) >= begin_row).astype(jnp.float32)
        output = attend(query_blk, key_blk, value_blk, state_prev, norm_prev, seg_blk, applies)
        state_tail, norm_tail = tail_state(key_blk, value_blk, tail_mask)
        carry_keep = 1.0 - reset_flag
        return ((state_tail + carry_keep * state_prev, norm_tail + carry_keep * norm_prev), output)
    initial = (jnp.zeros((HEADS, lifted_dim, HD), jnp.float32), jnp.zeros((HEADS, lifted_dim), jnp.float32))
    starts = jnp.arange(block_count, dtype=jnp.int32) * block_rows
    blocks = (queries.reshape(block_count, block_rows, HEADS, FEAT), key_rows.reshape(block_count, block_rows, HEADS, FEAT), value_rows.reshape(block_count, block_rows, HEADS, HD), segment.reshape(block_count, block_rows), starts)
    final_state, outputs = lax.scan(jax.checkpoint(block_step), initial, blocks)
    return outputs.reshape(row_count, HEADS, HD)

def block_layer(layer_in, lengths_now, params):
    gain_attn, gain_ffn, query_w, key_w, value_w, outgate_w, conv_w, mixout_w, gate_w, upward_w, down_w = params
    row_count = layer_in.shape[0]
    positions = jnp.arange(row_count, dtype=jnp.int32)
    first_len = lengths_now[0]
    second_len = lengths_now[1]
    segment = segment_of(positions, first_len, second_len)
    valid_rows = (positions < first_len + second_len).astype(jnp.float32)
    normed_one = low(normalize(layer_in, gain_attn))
    qk_share = query_w.shape[1] // N_HEAD
    value_share = value_w.shape[1] // N_HEAD
    hidden_share = gate_w.shape[1] // N_HEAD
    query_parts, key_parts, value_parts, gate_parts = ([], [], [], [])
    for group_index in range(N_HEAD):
        copy_one = low_back(normed_one)
        qk_cols = slice(group_index * qk_share, (group_index + 1) * qk_share)
        value_cols = slice(group_index * value_share, (group_index + 1) * value_share)
        query_parts.append(low_back(low(matmul(copy_one, query_w[:, qk_cols]))))
        key_parts.append(low_back(low(matmul(copy_one, key_w[:, qk_cols]))))
        value_parts.append(low_back(low(matmul(copy_one, value_w[:, value_cols]))))
        gate_parts.append(low_back(matmul(copy_one, outgate_w[:, value_cols])))
    queries = jnp.concatenate(query_parts, axis=1)
    key_all = jnp.concatenate(key_parts, axis=1)
    value_pre = jnp.concatenate(value_parts, axis=1)
    outgate = jnp.concatenate(gate_parts, axis=1)
    extended = jnp.concatenate([jnp.zeros((KW - 1, value_pre.shape[1]), jnp.float32), value_pre])
    seg_ext = jnp.concatenate([jnp.full((KW - 1,), -1, jnp.int32), segment])
    mixed_values = short_conv(extended, conv_w, seg_ext, segment)
    feat_scale = FEAT ** (-0.25)
    attended = attention_whole(queries.reshape(row_count, HEADS, FEAT) * feat_scale, key_all.reshape(row_count, HEADS, FEAT) * feat_scale, mixed_values.reshape(row_count, HEADS, HD), segment, first_len, second_len)
    gated = low(attended.reshape(row_count, HEADS * HD) * jax.nn.silu(outgate))
    mix_sum = jnp.zeros_like(layer_in)
    for group_index in range(N_HEAD):
        value_cols = slice(group_index * value_share, (group_index + 1) * value_share)
        mix_sum = mix_sum + low(matmul(gated[:, value_cols], mixout_w[value_cols, :]))
    hidden_one = layer_in + low_back(mix_sum)
    normed_two = low(normalize(hidden_one, gain_ffn))
    feed_sum = jnp.zeros_like(layer_in)
    for group_index in range(N_HEAD):
        copy_two = low_back(normed_two)
        hidden_cols = slice(group_index * hidden_share, (group_index + 1) * hidden_share)
        gate_pre = low_back(matmul(copy_two, gate_w[:, hidden_cols]))
        up_pre = low_back(matmul(copy_two, upward_w[:, hidden_cols]))
        activated = low(jax.nn.silu(gate_pre) * up_pre)
        feed_sum = feed_sum + low(matmul(activated, down_w[hidden_cols, :]))
    return (hidden_one + low_back(feed_sum)) * valid_rows[:, None]

def reference(inputs, out_grad, lengths, norm_attn, norm_ffn, w_query, w_key, w_value, w_output_gate, conv_kernel, w_out, w_gate, w_up, w_down):
    weights = tuple((tensor_item.astype(jnp.float32) for tensor_item in (norm_attn, norm_ffn, w_query, w_key, w_value, w_output_gate, conv_kernel, w_out, w_gate, w_up, w_down)))
    input_rows = inputs.astype(jnp.float32)
    offsets = jnp.zeros((N_SECTION,) + inputs.shape, jnp.float32)
    checked = jax.checkpoint(block_layer)

    def whole_run(offset_all, weight_all):
        section_rows = [[None] * MICRO for section_index in range(N_SECTION)]
        for micro_index in range(MICRO):
            current = input_rows[micro_index]
            for section_index in range(N_SECTION):
                current = low_back(current + offset_all[section_index, micro_index])
                params = tuple((tensor_item[section_index] for tensor_item in weight_all))
                current = low(checked(current, lengths[micro_index], params))
                section_rows[section_index][micro_index] = current
        stacked = jnp.stack([jnp.stack(per_section) for per_section in section_rows])
        return (stacked[N_SECTION - 1], stacked)
    final_rows, pull_back, stacked = jax.vjp(whole_run, offsets, weights, has_aux=True)
    grad_offsets, grad_weights = pull_back(out_grad.astype(jnp.float32))
    return (stacked.astype(jnp.bfloat16), grad_offsets.astype(jnp.bfloat16), grad_weights[0], grad_weights[1], grad_weights[2], grad_weights[3], grad_weights[4], grad_weights[5], grad_weights[6], grad_weights[7], grad_weights[8], grad_weights[9], grad_weights[10])
```

```python
import functools

import jax
import jax.numpy as jnp
import numpy as np
from jax import lax
from jax.experimental import pallas as pl
from jax.experimental.pallas import tpu as pltpu
from jax.sharding import PartitionSpec as P

HD = 112
FEAT = 16
KW = 3
EPS = 1e-05
LANES = 128
PSI = 256
PSI_SENT = 160
MESH = pl.DeviceIdType.MESH
F32 = jnp.float32
BF16 = jnp.bfloat16
VMEM_LIMIT = 60 << 20


def dot_nn(a, b):
    return lax.dot_general(a, b, (((1,), (0,)), ((), ())), preferred_element_type=F32)


def dot_nt(a, b):
    return lax.dot_general(a, b, (((1,), (1,)), ((), ())), preferred_element_type=F32)


def dot_tn(a, b):
    return lax.dot_general(a, b, (((0,), (0,)), ((), ())), preferred_element_type=F32)


def chunks(total, step, body):
    whole = total // step
    if whole > 1:

        def one(i, carry):
            body(pl.multiple_of(i * step, step), step)
            return carry

        lax.fori_loop(0, whole, one, 0)
    elif whole == 1:
        body(0, step)
    if total % step:
        body(whole * step, total % step)


def lift_tables(heads):
    first = np.zeros((heads * FEAT, heads * PSI), np.float32)
    second = np.zeros_like(first)
    second_key = np.zeros_like(first)
    for head in range(heads):
        row, col = head * FEAT, head * PSI
        for i in range(FEAT):
            first[row + i, col + 1 + i] = 1.0
        at = 1 + FEAT
        for i in range(FEAT):
            for j in range(i, FEAT):
                first[row + i, col + at] = 1.0
                second[row + j, col + at] = 1.0
                second_key[row + j, col + at] = 0.5 if i == j else 1.0
                at += 1
    return np.stack([first, second, second_key])


class Place:
    def __init__(self, lens, nz, nh, rows):
        self.sec, self.s, self.h = (lax.axis_index(a) for a in ("section", "seq", "head"))
        self.nz, self.nh, self.rows = nz, nh, rows
        self.l0 = lens[self.sec, 0]
        self.tot = self.l0 + lens[self.sec, 1]
        self.first = self.s * rows
        self.part = rows // nh
        self.mine = pl.ds(pl.multiple_of(self.h * self.part, self.part), self.part)

    def seg(self, pos):
        inside = (pos >= self.l0).astype(jnp.int32) + (pos >= self.tot).astype(jnp.int32)
        return jnp.where(pos >= 0, inside, -1)

    def pos(self, shift=0):
        return self.first + shift + lax.broadcasted_iota(jnp.int32, (self.rows, 1), 0)

    def same(self, shift):
        other = self.pos(shift)
        inside = other < self.nz * self.rows
        return (self.seg(other) == self.seg(self.pos())) & inside

    def allowed(self):
        shape = (self.rows, self.rows)
        row = lax.broadcasted_iota(jnp.int32, shape, 0)
        col = lax.broadcasted_iota(jnp.int32, shape, 1)
        return (col <= row) & (self.seg(self.first + col) == self.seg(self.first + row))

    def last_seg(self, block):
        return self.seg(block * self.rows + self.rows - 1)

    def prior_seg(self, block):
        return self.seg(block * self.rows - 1)

    def applies(self):
        return self.seg(self.pos()) == self.prior_seg(self.s)

    def tail(self):
        return self.seg(self.pos()) == self.last_seg(self.s)

    def peers(self):
        core = [(1 - self.sec, self.s, self.h)]
        seq = [(self.sec, (self.s + k) % self.nz, self.h) for k in range(1, self.nz)]
        head = [(self.sec, self.s, self.h ^ m) for m in range(1, self.nh)]
        return core, seq, head

    def barrier(self, core, seq, head):
        groups = self.peers()
        told = [d for use, g in zip((core, seq, head), groups) if use for d in g]
        sem = pltpu.get_barrier_semaphore()
        for device in told:
            pl.semaphore_signal(sem, 1, device_id=device, device_id_type=MESH)
        pl.semaphore_wait(sem, len(told))


def remote(src, dst, send, recv, device):
    return pltpu.make_async_remote_copy(
        src_ref=src, dst_ref=dst, send_sem=send, recv_sem=recv, device_id=device, device_id_type=MESH
    )


def scatter_start(at, buf, got, send, recv):
    sent = []
    for m in sorted(range(1, at.nh), reverse=True):
        peer = at.h ^ m
        rows = pl.ds(pl.multiple_of(peer * at.part, at.part), at.part)
        copy = remote(buf.at[rows], got.at[m - 1], send.at[m - 1], recv.at[m - 1], (at.sec, at.s, peer))
        copy.start()
        sent.append(copy)
    return sent


def scatter_sum(at, buf, got, sent):
    total = buf[at.mine].astype(F32)
    for copy in sent:
        copy.wait_recv()
    for m in range(1, at.nh):
        total = total + got[m - 1].astype(F32)
    return total


def gather_start(at, buf, send, recv):
    sent = []
    for m in sorted(range(1, at.nh), reverse=True):
        copy = remote(
            buf.at[at.mine], buf.at[at.mine], send.at[m - 1], recv.at[m - 1], (at.sec, at.s, at.h ^ m)
        )
        copy.start()
        sent.append(copy)
    return sent


def wait_recv(copies):
    for copy in copies:
        copy.wait_recv()


def wait_send(copies):
    for copy in copies:
        copy.wait_send()


def norm_rows(x, gain):
    return x * lax.rsqrt(jnp.mean(x * x, axis=-1, keepdims=True) + EPS) * gain


def norm_rows_back(x, gain, grad):
    inverse = lax.rsqrt(jnp.mean(x * x, axis=-1, keepdims=True) + EPS)
    unit = x * inverse
    scaled = grad * gain
    back = inverse * (scaled - unit * jnp.mean(scaled * unit, axis=-1, keepdims=True))
    return back, jnp.sum(grad * unit, axis=0, keepdims=True)


def lift_parts(low, tables, second, head):
    cols = slice(head * PSI, (head + 1) * PSI)
    lane = lax.broadcasted_iota(jnp.int32, (1, PSI), 1)
    one = dot_nn(low, tables[0, :, cols]) + (lane == 0).astype(F32)
    two = dot_nn(low, tables[second, :, cols]) + (lane <= FEAT).astype(F32)
    return one, two


def head_only(low, head):
    lane = lax.broadcasted_iota(jnp.int32, low.shape, 1)
    return jnp.where((lane >= head * FEAT) & (lane < (head + 1) * FEAT), low, jnp.zeros_like(low))


def convolve(at, u_s, taps, c_s, cx_s, heads):
    rows, width = at.rows, heads * HD
    out = taps[0:1, :width] * u_s[8 : 8 + rows, :width]
    for j in range(1, KW):
        shifted = u_s[8 - j : 8 - j + rows, :width]
        out = out + jnp.where(at.same(-j), shifted * taps[j : j + 1, :width], 0.0)
    c_s[0:rows, :width] = out
    lane = lax.broadcasted_iota(jnp.int32, (rows, LANES), 1)
    for head in range(heads):
        one = c_s[0:rows, head * HD : head * HD + LANES]
        cx_s[head] = jnp.where(lane < HD, one, jnp.where(lane == HD, 1.0, 0.0)).astype(BF16)


class Weights:
    def __init__(self, at, layer, own, other, slots, sems):
        self.at, self.layer, self.own, self.other, self.slots, self.sems = at, layer, own, other, slots, sems

    def _copy(self, src, i):
        return pltpu.make_async_copy(src[i].at[0], self.slots[i], self.sems.at[i])

    def start(self, i):
        @pl.when(self.at.sec == self.layer)
        def _():
            self._copy(self.own, i).start()

        @pl.when(self.at.sec != self.layer)
        def _():
            self._copy(self.other, i).start()

    def wait(self, i):
        self._copy(self.own, i).wait()


W_NAMES = ("q", "k", "v", "o", "out", "gate", "up", "down")


def fwd_kernel(layer, dims, *refs):
    nz, nh, rows, heads = dims
    refs = list(refs)

    def take(n):
        out = refs[:n]
        del refs[:n]
        return out

    lens, x_in, small_own = take(3)
    small_other = None if layer == 0 else take(1)[0]
    (tables,) = take(1)
    own = take(8)
    other = None if layer == 0 else take(8)
    if layer == 0:
        small_other = take(1)[0]
        other = take(8)
    xo_o, n1_o, n2_o, q_o, k_o, u_o, o_o, yx_o, sin_o, g_o, h_o, f_o, v_o = take(13)
    slots = take(8)
    (x_s, n1_s, n2_s, u_s, o_s, c_s, cx_s, yx_s, ss, sr, g_s, gb_s, p1, r1, p2, r2, f_s, v_s, t_s, xo_s, h_s, sm_s) = take(22)
    w_sem, io_sem, x_send, x_recv, e_send, e_recv, st_send, st_recv, head_send, head_recv = take(10)
    at = Place(lens, nz, nh, rows)
    d = x_s.shape[1]
    width = heads * HD
    core = (1 - at.sec, at.s, at.h)

    x_copy = pltpu.make_async_copy(x_in.at[at.sec] if layer == 0 else x_in, x_s, io_sem.at[0])
    x_copy.start()
    weights = Weights(at, layer, own, other, slots, w_sem)
    at.barrier(layer == 0, True, True)
    swaps = []
    if layer == 0:
        small_swap = remote(small_own, small_other, x_send.at[8], x_recv.at[8], core)
        small_swap.start()
        for i in range(8):
            swap = remote(own[i], other[i], x_send.at[i], x_recv.at[i], core)
            swap.start()
            swaps.append(swap)
        small_swap.wait_recv()
    small_copy = pltpu.make_async_copy(small_other, sm_s, io_sem.at[1])
    small_copy.start()

    def load(i):
        if layer == 0:

            @pl.when(at.sec == 1)
            def _():
                swaps[i].wait_recv()

        weights.start(i)

    if layer == 1:
        for i in range(8):
            load(i)
    else:
        for i in range(5):
            load(i)
    small_copy.wait()
    small = jnp.where(at.sec == layer, small_own[...], sm_s[...])
    gain_attn, gain_ffn, taps = small[0:1], small[1:2], small[2 : 2 + KW]
    x_copy.wait()
    n1_s[...] = norm_rows(x_s[...].astype(F32), gain_attn).astype(BF16)

    weights.wait(2)
    u_s[8 : 8 + rows, :width] = dot_nn(n1_s[...], slots[2][...]).astype(BF16).astype(F32)
    edge = remote(
        u_s.at[pl.ds(rows, 8)], u_s.at[pl.ds(0, 8)], e_send, e_recv, (at.sec, (at.s + 1) % nz, at.h)
    )

    @pl.when(at.s + 1 < nz)
    def _():
        edge.start()

    weights.wait(0)
    q_o[...] = (dot_nn(n1_s[...], slots[0][...]).astype(BF16).astype(F32) * 0.5).astype(BF16)
    weights.wait(1)
    k_o[...] = (dot_nn(n1_s[...], slots[1][...]).astype(BF16).astype(F32) * 0.5).astype(BF16)
    weights.wait(3)
    o_s[:, :width] = dot_nn(n1_s[...], slots[3][...])

    @pl.when(at.s > 0)
    def _():
        edge.wait_recv()

    convolve(at, u_s, taps, c_s, cx_s, heads)
    outs = [pltpu.make_async_copy(a, b, io_sem.at[2 + i]) for i, (a, b) in enumerate(((n1_s, n1_o), (u_s, u_o), (o_s, o_o)))]
    for copy in outs:
        copy.start()

    a_low, b_low = q_o[...], k_o[...]
    tail = at.tail()
    for head in range(heads):
        one, two = lift_parts(b_low, tables, 2, head)
        psi = jnp.where(tail, one * two, 0.0).astype(BF16)
        ss[head] = dot_tn(psi, cx_s[head])[:PSI_SENT].astype(BF16)
    for k in range(1, nz):

        @pl.when(at.s + k < nz)
        def _(k=k):
            remote(ss, sr.at[at.s], st_send.at[k - 1], st_recv.at[at.s], (at.sec, (at.s + k) % nz, at.h)).start()

    allowed = at.allowed()
    for head in range(heads):
        e = dot_nt(a_low, head_only(b_low, head))
        kern = jnp.where(allowed, 1.0 + e + 0.5 * e * e, 0.0).astype(BF16)
        yx_s[head] = dot_nn(kern, cx_s[head])
    for j in range(nz - 1):

        @pl.when(j < at.s)
        def _(j=j):
            remote(ss, sr.at[j], st_send.at[0], st_recv.at[j], core).wait_recv()

    prior = at.prior_seg(at.s)
    applies = at.applies()
    lane = lax.broadcasted_iota(jnp.int32, (rows, LANES), 1)
    sin_o[...] = jnp.zeros_like(sin_o)
    for head in range(heads):
        state = jnp.zeros((PSI_SENT, LANES), F32)
        for j in range(nz - 1):
            counts = (j < at.s) & (at.last_seg(j) == prior)
            state = state + jnp.where(counts, sr[j, head].astype(F32), 0.0)
        sin_o[head, 0:PSI_SENT] = state.astype(BF16)
        one, two = lift_parts(a_low, tables, 1, head)
        psi = (one * two).astype(BF16)
        yx = yx_s[head] + jnp.where(applies, dot_nn(psi, sin_o[head]), 0.0)
        yx_s[head] = yx
        gate = o_s[:, head * HD : head * HD + LANES]
        y = yx / yx[:, HD : HD + 1]
        g_s[:, head * HD : head * HD + LANES] = y * (gate * jax.nn.sigmoid(gate))
    gb_s[...] = g_s[:, :width].astype(BF16)
    outs2 = [pltpu.make_async_copy(a, b, io_sem.at[5 + i]) for i, (a, b) in enumerate(((yx_s, yx_o), (gb_s, g_o)))]
    for copy in outs2:
        copy.start()

    weights.wait(4)

    def mix_chunk(at_col, size):
        p1[:, pl.ds(at_col, size)] = dot_nn(gb_s[...], slots[4][:, pl.ds(at_col, size)]).astype(BF16)

    chunks(d, 256, mix_chunk)
    s1 = scatter_start(at, p1, r1, head_send.at[0], head_recv.at[0])
    if layer == 0:
        for i in range(5, 8):
            load(i)
    hidden = x_s[at.mine].astype(F32) + scatter_sum(at, p1, r1, s1)
    h_s[...] = hidden
    n2_s[at.mine] = norm_rows(hidden, gain_ffn).astype(BF16)
    s2 = gather_start(at, n2_s, head_send.at[1], head_recv.at[1])
    wait_recv(s2)
    outs3 = [pltpu.make_async_copy(a, b, io_sem.at[7 + i]) for i, (a, b) in enumerate(((n2_s, n2_o), (h_s, h_o)))]
    for copy in outs3:
        copy.start()

    weights.wait(5)
    weights.wait(6)

    def up_chunk(at_col, size):
        cols = pl.ds(at_col, size)
        f = dot_nn(n2_s[...], slots[5][:, cols])
        v = dot_nn(n2_s[...], slots[6][:, cols])
        f_s[:, cols] = f
        v_s[:, cols] = v
        t_s[:, cols] = (f * jax.nn.sigmoid(f) * v).astype(BF16)

    chunks(t_s.shape[1], 256, up_chunk)
    outs4 = [pltpu.make_async_copy(a, b, io_sem.at[9 + i]) for i, (a, b) in enumerate(((f_s, f_o), (v_s, v_o)))]
    for copy in outs4:
        copy.start()
    weights.wait(7)

    def down_chunk(at_col, size):
        p2[:, pl.ds(at_col, size)] = dot_nn(t_s[...], slots[7][:, pl.ds(at_col, size)]).astype(BF16)

    chunks(d, 256, down_chunk)
    s3 = scatter_start(at, p2, r2, head_send.at[2], head_recv.at[2])
    feed = scatter_sum(at, p2, r2, s3)
    my_pos = at.first + at.h * at.part + lax.broadcasted_iota(jnp.int32, (at.part, 1), 0)
    valid = my_pos < at.tot
    xo_s[at.mine] = jnp.where(valid, h_s[...] + feed, 0.0).astype(BF16)
    s4 = gather_start(at, xo_s, head_send.at[3], head_recv.at[3])
    wait_recv(s4)
    last = pltpu.make_async_copy(xo_s, xo_o, io_sem.at[11])
    last.start()
    wait_send(s1 + s2 + s3 + s4)

    @pl.when(at.s + 1 < nz)
    def _():
        edge.wait_send()

    for k in range(1, nz):

        @pl.when(at.s + k < nz)
        def _(k=k):
            remote(ss, sr.at[at.s], st_send.at[k - 1], st_recv.at[at.s], core).wait_send()

    if layer == 0:
        small_swap.wait_send()
        for i in range(8):
            swaps[i].wait_send()

            @pl.when(at.sec == 0)
            def _(i=i):
                swaps[i].wait_recv()

    for copy in outs + outs2 + outs3 + outs4 + [last]:
        copy.wait()


def bwd_kernel(layer, dims, *refs):
    nz, nh, rows, heads = dims
    refs = list(refs)

    def take(n):
        out = refs[:n]
        del refs[:n]
        return out

    lens, x_in, g_in, small_own, small_other, tables = take(6)
    own = take(8)
    other = take(8)
    n1_i, q_i, k_i, u_i, o_i, yx_i, sin_i, gb_i, h_i, f_i, v_i = take(11)
    ig_o, gains_o, conv_o, acat_o, aout_o = take(5)
    slots = take(8)
    (x_s, grad_s, n1_s, u_s, o_s, yx_s, gb_s, h_s, f_s, v_s) = take(10)
    (df_s, dv_s, p1, r1, p2, r2, dm_s, dh_s, dg_s, do_s, c_s, cx_s, dyx_s, ss, sr, st_s, da_s, db_s, dc_s, dcat_s, ig_s, acat_s, aout_s) = take(23)
    w_sem, io_sem, e_send, e_recv, st_send, st_recv, head_send, head_recv = take(8)
    at = Place(lens, nz, nh, rows)
    d = x_s.shape[1]
    width = heads * HD
    qk = heads * FEAT
    core = (1 - at.sec, at.s, at.h)

    loads = [
        pltpu.make_async_copy(a, b, io_sem.at[i])
        for i, (a, b) in enumerate(
            (
                (g_in.at[at.sec] if layer == 1 else g_in, grad_s),
                (f_i, f_s),
                (v_i, v_s),
                (h_i, h_s),
                (u_i, u_s),
                (o_i, o_s),
                (yx_i, yx_s),
                (gb_i, gb_s),
                (n1_i, n1_s),
                (x_in.at[at.sec] if layer == 0 else x_in, x_s),
            )
        )
    ]
    weights = Weights(at, layer, own, other, slots, w_sem)
    loads[0].start()
    weights.start(7)
    loads[1].start()
    loads[2].start()
    for i in (5, 6, 4):
        weights.start(i)
    for copy in loads[3:]:
        copy.start()
    for i in (0, 1, 2, 3):
        weights.start(i)
    at.barrier(False, True, True)
    small = jnp.where(at.sec == layer, small_own[...], small_other[...])
    gain_attn, gain_ffn, taps = small[0:1], small[1:2], small[2 : 2 + KW]
    valid = at.pos() < at.tot
    loads[0].wait()
    grad_s[...] = jnp.where(valid, grad_s[...].astype(F32), 0.0).astype(BF16)

    weights.wait(7)
    loads[1].wait()
    loads[2].wait()

    def down_chunk(at_row, size):
        cols = pl.ds(at_row, size)
        dt = dot_nt(grad_s[...], slots[7][cols, :])
        f = f_s[:, cols]
        sig = jax.nn.sigmoid(f)
        df_s[:, cols] = (dt * v_s[:, cols] * sig * (1.0 + f * (1.0 - sig))).astype(BF16)
        dv_s[:, cols] = (dt * f * sig).astype(BF16)

    chunks(df_s.shape[1], 256, down_chunk)
    weights.wait(5)
    weights.wait(6)

    def up_chunk(at_row, size):
        cols = pl.ds(at_row, size)
        part = dot_nt(df_s[...], slots[5][cols, :]) + dot_nt(dv_s[...], slots[6][cols, :])
        p1[:, cols] = part.astype(BF16)

    chunks(d, 256, up_chunk)
    s1 = scatter_start(at, p1, r1, head_send.at[0], head_recv.at[0])
    loads[3].wait()
    dn2 = scatter_sum(at, p1, r1, s1)
    back, gain_grad = norm_rows_back(h_s[...], gain_ffn, dn2)
    gains_o[1:2, :] = gain_grad
    dh = grad_s[at.mine].astype(F32) + back
    dh_s[...] = dh
    dm_s[at.mine] = dh.astype(BF16)
    s2 = gather_start(at, dm_s, head_send.at[1], head_recv.at[1])
    for copy in loads[4:]:
        copy.wait()
    for i in (4, 0, 1, 2, 3):
        weights.wait(i)
    convolve(at, u_s, taps, c_s, cx_s, heads)
    wait_recv(s2)

    def out_chunk(at_row, size):
        cols = pl.ds(at_row, size)
        dg_s[:, cols] = dot_nt(dm_s[...], slots[4][cols, :])

    chunks(width, 256, out_chunk)
    lane = lax.broadcasted_iota(jnp.int32, (rows, LANES), 1)
    applies = at.applies()
    tail = at.tail()
    a_low, b_low = q_i[...], k_i[...]
    for head in range(heads):
        cols = slice(head * HD, head * HD + LANES)
        gate, dg, yx = o_s[:, cols], dg_s[:, cols], yx_s[head]
        sig = jax.nn.sigmoid(gate)
        inverse = 1.0 / yx[:, HD : HD + 1]
        y = yx * inverse
        do_s[:, cols] = dg * y * sig * (1.0 + gate * (1.0 - sig))
        dy = jnp.where(lane < HD, dg * gate * sig, 0.0)
        dden = -jnp.sum(dy * y, axis=1, keepdims=True) * inverse
        dyx_s[head] = jnp.where(lane == HD, dden, dy * inverse).astype(BF16)
        one, two = lift_parts(a_low, tables, 1, head)
        psi = jnp.where(applies, one * two, 0.0).astype(BF16)
        ss[head] = dot_tn(psi, dyx_s[head])[:PSI_SENT].astype(BF16)
    for k in range(1, nz):

        @pl.when(at.s - k >= 0)
        def _(k=k):
            remote(ss, sr.at[at.s], st_send.at[k - 1], st_recv.at[at.s], (at.sec, (at.s + nz - k) % nz, at.h)).start()

    allowed = at.allowed()
    da_s[...] = jnp.zeros_like(da_s)
    db_s[...] = jnp.zeros_like(db_s)
    for head in range(heads):
        a_own, b_own = head_only(a_low, head), head_only(b_low, head)
        e = dot_nt(a_low, b_own)
        kern = jnp.where(allowed, 1.0 + e + 0.5 * e * e, 0.0).astype(BF16)
        dkern = dot_nt(dyx_s[head], cx_s[head])
        de = jnp.where(allowed, dkern * (1.0 + e), 0.0).astype(BF16)
        one, two = lift_parts(a_low, tables, 1, head)
        dpsi = jnp.where(applies, dot_nt(dyx_s[head], sin_i[head]), 0.0)
        pcols = slice(head * PSI, (head + 1) * PSI)
        da_s[...] += (
            dot_nn(de, b_own)
            + dot_nt((dpsi * two).astype(BF16), tables[0, :, pcols])
            + dot_nt((dpsi * one).astype(BF16), tables[1, :, pcols])
        )
        db_s[...] += dot_tn(de, a_own)
        yx_s[head] = dot_tn(kern, dyx_s[head])
    for j in range(1, nz):

        @pl.when(j > at.s)
        def _(j=j):
            remote(ss, sr.at[j], st_send.at[0], st_recv.at[j], core).wait_recv()

    mine_last = at.last_seg(at.s)
    st_s[...] = jnp.zeros_like(st_s)
    for head in range(heads):
        state = jnp.zeros((PSI_SENT, LANES), F32)
        for j in range(1, nz):
            counts = (j > at.s) & (at.prior_seg(j) == mine_last)
            state = state + jnp.where(counts, sr[j, head].astype(F32), 0.0)
        st_s[head, 0:PSI_SENT] = state.astype(BF16)
        one, two = lift_parts(b_low, tables, 2, head)
        psi = (one * two).astype(BF16)
        dpsi = jnp.where(tail, dot_nt(cx_s[head], st_s[head]), 0.0)
        pcols = slice(head * PSI, (head + 1) * PSI)
        db_s[...] += dot_nt((dpsi * two).astype(BF16), tables[0, :, pcols]) + dot_nt(
            (dpsi * one).astype(BF16), tables[2, :, pcols]
        )
        dc = yx_s[head] + jnp.where(tail, dot_nn(psi, st_s[head]), 0.0)
        dc_s[0:rows, head * HD : head * HD + LANES] = dc
    edge = remote(
        dc_s.at[pl.ds(0, 8)], dc_s.at[pl.ds(rows, 8)], e_send, e_recv, (at.sec, (at.s + nz - 1) % nz, at.h)
    )

    @pl.when(at.s > 0)
    def _():
        edge.start()

    dcat_s[:, 0:qk] = (da_s[...] * 0.5).astype(BF16)
    dcat_s[:, qk : 2 * qk] = (db_s[...] * 0.5).astype(BF16)
    dcat_s[:, 2 * qk + width :] = do_s[:, :width].astype(BF16)
    conv_o[...] = jnp.zeros_like(conv_o)
    for j in range(KW):
        product = dc_s[0:rows, :width] * u_s[8 - j : 8 - j + rows, :width]
        conv_o[j : j + 1, :width] = jnp.sum(jnp.where(at.same(-j), product, 0.0), axis=0, keepdims=True)

    @pl.when(at.s + 1 < nz)
    def _():
        edge.wait_recv()

    du = taps[0:1, :width] * dc_s[0:rows, :width]
    for j in range(1, KW):
        du = du + jnp.where(at.same(j), dc_s[j : j + rows, :width] * taps[j : j + 1, :width], 0.0)
    dcat_s[:, 2 * qk : 2 * qk + width] = du.astype(BF16)

    def proj_chunk(at_row, size):
        cols = pl.ds(at_row, size)
        part = (
            dot_nt(dcat_s[:, 0:qk], slots[0][cols, :])
            + dot_nt(dcat_s[:, qk : 2 * qk], slots[1][cols, :])
            + dot_nt(dcat_s[:, 2 * qk : 2 * qk + width], slots[2][cols, :])
            + dot_nt(dcat_s[:, 2 * qk + width :], slots[3][cols, :])
        )
        p2[:, cols] = part.astype(BF16)

    chunks(d, 256, proj_chunk)
    s3 = scatter_start(at, p2, r2, head_send.at[2], head_recv.at[2])

    def in_chunk(at_row, size):
        cols = pl.ds(at_row, size)
        acat_s[cols, :] = dot_tn(n1_s[:, cols], dcat_s[...]).astype(BF16)
        aout_s[:, cols] = dot_tn(gb_s[...], dm_s[:, cols]).astype(BF16)

    chunks(d, 256, in_chunk)
    outs = [pltpu.make_async_copy(a, b, io_sem.at[10 + i]) for i, (a, b) in enumerate(((acat_s, acat_o), (aout_s, aout_o)))]
    for copy in outs:
        copy.start()
    dn1 = scatter_sum(at, p2, r2, s3)
    back, gain_grad = norm_rows_back(x_s[at.mine].astype(F32), gain_attn, dn1)
    gains_o[0:1, :] = gain_grad
    gains_o[2:8, :] = jnp.zeros((6, d), F32)
    ig_s[at.mine] = (dh_s[...] + back).astype(BF16)
    s4 = gather_start(at, ig_s, head_send.at[3], head_recv.at[3])
    wait_recv(s4)
    last = pltpu.make_async_copy(ig_s, ig_o, io_sem.at[12])
    last.start()
    wait_send(s1 + s2 + s3 + s4)

    @pl.when(at.s > 0)
    def _():
        edge.wait_send()

    for k in range(1, nz):

        @pl.when(at.s - k >= 0)
        def _(k=k):
            remote(ss, sr.at[at.s], st_send.at[k - 1], st_recv.at[at.s], core).wait_send()

    for copy in outs + [last]:
        copy.wait()


def ffn_grad_kernel(dims, lens, n2_0, n2_1, g_0, g_1, *refs):
    nz, nh, rows, heads = dims
    refs = list(refs)

    def take(n):
        out = refs[:n]
        del refs[:n]
        return out

    own = take(3)
    other = take(3)
    outs = take(3)
    slots = [take(3), take(3)]
    n2_s, g_s, n2c, gc, t_s, df_s, dv_s = take(7)
    acc = take(3)
    send = take(3)
    got = take(3)
    w_sem, io_sem, x_send, x_recv = take(4)
    at = Place(lens, nz, nh, rows)
    d = n2_s.shape[2]
    block = d // nz
    core = (1 - at.sec, at.s, at.h)
    at.barrier(True, False, False)
    for role, source in ((0, other), (1, own)):
        for i in range(3):
            pltpu.make_async_copy(source[i].at[0], slots[role][i], w_sem.at[role, i]).start()

    def fetch(role, j, slot, go):
        where = pl.ds(pl.multiple_of(j * rows, rows), rows)
        for layer, n2_ref, g_ref in ((0, n2_0, g_0), (1, n2_1, g_1)):
            @pl.when((at.sec == layer) if role == 1 else (at.sec != layer))
            def _(n2_ref=n2_ref, g_ref=g_ref):
                for i, (src, dst) in enumerate(((n2_ref, n2_s), (g_ref, g_s))):
                    copy = pltpu.make_async_copy(src.at[where], dst.at[slot], io_sem.at[slot, i])
                    if go:
                        copy.start()
                    else:
                        copy.wait()

    fetch(0, 0, 0, True)
    swaps = []
    for role in range(2):
        gate, up, down = slots[role]
        for i in range(3):
            acc[i][...] = jnp.zeros_like(acc[i])

        def one(j, carry, role=role, gate=gate, up=up, down=down):
            slot = lax.rem(j, 2)
            fetch(role, j, slot, False)

            @pl.when(j + 1 < nz)
            def _():
                fetch(role, j + 1, lax.rem(j + 1, 2), True)

            if role == 0:

                @pl.when(j + 1 == nz)
                def _():
                    fetch(1, 0, 0 if nz % 2 == 0 else 1, True)

            pos = j * rows + lax.broadcasted_iota(jnp.int32, (rows, 1), 0)
            g_s[slot] = jnp.where(pos < at.tot, g_s[slot].astype(F32), 0.0).astype(BF16)
            for piece in range(nz):

                @pl.when(at.s == piece)
                def _(piece=piece):
                    n2c[...] = n2_s[slot, :, piece * block : (piece + 1) * block]
                    gc[...] = g_s[slot, :, piece * block : (piece + 1) * block]

            def hidden(at_col, size):
                cols = pl.ds(at_col, size)
                n2 = n2_s[slot]
                f = dot_nn(n2, gate[:, cols])
                v = dot_nn(n2, up[:, cols])
                dt = dot_nt(g_s[slot], down[cols, :])
                sig = jax.nn.sigmoid(f)
                t = (f * sig * v).astype(BF16)
                df = (dt * v * sig * (1.0 + f * (1.0 - sig))).astype(BF16)
                dv = (dt * f * sig).astype(BF16)
                acc[0][:, cols] += dot_tn(n2c[...], df)
                acc[1][:, cols] += dot_tn(n2c[...], dv)
                acc[2][:, cols] += dot_tn(gc[...], t)

            chunks(gate.shape[1], 256, hidden)
            return carry

        for i in range(3):
            pltpu.make_async_copy(own[i].at[0], slots[role][i], w_sem.at[role, i]).wait()
        lax.fori_loop(0, nz, one, 0)
        if role == 0:
            for i in range(3):
                send[i][...] = acc[i][...].astype(BF16)
                swap = remote(send[i], got[i], x_send.at[i], x_recv.at[i], core)
                swap.start()
                swaps.append(swap)
    for i in range(3):
        swaps[i].wait_recv()
        outs[i][...] = acc[i][...] + got[i][...].astype(F32)
    wait_send(swaps)


def swap_kernel(dims, a0, a1, b0, b1, x0, x1, g0, g1, a_o, b_o, x_o, g_o, a_s, b_s, a_r, b_r, io_sem, x_send, x_recv):
    sec, s, h = (lax.axis_index(a) for a in ("section", "seq", "head"))
    core = (1 - sec, s, h)
    sem = pltpu.get_barrier_semaphore()
    pl.semaphore_signal(sem, 1, device_id=core, device_id_type=MESH)
    pl.semaphore_wait(sem, 1)

    def moves(mine, his):
        out = [
            remote(his[0], a_r, x_send.at[0], x_recv.at[0], core),
            remote(his[1], b_r, x_send.at[1], x_recv.at[1], core),
            remote(his[2], x_o.at[sec], x_send.at[2], x_recv.at[2], core),
            remote(his[3], g_o.at[sec], x_send.at[3], x_recv.at[3], core),
        ]
        local = [
            pltpu.make_async_copy(mine[0], a_s, io_sem.at[0]),
            pltpu.make_async_copy(mine[1], b_s, io_sem.at[1]),
            pltpu.make_async_copy(mine[2], x_o.at[sec], io_sem.at[2]),
            pltpu.make_async_copy(mine[3], g_o.at[sec], io_sem.at[3]),
        ]
        return out, local

    sides = (((a0, b0, x0, g0), (a1, b1, x1, g1)), ((a1, b1, x1, g1), (a0, b0, x0, g0)))
    for here in range(2):

        @pl.when(sec == here)
        def _(here=here):
            out, local = moves(*sides[here])
            for copy in out + local:
                copy.start()

    out, local = moves(*sides[0])
    local[0].wait()
    out[0].wait_recv()
    a_s[...] = (a_s[...].astype(F32) + a_r[...].astype(F32)).astype(BF16)
    done_a = pltpu.make_async_copy(a_s, a_o, io_sem.at[4])
    done_a.start()
    local[1].wait()
    out[1].wait_recv()
    b_s[...] = (b_s[...].astype(F32) + b_r[...].astype(F32)).astype(BF16)
    done_b = pltpu.make_async_copy(b_s, b_o, io_sem.at[5])
    done_b.start()
    for copy in local[2:]:
        copy.wait()
    for copy in out[2:]:
        copy.wait_recv()
    for copy in out:
        copy.wait_send()
    done_a.wait()
    done_b.wait()


def shape(dims, kind=BF16):
    return jax.ShapeDtypeStruct(tuple(dims), kind)


ANY = pl.BlockSpec(memory_space=pl.ANY)
VM = pl.BlockSpec(memory_space=pltpu.VMEM)
SM = pl.BlockSpec(memory_space=pltpu.SMEM)
DMA = pltpu.SemaphoreType.DMA


def params(number):
    return pltpu.CompilerParams(collective_id=number, has_side_effects=True, vmem_limit_bytes=VMEM_LIMIT)


def shards(nz, nh, inputs, out_grad, lengths, norm_attn, norm_ffn, w_query, w_key, w_value, w_output_gate, conv_kernel, w_out, w_gate, w_up, w_down):
    micro, rows, d = inputs.shape
    heads = w_query.shape[2] // FEAT
    width, qk, ff = w_value.shape[2], w_query.shape[2], w_gate.shape[2]
    part = rows // nh
    dims = (nz, nh, rows, heads)
    wide = -(-width // LANES) * LANES + (LANES if (heads - 1) * HD + LANES > -(-width // LANES) * LANES else 0)
    tables = jnp.asarray(lift_tables(heads), BF16)
    own = (w_query, w_key, w_value, w_output_gate, w_out, w_gate, w_up, w_down)
    small_own = jnp.concatenate(
        [norm_attn, norm_ffn, jnp.pad(conv_kernel[0], ((0, 0), (0, d - width))), jnp.zeros((3, d), F32)]
    )
    w_slots = [pltpu.VMEM(w.shape[1:], BF16) for w in own]
    act = pltpu.VMEM((rows, d), BF16)
    headsum = pltpu.VMEM((nh - 1, part, d), BF16)

    def forward(layer, x, other_small, other):
        outs = [
            shape((rows, d)),
            shape((rows, d)),
            shape((rows, d)),
            shape((rows, qk)),
            shape((rows, qk)),
            shape((rows + 8, wide), F32),
            shape((rows, wide), F32),
            shape((heads, rows, LANES), F32),
            shape((heads, PSI, LANES)),
            shape((rows, width)),
            shape((part, d), F32),
            shape((rows, ff), F32),
            shape((rows, ff), F32),
        ]
        specs = [ANY, ANY, ANY, VM, VM, ANY, ANY, ANY, VM, ANY, ANY, ANY, ANY]
        ins = [lengths, x, small_own]
        in_specs = [SM, ANY, VM]
        if layer == 0:
            outs = [shape((8, d), F32)] + [shape(w.shape) for w in own] + outs
            specs = [ANY] * 9 + specs
        else:
            ins += [other_small]
            in_specs += [ANY]
        ins += [tables, *own]
        in_specs += [VM] + [ANY] * 8
        if layer == 1:
            ins += list(other)
            in_specs += [ANY] * 8
        scratch = w_slots + [
            act,
            act,
            act,
            pltpu.VMEM((rows + 8, wide), F32),
            pltpu.VMEM((rows, wide), F32),
            pltpu.VMEM((rows, wide), F32),
            pltpu.VMEM((heads, rows, LANES), BF16),
            pltpu.VMEM((heads, rows, LANES), F32),
            pltpu.VMEM((heads, PSI_SENT, LANES), BF16),
            pltpu.VMEM((nz, heads, PSI_SENT, LANES), BF16),
            pltpu.VMEM((rows, wide), F32),
            pltpu.VMEM((rows, width), BF16),
            act,
            headsum,
            act,
            headsum,
            pltpu.VMEM((rows, ff), F32),
            pltpu.VMEM((rows, ff), F32),
            pltpu.VMEM((rows, ff), BF16),
            act,
            pltpu.VMEM((part, d), F32),
            pltpu.VMEM((8, d), F32),
            DMA((8,)),
            DMA((12,)),
            DMA((9,)),
            DMA((9,)),
            DMA,
            DMA,
            DMA((nz,)),
            DMA((nz,)),
            DMA((4, nh - 1)),
            DMA((4, nh - 1)),
        ]
        return pl.pallas_call(
            functools.partial(fwd_kernel, layer, dims),
            out_shape=outs,
            in_specs=in_specs,
            out_specs=specs,
            scratch_shapes=scratch,
            compiler_params=params(layer),
        )(*ins)

    def backward(layer, x, grad, other_small, other, kept):
        outs = [shape((rows, d)), shape((8, d), F32), shape((8, wide), F32), shape((d, 2 * qk + 2 * width)), shape((width, d))]
        specs = [ANY, VM, VM, ANY, ANY]
        ins = [lengths, x, grad, small_own, other_small, tables, *own, *other, *kept]
        in_specs = [SM, ANY, ANY, VM, VM, VM] + [ANY] * 16 + [ANY, VM, VM, ANY, ANY, ANY, VM, ANY, ANY, ANY, ANY]
        scratch = w_slots + [
            act,
            act,
            act,
            pltpu.VMEM((rows + 8, wide), F32),
            pltpu.VMEM((rows, wide), F32),
            pltpu.VMEM((heads, rows, LANES), F32),
            pltpu.VMEM((rows, width), BF16),
            pltpu.VMEM((part, d), F32),
            pltpu.VMEM((rows, ff), F32),
            pltpu.VMEM((rows, ff), F32),
            pltpu.VMEM((rows, ff), BF16),
            pltpu.VMEM((rows, ff), BF16),
            act,
            headsum,
            act,
            headsum,
            act,
            pltpu.VMEM((part, d), F32),
            pltpu.VMEM((rows, wide), F32),
            pltpu.VMEM((rows, wide), F32),
            pltpu.VMEM((rows, wide), F32),
            pltpu.VMEM((heads, rows, LANES), BF16),
            pltpu.VMEM((heads, rows, LANES), BF16),
            pltpu.VMEM((heads, PSI_SENT, LANES), BF16),
            pltpu.VMEM((nz, heads, PSI_SENT, LANES), BF16),
            pltpu.VMEM((heads, PSI, LANES), BF16),
            pltpu.VMEM((rows, qk), F32),
            pltpu.VMEM((rows, qk), F32),
            pltpu.VMEM((rows + 8, wide), F32),
            pltpu.VMEM((rows, 2 * qk + 2 * width), BF16),
            act,
            pltpu.VMEM((d, 2 * qk + 2 * width), BF16),
            pltpu.VMEM((width, d), BF16),
            DMA((8,)),
            DMA((13,)),
            DMA,
            DMA,
            DMA((nz,)),
            DMA((nz,)),
            DMA((4, nh - 1)),
            DMA((4, nh - 1)),
        ]
        return pl.pallas_call(
            functools.partial(bwd_kernel, layer, dims),
            out_shape=outs,
            in_specs=in_specs,
            out_specs=specs,
            scratch_shapes=scratch,
            compiler_params=params(2 + layer),
        )(*ins)

    first = forward(0, inputs, None, None)
    other_small, other, kept_0 = first[0], first[1:9], first[9:]
    x_1, n2_0 = kept_0[0], kept_0[2]
    kept_1 = forward(1, x_1, other_small, other)
    x_2, n2_1 = kept_1[0], kept_1[2]

    def keep(kept):
        return (kept[1],) + tuple(kept[3:])

    ig_1, gains_1, conv_1, a_1, b_1 = backward(1, x_1, out_grad, other_small, other, keep(kept_1))
    ig_0, gains_0, conv_0, a_0, b_0 = backward(0, inputs, ig_1, other_small, other, keep(kept_0))

    def all_slots(block):
        return lax.all_gather(block, "seq", axis=0, tiled=True)

    sec = lax.axis_index("section")
    out_grad_mine = lax.dynamic_index_in_dim(out_grad, sec, 0, keepdims=False)
    block = d // nz
    ffn = [pltpu.VMEM(w.shape[1:], BF16) for w in own[5:]]
    grid_shapes = [(block, ff)] * 3
    g_gate, g_up, g_down = pl.pallas_call(
        functools.partial(ffn_grad_kernel, dims),
        out_shape=[shape(s, F32) for s in grid_shapes],
        in_specs=[SM] + [ANY] * 10,
        out_specs=[VM] * 3,
        scratch_shapes=ffn
        + ffn
        + [
            pltpu.VMEM((2, rows, d), BF16),
            pltpu.VMEM((2, rows, d), BF16),
            pltpu.VMEM((rows, block), BF16),
            pltpu.VMEM((rows, block), BF16),
            pltpu.VMEM((rows, ff), BF16),
            pltpu.VMEM((rows, ff), BF16),
            pltpu.VMEM((rows, ff), BF16),
        ]
        + [pltpu.VMEM(s, F32) for s in grid_shapes]
        + [pltpu.VMEM(s, BF16) for s in grid_shapes] * 2
        + [DMA((2, 3)), DMA((2, 2)), DMA((3,)), DMA((3,))],
        compiler_params=params(4),
    )(lengths, all_slots(n2_0), all_slots(n2_1), all_slots(ig_1), all_slots(out_grad_mine), *own[5:], *other[5:])

    a_sum, b_sum, section_out, input_grad = pl.pallas_call(
        functools.partial(swap_kernel, dims),
        out_shape=[shape(a_0.shape), shape(b_0.shape), shape((micro, rows, d)), shape((micro, rows, d))],
        in_specs=[ANY] * 8,
        out_specs=[ANY] * 4,
        scratch_shapes=[pltpu.VMEM(a_0.shape, BF16), pltpu.VMEM(b_0.shape, BF16)] * 2
        + [DMA((6,)), DMA((4,)), DMA((4,))],
        compiler_params=params(5),
    )(a_0, a_1, b_0, b_1, x_1, x_2, ig_0, ig_1)
    a_sum = lax.psum_scatter(a_sum, "seq", scatter_dimension=0, tiled=True).astype(F32)
    b_sum = lax.psum_scatter(b_sum, "seq", scatter_dimension=1, tiled=True).astype(F32)
    gains = lax.psum(jnp.stack([gains_0[:2], gains_1[:2]]), ("section", "seq", "head"))
    convs = lax.psum(jnp.stack([conv_0[:KW, :width], conv_1[:KW, :width]]), ("section", "seq"))
    gains = lax.dynamic_index_in_dim(gains, sec, 0, keepdims=False)
    convs = lax.dynamic_index_in_dim(convs, sec, 0, keepdims=True)
    return (
        section_out[None],
        input_grad[None],
        gains[0:1],
        gains[1:2],
        a_sum[None, :, 0:qk],
        a_sum[None, :, qk : 2 * qk],
        a_sum[None, :, 2 * qk : 2 * qk + width],
        a_sum[None, :, 2 * qk + width :],
        convs,
        b_sum[None],
        g_gate[None],
        g_up[None],
        g_down.T[None],
    )


def solution(mesh):
    return jax.shard_map(
        functools.partial(shards, mesh.shape["seq"], mesh.shape["head"]),
        mesh=mesh,
        in_specs=(
            P(None, "seq", None),
            P(None, "seq", None),
            P(),
            P("section", None),
            P("section", None),
            P("section", None, "head"),
            P("section", None, "head"),
            P("section", None, "head"),
            P("section", None, "head"),
            P("section", None, "head"),
            P("section", "head", None),
            P("section", None, "head"),
            P("section", None, "head"),
            P("section", "head", None),
        ),
        out_specs=(
            P("section", None, "seq", None),
            P("section", None, "seq", None),
            P("section", None),
            P("section", None),
            P("section", "seq", "head"),
            P("section", "seq", "head"),
            P("section", "seq", "head"),
            P("section", "seq", "head"),
            P("section", None, "head"),
            P("section", "head", "seq"),
            P("section", "seq", "head"),
            P("section", "seq", "head"),
            P("section", "head", "seq"),
        ),
        check_vma=False,
    )
```

```python
import functools

import jax
import jax.numpy as jnp
import numpy as np
from jax import lax
from jax.experimental import pallas as pl
from jax.experimental.pallas import tpu as pltpu
from jax.sharding import PartitionSpec as P

HD = 112
FEAT = 16
KW = 3
EPS = 1e-05
LANES = 128
PSI = 256
PSI_SENT = 160
MESH = pl.DeviceIdType.MESH
F32 = jnp.float32
BF16 = jnp.bfloat16
VMEM_LIMIT = 62 << 20


def dot_nn(a, b):
    return lax.dot_general(a, b, (((1,), (0,)), ((), ())), preferred_element_type=F32)


def dot_nt(a, b):
    return lax.dot_general(a, b, (((1,), (1,)), ((), ())), preferred_element_type=F32)


def dot_tn(a, b):
    return lax.dot_general(a, b, (((0,), (0,)), ((), ())), preferred_element_type=F32)


def chunks(total, step, body):
    whole = total // step
    if whole > 1:

        def one(i, carry):
            body(pl.multiple_of(i * step, step), step)
            return carry

        lax.fori_loop(0, whole, one, 0)
    elif whole == 1:
        body(0, step)
    if total % step:
        body(whole * step, total % step)


def lift_tables(heads):
    first = np.zeros((heads * FEAT, heads * PSI), np.float32)
    second = np.zeros_like(first)
    second_key = np.zeros_like(first)
    for head in range(heads):
        row, col = head * FEAT, head * PSI
        for i in range(FEAT):
            first[row + i, col + 1 + i] = 1.0
        at = 1 + FEAT
        for i in range(FEAT):
            for j in range(i, FEAT):
                first[row + i, col + at] = 1.0
                second[row + j, col + at] = 1.0
                second_key[row + j, col + at] = 0.5 if i == j else 1.0
                at += 1
    return np.stack([first, second, second_key])


class Place:
    def __init__(self, lens, nz, nh, rows):
        self.sec, self.s, self.h = (lax.axis_index(a) for a in ("section", "seq", "head"))
        self.nz, self.nh, self.rows = nz, nh, rows
        self.l0 = lens[self.sec, 0]
        self.tot = self.l0 + lens[self.sec, 1]
        self.first = self.s * rows
        self.part = rows // nh
        self.mine = pl.ds(pl.multiple_of(self.h * self.part, self.part), self.part)

    def seg(self, pos):
        inside = (pos >= self.l0).astype(jnp.int32) + (pos >= self.tot).astype(jnp.int32)
        return jnp.where(pos >= 0, inside, -1)

    def pos(self, shift=0):
        return self.first + shift + lax.broadcasted_iota(jnp.int32, (self.rows, 1), 0)

    def same(self, shift):
        other = self.pos(shift)
        inside = other < self.nz * self.rows
        return (self.seg(other) == self.seg(self.pos())) & inside

    def allowed(self):
        shape = (self.rows, self.rows)
        row = lax.broadcasted_iota(jnp.int32, shape, 0)
        col = lax.broadcasted_iota(jnp.int32, shape, 1)
        return (col <= row) & (self.seg(self.first + col) == self.seg(self.first + row))

    def last_seg(self, block):
        return self.seg(block * self.rows + self.rows - 1)

    def prior_seg(self, block):
        return self.seg(block * self.rows - 1)

    def applies(self):
        return self.seg(self.pos()) == self.prior_seg(self.s)

    def tail(self):
        return self.seg(self.pos()) == self.last_seg(self.s)

    def peers(self):
        core = [(1 - self.sec, self.s, self.h)]
        seq = [(self.sec, (self.s + k) % self.nz, self.h) for k in range(1, self.nz)]
        head = [(self.sec, self.s, self.h ^ m) for m in range(1, self.nh)]
        return core, seq, head

    def barrier(self, core, seq, head):
        groups = self.peers()
        told = [d for use, g in zip((core, seq, head), groups) if use for d in g]
        sem = pltpu.get_barrier_semaphore()
        for device in told:
            pl.semaphore_signal(sem, 1, device_id=device, device_id_type=MESH)
        pl.semaphore_wait(sem, len(told))


def remote(src, dst, send, recv, device):
    return pltpu.make_async_remote_copy(
        src_ref=src, dst_ref=dst, send_sem=send, recv_sem=recv, device_id=device, device_id_type=MESH
    )


def scatter_start(at, buf, got, send, recv):
    sent = []
    for m in sorted(range(1, at.nh), reverse=True):
        peer = at.h ^ m
        rows = pl.ds(pl.multiple_of(peer * at.part, at.part), at.part)
        copy = remote(buf.at[rows], got.at[m - 1], send.at[m - 1], recv.at[m - 1], (at.sec, at.s, peer))
        copy.start()
        sent.append(copy)
    return sent


def scatter_sum(at, buf, got, sent):
    total = buf[at.mine].astype(F32)
    for copy in sent:
        copy.wait_recv()
    for m in range(1, at.nh):
        total = total + got[m - 1].astype(F32)
    return total


def gather_start(at, buf, send, recv):
    sent = []
    for m in sorted(range(1, at.nh), reverse=True):
        copy = remote(
            buf.at[at.mine], buf.at[at.mine], send.at[m - 1], recv.at[m - 1], (at.sec, at.s, at.h ^ m)
        )
        copy.start()
        sent.append(copy)
    return sent


def wait_recv(copies):
    for copy in copies:
        copy.wait_recv()


def wait_send(copies):
    for copy in copies:
        copy.wait_send()


def norm_rows(x, gain):
    return x * lax.rsqrt(jnp.mean(x * x, axis=-1, keepdims=True) + EPS) * gain


def norm_rows_back(x, gain, grad):
    inverse = lax.rsqrt(jnp.mean(x * x, axis=-1, keepdims=True) + EPS)
    unit = x * inverse
    scaled = grad * gain
    back = inverse * (scaled - unit * jnp.mean(scaled * unit, axis=-1, keepdims=True))
    return back, jnp.sum(grad * unit, axis=0, keepdims=True)


def lift_parts(low, tables, second, head):
    cols = slice(head * PSI, (head + 1) * PSI)
    lane = lax.broadcasted_iota(jnp.int32, (1, PSI), 1)
    one = dot_nn(low, tables[0, :, cols]) + (lane == 0).astype(F32)
    two = dot_nn(low, tables[second, :, cols]) + (lane <= FEAT).astype(F32)
    return one, two


def head_only(low, head):
    lane = lax.broadcasted_iota(jnp.int32, low.shape, 1)
    return jnp.where((lane >= head * FEAT) & (lane < (head + 1) * FEAT), low, jnp.zeros_like(low))


def convolve(at, u_s, taps, c_s, cx_s, heads):
    rows, width = at.rows, heads * HD
    out = taps[0:1, :width] * u_s[8 : 8 + rows, :width]
    for j in range(1, KW):
        shifted = u_s[8 - j : 8 - j + rows, :width]
        out = out + jnp.where(at.same(-j), shifted * taps[j : j + 1, :width], 0.0)
    c_s[0:rows, :width] = out
    lane = lax.broadcasted_iota(jnp.int32, (rows, LANES), 1)
    for head in range(heads):
        one = c_s[0:rows, head * HD : head * HD + LANES]
        cx_s[head] = jnp.where(lane < HD, one, jnp.where(lane == HD, 1.0, 0.0)).astype(BF16)


def order(at, i):
    left, right = at.s, at.nz - 1 - at.s
    both = 2 * jnp.minimum(left, right)
    near = i <= both
    dist = jnp.where(near, (i + 1) // 2, i - both // 2)
    leftward = jnp.where(near, i % 2 == 1, left > right)
    return jnp.where(leftward, at.s - dist, at.s + dist)


class Ring:
    def __init__(self, at, src, dst, send, recv):
        self.at, self.src, self.dst, self.send, self.recv = at, src, dst, send, recv

    def _copy(self, way, k, block, first):
        at = self.at
        to = lax.rem(at.s + (1 if way == 0 else at.nz - 1), at.nz)
        src = self.src if first else self.dst.at[block]
        return remote(src, self.dst.at[block], self.send.at[way, k], self.recv.at[way, k], (at.sec, to, at.h))

    def step(self, k):
        at = self.at
        first = isinstance(k, int) and k == 0
        for way in range(2):
            block = at.s - k if way == 0 else at.s + k
            there = block >= 0 if way == 0 else block < at.nz
            onward = at.s + 1 < at.nz if way == 0 else at.s > 0
            if not first:

                @pl.when(there)
                def _(way=way, block=block):
                    self._copy(way, k - 1, block, False).wait_recv()

            if not isinstance(k, int) or k < at.nz - 1:

                @pl.when(there & onward & (k < at.nz - 1))
                def _(way=way, block=block):
                    self._copy(way, k, block, first).start()

    def drain(self):
        at = self.at
        for k in range(at.nz - 1):
            for way in range(2):
                block = at.s - k if way == 0 else at.s + k
                there = block >= 0 if way == 0 else block < at.nz
                onward = at.s + 1 < at.nz if way == 0 else at.s > 0

                @pl.when(there & onward)
                def _(way=way, k=k):
                    self._copy(way, k, at.s, True).wait_send()


class LineSum:
    def __init__(self, at, mine, peer, land, work, io, send, recv, peer_recv):
        self.at, self.mine, self.peer, self.land, self.work = at, mine, peer, land, work
        self.io, self.send, self.recv, self.peer_recv = io, send, recv, peer_recv

    def _hop(self, way, d):
        at = self.at
        to = lax.rem(at.s + (1 if way == 0 else at.nz - 1), at.nz)
        return remote(self.work.at[way], self.land.at[way, d], self.send.at[way, d], self.recv.at[way, d], (at.sec, to, at.h))

    def _load(self, src, slot):
        copy = pltpu.make_async_copy(src, self.work.at[slot], self.io)
        copy.start()
        copy.wait()

    def _add(self, slot, src):
        self._load(src, 2)
        self.work[slot] = (self.work[slot].astype(F32) + self.work[2].astype(F32)).astype(BF16)

    def _own(self, slot, d):
        at = self.at
        self._load(self.mine.at[d], slot)
        remote(self.mine.at[d], self.peer.at[d], self.peer_recv.at[d], self.peer_recv.at[d], (1 - at.sec, at.s, at.h)).wait_recv()
        self._add(slot, self.peer.at[d])

    def slot(self, i):
        at = self.at
        for way in range(2):
            begun = i - at.s if way == 0 else i - (at.nz - 1 - at.s)
            d = at.nz - 1 - begun if way == 0 else begun
            earlier = at.s > 0 if way == 0 else at.s < at.nz - 1

            @pl.when((begun >= 0) & (i < at.nz - 1))
            def _(way=way, d=d, begun=begun, earlier=earlier):
                @pl.when(begun > 0)
                def _():
                    self._hop(way, d + 1 if way == 0 else d - 1).wait_send()

                self._own(way, d)

                @pl.when(earlier)
                def _():
                    self._hop(way, d).wait_recv()
                    self._add(way, self.land.at[way, d])

                self._hop(way, d).start()

    def last(self):
        at = self.at

        @pl.when(at.s < at.nz - 1)
        def _():
            self._hop(0, at.s + 1).wait_send()

        @pl.when(at.s > 0)
        def _():
            self._hop(1, at.s - 1).wait_send()

        self._own(0, at.s)

        @pl.when(at.s > 0)
        def _():
            self._hop(0, at.s).wait_recv()
            self._add(0, self.land.at[0, at.s])

        @pl.when(at.s < at.nz - 1)
        def _():
            self._hop(1, at.s).wait_recv()
            self._add(0, self.land.at[1, at.s])


def taker(refs):
    refs = list(refs)

    def take(n):
        out = refs[:n]
        del refs[:n]
        return out

    return take


def weight_slots(cat, out, gate, up, down, qk, width):
    at_row, views = 0, []
    for size in (qk, qk, width, width):
        views.append(cat.at[pl.ds(at_row, size)])
        at_row += size
    return views + [out, gate, up, down]


SAVED = 11


def fwd_kernel(dims, *refs):
    nz, nh, rows, heads = dims
    take = taker(refs)
    lens, inputs, out_grad, small_own, tables = take(5)
    own = take(8)
    small_other = take(1)[0]
    other = take(8)
    saved = [take(SAVED), take(SAVED)]
    x_out, gath_g1, gath_n2, n2_out = take(4)
    mats = [take(5), take(5)]
    (x_s, n1_s, n2_s, qk_s, u_s, edge_s, o_s, c_s, cx_s, yx_s, ss, sr, sin_s, g_s, gb_s, part_s, got_s, f_s, v_s, t_s, xo_s, h_s, sm_s) = take(23)
    w_sem, io_sem, save_sem, x_send, x_recv, e_send, e_recv, st_send, st_recv, head_send, head_recv, r_send, r_recv = take(13)
    at = Place(lens, nz, nh, rows)
    d = x_s.shape[1]
    width, qk = heads * HD, heads * FEAT
    core = (1 - at.sec, at.s, at.h)
    slots = [weight_slots(*m, qk, width) for m in mats]

    x_copy = pltpu.make_async_copy(inputs.at[at.sec], x_s, io_sem.at[0])
    x_copy.start()

    def local(layer, i):
        return pltpu.make_async_copy(own[i].at[0], slots[layer][i], w_sem.at[i])

    def swap(layer, i):
        return remote(own[i].at[0], slots[layer][i], x_send.at[i], x_recv.at[i], core)

    def stash(layer, i):
        return pltpu.make_async_copy(slots[layer][i], other[i].at[0], w_sem.at[8 + i])

    for here in range(2):

        @pl.when(at.sec == here)
        def _(here=here):
            for i in (2, 0, 1, 3, 4, 5, 6, 7):
                local(here, i).start()

    at.barrier(True, True, True)
    small_swap = remote(small_own, small_other, x_send.at[8], x_recv.at[8], core)
    small_swap.start()
    for here in range(2):

        @pl.when(at.sec == here)
        def _(here=here):
            for i in (2, 0, 1, 3, 4, 5, 6, 7):
                swap(here, i).start()

    ring_g = Ring(at, out_grad.at[at.sec], gath_g1, r_send.at[0], r_recv.at[0])
    ring_n = Ring(at, gath_n2.at[at.s], gath_n2, r_send.at[1], r_recv.at[1])
    ring_g.step(0)
    small_swap.wait_recv()
    small_copy = pltpu.make_async_copy(small_other, sm_s, io_sem.at[1])
    small_copy.start()
    small_copy.wait()

    def wait_weight(layer, i):
        @pl.when(at.sec == layer)
        def _():
            local(layer, i).wait()

        @pl.when(at.sec != layer)
        def _():
            swap(layer, i).wait_recv()
            stash(layer, i).start()

    allowed = at.allowed()
    applies, tail, prior = at.applies(), at.tail(), at.prior_seg(at.s)
    my_pos = at.first + at.h * at.part + lax.broadcasted_iota(jnp.int32, (at.part, 1), 0)
    my_valid = my_pos < at.tot

    def layer_forward(layer, x_s, hooks):
        cat, w_out, w_gate, w_up, w_down = mats[layer]
        small = jnp.where(at.sec == layer, small_own[...], sm_s[...])
        gain_attn, gain_ffn, taps = small[0:1], small[1:2], small[2 : 2 + KW]
        keep = []

        def save(src, i):
            copy = pltpu.make_async_copy(src, saved[layer][i], save_sem.at[i])
            copy.start()
            keep.append(copy)

        n1_s[...] = norm_rows(x_s[...].astype(F32), gain_attn).astype(BF16)
        save(x_s.at[at.mine], 0)
        save(n1_s, 1)
        wait_weight(layer, 2)
        u_s[8 : 8 + rows, :width] = dot_nt(n1_s[...], cat[2 * qk : 2 * qk + width, :]).astype(BF16).astype(F32)
        edge = remote(
            u_s.at[pl.ds(rows, 8)], edge_s.at[layer], e_send.at[layer], e_recv.at[layer],
            (at.sec, lax.rem(at.s + 1, nz), at.h),
        )

        @pl.when(at.s + 1 < nz)
        def _():
            edge.start()

        wait_weight(layer, 0)
        wait_weight(layer, 1)
        low = dot_nt(n1_s[...], cat[0 : 2 * qk, :]).astype(BF16).astype(F32)
        qk_s[...] = (low * 0.5).astype(BF16)
        save(qk_s, 2)
        a_low, b_low = qk_s[:, 0:qk], qk_s[:, qk : 2 * qk]

        @pl.when(at.s > 0)
        def _():
            edge.wait_recv()

        u_s[0:8, :] = edge_s[layer]
        save(u_s, 3)
        convolve(at, u_s, taps, c_s, cx_s, heads)

        for head in range(heads):
            one, two = lift_parts(b_low, tables, 2, head)
            psi = jnp.where(tail, one * two, 0.0).astype(BF16)
            ss[layer, head] = dot_tn(psi, cx_s[head])[:PSI_SENT].astype(BF16)

        def state(k):
            return remote(
                ss.at[layer], sr.at[layer, at.s], st_send.at[layer, k - 1], st_recv.at[layer, at.s],
                (at.sec, lax.rem(at.s + k, nz), at.h),
            )

        for k in range(1, nz):

            @pl.when(at.s + k < nz)
            def _(k=k):
                state(k).start()

        wait_weight(layer, 3)
        o_s[:, :width] = dot_nt(n1_s[...], cat[2 * qk + width :, :])
        save(o_s, 4)
        for head in range(heads):
            e = dot_nt(a_low, head_only(b_low, head))
            kern = jnp.where(allowed, 1.0 + e + 0.5 * e * e, 0.0).astype(BF16)
            yx_s[head] = dot_nn(kern, cx_s[head])
        for j in range(nz - 1):

            @pl.when(j < at.s)
            def _(j=j):
                remote(ss.at[layer], sr.at[layer, j], st_send.at[layer, 0], st_recv.at[layer, j], core).wait_recv()

        hooks["states"]()
        sin_s[...] = jnp.zeros_like(sin_s)
        for head in range(heads):
            total = jnp.zeros((PSI_SENT, LANES), F32)
            for j in range(nz - 1):
                counts = (j < at.s) & (at.last_seg(j) == prior)
                total = total + jnp.where(counts, sr[layer, j, head].astype(F32), 0.0)
            sin_s[head, 0:PSI_SENT] = total.astype(BF16)
            one, two = lift_parts(a_low, tables, 1, head)
            psi = (one * two).astype(BF16)
            yx = yx_s[head] + jnp.where(applies, dot_nn(psi, sin_s[head]), 0.0)
            yx_s[head] = yx
            gate = o_s[:, head * HD : head * HD + LANES]
            y = yx / yx[:, HD : HD + 1]
            g_s[:, head * HD : head * HD + LANES] = y * (gate * jax.nn.sigmoid(gate))
        gb_s[...] = g_s[:, :width].astype(BF16)
        save(yx_s, 5)
        save(sin_s, 6)
        save(gb_s, 7)

        wait_weight(layer, 4)

        def mix_chunk(at_col, size):
            part_s[layer, 0, :, pl.ds(at_col, size)] = dot_nn(gb_s[...], w_out[:, pl.ds(at_col, size)]).astype(BF16)

        chunks(d, 256, mix_chunk)
        s1 = scatter_start(at, part_s.at[layer, 0], got_s, head_send.at[layer, 0], head_recv.at[layer, 0])
        hooks["rs1"]()
        hidden = x_s[at.mine].astype(F32) + scatter_sum(at, part_s.at[layer, 0], got_s, s1)
        h_s[...] = hidden
        n2_s[at.mine] = norm_rows(hidden, gain_ffn).astype(BF16)
        s2 = gather_start(at, n2_s, head_send.at[layer, 1], head_recv.at[layer, 1])
        save(h_s, 8)
        hooks["ag1"]()
        wait_recv(s2)
        hooks["n2"]()

        wait_weight(layer, 5)
        wait_weight(layer, 6)

        def up_chunk(at_row, size):
            cols = pl.ds(at_row, size)
            f = dot_nt(n2_s[...], w_gate[cols, :])
            v = dot_nt(n2_s[...], w_up[cols, :])
            f_s[:, cols] = f.astype(BF16)
            v_s[:, cols] = v.astype(BF16)
            t_s[:, cols] = (f * jax.nn.sigmoid(f) * v).astype(BF16)

        chunks(t_s.shape[1], 256, up_chunk)
        save(f_s, 9)
        save(v_s, 10)
        wait_weight(layer, 7)

        def down_chunk(at_col, size):
            part_s[layer, 1, :, pl.ds(at_col, size)] = dot_nn(t_s[...], w_down[:, pl.ds(at_col, size)]).astype(BF16)

        chunks(d, 256, down_chunk)
        s3 = scatter_start(at, part_s.at[layer, 1], got_s, head_send.at[layer, 2], head_recv.at[layer, 2])
        hooks["rs2"]()
        feed = scatter_sum(at, part_s.at[layer, 1], got_s, s3)
        xo_s[layer, at.mine] = jnp.where(my_valid, h_s[...] + feed, 0.0).astype(BF16)
        s4 = gather_start(at, xo_s.at[layer], head_send.at[layer, 3], head_recv.at[layer, 3])
        hooks["ag2"]()
        wait_recv(s4)
        for copy in keep:
            copy.wait()

        def finish():
            wait_send(s1 + s2 + s3 + s4)

            @pl.when(at.s + 1 < nz)
            def _():
                edge.wait_send()

            for k in range(1, nz):

                @pl.when(at.s + k < nz)
                def _(k=k):
                    state(k).wait_send()

        return finish

    def nothing():
        pass

    n2_copy = pltpu.make_async_copy(n2_s, gath_n2.at[at.s], io_sem.at[2])

    def ring_rest(ring):
        for k in range(3, nz - 1):
            ring.step(k)

    def n2_ready():
        n2_copy.start()

    x_copy.wait()
    finish_0 = layer_forward(
        0,
        x_s,
        dict(states=lambda: ring_g.step(1), rs1=nothing, ag1=nothing, n2=n2_ready, rs2=lambda: ring_g.step(2), ag2=nothing),
    )
    finish_0()
    n2_copy.wait()
    ring_rest(ring_g)
    ring_g.step(nz - 1)
    ring_n.step(0)

    def out_copy(layer):
        near = pltpu.make_async_copy(xo_s.at[layer], x_out.at[at.sec], io_sem.at[3])
        far = remote(xo_s.at[layer], x_out.at[at.sec], x_send.at[9], x_recv.at[9], core)
        return near, far

    def send_out(layer):
        near, far = out_copy(layer)

        @pl.when(at.sec == layer)
        def _():
            near.start()

        @pl.when(at.sec != layer)
        def _():
            far.start()

    send_out(0)
    n2_last = pltpu.make_async_copy(n2_s, n2_out, io_sem.at[4])
    finish_1 = layer_forward(
        1,
        xo_s.at[0],
        dict(states=lambda: ring_n.step(1), rs1=nothing, ag1=nothing, n2=n2_last.start, rs2=lambda: ring_n.step(2), ag2=nothing),
    )
    send_out(1)
    finish_1()
    ring_rest(ring_n)
    ring_n.step(nz - 1)
    n2_last.wait()
    ring_g.drain()
    ring_n.drain()
    near, far = out_copy(0)
    near.wait()
    far.wait_send()
    far.wait_recv()
    small_swap.wait_send()
    for here in range(2):

        @pl.when(at.sec == here)
        def _(here=here):
            for i in range(8):
                swap(here, i).wait_send()
                stash(1 - here, i).wait()


def bwd_kernel(dims, *refs):
    nz, nh, rows, heads = dims
    take = taker(refs)
    lens, inputs_grad, small_own, small_other, tables = take(5)
    own = take(8)
    other = take(8)
    saved = [take(SAVED), take(SAVED)]
    gath_g1, gath_n2_0, n2_1 = take(3)
    ig_o, gains_o, att_o = take(3)
    ffn_o = take(3)
    gath_n2_1, gath_g0 = take(2)
    a_mine, a_peer, a_land = take(3)
    wr_o = take(3)
    mats = take(5)
    keep_s = take(SAVED)
    (grad_s, part_s, got_s, dm_s, dh_s, dg_s, do_s, cx_s, dyx_s, ss, sr, st_s, da_s, db_s, dc_s, edge_s, dcat_s, ig_s) = take(18)
    gsum_s, gpeer_s, gtot_s, gz_s, gh_s = take(5)
    acc = take(3)
    wx_s = take(3)
    blk_n2, blk_g, n2t_s, gt_s = take(4)
    a_s, work_s = take(2)
    (w_sem, io_sem, keep_sem, e_send, e_recv, st_send, st_recv, head_send, head_recv, r_send, r_recv) = take(11)
    (wx_send, wx_recv, ap_send, ap_recv, l_send, l_recv, x_send, x_recv, gz_send, gz_recv, gh_send, gh_recv) = take(12)
    x_s, n1_s, qk_s, u_s, o_s, yx_s, sin_s, gb_s, h_s, f_s, v_s = keep_s
    df_s, dv_s = f_s, v_s
    at = Place(lens, nz, nh, rows)
    cat, w_out, w_gate, w_up, w_down = mats
    d = n1_s.shape[1]
    width, qk = heads * HD, heads * FEAT
    block = d // nz
    core = (1 - at.sec, at.s, at.h)
    slots = weight_slots(*mats, qk, width)

    def weight_start(layer, i):
        @pl.when(at.sec == layer)
        def _():
            pltpu.make_async_copy(own[i].at[0], slots[i], w_sem.at[i]).start()

        @pl.when(at.sec != layer)
        def _():
            pltpu.make_async_copy(other[i].at[0], slots[i], w_sem.at[i]).start()

    def weight_wait(i):
        pltpu.make_async_copy(own[i].at[0], slots[i], w_sem.at[i]).wait()

    def keep_copy(layer, i):
        return pltpu.make_async_copy(saved[layer][i], keep_s[i], keep_sem.at[i])

    ring_n = Ring(at, n2_1, gath_n2_1, r_send.at[0], r_recv.at[0])
    ring_g = Ring(at, ig_s.at[1], gath_g0, r_send.at[1], r_recv.at[1])
    line = [
        LineSum(at, a_mine.at[0], a_peer.at[0], a_land.at[0], work_s, io_sem.at[4], l_send.at[0], l_recv.at[0], ap_recv),
        LineSum(at, a_mine.at[1], a_peer.at[1], a_land.at[1], work_s, io_sem.at[4], l_send.at[1], l_recv.at[1], ap_recv),
    ]

    def piece(layer, i):
        which = order(at, i)
        if isinstance(i, int) and i == 0:
            n2_src = n2_1 if layer == 1 else gath_n2_0.at[at.s]
            g_src = inputs_grad.at[at.sec] if layer == 1 else ig_s.at[1]
        else:
            n2_src = (gath_n2_1 if layer == 1 else gath_n2_0).at[which]
            g_src = (gath_g1 if layer == 1 else gath_g0).at[which]
        loads = [pltpu.make_async_copy(n2_src, blk_n2, io_sem.at[0]), pltpu.make_async_copy(g_src, blk_g, io_sem.at[1])]
        for copy in loads:
            copy.start()
        for copy in loads:
            copy.wait()
        pos = which * rows + lax.broadcasted_iota(jnp.int32, (rows, 1), 0)
        blk_g[...] = jnp.where(pos < at.tot, blk_g[...].astype(F32), 0.0).astype(BF16)
        for part in range(nz):

            @pl.when(at.s == part)
            def _(part=part):
                n2t_s[...] = blk_n2[:, part * block : (part + 1) * block].T
                gt_s[...] = blk_g[:, part * block : (part + 1) * block].T

        def hidden(at_row, size):
            cols = pl.ds(at_row, size)
            f = dot_nt(blk_n2[...], w_gate[cols, :])
            v = dot_nt(blk_n2[...], w_up[cols, :])
            dt = dot_nt(blk_g[...], w_down[cols, :])
            sig = jax.nn.sigmoid(f)
            act = f * sig
            t = (act * v).astype(BF16)
            df = (dt * v * (sig + act * (1.0 - sig))).astype(BF16)
            dv = (dt * act).astype(BF16)
            parts = (dot_nn(n2t_s[...], df), dot_nn(n2t_s[...], dv), dot_nn(gt_s[...], t))
            for total, new in zip(acc, parts):
                if isinstance(i, int) and i == 0:
                    total[:, cols] = new
                else:
                    total[:, cols] += new

        chunks(w_gate.shape[0], 640, hidden)

    def ffn_swap(i):
        return remote(wx_s[i], wr_o[i], wx_send.at[i], wx_recv.at[i], core)

    def ffn_send(layer):
        @pl.when(at.sec != layer)
        def _():
            for i in range(3):
                wx_s[i][...] = acc[i][...].astype(BF16)
                ffn_swap(i).start()

    def ffn_take(layer):
        @pl.when(at.sec == layer)
        def _():
            copies = []
            if layer == 0:
                for i in range(3):
                    ffn_swap(i).wait_send()
            loads = [pltpu.make_async_copy(wr_o[i], wx_s[i], io_sem.at[9 + i]) for i in range(3)]
            for i in range(3):
                ffn_swap(i).wait_recv()
                loads[i].start()
            for i in range(3):
                loads[i].wait()
                acc[i][...] += wx_s[i][...].astype(F32)
                copy = pltpu.make_async_copy(acc[i], ffn_o[i], io_sem.at[5 + i])
                copy.start()
                copies.append(copy)
            for copy in copies:
                copy.wait()

    def ig_copy(layer):
        near = pltpu.make_async_copy(ig_s.at[layer], ig_o.at[at.sec], io_sem.at[3])
        far = remote(ig_s.at[layer], ig_o.at[at.sec], x_send.at[0], x_recv.at[0], core)
        return near, far

    def ig_send(layer):
        near, far = ig_copy(layer)

        @pl.when(at.sec == layer)
        def _():
            near.start()

        @pl.when(at.sec != layer)
        def _():
            far.start()

    allowed = at.allowed()
    applies, tail, mine_last = at.applies(), at.tail(), at.last_seg(at.s)
    valid = at.pos() < at.tot
    lane = lax.broadcasted_iota(jnp.int32, (rows, LANES), 1)

    def peer_chunk(layer, i):
        return remote(a_s.at[i], a_peer.at[layer, i], ap_send.at[i], ap_recv.at[i], core)

    def mine_chunk(layer, i):
        return pltpu.make_async_copy(a_s.at[i], a_mine.at[layer, i], ap_send.at[i])

    def mixer_grads(layer):
        for i in range(nz):
            cols = slice(i * block, (i + 1) * block)
            a_s[i, :, 0 : 2 * qk + 2 * width] = dot_tn(n1_s[:, cols], dcat_s[...]).astype(BF16)
            a_s[i, :, 2 * qk + 2 * width :] = dot_tn(dm_s[:, cols], gb_s[...]).astype(BF16)

            @pl.when(at.sec != layer)
            def _(i=i):
                peer_chunk(layer, i).start()

            @pl.when(at.sec == layer)
            def _(i=i):
                mine_chunk(layer, i).start()

    def mixer_sent(layer):
        for i in range(nz):

            @pl.when(at.sec != layer)
            def _(i=i):
                peer_chunk(layer, i).wait_send()

            @pl.when(at.sec == layer)
            def _(i=i):
                mine_chunk(layer, i).wait()

    def layer_backward(layer, hooks):
        small = jnp.where(at.sec == layer, small_own[...], small_other[...])
        gain_attn, gain_ffn, taps = small[0:1], small[1:2], small[2 : 2 + KW]
        hooks["begin"]()

        weight_wait(7)
        keep_copy(layer, 9).wait()
        keep_copy(layer, 10).wait()

        def down_chunk(at_row, size):
            cols = pl.ds(at_row, size)
            dt = dot_nt(grad_s[...], w_down[cols, :])
            f = f_s[:, cols].astype(F32)
            v = v_s[:, cols].astype(F32)
            sig = jax.nn.sigmoid(f)
            df_s[:, cols] = (dt * v * sig * (1.0 + f * (1.0 - sig))).astype(BF16)
            dv_s[:, cols] = (dt * f * sig).astype(BF16)

        chunks(df_s.shape[1], 256, down_chunk)
        weight_wait(5)
        weight_wait(6)

        def up_chunk(at_col, size):
            cols = pl.ds(at_col, size)
            part = dot_nn(df_s[...], w_gate[:, cols]) + dot_nn(dv_s[...], w_up[:, cols])
            part_s[0, :, cols] = part.astype(BF16)

        chunks(d, 256, up_chunk)
        s1 = scatter_start(at, part_s.at[0], got_s, head_send.at[layer, 0], head_recv.at[layer, 0])
        hooks["rs1"]()
        keep_copy(layer, 8).wait()
        dn2 = scatter_sum(at, part_s.at[0], got_s, s1)
        back, gain_grad = norm_rows_back(h_s[...], gain_ffn, dn2)
        gsum_s[layer, 1:2, :] = gain_grad
        dh = grad_s[at.mine].astype(F32) + back
        dh_s[...] = dh
        dm_s[at.mine] = dh.astype(BF16)
        s2 = gather_start(at, dm_s, head_send.at[layer, 1], head_recv.at[layer, 1])
        for i in range(8):
            keep_copy(layer, i).wait()
        for i in (4, 0, 1, 2, 3):
            weight_wait(i)
        convolve(at, u_s, taps, do_s, cx_s, heads)
        a_low, b_low = qk_s[:, 0:qk], qk_s[:, qk : 2 * qk]
        hooks["ag1"]()
        wait_recv(s2)

        def out_chunk(at_row, size):
            cols = pl.ds(at_row, size)
            dg_s[:, cols] = dot_nt(dm_s[...], w_out[cols, :])

        chunks(width, 256, out_chunk)
        for head in range(heads):
            cols = slice(head * HD, head * HD + LANES)
            gate, dg, yx = o_s[:, cols], dg_s[:, cols], yx_s[head]
            sig = jax.nn.sigmoid(gate)
            inverse = 1.0 / yx[:, HD : HD + 1]
            y = yx * inverse
            do_s[:, cols] = dg * y * sig * (1.0 + gate * (1.0 - sig))
            dy = jnp.where(lane < HD, dg * gate * sig, 0.0)
            dden = -jnp.sum(dy * y, axis=1, keepdims=True) * inverse
            dyx_s[head] = jnp.where(lane == HD, dden, dy * inverse).astype(BF16)
            one, two = lift_parts(a_low, tables, 1, head)
            psi = jnp.where(applies, one * two, 0.0).astype(BF16)
            ss[layer, head] = dot_tn(psi, dyx_s[head])[:PSI_SENT].astype(BF16)

        def state(k):
            return remote(
                ss.at[layer], sr.at[layer, at.s], st_send.at[layer, k - 1], st_recv.at[layer, at.s],
                (at.sec, lax.rem(at.s + nz - k, nz), at.h),
            )

        for k in range(1, nz):

            @pl.when(at.s - k >= 0)
            def _(k=k):
                state(k).start()

        da_s[...] = jnp.zeros_like(da_s)
        db_s[...] = jnp.zeros_like(db_s)
        for head in range(heads):
            a_own, b_own = head_only(a_low, head), head_only(b_low, head)
            e = dot_nt(a_low, b_own)
            kern = jnp.where(allowed, 1.0 + e + 0.5 * e * e, 0.0).astype(BF16)
            dkern = dot_nt(dyx_s[head], cx_s[head])
            de = jnp.where(allowed, dkern * (1.0 + e), 0.0).astype(BF16)
            one, two = lift_parts(a_low, tables, 1, head)
            dpsi = jnp.where(applies, dot_nt(dyx_s[head], sin_s[head]), 0.0)
            pcols = slice(head * PSI, (head + 1) * PSI)
            da_s[...] += (
                dot_nn(de, b_own)
                + dot_nt((dpsi * two).astype(BF16), tables[0, :, pcols])
                + dot_nt((dpsi * one).astype(BF16), tables[1, :, pcols])
            )
            db_s[...] += dot_tn(de, a_own)
            yx_s[head] = dot_tn(kern, dyx_s[head])
        for j in range(1, nz):

            @pl.when(j > at.s)
            def _(j=j):
                remote(ss.at[layer], sr.at[layer, j], st_send.at[layer, 0], st_recv.at[layer, j], core).wait_recv()

        hooks["states"]()
        st_s[...] = jnp.zeros_like(st_s)
        for head in range(heads):
            total = jnp.zeros((PSI_SENT, LANES), F32)
            for j in range(1, nz):
                counts = (j > at.s) & (at.prior_seg(j) == mine_last)
                total = total + jnp.where(counts, sr[layer, j, head].astype(F32), 0.0)
            st_s[head, 0:PSI_SENT] = total.astype(BF16)
            one, two = lift_parts(b_low, tables, 2, head)
            psi = (one * two).astype(BF16)
            dpsi = jnp.where(tail, dot_nt(cx_s[head], st_s[head]), 0.0)
            pcols = slice(head * PSI, (head + 1) * PSI)
            db_s[...] += dot_nt((dpsi * two).astype(BF16), tables[0, :, pcols]) + dot_nt(
                (dpsi * one).astype(BF16), tables[2, :, pcols]
            )
            dc = yx_s[head] + jnp.where(tail, dot_nn(psi, st_s[head]), 0.0)
            dc_s[0:rows, head * HD : head * HD + LANES] = dc
        edge = remote(
            dc_s.at[pl.ds(0, 8)], edge_s.at[layer], e_send.at[layer], e_recv.at[layer],
            (at.sec, lax.rem(at.s + nz - 1, nz), at.h),
        )

        @pl.when(at.s > 0)
        def _():
            edge.start()

        dcat_s[:, 0:qk] = (da_s[...] * 0.5).astype(BF16)
        dcat_s[:, qk : 2 * qk] = (db_s[...] * 0.5).astype(BF16)
        dcat_s[:, 2 * qk + width :] = do_s[:, :width].astype(BF16)
        gsum_s[layer, 2:8, :] = jnp.zeros((6, d), F32)
        for j in range(KW):
            product = dc_s[0:rows, :width] * u_s[8 - j : 8 - j + rows, :width]
            gsum_s[layer, 2 + j : 3 + j, :width] = jnp.sum(jnp.where(at.same(-j), product, 0.0), axis=0, keepdims=True)

        @pl.when(at.s + 1 < nz)
        def _():
            edge.wait_recv()

        dc_s[rows : rows + 8, :] = edge_s[layer]
        du = taps[0:1, :width] * dc_s[0:rows, :width]
        for j in range(1, KW):
            du = du + jnp.where(at.same(j), dc_s[j : j + rows, :width] * taps[j : j + 1, :width], 0.0)
        dcat_s[:, 2 * qk : 2 * qk + width] = du.astype(BF16)

        def proj_chunk(at_col, size):
            cols = pl.ds(at_col, size)
            part_s[1, :, cols] = dot_nn(dcat_s[...], cat[:, cols]).astype(BF16)

        chunks(d, 256, proj_chunk)
        s3 = scatter_start(at, part_s.at[1], got_s, head_send.at[layer, 2], head_recv.at[layer, 2])
        mixer_grads(layer)
        hooks["rs2"]()
        dn1 = scatter_sum(at, part_s.at[1], got_s, s3)
        back, gain_grad = norm_rows_back(x_s[...].astype(F32), gain_attn, dn1)
        gsum_s[layer, 0:1, :] = gain_grad
        ig_s[layer, at.mine] = (dh_s[...] + back).astype(BF16)
        s4 = gather_start(at, ig_s.at[layer], head_send.at[layer, 3], head_recv.at[layer, 3])
        hooks["ag2"]()
        wait_recv(s4)
        ig_send(layer)
        wait_send(s1 + s3)

        def finish():
            wait_send(s2 + s4)

            @pl.when(at.s > 0)
            def _():
                edge.wait_send()

            for k in range(1, nz):

                @pl.when(at.s - k >= 0)
                def _(k=k):
                    state(k).wait_send()

        return finish

    def rest(layer, ring):
        for k in range(3, min(nz, 4)):
            ring.step(k)
            piece(layer, k)

        def one(k, carry):
            ring.step(k)
            piece(layer, k)
            return carry

        if nz > 4:
            lax.fori_loop(4, nz, one, 0)

    def owner(layer, what):
        @pl.when(at.sec == layer)
        def _():
            what()

    g_copy = pltpu.make_async_copy(inputs_grad.at[at.sec], grad_s, io_sem.at[2])
    g_copy.start()
    for i in (7, 5, 6, 4, 0, 1, 2, 3):
        weight_start(1, i)
    for i in (9, 10, 8, 3, 2, 4, 5, 6, 7, 1, 0):
        keep_copy(1, i).start()
    at.barrier(True, True, True)
    ring_n.step(0)
    g_copy.wait()
    grad_s[...] = jnp.where(valid, grad_s[...].astype(F32), 0.0).astype(BF16)

    def b1_ag1():
        ring_n.step(1)
        piece(1, 1)

    def b1_ag2():
        for i in (4, 0, 1, 2, 3):
            weight_start(0, i)
        for i in (9, 10, 8, 3, 2, 4, 5, 6, 7, 1, 0):
            keep_copy(0, i).start()
        rest(1, ring_n)
        for i in (7, 5, 6):
            weight_start(0, i)
        ffn_send(1)

    def nothing():
        pass

    def b1_states():
        ring_n.step(2)

    def b1_rs2():
        piece(1, 2)

    finish_1 = layer_backward(
        1, dict(begin=nothing, rs1=lambda: piece(1, 0), ag1=b1_ag1, states=b1_states, rs2=b1_rs2, ag2=b1_ag2)
    )
    finish_1()
    grad_s[...] = jnp.where(valid, ig_s[1].astype(F32), 0.0).astype(BF16)

    def b0_begin():
        ring_g.step(0)
        mixer_sent(1)
        owner(1, lambda: line[1].slot(0))

    def b0_rs1():
        ffn_take(1)
        piece(0, 0)

    def b0_ag1():
        ring_g.step(1)
        piece(0, 1)

    def b0_states():
        ring_g.step(2)
        owner(1, lambda: line[1].slot(1))

    def b0_rs2():
        piece(0, 2)
        owner(1, lambda: line[1].slot(2))

    def b0_ag2():
        rest(0, ring_g)
        ffn_send(0)

    finish_0 = layer_backward(
        0, dict(begin=b0_begin, rs1=b0_rs1, ag1=b0_ag1, states=b0_states, rs2=b0_rs2, ag2=b0_ag2)
    )

    gain_swap = remote(gsum_s.at[1 - at.sec], gpeer_s, x_send.at[1], x_recv.at[1], core)
    gain_swap.start()

    def line_end(layer, begin):
        for i in range(begin, nz - 1):
            line[layer].slot(i)
        line[layer].last()
        copy = pltpu.make_async_copy(work_s.at[0], att_o, io_sem.at[8])
        copy.start()
        copy.wait()

    owner(1, lambda: line_end(1, 3))
    mixer_sent(0)
    gain_swap.wait_recv()
    gtot_s[0] = gsum_s[at.sec] + gpeer_s[...]

    def gain_seq(k):
        to = lax.rem(at.s + k, nz)
        return remote(gtot_s.at[0], gz_s.at[k - 1], gz_send.at[k - 1], gz_recv.at[k - 1], (at.sec, to, at.h))

    for k in range(1, nz):
        gain_seq(k).start()
    ffn_take(0)
    for k in range(1, nz):
        gain_seq(k).wait_recv()
    total = gtot_s[0]
    for k in range(1, nz):
        total = total + gz_s[k - 1]
    gtot_s[1] = total

    def gain_head(m):
        return remote(gtot_s.at[1], gh_s.at[m - 1], gh_send.at[m - 1], gh_recv.at[m - 1], (at.sec, at.s, at.h ^ m))

    for m in range(1, nh):
        gain_head(m).start()
    owner(0, lambda: line_end(0, 0))
    for m in range(1, nh):
        gain_head(m).wait_recv()
    total = gtot_s[1, 0:2]
    for m in range(1, nh):
        total = total + gh_s[m - 1, 0:2]
    gains_o[...] = gtot_s[1]
    gains_o[0:2, :] = total

    finish_0()
    ring_n.drain()
    ring_g.drain()
    gain_swap.wait_send()
    for k in range(1, nz):
        gain_seq(k).wait_send()
    for m in range(1, nh):
        gain_head(m).wait_send()
    owner(1, lambda: wait_send([ffn_swap(i) for i in range(3)]))
    near, far = ig_copy(0)
    near.wait()
    far.wait_send()
    far.wait_recv()


def shape(dims, kind=BF16):
    return jax.ShapeDtypeStruct(tuple(dims), kind)


ANY = pl.BlockSpec(memory_space=pl.ANY)
VM = pl.BlockSpec(memory_space=pltpu.VMEM)
SM = pl.BlockSpec(memory_space=pltpu.SMEM)
DMA = pltpu.SemaphoreType.DMA


def params(number):
    return pltpu.CompilerParams(collective_id=number, has_side_effects=True, vmem_limit_bytes=VMEM_LIMIT)


def shards(nz, nh, inputs, out_grad, lengths, norm_attn, norm_ffn, w_query, w_key, w_value, w_output_gate, conv_kernel, w_out, w_gate, w_up, w_down):
    micro, rows, d = inputs.shape
    heads = w_query.shape[2] // FEAT
    width, qk, ff = w_value.shape[2], w_query.shape[2], w_gate.shape[2]
    part, block = rows // nh, d // nz
    dims = (nz, nh, rows, heads)
    wide = -(-((heads - 1) * HD + LANES) // LANES) * LANES
    total = 2 * qk + 3 * width
    tables = jnp.asarray(lift_tables(heads), BF16)
    turned = [jnp.swapaxes(w, 1, 2) for w in (w_query, w_key, w_value, w_output_gate)]
    own = (*turned, w_out, jnp.swapaxes(w_gate, 1, 2), jnp.swapaxes(w_up, 1, 2), w_down)
    small_own = jnp.concatenate(
        [norm_attn, norm_ffn, jnp.pad(conv_kernel[0], ((0, 0), (0, d - width))), jnp.zeros((3, d), F32)]
    )

    def vm(dims, kind=BF16):
        return pltpu.VMEM(tuple(dims), kind)

    mats = [vm((2 * qk + 2 * width, d)), vm((width, d)), vm((ff, d)), vm((ff, d)), vm((ff, d))]
    act = vm((rows, d))
    kept = [
        ((part, d), BF16),
        ((rows, d), BF16),
        ((rows, 2 * qk), BF16),
        ((rows + 8, wide), F32),
        ((rows, wide), F32),
        ((heads, rows, LANES), F32),
        ((heads, PSI, LANES), BF16),
        ((rows, width), BF16),
        ((part, d), F32),
        ((rows, ff), BF16),
        ((rows, ff), BF16),
    ]
    keep_shapes = [shape(*k) for k in kept]
    gathered = shape((nz, rows, d))
    outs = (
        [shape((8, d), F32)]
        + [shape(w.shape) for w in own]
        + keep_shapes * 2
        + [shape((micro, rows, d)), gathered, gathered, shape((rows, d))]
    )
    scratch = (
        mats
        + mats
        + [
            act,
            act,
            act,
            vm((rows, 2 * qk)),
            vm((rows + 8, wide), F32),
            vm((2, 8, wide), F32),
            vm((rows, wide), F32),
            vm((rows, wide), F32),
            vm((heads, rows, LANES)),
            vm((heads, rows, LANES), F32),
            vm((2, heads, PSI_SENT, LANES)),
            vm((2, nz, heads, PSI_SENT, LANES)),
            vm((heads, PSI, LANES)),
            vm((rows, wide), F32),
            vm((rows, width)),
            vm((2, 2, rows, d)),
            vm((nh - 1, part, d)),
            vm((rows, ff)),
            vm((rows, ff)),
            vm((rows, ff)),
            vm((2, rows, d)),
            vm((part, d), F32),
            vm((8, d), F32),
            DMA((16,)),
            DMA((5,)),
            DMA((SAVED,)),
            DMA((10,)),
            DMA((10,)),
            DMA((2,)),
            DMA((2,)),
            DMA((2, nz)),
            DMA((2, nz)),
            DMA((2, 4, nh - 1)),
            DMA((2, 4, nh - 1)),
            DMA((2, 2, nz - 1)),
            DMA((2, 2, nz - 1)),
        ]
    )
    first = pl.pallas_call(
        functools.partial(fwd_kernel, dims),
        out_shape=outs,
        in_specs=[SM, ANY, ANY, VM, VM] + [ANY] * 8,
        out_specs=[ANY] * len(outs),
        scratch_shapes=scratch,
        compiler_params=params(0),
    )(lengths, inputs, out_grad, small_own, tables, *own)
    small_other, other = first[0], first[1:9]
    saved = first[9 : 9 + 2 * SAVED]
    section_out, gath_g1, gath_n2_0, n2_1 = first[9 + 2 * SAVED :]

    outs = (
        [shape((micro, rows, d)), shape((8, d), F32), shape((block, total))]
        + [shape((block, ff), F32)] * 3
        + [gathered, gathered]
        + [shape((2, nz, block, total)), shape((2, nz, block, total)), shape((2, 2, nz, block, total))]
        + [shape((block, ff))] * 3
    )
    out_specs = [ANY, VM] + [ANY] * (len(outs) - 2)
    scratch = (
        mats
        + [vm(*k) for k in kept]
        + [
            act,
            vm((2, rows, d)),
            vm((nh - 1, part, d)),
            act,
            vm((part, d), F32),
            vm((rows, wide), F32),
            vm((rows, wide), F32),
            vm((heads, rows, LANES)),
            vm((heads, rows, LANES)),
            vm((2, heads, PSI_SENT, LANES)),
            vm((2, nz, heads, PSI_SENT, LANES)),
            vm((heads, PSI, LANES)),
            vm((rows, qk), F32),
            vm((rows, qk), F32),
            vm((rows + 8, wide), F32),
            vm((2, 8, wide), F32),
            vm((rows, 2 * qk + 2 * width)),
            vm((2, rows, d)),
            vm((2, 8, d), F32),
            vm((8, d), F32),
            vm((2, 8, d), F32),
            vm((nz - 1, 8, d), F32),
            vm((nh - 1, 8, d), F32),
        ]
        + [vm((block, ff), F32)] * 3
        + [vm((block, ff))] * 3
        + [act, act, vm((block, rows)), vm((block, rows)), vm((nz, block, total)), vm((3, block, total))]
        + [
            DMA((8,)),
            DMA((12,)),
            DMA((SAVED,)),
            DMA((2,)),
            DMA((2,)),
            DMA((2, nz)),
            DMA((2, nz)),
            DMA((2, 4, nh - 1)),
            DMA((2, 4, nh - 1)),
            DMA((2, 2, nz - 1)),
            DMA((2, 2, nz - 1)),
            DMA((3,)),
            DMA((3,)),
            DMA((nz,)),
            DMA((nz,)),
            DMA((2, 2, nz)),
            DMA((2, 2, nz)),
            DMA((2,)),
            DMA((2,)),
            DMA((nz - 1,)),
            DMA((nz - 1,)),
            DMA((nh - 1,)),
            DMA((nh - 1,)),
        ]
    )
    second = pl.pallas_call(
        functools.partial(bwd_kernel, dims),
        out_shape=outs,
        in_specs=[SM, ANY, VM, VM, VM] + [ANY] * (16 + 2 * SAVED + 3),
        out_specs=out_specs,
        scratch_shapes=scratch,
        compiler_params=params(1),
    )(lengths, out_grad, small_own, small_other, tables, *own, *other, *saved, gath_g1, gath_n2_0, n2_1)
    input_grad, gains, att, g_gate, g_up, g_down = second[:6]
    att = att.astype(F32)
    return (
        section_out[None],
        input_grad[None],
        gains[0:1],
        gains[1:2],
        att[None, :, 0:qk],
        att[None, :, qk : 2 * qk],
        att[None, :, 2 * qk : 2 * qk + width],
        att[None, :, 2 * qk + width : 2 * qk + 2 * width],
        gains[None, 2 : 2 + KW, :width],
        att[:, 2 * qk + 2 * width :].T[None],
        g_gate[None],
        g_up[None],
        g_down.T[None],
    )


def solution(mesh):
    return jax.shard_map(
        functools.partial(shards, mesh.shape["seq"], mesh.shape["head"]),
        mesh=mesh,
        in_specs=(
            P(None, "seq", None),
            P(None, "seq", None),
            P(),
            P("section", None),
            P("section", None),
            P("section", None, "head"),
            P("section", None, "head"),
            P("section", None, "head"),
            P("section", None, "head"),
            P("section", None, "head"),
            P("section", "head", None),
            P("section", None, "head"),
            P("section", None, "head"),
            P("section", "head", None),
        ),
        out_specs=(
            P("section", None, "seq", None),
            P("section", None, "seq", None),
            P("section", None),
            P("section", None),
            P("section", "seq", "head"),
            P("section", "seq", "head"),
            P("section", "seq", "head"),
            P("section", "seq", "head"),
            P("section", None, "head"),
            P("section", "head", "seq"),
            P("section", "seq", "head"),
            P("section", "seq", "head"),
            P("section", "head", "seq"),
        ),
        check_vma=False,
    )
```

```python
import functools

import jax
import jax.numpy as jnp
import numpy as np
from jax import lax
from jax.experimental import pallas as pl
from jax.experimental.pallas import tpu as pltpu
from jax.sharding import PartitionSpec as P

HD = 112
FEAT = 16
KW = 3
EPS = 1e-05
LANES = 128
PSI = 256
PSI_SENT = 160
MESH = pl.DeviceIdType.MESH
F32 = jnp.float32
BF16 = jnp.bfloat16
VMEM_LIMIT = 62 << 20


def dot_nn(a, b):
    return lax.dot_general(a, b, (((1,), (0,)), ((), ())), preferred_element_type=F32)


def dot_nt(a, b):
    return lax.dot_general(a, b, (((1,), (1,)), ((), ())), preferred_element_type=F32)


def dot_tn(a, b):
    return lax.dot_general(a, b, (((0,), (0,)), ((), ())), preferred_element_type=F32)


def chunks(total, step, body):
    whole = total // step
    if whole > 1:

        def one(i, carry):
            body(pl.multiple_of(i * step, step), step)
            return carry

        lax.fori_loop(0, whole, one, 0)
    elif whole == 1:
        body(0, step)
    if total % step:
        body(whole * step, total % step)


def lift_tables(heads):
    first = np.zeros((heads * FEAT, heads * PSI), np.float32)
    second = np.zeros_like(first)
    second_key = np.zeros_like(first)
    for head in range(heads):
        row, col = head * FEAT, head * PSI
        for i in range(FEAT):
            first[row + i, col + 1 + i] = 1.0
        at = 1 + FEAT
        for i in range(FEAT):
            for j in range(i, FEAT):
                first[row + i, col + at] = 1.0
                second[row + j, col + at] = 1.0
                second_key[row + j, col + at] = 0.5 if i == j else 1.0
                at += 1
    return np.stack([first, second, second_key])


class Place:
    def __init__(self, lens, nz, nh, rows):
        self.sec, self.s, self.h = (lax.axis_index(a) for a in ("section", "seq", "head"))
        self.nz, self.nh, self.rows = nz, nh, rows
        self.l0 = lens[self.sec, 0]
        self.tot = self.l0 + lens[self.sec, 1]
        self.first = self.s * rows
        self.part = rows // nh
        self.mine = pl.ds(pl.multiple_of(self.h * self.part, self.part), self.part)

    def seg(self, pos):
        inside = (pos >= self.l0).astype(jnp.int32) + (pos >= self.tot).astype(jnp.int32)
        return jnp.where(pos >= 0, inside, -1)

    def pos(self, shift=0):
        return self.first + shift + lax.broadcasted_iota(jnp.int32, (self.rows, 1), 0)

    def same(self, shift):
        other = self.pos(shift)
        inside = other < self.nz * self.rows
        return (self.seg(other) == self.seg(self.pos())) & inside

    def allowed(self):
        shape = (self.rows, self.rows)
        row = lax.broadcasted_iota(jnp.int32, shape, 0)
        col = lax.broadcasted_iota(jnp.int32, shape, 1)
        return (col <= row) & (self.seg(self.first + col) == self.seg(self.first + row))

    def last_seg(self, block):
        return self.seg(block * self.rows + self.rows - 1)

    def prior_seg(self, block):
        return self.seg(block * self.rows - 1)

    def applies(self):
        return self.seg(self.pos()) == self.prior_seg(self.s)

    def tail(self):
        return self.seg(self.pos()) == self.last_seg(self.s)

    def peers(self):
        core = [(1 - self.sec, self.s, self.h)]
        seq = [(self.sec, (self.s + k) % self.nz, self.h) for k in range(1, self.nz)]
        head = [(self.sec, self.s, self.h ^ m) for m in range(1, self.nh)]
        return core, seq, head

    def barrier(self, core, seq, head):
        groups = self.peers()
        told = [d for use, g in zip((core, seq, head), groups) if use for d in g]
        sem = pltpu.get_barrier_semaphore()
        for device in told:
            pl.semaphore_signal(sem, 1, device_id=device, device_id_type=MESH)
        pl.semaphore_wait(sem, len(told))


def remote(src, dst, send, recv, device):
    return pltpu.make_async_remote_copy(
        src_ref=src, dst_ref=dst, send_sem=send, recv_sem=recv, device_id=device, device_id_type=MESH
    )


def half_cols(buf, half):
    size = buf.shape[-1] // 2
    return pl.ds(half * size, size)


def scatter_start(at, buf, got, send, recv, half):
    sent = []
    cols = half_cols(buf, half)
    for m in sorted(range(1, at.nh), reverse=True):
        peer = at.h ^ m
        rows = pl.ds(pl.multiple_of(peer * at.part, at.part), at.part)
        sem = half * (at.nh - 1) + m - 1
        copy = remote(
            buf.at[rows, cols], got.at[m - 1, :, cols], send.at[sem], recv.at[sem], (at.sec, at.s, peer)
        )
        copy.start()
        sent.append(copy)
    return sent


def scatter_sum(at, buf, got, sent):
    total = buf[at.mine].astype(F32)
    for copy in sent:
        copy.wait_recv()
    for m in range(1, at.nh):
        total = total + got[m - 1].astype(F32)
    return total


def gather_start(at, buf, send, recv):
    sent = []
    for m in sorted(range(1, at.nh), reverse=True):
        copy = remote(
            buf.at[at.mine], buf.at[at.mine], send.at[m - 1], recv.at[m - 1], (at.sec, at.s, at.h ^ m)
        )
        copy.start()
        sent.append(copy)
    return sent


def wait_recv(copies):
    for copy in copies:
        copy.wait_recv()


def wait_send(copies):
    for copy in copies:
        copy.wait_send()


def norm_rows(x, gain):
    return x * lax.rsqrt(jnp.mean(x * x, axis=-1, keepdims=True) + EPS) * gain


def norm_rows_back(x, gain, grad):
    inverse = lax.rsqrt(jnp.mean(x * x, axis=-1, keepdims=True) + EPS)
    unit = x * inverse
    scaled = grad * gain
    back = inverse * (scaled - unit * jnp.mean(scaled * unit, axis=-1, keepdims=True))
    return back, jnp.sum(grad * unit, axis=0, keepdims=True)


def lift_parts(low, tables, second, head):
    cols = slice(head * PSI, (head + 1) * PSI)
    lane = lax.broadcasted_iota(jnp.int32, (1, PSI), 1)
    one = dot_nn(low, tables[0, :, cols]) + (lane == 0).astype(F32)
    two = dot_nn(low, tables[second, :, cols]) + (lane <= FEAT).astype(F32)
    return one, two


def head_only(low, head):
    lane = lax.broadcasted_iota(jnp.int32, low.shape, 1)
    return jnp.where((lane >= head * FEAT) & (lane < (head + 1) * FEAT), low, jnp.zeros_like(low))


def convolve(at, u_s, taps, c_s, cx_s, heads):
    rows, width = at.rows, heads * HD
    out = taps[0:1, :width] * u_s[8 : 8 + rows, :width]
    for j in range(1, KW):
        shifted = u_s[8 - j : 8 - j + rows, :width]
        out = out + jnp.where(at.same(-j), shifted * taps[j : j + 1, :width], 0.0)
    c_s[0:rows, :width] = out
    lane = lax.broadcasted_iota(jnp.int32, (rows, LANES), 1)
    for head in range(heads):
        one = c_s[0:rows, head * HD : head * HD + LANES]
        cx_s[head] = jnp.where(lane < HD, one, jnp.where(lane == HD, 1.0, 0.0)).astype(BF16)


def order(at, i):
    left, right = at.s, at.nz - 1 - at.s
    both = 2 * jnp.minimum(left, right)
    near = i <= both
    dist = jnp.where(near, (i + 1) // 2, i - both // 2)
    leftward = jnp.where(near, i % 2 == 1, left > right)
    return jnp.where(leftward, at.s - dist, at.s + dist)


class Ring:
    def __init__(self, at, src, dst, send, recv, pair_send, pair_recv):
        self.at, self.src, self.dst, self.send, self.recv = at, src, dst, send, recv
        self.pair_send, self.pair_recv = pair_send, pair_recv

    def _view(self, c):
        at = self.at
        rows, cols = at.rows // 2, self.dst.shape[-1] // 2
        bit = lax.rem(at.h // (1 << c), 2)
        return pl.ds(pl.multiple_of(bit * rows, rows), rows), pl.ds(c * cols, cols)

    def _ways(self, k):
        at = self.at
        right = (at.s - k, at.s - k >= 0, at.s + 1 < at.nz, lax.rem(at.s + 1, at.nz))
        left = (at.s + k, at.s + k < at.nz, at.s > 0, lax.rem(at.s + at.nz - 1, at.nz))
        return right, left

    def _copies(self, way, k, block, to, first):
        at = self.at
        for c in range(2):
            rows, cols = self._view(c)
            src = self.src.at[rows, cols] if first else self.dst.at[block, rows, cols]
            yield remote(
                src, self.dst.at[block, rows, cols], self.send.at[way, k, c], self.recv.at[way, k, c], (at.sec, to, at.h)
            )

    def _pairs(self, way, k, block):
        at = self.at
        for c in range(2):
            rows, cols = self._view(c)
            view = self.dst.at[block, rows, cols]
            yield remote(view, view, self.pair_send.at[way, k, c], self.pair_recv.at[way, k, c], (at.sec, at.s, at.h ^ (1 << c)))

    def step(self, k):
        at = self.at
        first = isinstance(k, int) and k == 0
        for way, (block, there, onward, to) in enumerate(self._ways(k)):
            if not first:

                @pl.when(there)
                def _(way=way, block=block, to=to):
                    wait_recv(self._copies(way, k - 1, block, to, False))

            if not isinstance(k, int) or k < at.nz - 1:

                @pl.when(there & onward & (k < at.nz - 1))
                def _(way=way, block=block, to=to):
                    for copy in self._copies(way, k, block, to, first):
                        copy.start()

    def pair(self, k):
        for way, (block, there, _, _) in enumerate(self._ways(k + 1)):

            @pl.when(there)
            def _(way=way, block=block):
                for copy in self._pairs(way, k, block):
                    copy.start()

    def ready(self, k):
        for way, (block, there, _, _) in enumerate(self._ways(k + 1)):

            @pl.when(there)
            def _(way=way, block=block):
                wait_recv(self._pairs(way, k, block))

    def drain(self):
        def one(k, carry):
            for way, (_, there, onward, to) in enumerate(self._ways(k)):

                @pl.when(there & onward)
                def _(way=way, to=to):
                    wait_send(self._copies(way, k, self.at.s, to, False))

            for way, (_, there, _, _) in enumerate(self._ways(k + 1)):

                @pl.when(there)
                def _(way=way):
                    wait_send(self._pairs(way, k, self.at.s))

            return carry

        lax.fori_loop(0, self.at.nz - 1, one, 0)


def upward(begin, end, body):
    if end > begin:

        def one(k, carry):
            body(k)
            return carry

        lax.fori_loop(begin, end, one, 0)


class LineSum:
    def __init__(self, at, mine, peer, land, work, io, send, recv, peer_recv):
        self.at, self.mine, self.peer, self.land, self.work = at, mine, peer, land, work
        self.io, self.send, self.recv, self.peer_recv = io, send, recv, peer_recv

    def _hop(self, way, d):
        at = self.at
        to = lax.rem(at.s + (1 if way == 0 else at.nz - 1), at.nz)
        return remote(self.work.at[way], self.land.at[way, d], self.send.at[way, d], self.recv.at[way, d], (at.sec, to, at.h))

    def _load(self, src, slot):
        copy = pltpu.make_async_copy(src, self.work.at[slot], self.io)
        copy.start()
        copy.wait()

    def _add(self, slot, src):
        self._load(src, 2)
        self.work[slot] = (self.work[slot].astype(F32) + self.work[2].astype(F32)).astype(BF16)

    def _own(self, slot, d):
        at = self.at
        remote(self.mine.at[d], self.peer.at[d], self.peer_recv.at[d], self.peer_recv.at[d], (1 - at.sec, at.s, at.h)).wait_recv()
        self._load(self.peer.at[d], 2)
        self.work[slot] = (self.mine[d].astype(F32) + self.work[2].astype(F32)).astype(BF16)

    def slot(self, i):
        at = self.at
        for way in range(2):
            begun = i - at.s if way == 0 else i - (at.nz - 1 - at.s)
            d = at.nz - 1 - begun if way == 0 else begun
            earlier = at.s > 0 if way == 0 else at.s < at.nz - 1

            @pl.when((begun >= 0) & (i < at.nz - 1))
            def _(way=way, d=d, begun=begun, earlier=earlier):
                @pl.when(begun > 0)
                def _():
                    self._hop(way, d + 1 if way == 0 else d - 1).wait_send()

                self._own(way, d)

                @pl.when(earlier)
                def _():
                    self._hop(way, d).wait_recv()
                    self._add(way, self.land.at[way, d])

                self._hop(way, d).start()

    def last(self):
        at = self.at

        @pl.when(at.s < at.nz - 1)
        def _():
            self._hop(0, at.s + 1).wait_send()

        @pl.when(at.s > 0)
        def _():
            self._hop(1, at.s - 1).wait_send()

        self._own(0, at.s)

        @pl.when(at.s > 0)
        def _():
            self._hop(0, at.s).wait_recv()
            self._add(0, self.land.at[0, at.s])

        @pl.when(at.s < at.nz - 1)
        def _():
            self._hop(1, at.s).wait_recv()
            self._add(0, self.land.at[1, at.s])


def taker(refs):
    refs = list(refs)

    def take(n):
        out = refs[:n]
        del refs[:n]
        return out

    return take


def weight_slots(cat, out, gate, up, down, qk, width):
    at_row, views = 0, []
    for size in (qk, qk, width, width):
        views.append(cat.at[pl.ds(at_row, size)])
        at_row += size
    return views + [out, gate, up, down]


SAVED = 11


def fwd_kernel(dims, *refs):
    nz, nh, rows, heads = dims
    take = taker(refs)
    lens, inputs, out_grad, small_own, tables = take(5)
    own = take(8)
    small_other = take(1)[0]
    other = take(8)
    saved = [take(SAVED), take(SAVED)]
    x_out, gath_g1, gath_n2, n2_out = take(4)
    mats = [take(5), take(5)]
    (x_s, n1_s, n2_s, qk_s, u_s, edge_s, o_s, c_s, cx_s, yx_s, ss, sr, sin_s, g_s, gb_s, part_s, got_s, f_s, v_s, t_s, xo_s, h_s, sm_s) = take(23)
    w_sem, io_sem, save_sem, x_send, x_recv, e_send, e_recv, st_send, st_recv, head_send, head_recv = take(11)
    r_send, r_recv, p_send, p_recv = take(4)
    at = Place(lens, nz, nh, rows)
    d = x_s.shape[1]
    width, qk = heads * HD, heads * FEAT
    core = (1 - at.sec, at.s, at.h)
    slots = [weight_slots(*m, qk, width) for m in mats]

    x_copy = pltpu.make_async_copy(inputs.at[at.sec], x_s, io_sem.at[0])
    x_copy.start()

    def local(layer, i):
        return pltpu.make_async_copy(own[i].at[0], slots[layer][i], w_sem.at[i])

    def swap(layer, i):
        return remote(own[i].at[0], slots[layer][i], x_send.at[i], x_recv.at[i], core)

    def stash(layer, i):
        return pltpu.make_async_copy(slots[layer][i], other[i].at[0], w_sem.at[8 + i])

    for here in range(2):

        @pl.when(at.sec == here)
        def _(here=here):
            for i in (2, 0, 1, 3, 4, 5, 6, 7):
                local(here, i).start()

    at.barrier(True, True, True)
    small_swap = remote(small_own, small_other, x_send.at[8], x_recv.at[8], core)
    small_swap.start()
    for here in range(2):

        @pl.when(at.sec == here)
        def _(here=here):
            for i in (2, 0, 1, 3, 4, 5, 6, 7):
                swap(here, i).start()

    ring_g = Ring(at, out_grad.at[at.sec], gath_g1, r_send.at[0], r_recv.at[0], p_send.at[0], p_recv.at[0])
    ring_n = Ring(at, gath_n2.at[at.s], gath_n2, r_send.at[1], r_recv.at[1], p_send.at[1], p_recv.at[1])
    ring_g.step(0)
    small_swap.wait_recv()
    small_copy = pltpu.make_async_copy(small_other, sm_s, io_sem.at[1])
    small_copy.start()
    small_copy.wait()

    def wait_weight(layer, i):
        @pl.when(at.sec == layer)
        def _():
            local(layer, i).wait()

        @pl.when(at.sec != layer)
        def _():
            swap(layer, i).wait_recv()
            stash(layer, i).start()

    allowed = at.allowed()
    applies, tail, prior = at.applies(), at.tail(), at.prior_seg(at.s)
    my_pos = at.first + at.h * at.part + lax.broadcasted_iota(jnp.int32, (at.part, 1), 0)
    my_valid = my_pos < at.tot

    def layer_forward(layer, x_s, hooks):
        cat, w_out, w_gate, w_up, w_down = mats[layer]
        small = jnp.where(at.sec == layer, small_own[...], sm_s[...])
        gain_attn, gain_ffn, taps = small[0:1], small[1:2], small[2 : 2 + KW]
        keep = []

        def save(src, i):
            copy = pltpu.make_async_copy(src, saved[layer][i], save_sem.at[i])
            copy.start()
            keep.append(copy)

        hooks["begin"]()
        n1_s[...] = norm_rows(x_s[...].astype(F32), gain_attn).astype(BF16)
        save(x_s.at[at.mine], 0)
        save(n1_s, 1)
        wait_weight(layer, 2)
        u_s[8 : 8 + rows, :width] = dot_nt(n1_s[...], cat[2 * qk : 2 * qk + width, :]).astype(BF16).astype(F32)
        edge = remote(
            u_s.at[pl.ds(rows, 8)], edge_s.at[layer], e_send.at[layer], e_recv.at[layer],
            (at.sec, lax.rem(at.s + 1, nz), at.h),
        )

        @pl.when(at.s + 1 < nz)
        def _():
            edge.start()

        wait_weight(layer, 0)
        wait_weight(layer, 1)
        low = dot_nt(n1_s[...], cat[0 : 2 * qk, :]).astype(BF16).astype(F32)
        qk_s[...] = (low * 0.5).astype(BF16)
        save(qk_s, 2)
        a_low, b_low = qk_s[:, 0:qk], qk_s[:, qk : 2 * qk]

        @pl.when(at.s > 0)
        def _():
            edge.wait_recv()

        u_s[0:8, :] = edge_s[layer]
        save(u_s, 3)
        convolve(at, u_s, taps, c_s, cx_s, heads)

        for head in range(heads):
            one, two = lift_parts(b_low, tables, 2, head)
            psi = jnp.where(tail, one * two, 0.0).astype(BF16)
            ss[layer, head] = dot_tn(psi, cx_s[head])[:PSI_SENT].astype(BF16)

        def state(k):
            return remote(
                ss.at[layer], sr.at[layer, at.s], st_send.at[layer, k - 1], st_recv.at[layer, at.s],
                (at.sec, lax.rem(at.s + k, nz), at.h),
            )

        for k in range(1, nz):

            @pl.when(at.s + k < nz)
            def _(k=k):
                state(k).start()

        wait_weight(layer, 3)
        o_s[:, :width] = dot_nt(n1_s[...], cat[2 * qk + width :, :])
        save(o_s, 4)
        for head in range(heads):
            e = dot_nt(a_low, head_only(b_low, head))
            kern = jnp.where(allowed, 1.0 + e + 0.5 * e * e, 0.0).astype(BF16)
            yx_s[head] = dot_nn(kern, cx_s[head])
        for j in range(nz - 1):

            @pl.when(j < at.s)
            def _(j=j):
                remote(ss.at[layer], sr.at[layer, j], st_send.at[layer, 0], st_recv.at[layer, j], core).wait_recv()

        hooks["states"]()
        sin_s[...] = jnp.zeros_like(sin_s)
        for head in range(heads):
            total = jnp.zeros((PSI_SENT, LANES), F32)
            for j in range(nz - 1):
                counts = (j < at.s) & (at.last_seg(j) == prior)
                total = total + jnp.where(counts, sr[layer, j, head].astype(F32), 0.0)
            sin_s[head, 0:PSI_SENT] = total.astype(BF16)
            one, two = lift_parts(a_low, tables, 1, head)
            psi = (one * two).astype(BF16)
            yx = yx_s[head] + jnp.where(applies, dot_nn(psi, sin_s[head]), 0.0)
            yx_s[head] = yx
            gate = o_s[:, head * HD : head * HD + LANES]
            y = yx / yx[:, HD : HD + 1]
            g_s[:, head * HD : head * HD + LANES] = y * (gate * jax.nn.sigmoid(gate))
        gb_s[...] = g_s[:, :width].astype(BF16)
        save(yx_s, 5)
        save(sin_s, 6)
        save(gb_s, 7)

        wait_weight(layer, 4)

        s1 = []
        for half in range(2):
            cols = half_cols(w_out, half)
            part_s[layer, 0, :, cols] = dot_nn(gb_s[...], w_out[:, cols]).astype(BF16)
            s1 += scatter_start(at, part_s.at[layer, 0], got_s, head_send.at[layer, 0], head_recv.at[layer, 0], half)
        hooks["rs1"]()
        hidden = x_s[at.mine].astype(F32) + scatter_sum(at, part_s.at[layer, 0], got_s, s1)
        h_s[...] = hidden
        n2_s[at.mine] = norm_rows(hidden, gain_ffn).astype(BF16)
        s2 = gather_start(at, n2_s, head_send.at[layer, 1], head_recv.at[layer, 1])
        save(h_s, 8)
        hooks["ag1"]()
        wait_recv(s2)
        hooks["n2"]()

        wait_weight(layer, 5)
        wait_weight(layer, 6)

        def up_chunk(at_row, size):
            cols = pl.ds(at_row, size)
            f = dot_nt(n2_s[...], w_gate[cols, :])
            v = dot_nt(n2_s[...], w_up[cols, :])
            f_s[:, cols] = f.astype(BF16)
            v_s[:, cols] = v.astype(BF16)
            t_s[:, cols] = (f * jax.nn.sigmoid(f) * v).astype(BF16)

        chunks(t_s.shape[1], 256, up_chunk)
        save(f_s, 9)
        save(v_s, 10)
        wait_weight(layer, 7)

        s3 = []
        for half in range(2):
            cols = half_cols(w_down, half)
            part_s[layer, 1, :, cols] = dot_nn(t_s[...], w_down[:, cols]).astype(BF16)
            s3 += scatter_start(at, part_s.at[layer, 1], got_s, head_send.at[layer, 2], head_recv.at[layer, 2], half)
        hooks["rs2"]()
        feed = scatter_sum(at, part_s.at[layer, 1], got_s, s3)
        xo_s[layer, at.mine] = jnp.where(my_valid, h_s[...] + feed, 0.0).astype(BF16)
        s4 = gather_start(at, xo_s.at[layer], head_send.at[layer, 3], head_recv.at[layer, 3])
        hooks["ag2"]()
        wait_recv(s4)
        for copy in keep:
            copy.wait()

        def finish():
            wait_send(s1 + s2 + s3 + s4)

            @pl.when(at.s + 1 < nz)
            def _():
                edge.wait_send()

            for k in range(1, nz):

                @pl.when(at.s + k < nz)
                def _(k=k):
                    state(k).wait_send()

        return finish

    def nothing():
        pass

    n2_copy = pltpu.make_async_copy(n2_s, gath_n2.at[at.s], io_sem.at[2])

    def n2_ready():
        n2_copy.start()
        ring_g.step(2)

    def f0_rs2():
        n2_copy.wait()
        ring_n.step(0)

    def f1_begin():
        upward(3, nz, ring_g.step)
        upward(0, nz - 1, ring_g.pair)
        ring_n.step(1)

    def f1_states():
        ring_n.pair(0)

    def f1_rs1():
        ring_n.step(2)

    def f1_n2():
        n2_last.start()
        upward(3, nz, ring_n.step)
        upward(1, nz - 1, ring_n.pair)

    x_copy.wait()
    finish_0 = layer_forward(
        0, x_s, dict(begin=nothing, states=nothing, rs1=lambda: ring_g.step(1), ag1=nothing, n2=n2_ready, rs2=f0_rs2, ag2=nothing)
    )
    finish_0()

    def out_copy(layer):
        near = pltpu.make_async_copy(xo_s.at[layer], x_out.at[at.sec], io_sem.at[3])
        far = remote(xo_s.at[layer], x_out.at[at.sec], x_send.at[9], x_recv.at[9], core)
        return near, far

    def send_out(layer):
        near, far = out_copy(layer)

        @pl.when(at.sec == layer)
        def _():
            near.start()

        @pl.when(at.sec != layer)
        def _():
            far.start()

    send_out(0)
    n2_last = pltpu.make_async_copy(n2_s, n2_out, io_sem.at[4])
    finish_1 = layer_forward(
        1, xo_s.at[0], dict(begin=f1_begin, states=f1_states, rs1=f1_rs1, ag1=nothing, n2=f1_n2, rs2=nothing, ag2=nothing)
    )
    send_out(1)
    finish_1()
    upward(0, nz - 1, ring_g.ready)
    upward(0, nz - 1, ring_n.ready)
    n2_last.wait()
    ring_g.drain()
    ring_n.drain()
    near, far = out_copy(0)
    near.wait()
    far.wait_send()
    far.wait_recv()
    small_swap.wait_send()
    for here in range(2):

        @pl.when(at.sec == here)
        def _(here=here):
            for i in range(8):
                swap(here, i).wait_send()
                stash(1 - here, i).wait()


def bwd_kernel(dims, *refs):
    nz, nh, rows, heads = dims
    take = taker(refs)
    lens, inputs_grad, small_own, small_other, tables = take(5)
    own = take(8)
    other = take(8)
    saved = [take(SAVED), take(SAVED)]
    gath_g1, gath_n2_0, n2_1 = take(3)
    ig_o, gains_o = take(2)
    att_o = take(2)
    ffn_o = take(3)
    gath_n2_1, gath_g0 = take(2)
    a_peer, a_land = take(2), take(2)
    wr_o = take(3)
    mats = take(5)
    keep_s = take(SAVED)
    (grad_s, part_s, got_s, dm_s, dh_s, dg_s, do_s, cx_s, dyx_s, ss, sr, st_s, da_s, db_s, dc_s, edge_s, dcat_s, ig_s) = take(18)
    gsum_s, gpeer_s, gtot_s, gz_s, gh_s = take(5)
    acc = take(3)
    wx_s = take(3)
    blk_n2, blk_g, n2t_s, gt_s = take(4)
    a_s, work_s = take(2), take(2)
    (w_sem, io_sem, keep_sem, e_send, e_recv, st_send, st_recv, head_send, head_recv, r_send, r_recv, p_send, p_recv) = take(13)
    (wx_send, wx_recv, ap_send, ap_recv, l_send, l_recv, x_send, x_recv, gz_send, gz_recv, gh_send, gh_recv) = take(12)
    x_s, n1_s, qk_s, u_s, o_s, yx_s, sin_s, gb_s, h_s, f_s, v_s = keep_s
    df_s, dv_s = f_s, v_s
    at = Place(lens, nz, nh, rows)
    cat, w_out, w_gate, w_up, w_down = mats
    d = n1_s.shape[1]
    width, qk = heads * HD, heads * FEAT
    block = d // nz
    core = (1 - at.sec, at.s, at.h)
    slots = weight_slots(*mats, qk, width)

    def weight_start(layer, i):
        @pl.when(at.sec == layer)
        def _():
            pltpu.make_async_copy(own[i].at[0], slots[i], w_sem.at[i]).start()

        @pl.when(at.sec != layer)
        def _():
            pltpu.make_async_copy(other[i].at[0], slots[i], w_sem.at[i]).start()

    def weight_wait(i):
        pltpu.make_async_copy(own[i].at[0], slots[i], w_sem.at[i]).wait()

    def keep_copy(layer, i):
        return pltpu.make_async_copy(saved[layer][i], keep_s[i], keep_sem.at[i])

    ring_n = Ring(at, n2_1, gath_n2_1, r_send.at[0], r_recv.at[0], p_send.at[0], p_recv.at[0])
    ring_g = Ring(at, ig_s.at[1], gath_g0, r_send.at[1], r_recv.at[1], p_send.at[1], p_recv.at[1])
    line = [
        [
            LineSum(
                at, a_s[g], a_peer[g].at[layer], a_land[g].at[layer], work_s[g], io_sem.at[4],
                l_send.at[layer, g], l_recv.at[layer, g], ap_recv.at[layer, g],
            )
            for g in range(2)
        ]
        for layer in range(2)
    ]

    def piece(layer, i):
        which = order(at, i)
        if isinstance(i, int) and i == 0:
            n2_src = n2_1 if layer == 1 else gath_n2_0.at[at.s]
            g_src = inputs_grad.at[at.sec] if layer == 1 else ig_s.at[1]
        else:
            n2_src = (gath_n2_1 if layer == 1 else gath_n2_0).at[which]
            g_src = (gath_g1 if layer == 1 else gath_g0).at[which]
        loads = [pltpu.make_async_copy(n2_src, blk_n2, io_sem.at[0]), pltpu.make_async_copy(g_src, blk_g, io_sem.at[1])]
        for copy in loads:
            copy.start()
        for copy in loads:
            copy.wait()
        pos = which * rows + lax.broadcasted_iota(jnp.int32, (rows, 1), 0)
        blk_g[...] = jnp.where(pos < at.tot, blk_g[...].astype(F32), 0.0).astype(BF16)
        for part in range(nz):

            @pl.when(at.s == part)
            def _(part=part):
                n2t_s[...] = blk_n2[:, part * block : (part + 1) * block].T
                gt_s[...] = blk_g[:, part * block : (part + 1) * block].T

        def hidden(at_row, size):
            cols = pl.ds(at_row, size)
            f = dot_nt(blk_n2[...], w_gate[cols, :])
            v = dot_nt(blk_n2[...], w_up[cols, :])
            dt = dot_nt(blk_g[...], w_down[cols, :])
            sig = jax.nn.sigmoid(f)
            act = f * sig
            t = (act * v).astype(BF16)
            df = (dt * v * (sig + act * (1.0 - sig))).astype(BF16)
            dv = (dt * act).astype(BF16)
            parts = (dot_nn(n2t_s[...], df), dot_nn(n2t_s[...], dv), dot_nn(gt_s[...], t))
            for total, new in zip(acc, parts):
                if isinstance(i, int) and i == 0:
                    total[:, cols] = new
                else:
                    total[:, cols] += new

        chunks(w_gate.shape[0], 640, hidden)

    def ffn_swap(i):
        return remote(wx_s[i], wr_o[i], wx_send.at[i], wx_recv.at[i], core)

    def ffn_send(layer):
        @pl.when(at.sec != layer)
        def _():
            for i in range(3):
                wx_s[i][...] = acc[i][...].astype(BF16)
                ffn_swap(i).start()

    def ffn_take(layer):
        @pl.when(at.sec == layer)
        def _():
            copies = []
            if layer == 0:
                for i in range(3):
                    ffn_swap(i).wait_send()
            loads = [pltpu.make_async_copy(wr_o[i], wx_s[i], io_sem.at[9 + i]) for i in range(3)]
            for i in range(3):
                ffn_swap(i).wait_recv()
                loads[i].start()
            for i in range(3):
                loads[i].wait()
                acc[i][...] += wx_s[i][...].astype(F32)
                copy = pltpu.make_async_copy(acc[i], ffn_o[i], io_sem.at[5 + i])
                copy.start()
                copies.append(copy)
            for copy in copies:
                copy.wait()

    def ig_copy(layer):
        near = pltpu.make_async_copy(ig_s.at[layer], ig_o.at[at.sec], io_sem.at[3])
        far = remote(ig_s.at[layer], ig_o.at[at.sec], x_send.at[0], x_recv.at[0], core)
        return near, far

    def ig_send(layer):
        near, far = ig_copy(layer)

        @pl.when(at.sec == layer)
        def _():
            near.start()

        @pl.when(at.sec != layer)
        def _():
            far.start()

    allowed = at.allowed()
    applies, tail, mine_last = at.applies(), at.tail(), at.last_seg(at.s)
    valid = at.pos() < at.tot
    lane = lax.broadcasted_iota(jnp.int32, (rows, LANES), 1)

    def line_core(layer, g):
        return 1 if layer == 1 or g == 1 else 0

    def peer_chunk(layer, g, i):
        return remote(a_s[g].at[i], a_peer[g].at[layer, i], ap_send.at[g, i], ap_recv.at[layer, g, i], core)

    def mixer_grads(layer, g):
        late = 2 * qk + width
        for i in range(nz):
            cols = slice(i * block, (i + 1) * block)
            if g == 0:
                a_s[0][i, :, 0:width] = dot_tn(n1_s[:, cols], dcat_s[:, late:]).astype(BF16)
                a_s[0][i, :, width:] = dot_tn(dm_s[:, cols], gb_s[...]).astype(BF16)
            else:
                a_s[1][i] = dot_tn(n1_s[:, cols], dcat_s[:, 0:late]).astype(BF16)

            @pl.when(at.sec != line_core(layer, g))
            def _(i=i):
                peer_chunk(layer, g, i).start()

    def mixer_sent(layer, g):
        for i in range(nz):

            @pl.when(at.sec != line_core(layer, g))
            def _(i=i):
                peer_chunk(layer, g, i).wait_send()

    def layer_backward(layer, hooks):
        small = jnp.where(at.sec == layer, small_own[...], small_other[...])
        gain_attn, gain_ffn, taps = small[0:1], small[1:2], small[2 : 2 + KW]
        hooks["begin"]()

        weight_wait(7)
        keep_copy(layer, 9).wait()
        keep_copy(layer, 10).wait()

        def down_chunk(at_row, size):
            cols = pl.ds(at_row, size)
            dt = dot_nt(grad_s[...], w_down[cols, :])
            f = f_s[:, cols].astype(F32)
            v = v_s[:, cols].astype(F32)
            sig = jax.nn.sigmoid(f)
            df_s[:, cols] = (dt * v * sig * (1.0 + f * (1.0 - sig))).astype(BF16)
            dv_s[:, cols] = (dt * f * sig).astype(BF16)

        chunks(df_s.shape[1], 256, down_chunk)
        weight_wait(5)
        weight_wait(6)

        s1 = []
        for half in range(2):
            cols = half_cols(w_up, half)
            part = dot_nn(df_s[...], w_gate[:, cols]) + dot_nn(dv_s[...], w_up[:, cols])
            part_s[:, cols] = part.astype(BF16)
            s1 += scatter_start(at, part_s, got_s, head_send.at[layer, 0], head_recv.at[layer, 0], half)
        hooks["rs1"]()
        keep_copy(layer, 8).wait()
        dn2 = scatter_sum(at, part_s, got_s, s1)
        back, gain_grad = norm_rows_back(h_s[...], gain_ffn, dn2)
        gsum_s[layer, 1:2, :] = gain_grad
        dh = grad_s[at.mine].astype(F32) + back
        dh_s[...] = dh
        dm_s[at.mine] = dh.astype(BF16)
        s2 = gather_start(at, dm_s, head_send.at[layer, 1], head_recv.at[layer, 1])
        for i in range(8):
            keep_copy(layer, i).wait()
        for i in (4, 0, 1, 2, 3):
            weight_wait(i)
        convolve(at, u_s, taps, do_s, cx_s, heads)
        a_low, b_low = qk_s[:, 0:qk], qk_s[:, qk : 2 * qk]
        hooks["ag1"]()
        wait_recv(s2)
        hooks["dm"]()

        def out_chunk(at_row, size):
            cols = pl.ds(at_row, size)
            dg_s[:, cols] = dot_nt(dm_s[...], w_out[cols, :])

        chunks(width, 256, out_chunk)
        for head in range(heads):
            cols = slice(head * HD, head * HD + LANES)
            gate, dg, yx = o_s[:, cols], dg_s[:, cols], yx_s[head]
            sig = jax.nn.sigmoid(gate)
            inverse = 1.0 / yx[:, HD : HD + 1]
            y = yx * inverse
            do_s[:, cols] = dg * y * sig * (1.0 + gate * (1.0 - sig))
            dy = jnp.where(lane < HD, dg * gate * sig, 0.0)
            dden = -jnp.sum(dy * y, axis=1, keepdims=True) * inverse
            dyx_s[head] = jnp.where(lane == HD, dden, dy * inverse).astype(BF16)
            one, two = lift_parts(a_low, tables, 1, head)
            psi = jnp.where(applies, one * two, 0.0).astype(BF16)
            ss[layer, head] = dot_tn(psi, dyx_s[head])[:PSI_SENT].astype(BF16)
        dcat_s[:, 2 * qk + width :] = do_s[:, :width].astype(BF16)

        def state(k):
            return remote(
                ss.at[layer], sr.at[layer, at.s], st_send.at[layer, k - 1], st_recv.at[layer, at.s],
                (at.sec, lax.rem(at.s + nz - k, nz), at.h),
            )

        for k in range(1, nz):

            @pl.when(at.s - k >= 0)
            def _(k=k):
                state(k).start()

        da_s[...] = jnp.zeros_like(da_s)
        db_s[...] = jnp.zeros_like(db_s)
        for head in range(heads):
            a_own, b_own = head_only(a_low, head), head_only(b_low, head)
            e = dot_nt(a_low, b_own)
            kern = jnp.where(allowed, 1.0 + e + 0.5 * e * e, 0.0).astype(BF16)
            dkern = dot_nt(dyx_s[head], cx_s[head])
            de = jnp.where(allowed, dkern * (1.0 + e), 0.0).astype(BF16)
            one, two = lift_parts(a_low, tables, 1, head)
            dpsi = jnp.where(applies, dot_nt(dyx_s[head], sin_s[head]), 0.0)
            pcols = slice(head * PSI, (head + 1) * PSI)
            da_s[...] += (
                dot_nn(de, b_own)
                + dot_nt((dpsi * two).astype(BF16), tables[0, :, pcols])
                + dot_nt((dpsi * one).astype(BF16), tables[1, :, pcols])
            )
            db_s[...] += dot_tn(de, a_own)
            yx_s[head] = dot_tn(kern, dyx_s[head])
        hooks["local"]()
        for j in range(1, nz):

            @pl.when(j > at.s)
            def _(j=j):
                remote(ss.at[layer], sr.at[layer, j], st_send.at[layer, 0], st_recv.at[layer, j], core).wait_recv()

        hooks["states"]()
        st_s[...] = jnp.zeros_like(st_s)
        for head in range(heads):
            total = jnp.zeros((PSI_SENT, LANES), F32)
            for j in range(1, nz):
                counts = (j > at.s) & (at.prior_seg(j) == mine_last)
                total = total + jnp.where(counts, sr[layer, j, head].astype(F32), 0.0)
            st_s[head, 0:PSI_SENT] = total.astype(BF16)
            one, two = lift_parts(b_low, tables, 2, head)
            psi = (one * two).astype(BF16)
            dpsi = jnp.where(tail, dot_nt(cx_s[head], st_s[head]), 0.0)
            pcols = slice(head * PSI, (head + 1) * PSI)
            db_s[...] += dot_nt((dpsi * two).astype(BF16), tables[0, :, pcols]) + dot_nt(
                (dpsi * one).astype(BF16), tables[2, :, pcols]
            )
            dc = yx_s[head] + jnp.where(tail, dot_nn(psi, st_s[head]), 0.0)
            dc_s[0:rows, head * HD : head * HD + LANES] = dc
        edge = remote(
            dc_s.at[pl.ds(0, 8)], edge_s.at[layer], e_send.at[layer], e_recv.at[layer],
            (at.sec, lax.rem(at.s + nz - 1, nz), at.h),
        )

        @pl.when(at.s > 0)
        def _():
            edge.start()

        dcat_s[:, 0:qk] = (da_s[...] * 0.5).astype(BF16)
        dcat_s[:, qk : 2 * qk] = (db_s[...] * 0.5).astype(BF16)
        gsum_s[layer, 2:8, :] = jnp.zeros((6, d), F32)
        for j in range(KW):
            product = dc_s[0:rows, :width] * u_s[8 - j : 8 - j + rows, :width]
            gsum_s[layer, 2 + j : 3 + j, :width] = jnp.sum(jnp.where(at.same(-j), product, 0.0), axis=0, keepdims=True)

        @pl.when(at.s + 1 < nz)
        def _():
            edge.wait_recv()

        dc_s[rows : rows + 8, :] = edge_s[layer]
        du = taps[0:1, :width] * dc_s[0:rows, :width]
        for j in range(1, KW):
            du = du + jnp.where(at.same(j), dc_s[j : j + rows, :width] * taps[j : j + 1, :width], 0.0)
        dcat_s[:, 2 * qk : 2 * qk + width] = du.astype(BF16)

        wait_send(s1)
        s3 = []
        for half in range(2):
            cols = half_cols(cat, half)
            part_s[:, cols] = dot_nn(dcat_s[...], cat[:, cols]).astype(BF16)
            s3 += scatter_start(at, part_s, got_s, head_send.at[layer, 2], head_recv.at[layer, 2], half)
        hooks["rs2"]()
        dn1 = scatter_sum(at, part_s, got_s, s3)
        back, gain_grad = norm_rows_back(x_s[...].astype(F32), gain_attn, dn1)
        gsum_s[layer, 0:1, :] = gain_grad
        ig_s[layer, at.mine] = (dh_s[...] + back).astype(BF16)
        s4 = gather_start(at, ig_s.at[layer], head_send.at[layer, 3], head_recv.at[layer, 3])
        hooks["ag2"]()
        wait_recv(s4)
        ig_send(layer)
        wait_send(s3)

        def finish():
            wait_send(s2 + s4)

            @pl.when(at.s > 0)
            def _():
                edge.wait_send()

            for k in range(1, nz):

                @pl.when(at.s - k >= 0)
                def _(k=k):
                    state(k).wait_send()

        return finish

    def owner(layer, what):
        @pl.when(at.sec == layer)
        def _():
            what()

    g_copy = pltpu.make_async_copy(inputs_grad.at[at.sec], grad_s, io_sem.at[2])
    g_copy.start()
    for i in (7, 5, 6, 4, 0, 1, 2, 3):
        weight_start(1, i)
    for i in (9, 10, 8, 3, 2, 4, 5, 6, 7, 1, 0):
        keep_copy(1, i).start()
    at.barrier(True, True, True)
    ring_n.step(0)
    g_copy.wait()
    grad_s[...] = jnp.where(valid, grad_s[...].astype(F32), 0.0).astype(BF16)

    def slot(layer, g, i):
        owner(line_core(layer, g), lambda: line[layer][g].slot(i))

    def far_sum(g):
        return remote(work_s[g].at[0], att_o[g], x_send.at[2], x_recv.at[2], core)

    def line_last(layer, g):
        def go():
            upward(3, nz - 1, line[layer][g].slot)
            line[layer][g].last()
            if line_core(layer, g) == layer:
                copy = pltpu.make_async_copy(work_s[g].at[0], att_o[g], io_sem.at[8])
                copy.start()
                copy.wait()
            else:
                far_sum(g).start()

        owner(line_core(layer, g), go)

    def pieces(layer, ring, begin, end):
        def one(k):
            ring.ready(k - 1)
            piece(layer, k)

        upward(begin, end, one)

    def spread(ring):
        upward(3, nz, ring.step)
        upward(1, nz - 1, ring.pair)

    def nothing():
        pass

    def b1_rs1():
        ring_n.step(1)
        ring_n.pair(0)
        piece(1, 0)

    def b1_ag1():
        ring_n.step(2)
        pieces(1, ring_n, 1, 2)

    def b1_local():
        mixer_grads(1, 0)

    def b1_rs2():
        mixer_grads(1, 1)
        slot(1, 0, 0)
        pieces(1, ring_n, 2, 3)

    def b1_ag2():
        for i in (4, 0, 1, 2, 3):
            weight_start(0, i)
        for i in (9, 10, 8, 3, 2, 4, 5, 6, 7, 1, 0):
            keep_copy(0, i).start()
        slot(1, 0, 1)
        slot(1, 1, 0)
        pieces(1, ring_n, 3, nz)
        for i in (7, 5, 6):
            weight_start(0, i)
        ffn_send(1)

    finish_1 = layer_backward(
        1,
        dict(
            begin=nothing, rs1=b1_rs1, ag1=b1_ag1, dm=lambda: spread(ring_n), local=b1_local,
            states=nothing, rs2=b1_rs2, ag2=b1_ag2,
        ),
    )
    finish_1()
    grad_s[...] = jnp.where(valid, ig_s[1].astype(F32), 0.0).astype(BF16)

    def b0_begin():
        ring_g.step(0)
        slot(1, 0, 2)
        slot(1, 1, 1)

    def b0_rs1():
        ffn_take(1)
        ring_g.step(1)
        ring_g.pair(0)
        piece(0, 0)

    def b0_ag1():
        ring_g.step(2)
        slot(1, 1, 2)
        pieces(0, ring_g, 1, 2)

    def b0_local():
        line_last(1, 0)
        mixer_sent(1, 0)
        mixer_grads(0, 0)

    def b0_states():
        line_last(1, 1)

    def b0_rs2():
        mixer_sent(1, 1)
        mixer_grads(0, 1)
        slot(0, 0, 0)
        pieces(0, ring_g, 2, 3)

    def b0_ag2():
        slot(0, 0, 1)
        slot(0, 1, 0)
        pieces(0, ring_g, 3, nz)
        ffn_send(0)

    finish_0 = layer_backward(
        0,
        dict(
            begin=b0_begin, rs1=b0_rs1, ag1=b0_ag1, dm=lambda: spread(ring_g), local=b0_local,
            states=b0_states, rs2=b0_rs2, ag2=b0_ag2,
        ),
    )

    gain_swap = remote(gsum_s.at[1 - at.sec], gpeer_s, x_send.at[1], x_recv.at[1], core)
    gain_swap.start()

    slot(0, 0, 2)
    slot(0, 1, 1)
    slot(0, 1, 2)
    gain_swap.wait_recv()
    gtot_s[0] = gsum_s[at.sec] + gpeer_s[...]

    def gain_seq(k):
        to = lax.rem(at.s + k, nz)
        return remote(gtot_s.at[0], gz_s.at[k - 1], gz_send.at[k - 1], gz_recv.at[k - 1], (at.sec, to, at.h))

    for k in range(1, nz):
        gain_seq(k).start()
    line_last(0, 1)
    line_last(0, 0)
    for k in range(1, nz):
        gain_seq(k).wait_recv()
    total = gtot_s[0]
    for k in range(1, nz):
        total = total + gz_s[k - 1]
    gtot_s[1] = total

    def gain_head(m):
        return remote(gtot_s.at[1], gh_s.at[m - 1], gh_send.at[m - 1], gh_recv.at[m - 1], (at.sec, at.s, at.h ^ m))

    for m in range(1, nh):
        gain_head(m).start()
    ffn_take(0)
    mixer_sent(0, 0)
    mixer_sent(0, 1)
    owner(0, lambda: far_sum(1).wait_recv())
    owner(1, lambda: far_sum(1).wait_send())
    for m in range(1, nh):
        gain_head(m).wait_recv()
    total = gtot_s[1, 0:2]
    for m in range(1, nh):
        total = total + gh_s[m - 1, 0:2]
    gains_o[...] = gtot_s[1]
    gains_o[0:2, :] = total

    finish_0()
    ring_n.drain()
    ring_g.drain()
    gain_swap.wait_send()
    for k in range(1, nz):
        gain_seq(k).wait_send()
    for m in range(1, nh):
        gain_head(m).wait_send()
    owner(1, lambda: wait_send([ffn_swap(i) for i in range(3)]))
    near, far = ig_copy(0)
    near.wait()
    far.wait_send()
    far.wait_recv()


def final_kernel(qk, width, *refs):
    take = taker(refs)
    whole, (early, late), out, parts, (sems,) = take(5), take(2), take(5), take(5), take(1)
    copies = [pltpu.make_async_copy(a, b, sems.at[i]) for i, (a, b) in enumerate(zip(whole, out))]
    for copy in copies:
        copy.start()
    g_q, g_k, g_v, g_o, g_out = parts
    turned = late[:, 0 : 2 * qk].astype(F32).T
    g_q[...] = turned[0:qk]
    g_k[...] = turned[qk : 2 * qk]
    g_v[...] = late[:, 2 * qk :].astype(F32)
    g_o[...] = early[:, 0:width].astype(F32)
    g_out[...] = early[:, width:].astype(F32).T
    for copy in copies:
        copy.wait()


def shape(dims, kind=BF16):
    return jax.ShapeDtypeStruct(tuple(dims), kind)


ANY = pl.BlockSpec(memory_space=pl.ANY)
VM = pl.BlockSpec(memory_space=pltpu.VMEM)
SM = pl.BlockSpec(memory_space=pltpu.SMEM)
DMA = pltpu.SemaphoreType.DMA


def params(number):
    return pltpu.CompilerParams(collective_id=number, has_side_effects=True, vmem_limit_bytes=VMEM_LIMIT)


def shards(nz, nh, inputs, out_grad, lengths, norm_attn, norm_ffn, w_query, w_key, w_value, w_output_gate, conv_kernel, w_out, w_gate, w_up, w_down):
    micro, rows, d = inputs.shape
    heads = w_query.shape[2] // FEAT
    width, qk, ff = w_value.shape[2], w_query.shape[2], w_gate.shape[2]
    part, block = rows // nh, d // nz
    dims = (nz, nh, rows, heads)
    wide = -(-((heads - 1) * HD + LANES) // LANES) * LANES
    groups = (2 * width, 2 * qk + width)
    tables = jnp.asarray(lift_tables(heads), BF16)
    turned = [jnp.swapaxes(w, 1, 2) for w in (w_query, w_key, w_value, w_output_gate)]
    own = (*turned, w_out, jnp.swapaxes(w_gate, 1, 2), jnp.swapaxes(w_up, 1, 2), w_down)
    small_own = jnp.concatenate(
        [norm_attn, norm_ffn, jnp.pad(conv_kernel[0], ((0, 0), (0, d - width))), jnp.zeros((3, d), F32)]
    )

    def vm(dims, kind=BF16):
        return pltpu.VMEM(tuple(dims), kind)

    mats = [vm((2 * qk + 2 * width, d)), vm((width, d)), vm((ff, d)), vm((ff, d)), vm((ff, d))]
    act = vm((rows, d))
    kept = [
        ((part, d), BF16),
        ((rows, d), BF16),
        ((rows, 2 * qk), BF16),
        ((rows + 8, wide), F32),
        ((rows, wide), F32),
        ((heads, rows, LANES), F32),
        ((heads, PSI, LANES), BF16),
        ((rows, width), BF16),
        ((part, d), F32),
        ((rows, ff), BF16),
        ((rows, ff), BF16),
    ]
    keep_shapes = [shape(*k) for k in kept]
    gathered = shape((nz, rows, d))
    outs = (
        [shape((8, d), F32)]
        + [shape(w.shape) for w in own]
        + keep_shapes * 2
        + [shape((micro, rows, d)), gathered, gathered, shape((rows, d))]
    )
    scratch = (
        mats
        + mats
        + [
            act,
            act,
            act,
            vm((rows, 2 * qk)),
            vm((rows + 8, wide), F32),
            vm((2, 8, wide), F32),
            vm((rows, wide), F32),
            vm((rows, wide), F32),
            vm((heads, rows, LANES)),
            vm((heads, rows, LANES), F32),
            vm((2, heads, PSI_SENT, LANES)),
            vm((2, nz, heads, PSI_SENT, LANES)),
            vm((heads, PSI, LANES)),
            vm((rows, wide), F32),
            vm((rows, width)),
            vm((2, 2, rows, d)),
            vm((nh - 1, part, d)),
            vm((rows, ff)),
            vm((rows, ff)),
            vm((rows, ff)),
            vm((2, rows, d)),
            vm((part, d), F32),
            vm((8, d), F32),
            DMA((16,)),
            DMA((5,)),
            DMA((SAVED,)),
            DMA((10,)),
            DMA((10,)),
            DMA((2,)),
            DMA((2,)),
            DMA((2, nz)),
            DMA((2, nz)),
            DMA((2, 4, 2 * (nh - 1))),
            DMA((2, 4, 2 * (nh - 1))),
            DMA((2, 2, nz - 1, 2)),
            DMA((2, 2, nz - 1, 2)),
            DMA((2, 2, nz - 1, 2)),
            DMA((2, 2, nz - 1, 2)),
        ]
    )
    first = pl.pallas_call(
        functools.partial(fwd_kernel, dims),
        out_shape=outs,
        in_specs=[SM, ANY, ANY, VM, VM] + [ANY] * 8,
        out_specs=[ANY] * len(outs),
        scratch_shapes=scratch,
        compiler_params=params(0),
    )(lengths, inputs, out_grad, small_own, tables, *own)
    small_other, other = first[0], first[1:9]
    saved = first[9 : 9 + 2 * SAVED]
    section_out, gath_g1, gath_n2_0, n2_1 = first[9 + 2 * SAVED :]

    outs = (
        [shape((micro, rows, d)), shape((8, d), F32)]
        + [shape((block, g)) for g in groups]
        + [shape((block, ff), F32)] * 3
        + [gathered, gathered]
        + [shape((2, nz, block, g)) for g in groups]
        + [shape((2, 2, nz, block, g)) for g in groups]
        + [shape((block, ff))] * 3
    )
    out_specs = [ANY, VM] + [ANY] * (len(outs) - 2)
    scratch = (
        mats
        + [vm(*k) for k in kept]
        + [
            act,
            act,
            vm((nh - 1, part, d)),
            act,
            vm((part, d), F32),
            vm((rows, wide), F32),
            vm((rows, wide), F32),
            vm((heads, rows, LANES)),
            vm((heads, rows, LANES)),
            vm((2, heads, PSI_SENT, LANES)),
            vm((2, nz, heads, PSI_SENT, LANES)),
            vm((heads, PSI, LANES)),
            vm((rows, qk), F32),
            vm((rows, qk), F32),
            vm((rows + 8, wide), F32),
            vm((2, 8, wide), F32),
            vm((rows, 2 * qk + 2 * width)),
            vm((2, rows, d)),
            vm((2, 8, d), F32),
            vm((8, d), F32),
            vm((2, 8, d), F32),
            vm((nz - 1, 8, d), F32),
            vm((nh - 1, 8, d), F32),
        ]
        + [vm((block, ff), F32)] * 3
        + [vm((block, ff))] * 3
        + [act, act, vm((block, rows)), vm((block, rows))]
        + [vm((nz, block, g)) for g in groups]
        + [vm((3, block, g)) for g in groups]
        + [
            DMA((8,)),
            DMA((12,)),
            DMA((SAVED,)),
            DMA((2,)),
            DMA((2,)),
            DMA((2, nz)),
            DMA((2, nz)),
            DMA((2, 4, 2 * (nh - 1))),
            DMA((2, 4, 2 * (nh - 1))),
            DMA((2, 2, nz - 1, 2)),
            DMA((2, 2, nz - 1, 2)),
            DMA((2, 2, nz - 1, 2)),
            DMA((2, 2, nz - 1, 2)),
            DMA((3,)),
            DMA((3,)),
            DMA((2, nz)),
            DMA((2, 2, nz)),
            DMA((2, 2, 2, nz)),
            DMA((2, 2, 2, nz)),
            DMA((3,)),
            DMA((3,)),
            DMA((nz - 1,)),
            DMA((nz - 1,)),
            DMA((nh - 1,)),
            DMA((nh - 1,)),
        ]
    )
    second = pl.pallas_call(
        functools.partial(bwd_kernel, dims),
        out_shape=outs,
        in_specs=[SM, ANY, VM, VM, VM] + [ANY] * (16 + 2 * SAVED + 3),
        out_specs=out_specs,
        scratch_shapes=scratch,
        compiler_params=params(1),
    )(lengths, out_grad, small_own, small_other, tables, *own, *other, *saved, gath_g1, gath_n2_0, n2_1)
    input_grad, gains, att_early, att_late, g_gate, g_up, g_down = second[:7]
    finals = [
        shape((micro, rows, d)),
        shape((micro, rows, d)),
        shape((block, ff), F32),
        shape((block, ff), F32),
        shape((block, ff), F32),
        shape((qk, block), F32),
        shape((qk, block), F32),
        shape((block, width), F32),
        shape((block, width), F32),
        shape((width, block), F32),
    ]
    section_out, input_grad, g_gate, g_up, g_down, g_q, g_k, g_v, g_o, g_out = pl.pallas_call(
        functools.partial(final_kernel, qk, width),
        out_shape=finals,
        in_specs=[ANY] * 5 + [VM] * 2,
        out_specs=[ANY] * 5 + [VM] * 5,
        scratch_shapes=[DMA((5,))],
        compiler_params=pltpu.CompilerParams(vmem_limit_bytes=VMEM_LIMIT),
    )(section_out, input_grad, g_gate, g_up, g_down, att_early, att_late)
    return (
        section_out[None],
        input_grad[None],
        gains[0:1],
        gains[1:2],
        g_q.T[None],
        g_k.T[None],
        g_v[None],
        g_o[None],
        gains[None, 2 : 2 + KW, :width],
        g_out[None],
        g_gate[None],
        g_up[None],
        g_down.T[None],
    )


def solution(mesh):
    return jax.shard_map(
        functools.partial(shards, mesh.shape["seq"], mesh.shape["head"]),
        mesh=mesh,
        in_specs=(
            P(None, "seq", None),
            P(None, "seq", None),
            P(),
            P("section", None),
            P("section", None),
            P("section", None, "head"),
            P("section", None, "head"),
            P("section", None, "head"),
            P("section", None, "head"),
            P("section", None, "head"),
            P("section", "head", None),
            P("section", None, "head"),
            P("section", None, "head"),
            P("section", "head", None),
        ),
        out_specs=(
            P("section", None, "seq", None),
            P("section", None, "seq", None),
            P("section", None),
            P("section", None),
            P("section", "seq", "head"),
            P("section", "seq", "head"),
            P("section", "seq", "head"),
            P("section", "seq", "head"),
            P("section", None, "head"),
            P("section", "head", "seq"),
            P("section", "seq", "head"),
            P("section", "seq", "head"),
            P("section", "head", "seq"),
        ),
        check_vma=False,
    )
```

```python
import functools

import jax
import jax.numpy as jnp
import numpy as np
from jax import lax
from jax.experimental import pallas as pl
from jax.experimental.pallas import tpu as pltpu
from jax.sharding import PartitionSpec as P

HD = 112
FEAT = 16
KW = 3
EPS = 1e-05
LANES = 128
PSI = 256
PSI_SENT = 160
MESH = pl.DeviceIdType.MESH
F32 = jnp.float32
BF16 = jnp.bfloat16
VMEM_LIMIT = 62 << 20


def dot_nn(a, b):
    return lax.dot_general(a, b, (((1,), (0,)), ((), ())), preferred_element_type=F32)


def dot_nt(a, b):
    return lax.dot_general(a, b, (((1,), (1,)), ((), ())), preferred_element_type=F32)


def dot_tn(a, b):
    return lax.dot_general(a, b, (((0,), (0,)), ((), ())), preferred_element_type=F32)


def chunks(total, step, body):
    whole = total // step
    if whole > 1:

        def one(i, carry):
            body(pl.multiple_of(i * step, step), step)
            return carry

        lax.fori_loop(0, whole, one, 0)
    elif whole == 1:
        body(0, step)
    if total % step:
        body(whole * step, total % step)


def lift_tables(heads):
    first = np.zeros((heads * FEAT, heads * PSI), np.float32)
    second = np.zeros_like(first)
    second_key = np.zeros_like(first)
    for head in range(heads):
        row, col = head * FEAT, head * PSI
        for i in range(FEAT):
            first[row + i, col + 1 + i] = 1.0
        at = 1 + FEAT
        for i in range(FEAT):
            for j in range(i, FEAT):
                first[row + i, col + at] = 1.0
                second[row + j, col + at] = 1.0
                second_key[row + j, col + at] = 0.5 if i == j else 1.0
                at += 1
    return np.stack([first, second, second_key])


class Place:
    def __init__(self, lens, nz, nh, rows):
        self.sec, self.s, self.h = (lax.axis_index(a) for a in ("section", "seq", "head"))
        self.nz, self.nh, self.rows = nz, nh, rows
        self.l0 = lens[self.sec, 0]
        self.tot = self.l0 + lens[self.sec, 1]
        self.first = self.s * rows
        self.part = rows // nh
        self.mine = pl.ds(pl.multiple_of(self.h * self.part, self.part), self.part)

    def seg(self, pos):
        inside = (pos >= self.l0).astype(jnp.int32) + (pos >= self.tot).astype(jnp.int32)
        return jnp.where(pos >= 0, inside, -1)

    def pos(self, shift=0):
        return self.first + shift + lax.broadcasted_iota(jnp.int32, (self.rows, 1), 0)

    def same(self, shift):
        other = self.pos(shift)
        inside = other < self.nz * self.rows
        return (self.seg(other) == self.seg(self.pos())) & inside

    def allowed(self):
        shape = (self.rows, self.rows)
        row = lax.broadcasted_iota(jnp.int32, shape, 0)
        col = lax.broadcasted_iota(jnp.int32, shape, 1)
        return (col <= row) & (self.seg(self.first + col) == self.seg(self.first + row))

    def last_seg(self, block):
        return self.seg(block * self.rows + self.rows - 1)

    def prior_seg(self, block):
        return self.seg(block * self.rows - 1)

    def applies(self):
        return self.seg(self.pos()) == self.prior_seg(self.s)

    def tail(self):
        return self.seg(self.pos()) == self.last_seg(self.s)

    def peers(self):
        core = [(1 - self.sec, self.s, self.h)]
        seq = [(self.sec, (self.s + k) % self.nz, self.h) for k in range(1, self.nz)]
        head = [(self.sec, self.s, self.h ^ m) for m in range(1, self.nh)]
        return core, seq, head

    def barrier(self, core, seq, head):
        groups = self.peers()
        told = [d for use, g in zip((core, seq, head), groups) if use for d in g]
        sem = pltpu.get_barrier_semaphore()
        for device in told:
            pl.semaphore_signal(sem, 1, device_id=device, device_id_type=MESH)
        pl.semaphore_wait(sem, len(told))


def remote(src, dst, send, recv, device):
    return pltpu.make_async_remote_copy(
        src_ref=src, dst_ref=dst, send_sem=send, recv_sem=recv, device_id=device, device_id_type=MESH
    )


def half_cols(buf, half):
    size = buf.shape[-1] // 2
    return pl.ds(half * size, size)


def scatter_start(at, buf, got, send, recv, half):
    sent = []
    cols = half_cols(buf, half)
    for m in sorted(range(1, at.nh), reverse=True):
        peer = at.h ^ m
        rows = pl.ds(pl.multiple_of(peer * at.part, at.part), at.part)
        sem = half * (at.nh - 1) + m - 1
        copy = remote(
            buf.at[rows, cols], got.at[m - 1, :, cols], send.at[sem], recv.at[sem], (at.sec, at.s, peer)
        )
        copy.start()
        sent.append(copy)
    return sent


def scatter_sum(at, buf, got, sent):
    total = buf[at.mine].astype(F32)
    for copy in sent:
        copy.wait_recv()
    for m in range(1, at.nh):
        total = total + got[m - 1].astype(F32)
    return total


def gather_start(at, buf, send, recv):
    sent = []
    for m in sorted(range(1, at.nh), reverse=True):
        copy = remote(
            buf.at[at.mine], buf.at[at.mine], send.at[m - 1], recv.at[m - 1], (at.sec, at.s, at.h ^ m)
        )
        copy.start()
        sent.append(copy)
    return sent


def wait_recv(copies):
    for copy in copies:
        copy.wait_recv()


def wait_send(copies):
    for copy in copies:
        copy.wait_send()


def norm_rows(x, gain):
    return x * lax.rsqrt(jnp.mean(x * x, axis=-1, keepdims=True) + EPS) * gain


def norm_rows_back(x, gain, grad):
    inverse = lax.rsqrt(jnp.mean(x * x, axis=-1, keepdims=True) + EPS)
    unit = x * inverse
    scaled = grad * gain
    back = inverse * (scaled - unit * jnp.mean(scaled * unit, axis=-1, keepdims=True))
    return back, jnp.sum(grad * unit, axis=0, keepdims=True)


def lift_parts(low, tables, second, head):
    cols = slice(head * PSI, (head + 1) * PSI)
    lane = lax.broadcasted_iota(jnp.int32, (1, PSI), 1)
    one = dot_nn(low, tables[0, :, cols]) + (lane == 0).astype(F32)
    two = dot_nn(low, tables[second, :, cols]) + (lane <= FEAT).astype(F32)
    return one, two


def head_only(low, head):
    lane = lax.broadcasted_iota(jnp.int32, low.shape, 1)
    return jnp.where((lane >= head * FEAT) & (lane < (head + 1) * FEAT), low, jnp.zeros_like(low))


def convolve(at, u_s, taps, c_s, cx_s, heads):
    rows, width = at.rows, heads * HD
    out = taps[0:1, :width] * u_s[8 : 8 + rows, :width]
    for j in range(1, KW):
        shifted = u_s[8 - j : 8 - j + rows, :width]
        out = out + jnp.where(at.same(-j), shifted * taps[j : j + 1, :width], 0.0)
    c_s[0:rows, :width] = out
    lane = lax.broadcasted_iota(jnp.int32, (rows, LANES), 1)
    for head in range(heads):
        one = c_s[0:rows, head * HD : head * HD + LANES]
        cx_s[head] = jnp.where(lane < HD, one, jnp.where(lane == HD, 1.0, 0.0)).astype(BF16)


def order(at, i):
    left, right = at.s, at.nz - 1 - at.s
    both = 2 * jnp.minimum(left, right)
    near = i <= both
    dist = jnp.where(near, (i + 1) // 2, i - both // 2)
    leftward = jnp.where(near, i % 2 == 1, left > right)
    return jnp.where(leftward, at.s - dist, at.s + dist)


class Ring:
    def __init__(self, at, src, dst, send, recv, pair_send, pair_recv):
        self.at, self.src, self.dst, self.send, self.recv = at, src, dst, send, recv
        self.pair_send, self.pair_recv = pair_send, pair_recv

    def _view(self, c):
        at = self.at
        rows, cols = at.rows // 2, self.dst.shape[-1] // 2
        bit = lax.rem(at.h // (1 << c), 2)
        return pl.ds(pl.multiple_of(bit * rows, rows), rows), pl.ds(c * cols, cols)

    def _ways(self, k):
        at = self.at
        right = (at.s - k, at.s - k >= 0, at.s + 1 < at.nz, lax.rem(at.s + 1, at.nz))
        left = (at.s + k, at.s + k < at.nz, at.s > 0, lax.rem(at.s + at.nz - 1, at.nz))
        return right, left

    def _copies(self, way, k, block, to, first):
        at = self.at
        for c in range(2):
            rows, cols = self._view(c)
            src = self.src.at[rows, cols] if first else self.dst.at[block, rows, cols]
            yield remote(
                src, self.dst.at[block, rows, cols], self.send.at[way, k, c], self.recv.at[way, k, c], (at.sec, to, at.h)
            )

    def _pairs(self, way, k, block):
        at = self.at
        for c in range(2):
            rows, cols = self._view(c)
            view = self.dst.at[block, rows, cols]
            yield remote(view, view, self.pair_send.at[way, k, c], self.pair_recv.at[way, k, c], (at.sec, at.s, at.h ^ (1 << c)))

    def step(self, k):
        at = self.at
        first = isinstance(k, int) and k == 0
        for way, (block, there, onward, to) in enumerate(self._ways(k)):
            if not first:

                @pl.when(there)
                def _(way=way, block=block, to=to):
                    wait_recv(self._copies(way, k - 1, block, to, False))

            if not isinstance(k, int) or k < at.nz - 1:

                @pl.when(there & onward & (k < at.nz - 1))
                def _(way=way, block=block, to=to):
                    for copy in self._copies(way, k, block, to, first):
                        copy.start()

    def pair(self, k):
        for way, (block, there, _, _) in enumerate(self._ways(k + 1)):

            @pl.when(there)
            def _(way=way, block=block):
                for copy in self._pairs(way, k, block):
                    copy.start()

    def ready(self, k):
        for way, (block, there, _, _) in enumerate(self._ways(k + 1)):

            @pl.when(there)
            def _(way=way, block=block):
                wait_recv(self._pairs(way, k, block))

    def drain(self, line=True, pairs=True):
        def one(k, carry):
            for way, (_, there, onward, to) in enumerate(self._ways(k) if line else ()):

                @pl.when(there & onward)
                def _(way=way, to=to):
                    wait_send(self._copies(way, k, self.at.s, to, False))

            for way, (_, there, _, _) in enumerate(self._ways(k + 1) if pairs else ()):

                @pl.when(there)
                def _(way=way):
                    wait_send(self._pairs(way, k, self.at.s))

            return carry

        lax.fori_loop(0, self.at.nz - 1, one, 0)


def upward(begin, end, body):
    if end > begin:

        def one(k, carry):
            body(k)
            return carry

        lax.fori_loop(begin, end, one, 0)


class LineSum:
    def __init__(self, at, mine, peer, land, work, io, send, recv, peer_recv):
        self.at, self.mine, self.peer, self.land, self.work = at, mine, peer, land, work
        self.io, self.send, self.recv, self.peer_recv = io, send, recv, peer_recv

    def _hop(self, way, d):
        at = self.at
        to = lax.rem(at.s + (1 if way == 0 else at.nz - 1), at.nz)
        return remote(self.work.at[way], self.land.at[way, d], self.send.at[way, d], self.recv.at[way, d], (at.sec, to, at.h))

    def _load(self, src, slot):
        copy = pltpu.make_async_copy(src, self.work.at[slot], self.io)
        copy.start()
        copy.wait()

    def _add(self, slot, src):
        self._load(src, 2)
        self.work[slot] = (self.work[slot].astype(F32) + self.work[2].astype(F32)).astype(BF16)

    def _own(self, slot, d):
        at = self.at
        remote(self.mine.at[d], self.peer.at[d], self.peer_recv.at[d], self.peer_recv.at[d], (1 - at.sec, at.s, at.h)).wait_recv()
        self._load(self.peer.at[d], 2)
        self.work[slot] = (self.mine[d].astype(F32) + self.work[2].astype(F32)).astype(BF16)

    def slot(self, i):
        at = self.at
        for way in range(2):
            begun = i - at.s if way == 0 else i - (at.nz - 1 - at.s)
            d = at.nz - 1 - begun if way == 0 else begun
            earlier = at.s > 0 if way == 0 else at.s < at.nz - 1

            @pl.when((begun >= 0) & (i < at.nz - 1))
            def _(way=way, d=d, begun=begun, earlier=earlier):
                @pl.when(begun > 0)
                def _():
                    self._hop(way, d + 1 if way == 0 else d - 1).wait_send()

                self._own(way, d)

                @pl.when(earlier)
                def _():
                    self._hop(way, d).wait_recv()
                    self._add(way, self.land.at[way, d])

                self._hop(way, d).start()

    def last(self):
        at = self.at

        @pl.when(at.s < at.nz - 1)
        def _():
            self._hop(0, at.s + 1).wait_send()

        @pl.when(at.s > 0)
        def _():
            self._hop(1, at.s - 1).wait_send()

        self._own(0, at.s)

        @pl.when(at.s > 0)
        def _():
            self._hop(0, at.s).wait_recv()
            self._add(0, self.land.at[0, at.s])

        @pl.when(at.s < at.nz - 1)
        def _():
            self._hop(1, at.s).wait_recv()
            self._add(0, self.land.at[1, at.s])


def taker(refs):
    refs = list(refs)

    def take(n):
        out = refs[:n]
        del refs[:n]
        return out

    return take


def weight_slots(cat, out, gate, up, down, qk, width):
    at_row, views = 0, []
    for size in (qk, qk, width, width):
        views.append(cat.at[pl.ds(at_row, size)])
        at_row += size
    return views + [out, gate, up, down]


SAVED = 11


def fwd_kernel(dims, *refs):
    nz, nh, rows, heads = dims
    take = taker(refs)
    lens, inputs, out_grad, small_own, tables = take(5)
    own = take(8)
    small_other = take(1)[0]
    other = take(8)
    saved = [take(SAVED), take(SAVED)]
    x_out, gath_g1, gath_n2, n2_out = take(4)
    mats = [take(5), take(5)]
    (x_s, n1_s, n2_s, qk_s, u_s, edge_s, o_s, c_s, cx_s, yx_s, ss, sr, sin_s, g_s, gb_s, part_s, got_s, f_s, v_s, t_s, xo_s, h_s, sm_s) = take(23)
    w_sem, io_sem, save_sem, x_send, x_recv, e_send, e_recv, st_send, st_recv, head_send, head_recv = take(11)
    r_send, r_recv, p_send, p_recv = take(4)
    at = Place(lens, nz, nh, rows)
    d = x_s.shape[1]
    width, qk = heads * HD, heads * FEAT
    core = (1 - at.sec, at.s, at.h)
    slots = [weight_slots(*m, qk, width) for m in mats]

    x_copy = pltpu.make_async_copy(inputs.at[at.sec], x_s, io_sem.at[0])
    x_copy.start()

    def local(layer, i):
        return pltpu.make_async_copy(own[i].at[0], slots[layer][i], w_sem.at[i])

    def swap(layer, i):
        return remote(own[i].at[0], slots[layer][i], x_send.at[i], x_recv.at[i], core)

    def stash(layer, i):
        return pltpu.make_async_copy(slots[layer][i], other[i].at[0], w_sem.at[8 + i])

    for here in range(2):

        @pl.when(at.sec == here)
        def _(here=here):
            for i in (2, 0, 1, 3, 4, 5, 6, 7):
                local(here, i).start()

    at.barrier(True, True, True)
    small_swap = remote(small_own, small_other, x_send.at[8], x_recv.at[8], core)
    small_swap.start()
    for here in range(2):

        @pl.when(at.sec == here)
        def _(here=here):
            for i in (2, 0, 1, 3, 4, 5, 6, 7):
                swap(here, i).start()

    ring_g = Ring(at, out_grad.at[at.sec], gath_g1, r_send.at[0], r_recv.at[0], p_send.at[0], p_recv.at[0])
    ring_n = Ring(at, gath_n2.at[at.s], gath_n2, r_send.at[1], r_recv.at[1], p_send.at[1], p_recv.at[1])
    small_swap.wait_recv()
    small_copy = pltpu.make_async_copy(small_other, sm_s, io_sem.at[1])
    small_copy.start()
    small_copy.wait()

    def wait_weight(layer, i):
        @pl.when(at.sec == layer)
        def _():
            local(layer, i).wait()

        @pl.when(at.sec != layer)
        def _():
            swap(layer, i).wait_recv()
            stash(layer, i).start()

    allowed = at.allowed()
    applies, tail, prior = at.applies(), at.tail(), at.prior_seg(at.s)
    my_pos = at.first + at.h * at.part + lax.broadcasted_iota(jnp.int32, (at.part, 1), 0)
    my_valid = my_pos < at.tot

    def layer_forward(layer, x_s, hooks):
        cat, w_out, w_gate, w_up, w_down = mats[layer]
        small = jnp.where(at.sec == layer, small_own[...], sm_s[...])
        gain_attn, gain_ffn, taps = small[0:1], small[1:2], small[2 : 2 + KW]
        keep = []

        def save(src, i):
            copy = pltpu.make_async_copy(src, saved[layer][i], save_sem.at[i])
            copy.start()
            keep.append(copy)

        hooks["begin"]()
        n1_s[...] = norm_rows(x_s[...].astype(F32), gain_attn).astype(BF16)
        save(x_s.at[at.mine], 0)
        save(n1_s, 1)
        wait_weight(layer, 2)
        u_s[8 : 8 + rows, :width] = dot_nt(n1_s[...], cat[2 * qk : 2 * qk + width, :]).astype(BF16).astype(F32)
        edge = remote(
            u_s.at[pl.ds(rows, 8)], edge_s.at[layer], e_send.at[layer], e_recv.at[layer],
            (at.sec, lax.rem(at.s + 1, nz), at.h),
        )

        @pl.when(at.s + 1 < nz)
        def _():
            edge.start()

        wait_weight(layer, 0)
        wait_weight(layer, 1)
        low = dot_nt(n1_s[...], cat[0 : 2 * qk, :]).astype(BF16).astype(F32)
        qk_s[...] = (low * 0.5).astype(BF16)
        save(qk_s, 2)
        a_low, b_low = qk_s[:, 0:qk], qk_s[:, qk : 2 * qk]

        @pl.when(at.s > 0)
        def _():
            edge.wait_recv()

        u_s[0:8, :] = edge_s[layer]
        save(u_s, 3)
        convolve(at, u_s, taps, c_s, cx_s, heads)

        for head in range(heads):
            one, two = lift_parts(b_low, tables, 2, head)
            psi = jnp.where(tail, one * two, 0.0).astype(BF16)
            ss[layer, head] = dot_tn(psi, cx_s[head])[:PSI_SENT].astype(BF16)

        def state(k):
            return remote(
                ss.at[layer], sr.at[layer, at.s], st_send.at[layer, k - 1], st_recv.at[layer, at.s],
                (at.sec, lax.rem(at.s + k, nz), at.h),
            )

        for k in range(1, nz):

            @pl.when(at.s + k < nz)
            def _(k=k):
                state(k).start()

        wait_weight(layer, 3)
        o_s[:, :width] = dot_nt(n1_s[...], cat[2 * qk + width :, :])
        save(o_s, 4)
        for head in range(heads):
            e = dot_nt(a_low, head_only(b_low, head))
            kern = jnp.where(allowed, 1.0 + e + 0.5 * e * e, 0.0).astype(BF16)
            yx_s[head] = dot_nn(kern, cx_s[head])
        for j in range(nz - 1):

            @pl.when(j < at.s)
            def _(j=j):
                remote(ss.at[layer], sr.at[layer, j], st_send.at[layer, 0], st_recv.at[layer, j], core).wait_recv()

        hooks["states"]()
        sin_s[...] = jnp.zeros_like(sin_s)
        for head in range(heads):
            total = jnp.zeros((PSI_SENT, LANES), F32)
            for j in range(nz - 1):
                counts = (j < at.s) & (at.last_seg(j) == prior)
                total = total + jnp.where(counts, sr[layer, j, head].astype(F32), 0.0)
            sin_s[head, 0:PSI_SENT] = total.astype(BF16)
            one, two = lift_parts(a_low, tables, 1, head)
            psi = (one * two).astype(BF16)
            yx = yx_s[head] + jnp.where(applies, dot_nn(psi, sin_s[head]), 0.0)
            yx_s[head] = yx
            gate = o_s[:, head * HD : head * HD + LANES]
            y = yx / yx[:, HD : HD + 1]
            g_s[:, head * HD : head * HD + LANES] = y * (gate * jax.nn.sigmoid(gate))
        gb_s[...] = g_s[:, :width].astype(BF16)
        save(yx_s, 5)
        save(sin_s, 6)
        save(gb_s, 7)

        wait_weight(layer, 4)

        s1 = []
        for half in range(2):
            cols = half_cols(w_out, half)
            part_s[layer, 0, :, cols] = dot_nn(gb_s[...], w_out[:, cols]).astype(BF16)
            s1 += scatter_start(at, part_s.at[layer, 0], got_s, head_send.at[layer, 0], head_recv.at[layer, 0], half)
        hooks["rs1"]()
        hidden = x_s[at.mine].astype(F32) + scatter_sum(at, part_s.at[layer, 0], got_s, s1)
        h_s[...] = hidden
        n2_s[at.mine] = norm_rows(hidden, gain_ffn).astype(BF16)
        s2 = gather_start(at, n2_s, head_send.at[layer, 1], head_recv.at[layer, 1])
        save(h_s, 8)
        hooks["ag1"]()
        wait_recv(s2)
        hooks["n2"]()

        wait_weight(layer, 5)
        wait_weight(layer, 6)

        def up_chunk(at_row, size):
            cols = pl.ds(at_row, size)
            f = dot_nt(n2_s[...], w_gate[cols, :])
            v = dot_nt(n2_s[...], w_up[cols, :])
            f_s[:, cols] = f.astype(BF16)
            v_s[:, cols] = v.astype(BF16)
            t_s[:, cols] = (f * jax.nn.sigmoid(f) * v).astype(BF16)

        chunks(t_s.shape[1], 256, up_chunk)
        save(f_s, 9)
        save(v_s, 10)
        wait_weight(layer, 7)

        s3 = []
        for half in range(2):
            cols = half_cols(w_down, half)
            part_s[layer, 1, :, cols] = dot_nn(t_s[...], w_down[:, cols]).astype(BF16)
            s3 += scatter_start(at, part_s.at[layer, 1], got_s, head_send.at[layer, 2], head_recv.at[layer, 2], half)
        hooks["rs2"]()
        feed = scatter_sum(at, part_s.at[layer, 1], got_s, s3)
        xo_s[layer, at.mine] = jnp.where(my_valid, h_s[...] + feed, 0.0).astype(BF16)
        s4 = gather_start(at, xo_s.at[layer], head_send.at[layer, 3], head_recv.at[layer, 3])
        hooks["ag2"]()
        wait_recv(s4)
        for copy in keep:
            copy.wait()

        def finish():
            wait_send(s1 + s2 + s3 + s4)

            @pl.when(at.s + 1 < nz)
            def _():
                edge.wait_send()

            for k in range(1, nz):

                @pl.when(at.s + k < nz)
                def _(k=k):
                    state(k).wait_send()

        return finish

    def nothing():
        pass

    n2_copy = pltpu.make_async_copy(n2_s, gath_n2.at[at.s], io_sem.at[2])

    def f0_n2():
        n2_copy.start()
        ring_g.step(1)

    def f1_begin():
        n2_copy.wait()
        upward(3, nz, ring_g.step)
        upward(0, nz - 1, ring_g.pair)
        ring_n.step(0)

    def f1_n2():
        n2_last.start()
        ring_n.step(2)

    x_copy.wait()
    finish_0 = layer_forward(
        0, x_s, dict(begin=nothing, states=nothing, rs1=lambda: ring_g.step(0), ag1=nothing, n2=f0_n2, rs2=nothing, ag2=lambda: ring_g.step(2))
    )
    finish_0()

    def out_copy(layer):
        near = pltpu.make_async_copy(xo_s.at[layer], x_out.at[at.sec], io_sem.at[3])
        far = remote(xo_s.at[layer], x_out.at[at.sec], x_send.at[9], x_recv.at[9], core)
        return near, far

    def send_out(layer):
        near, far = out_copy(layer)

        @pl.when(at.sec == layer)
        def _():
            near.start()

        @pl.when(at.sec != layer)
        def _():
            far.start()

    send_out(0)
    n2_last = pltpu.make_async_copy(n2_s, n2_out, io_sem.at[4])
    finish_1 = layer_forward(
        1, xo_s.at[0], dict(begin=f1_begin, states=nothing, rs1=lambda: ring_n.step(1), ag1=nothing, n2=f1_n2, rs2=nothing, ag2=nothing)
    )
    send_out(1)
    finish_1()
    upward(0, nz - 1, ring_g.ready)
    upward(3, nz, ring_n.step)
    n2_last.wait()
    ring_g.drain()
    ring_n.drain(pairs=False)
    near, far = out_copy(0)
    near.wait()
    far.wait_send()
    far.wait_recv()
    small_swap.wait_send()
    for here in range(2):

        @pl.when(at.sec == here)
        def _(here=here):
            for i in range(8):
                swap(here, i).wait_send()
                stash(1 - here, i).wait()


def bwd_kernel(dims, *refs):
    nz, nh, rows, heads = dims
    take = taker(refs)
    lens, inputs_grad, small_own, small_other, tables = take(5)
    own = take(8)
    other = take(8)
    saved = [take(SAVED), take(SAVED)]
    gath_g1, _, n2_1 = take(3)
    ig_o, gains_o = take(2)
    att_o = take(2)
    ffn_o = take(3)
    gath_n2_1, gath_g0, gath_n2_0 = take(3)
    a_peer, a_land = take(2), take(2)
    wr_o = take(3)
    mats = take(5)
    keep_s = take(SAVED)
    (grad_s, part_s, got_s, dm_s, dh_s, dg_s, do_s, cx_s, dyx_s, ss, sr, st_s, da_s, db_s, dc_s, edge_s, dcat_s, ig_s) = take(18)
    gsum_s, gpeer_s, gtot_s, gz_s, gh_s = take(5)
    acc = take(3)
    wx_s = take(3)
    blk_n2, blk_g, n2t_s, gt_s = take(4)
    a_s, work_s = take(2), take(2)
    (w_sem, io_sem, keep_sem, e_send, e_recv, st_send, st_recv, head_send, head_recv, r_send, r_recv, p_send, p_recv) = take(13)
    (wx_send, wx_recv, ap_send, ap_recv, l_send, l_recv, x_send, x_recv, gz_send, gz_recv, gh_send, gh_recv) = take(12)
    x_s, n1_s, qk_s, u_s, o_s, yx_s, sin_s, gb_s, h_s, f_s, v_s = keep_s
    df_s, dv_s = f_s, v_s
    at = Place(lens, nz, nh, rows)
    cat, w_out, w_gate, w_up, w_down = mats
    d = n1_s.shape[1]
    width, qk = heads * HD, heads * FEAT
    block = d // nz
    core = (1 - at.sec, at.s, at.h)
    slots = weight_slots(*mats, qk, width)

    def weight_start(layer, i):
        @pl.when(at.sec == layer)
        def _():
            pltpu.make_async_copy(own[i].at[0], slots[i], w_sem.at[i]).start()

        @pl.when(at.sec != layer)
        def _():
            pltpu.make_async_copy(other[i].at[0], slots[i], w_sem.at[i]).start()

    def weight_wait(i):
        pltpu.make_async_copy(own[i].at[0], slots[i], w_sem.at[i]).wait()

    def keep_copy(layer, i):
        return pltpu.make_async_copy(saved[layer][i], keep_s[i], keep_sem.at[i])

    ring_n = Ring(at, n2_1, gath_n2_1, r_send.at[0], r_recv.at[0], p_send.at[0], p_recv.at[0])
    ring_g = Ring(at, ig_s.at[1], gath_g0, r_send.at[1], r_recv.at[1], p_send.at[1], p_recv.at[1])
    ring_0 = Ring(at, None, gath_n2_0, None, None, p_send.at[2], p_recv.at[2])
    line = [
        [
            LineSum(
                at, a_s[g], a_peer[g].at[layer], a_land[g].at[layer], work_s[g], io_sem.at[4],
                l_send.at[layer, g], l_recv.at[layer, g], ap_recv.at[layer, g],
            )
            for g in range(2)
        ]
        for layer in range(2)
    ]

    def piece(layer, i):
        which = order(at, i)
        if isinstance(i, int) and i == 0:
            n2_src = n2_1 if layer == 1 else gath_n2_0.at[at.s]
            g_src = inputs_grad.at[at.sec] if layer == 1 else ig_s.at[1]
        else:
            n2_src = (gath_n2_1 if layer == 1 else gath_n2_0).at[which]
            g_src = (gath_g1 if layer == 1 else gath_g0).at[which]
        loads = [pltpu.make_async_copy(n2_src, blk_n2, io_sem.at[0]), pltpu.make_async_copy(g_src, blk_g, io_sem.at[1])]
        for copy in loads:
            copy.start()
        for copy in loads:
            copy.wait()
        pos = which * rows + lax.broadcasted_iota(jnp.int32, (rows, 1), 0)
        blk_g[...] = jnp.where(pos < at.tot, blk_g[...].astype(F32), 0.0).astype(BF16)
        for part in range(nz):

            @pl.when(at.s == part)
            def _(part=part):
                n2t_s[...] = blk_n2[:, part * block : (part + 1) * block].T
                gt_s[...] = blk_g[:, part * block : (part + 1) * block].T

        def hidden(at_row, size):
            cols = pl.ds(at_row, size)
            f = dot_nt(blk_n2[...], w_gate[cols, :])
            v = dot_nt(blk_n2[...], w_up[cols, :])
            dt = dot_nt(blk_g[...], w_down[cols, :])
            sig = jax.nn.sigmoid(f)
            act = f * sig
            t = (act * v).astype(BF16)
            df = (dt * v * (sig + act * (1.0 - sig))).astype(BF16)
            dv = (dt * act).astype(BF16)
            parts = (dot_nn(n2t_s[...], df), dot_nn(n2t_s[...], dv), dot_nn(gt_s[...], t))
            for total, new in zip(acc, parts):
                if isinstance(i, int) and i == 0:
                    total[:, cols] = new
                else:
                    total[:, cols] += new

        chunks(w_gate.shape[0], 640, hidden)

    def ffn_swap(i):
        return remote(wx_s[i], wr_o[i], wx_send.at[i], wx_recv.at[i], core)

    def ffn_own(i):
        return pltpu.make_async_copy(acc[i], ffn_o[i], io_sem.at[5 + i])

    def ffn_send(layer):
        @pl.when(at.sec != layer)
        def _():
            for i in range(3):
                wx_s[i][...] = acc[i][...].astype(BF16)
                ffn_swap(i).start()

        @pl.when(at.sec == layer)
        def _():
            for i in range(3):
                ffn_own(i).start()

    def ffn_done(layer):
        @pl.when(at.sec == layer)
        def _():
            for i in range(3):
                ffn_own(i).wait()

    def ig_copy(layer):
        near = pltpu.make_async_copy(ig_s.at[layer], ig_o.at[at.sec], io_sem.at[3])
        far = remote(ig_s.at[layer], ig_o.at[at.sec], x_send.at[0], x_recv.at[0], core)
        return near, far

    def ig_send(layer):
        near, far = ig_copy(layer)

        @pl.when(at.sec == layer)
        def _():
            near.start()

        @pl.when(at.sec != layer)
        def _():
            far.start()

    allowed = at.allowed()
    applies, tail, mine_last = at.applies(), at.tail(), at.last_seg(at.s)
    valid = at.pos() < at.tot
    lane = lax.broadcasted_iota(jnp.int32, (rows, LANES), 1)

    def line_core(layer, g):
        return 1 if layer == 0 and g == 1 else 0

    def peer_chunk(layer, g, i):
        return remote(a_s[g].at[i], a_peer[g].at[layer, i], ap_send.at[g, i], ap_recv.at[layer, g, i], core)

    def mixer_grads(layer, g):
        late = 2 * qk + width
        for i in range(nz):
            cols = slice(i * block, (i + 1) * block)
            if g == 0:
                a_s[0][i, :, 0:width] = dot_tn(n1_s[:, cols], dcat_s[:, late:]).astype(BF16)
                a_s[0][i, :, width:] = dot_tn(dm_s[:, cols], gb_s[...]).astype(BF16)
            else:
                a_s[1][i] = dot_tn(n1_s[:, cols], dcat_s[:, 0:late]).astype(BF16)

            @pl.when(at.sec != line_core(layer, g))
            def _(i=i):
                peer_chunk(layer, g, i).start()

    def mixer_sent(layer, g):
        for i in range(nz):

            @pl.when(at.sec != line_core(layer, g))
            def _(i=i):
                peer_chunk(layer, g, i).wait_send()

    def layer_backward(layer, hooks):
        small = jnp.where(at.sec == layer, small_own[...], small_other[...])
        gain_attn, gain_ffn, taps = small[0:1], small[1:2], small[2 : 2 + KW]
        hooks["begin"]()

        weight_wait(7)
        keep_copy(layer, 9).wait()
        keep_copy(layer, 10).wait()

        def down_chunk(at_row, size):
            cols = pl.ds(at_row, size)
            dt = dot_nt(grad_s[...], w_down[cols, :])
            f = f_s[:, cols].astype(F32)
            v = v_s[:, cols].astype(F32)
            sig = jax.nn.sigmoid(f)
            df_s[:, cols] = (dt * v * sig * (1.0 + f * (1.0 - sig))).astype(BF16)
            dv_s[:, cols] = (dt * f * sig).astype(BF16)

        chunks(df_s.shape[1], 256, down_chunk)
        weight_wait(5)
        weight_wait(6)

        s1 = []
        for half in range(2):
            cols = half_cols(w_up, half)
            part = dot_nn(df_s[...], w_gate[:, cols]) + dot_nn(dv_s[...], w_up[:, cols])
            part_s[:, cols] = part.astype(BF16)
            s1 += scatter_start(at, part_s, got_s, head_send.at[layer, 0], head_recv.at[layer, 0], half)
        hooks["rs1"]()
        keep_copy(layer, 8).wait()
        dn2 = scatter_sum(at, part_s, got_s, s1)
        back, gain_grad = norm_rows_back(h_s[...], gain_ffn, dn2)
        gsum_s[layer, 1:2, :] = gain_grad
        dh = grad_s[at.mine].astype(F32) + back
        dh_s[...] = dh
        dm_s[at.mine] = dh.astype(BF16)
        s2 = gather_start(at, dm_s, head_send.at[layer, 1], head_recv.at[layer, 1])
        for i in range(8):
            keep_copy(layer, i).wait()
        for i in (4, 0, 1, 2, 3):
            weight_wait(i)
        convolve(at, u_s, taps, do_s, cx_s, heads)
        a_low, b_low = qk_s[:, 0:qk], qk_s[:, qk : 2 * qk]
        hooks["ag1"]()
        wait_recv(s2)
        hooks["dm"]()

        def out_chunk(at_row, size):
            cols = pl.ds(at_row, size)
            dg_s[:, cols] = dot_nt(dm_s[...], w_out[cols, :])

        chunks(width, 256, out_chunk)
        for head in range(heads):
            cols = slice(head * HD, head * HD + LANES)
            gate, dg, yx = o_s[:, cols], dg_s[:, cols], yx_s[head]
            sig = jax.nn.sigmoid(gate)
            inverse = 1.0 / yx[:, HD : HD + 1]
            y = yx * inverse
            do_s[:, cols] = dg * y * sig * (1.0 + gate * (1.0 - sig))
            dy = jnp.where(lane < HD, dg * gate * sig, 0.0)
            dden = -jnp.sum(dy * y, axis=1, keepdims=True) * inverse
            dyx_s[head] = jnp.where(lane == HD, dden, dy * inverse).astype(BF16)
            one, two = lift_parts(a_low, tables, 1, head)
            psi = jnp.where(applies, one * two, 0.0).astype(BF16)
            ss[layer, head] = dot_tn(psi, dyx_s[head])[:PSI_SENT].astype(BF16)
        dcat_s[:, 2 * qk + width :] = do_s[:, :width].astype(BF16)

        def state(k):
            return remote(
                ss.at[layer], sr.at[layer, at.s], st_send.at[layer, k - 1], st_recv.at[layer, at.s],
                (at.sec, lax.rem(at.s + nz - k, nz), at.h),
            )

        for k in range(1, nz):

            @pl.when(at.s - k >= 0)
            def _(k=k):
                state(k).start()

        da_s[...] = jnp.zeros_like(da_s)
        db_s[...] = jnp.zeros_like(db_s)
        for head in range(heads):
            a_own, b_own = head_only(a_low, head), head_only(b_low, head)
            e = dot_nt(a_low, b_own)
            kern = jnp.where(allowed, 1.0 + e + 0.5 * e * e, 0.0).astype(BF16)
            dkern = dot_nt(dyx_s[head], cx_s[head])
            de = jnp.where(allowed, dkern * (1.0 + e), 0.0).astype(BF16)
            one, two = lift_parts(a_low, tables, 1, head)
            dpsi = jnp.where(applies, dot_nt(dyx_s[head], sin_s[head]), 0.0)
            pcols = slice(head * PSI, (head + 1) * PSI)
            da_s[...] += (
                dot_nn(de, b_own)
                + dot_nt((dpsi * two).astype(BF16), tables[0, :, pcols])
                + dot_nt((dpsi * one).astype(BF16), tables[1, :, pcols])
            )
            db_s[...] += dot_tn(de, a_own)
            yx_s[head] = dot_tn(kern, dyx_s[head])
        hooks["local"]()
        for j in range(1, nz):

            @pl.when(j > at.s)
            def _(j=j):
                remote(ss.at[layer], sr.at[layer, j], st_send.at[layer, 0], st_recv.at[layer, j], core).wait_recv()

        hooks["states"]()
        st_s[...] = jnp.zeros_like(st_s)
        for head in range(heads):
            total = jnp.zeros((PSI_SENT, LANES), F32)
            for j in range(1, nz):
                counts = (j > at.s) & (at.prior_seg(j) == mine_last)
                total = total + jnp.where(counts, sr[layer, j, head].astype(F32), 0.0)
            st_s[head, 0:PSI_SENT] = total.astype(BF16)
            one, two = lift_parts(b_low, tables, 2, head)
            psi = (one * two).astype(BF16)
            dpsi = jnp.where(tail, dot_nt(cx_s[head], st_s[head]), 0.0)
            pcols = slice(head * PSI, (head + 1) * PSI)
            db_s[...] += dot_nt((dpsi * two).astype(BF16), tables[0, :, pcols]) + dot_nt(
                (dpsi * one).astype(BF16), tables[2, :, pcols]
            )
            dc = yx_s[head] + jnp.where(tail, dot_nn(psi, st_s[head]), 0.0)
            dc_s[0:rows, head * HD : head * HD + LANES] = dc
        edge = remote(
            dc_s.at[pl.ds(0, 8)], edge_s.at[layer], e_send.at[layer], e_recv.at[layer],
            (at.sec, lax.rem(at.s + nz - 1, nz), at.h),
        )

        @pl.when(at.s > 0)
        def _():
            edge.start()

        dcat_s[:, 0:qk] = (da_s[...] * 0.5).astype(BF16)
        dcat_s[:, qk : 2 * qk] = (db_s[...] * 0.5).astype(BF16)
        gsum_s[layer, 2:8, :] = jnp.zeros((6, d), F32)
        for j in range(KW):
            product = dc_s[0:rows, :width] * u_s[8 - j : 8 - j + rows, :width]
            gsum_s[layer, 2 + j : 3 + j, :width] = jnp.sum(jnp.where(at.same(-j), product, 0.0), axis=0, keepdims=True)

        @pl.when(at.s + 1 < nz)
        def _():
            edge.wait_recv()

        dc_s[rows : rows + 8, :] = edge_s[layer]
        du = taps[0:1, :width] * dc_s[0:rows, :width]
        for j in range(1, KW):
            du = du + jnp.where(at.same(j), dc_s[j : j + rows, :width] * taps[j : j + 1, :width], 0.0)
        dcat_s[:, 2 * qk : 2 * qk + width] = du.astype(BF16)

        wait_send(s1)
        s3 = []
        for half in range(2):
            cols = half_cols(cat, half)
            part_s[:, cols] = dot_nn(dcat_s[...], cat[:, cols]).astype(BF16)
            s3 += scatter_start(at, part_s, got_s, head_send.at[layer, 2], head_recv.at[layer, 2], half)
        hooks["rs2"]()
        dn1 = scatter_sum(at, part_s, got_s, s3)
        back, gain_grad = norm_rows_back(x_s[...].astype(F32), gain_attn, dn1)
        gsum_s[layer, 0:1, :] = gain_grad
        ig_s[layer, at.mine] = (dh_s[...] + back).astype(BF16)
        s4 = gather_start(at, ig_s.at[layer], head_send.at[layer, 3], head_recv.at[layer, 3])
        hooks["ag2"]()
        wait_recv(s4)
        ig_send(layer)
        wait_send(s3)

        def finish():
            wait_send(s2 + s4)

            @pl.when(at.s > 0)
            def _():
                edge.wait_send()

            for k in range(1, nz):

                @pl.when(at.s - k >= 0)
                def _(k=k):
                    state(k).wait_send()

        return finish

    def owner(layer, what):
        @pl.when(at.sec == layer)
        def _():
            what()

    g_copy = pltpu.make_async_copy(inputs_grad.at[at.sec], grad_s, io_sem.at[2])
    g_copy.start()
    for i in (7, 5, 6, 4, 0, 1, 2, 3):
        weight_start(1, i)
    for i in (9, 10, 8, 3, 2, 4, 5, 6, 7, 1, 0):
        keep_copy(1, i).start()
    at.barrier(True, True, True)
    ring_n.step(0)
    g_copy.wait()
    grad_s[...] = jnp.where(valid, grad_s[...].astype(F32), 0.0).astype(BF16)

    def slot(layer, g, i):
        owner(line_core(layer, g), lambda: line[layer][g].slot(i))

    def far_sum(g):
        return remote(work_s[g].at[0], att_o[g], x_send.at[2 + g], x_recv.at[2 + g], core)

    def line_last(layer, g):
        def go():
            upward(3, nz - 1, line[layer][g].slot)
            line[layer][g].last()
            if line_core(layer, g) == layer:
                copy = pltpu.make_async_copy(work_s[g].at[0], att_o[g], io_sem.at[8])
                copy.start()
                copy.wait()
            else:
                far_sum(g).start()

        owner(line_core(layer, g), go)

    def pieces(layer, ring, begin, end):
        def one(k):
            ring.ready(k - 1)
            if layer == 0:
                ring_0.ready(k - 1)
            piece(layer, k)

        upward(begin, end, one)

    def spread(ring):
        upward(3, nz, ring.step)
        upward(1, nz - 1, ring.pair)

    def nothing():
        pass

    def b1_rs1():
        ring_n.step(1)
        ring_n.pair(0)
        piece(1, 0)

    def b1_ag1():
        ring_n.step(2)
        pieces(1, ring_n, 1, 2)

    def b1_local():
        upward(0, nz - 1, ring_0.pair)
        mixer_grads(1, 0)

    def b1_rs2():
        mixer_grads(1, 1)
        slot(1, 0, 0)
        pieces(1, ring_n, 2, 3)

    def b1_ag2():
        for i in (4, 0, 1, 2, 3):
            weight_start(0, i)
        for i in (9, 10, 8, 3, 2, 4, 5, 6, 7, 1, 0):
            keep_copy(0, i).start()
        slot(1, 0, 1)
        pieces(1, ring_n, 3, nz)
        for i in (7, 5, 6):
            weight_start(0, i)
        ffn_send(1)

    finish_1 = layer_backward(
        1,
        dict(
            begin=nothing, rs1=b1_rs1, ag1=b1_ag1, dm=lambda: spread(ring_n), local=b1_local,
            states=nothing, rs2=b1_rs2, ag2=b1_ag2,
        ),
    )
    finish_1()
    grad_s[...] = jnp.where(valid, ig_s[1].astype(F32), 0.0).astype(BF16)

    def b0_begin():
        ring_g.step(0)
        slot(1, 0, 2)
        slot(1, 1, 0)

    def b0_rs1():
        ffn_done(1)
        ring_g.step(1)
        ring_g.pair(0)
        piece(0, 0)
        slot(1, 1, 1)

    def b0_ag1():
        ring_g.step(2)
        pieces(0, ring_g, 1, 2)
        slot(1, 1, 2)

    def b0_local():
        line_last(1, 0)
        mixer_sent(1, 0)
        mixer_grads(0, 0)

    def b0_states():
        line_last(1, 1)

    def b0_rs2():
        mixer_sent(1, 1)
        mixer_grads(0, 1)
        owner(0, lambda: far_sum(0).wait_send())
        slot(0, 0, 0)
        pieces(0, ring_g, 2, 3)

    def b0_ag2():
        slot(0, 0, 1)
        slot(0, 1, 0)
        pieces(0, ring_g, 3, nz)
        ffn_send(0)

    finish_0 = layer_backward(
        0,
        dict(
            begin=b0_begin, rs1=b0_rs1, ag1=b0_ag1, dm=lambda: spread(ring_g), local=b0_local,
            states=b0_states, rs2=b0_rs2, ag2=b0_ag2,
        ),
    )

    gain_swap = remote(gsum_s.at[1 - at.sec], gpeer_s, x_send.at[1], x_recv.at[1], core)
    gain_swap.start()

    slot(0, 0, 2)
    slot(0, 1, 1)
    slot(0, 1, 2)
    gain_swap.wait_recv()
    gtot_s[0] = gsum_s[at.sec] + gpeer_s[...]

    def gain_seq(k):
        to = lax.rem(at.s + k, nz)
        return remote(gtot_s.at[0], gz_s.at[k - 1], gz_send.at[k - 1], gz_recv.at[k - 1], (at.sec, to, at.h))

    for k in range(1, nz):
        gain_seq(k).start()
    line_last(0, 1)
    line_last(0, 0)
    for k in range(1, nz):
        gain_seq(k).wait_recv()
    total = gtot_s[0]
    for k in range(1, nz):
        total = total + gz_s[k - 1]
    gtot_s[1] = total

    def gain_head(m):
        return remote(gtot_s.at[1], gh_s.at[m - 1], gh_send.at[m - 1], gh_recv.at[m - 1], (at.sec, at.s, at.h ^ m))

    for m in range(1, nh):
        gain_head(m).start()
    ffn_done(0)
    mixer_sent(0, 0)
    mixer_sent(0, 1)
    far_sum(1).wait()
    owner(1, lambda: far_sum(0).wait_recv())
    for m in range(1, nh):
        gain_head(m).wait_recv()
    total = gtot_s[1, 0:2]
    for m in range(1, nh):
        total = total + gh_s[m - 1, 0:2]
    gains_o[...] = gtot_s[1]
    gains_o[0:2, :] = total

    finish_0()
    ring_n.drain()
    ring_g.drain()
    ring_0.drain(line=False)
    gain_swap.wait_send()
    for k in range(1, nz):
        gain_seq(k).wait_send()
    for m in range(1, nh):
        gain_head(m).wait_send()
    for i in range(3):
        ffn_swap(i).wait()
    near, far = ig_copy(0)
    near.wait()
    far.wait_send()
    far.wait_recv()


def final_kernel(qk, width, *refs):
    take = taker(refs)
    whole, far, (early, late), out, parts, held, held_far, (sems,) = take(5), take(3), take(2), take(5), take(5), take(5), take(3), take(1)
    loads = [pltpu.make_async_copy(a, b, sems.at[i]) for i, (a, b) in enumerate(zip(whole + far, held + held_far))]
    stores = [pltpu.make_async_copy(a, b, sems.at[8 + i]) for i, (a, b) in enumerate(zip(held, out))]
    for copy in loads:
        copy.start()
    g_q, g_k, g_v, g_o, g_out = parts
    turned = late[:, 0 : 2 * qk].astype(F32).T
    g_q[...] = turned[0:qk]
    g_k[...] = turned[qk : 2 * qk]
    g_v[...] = late[:, 2 * qk :].astype(F32)
    g_o[...] = early[:, 0:width].astype(F32)
    g_out[...] = early[:, width:].astype(F32).T
    for i in range(5):
        loads[i].wait()
        if i >= 2:
            loads[i + 3].wait()
            held[i][...] += held_far[i - 2][...].astype(F32)
        stores[i].start()
    for copy in stores:
        copy.wait()


def shape(dims, kind=BF16):
    return jax.ShapeDtypeStruct(tuple(dims), kind)


ANY = pl.BlockSpec(memory_space=pl.ANY)
VM = pl.BlockSpec(memory_space=pltpu.VMEM)
SM = pl.BlockSpec(memory_space=pltpu.SMEM)
DMA = pltpu.SemaphoreType.DMA


def params(number):
    return pltpu.CompilerParams(collective_id=number, has_side_effects=True, vmem_limit_bytes=VMEM_LIMIT)


def shards(nz, nh, inputs, out_grad, lengths, norm_attn, norm_ffn, w_query, w_key, w_value, w_output_gate, conv_kernel, w_out, w_gate, w_up, w_down):
    micro, rows, d = inputs.shape
    heads = w_query.shape[2] // FEAT
    width, qk, ff = w_value.shape[2], w_query.shape[2], w_gate.shape[2]
    part, block = rows // nh, d // nz
    dims = (nz, nh, rows, heads)
    wide = -(-((heads - 1) * HD + LANES) // LANES) * LANES
    groups = (2 * width, 2 * qk + width)
    tables = jnp.asarray(lift_tables(heads), BF16)
    turned = [jnp.swapaxes(w, 1, 2) for w in (w_query, w_key, w_value, w_output_gate)]
    own = (*turned, w_out, jnp.swapaxes(w_gate, 1, 2), jnp.swapaxes(w_up, 1, 2), w_down)
    small_own = jnp.concatenate(
        [norm_attn, norm_ffn, jnp.pad(conv_kernel[0], ((0, 0), (0, d - width))), jnp.zeros((3, d), F32)]
    )

    def vm(dims, kind=BF16):
        return pltpu.VMEM(tuple(dims), kind)

    mats = [vm((2 * qk + 2 * width, d)), vm((width, d)), vm((ff, d)), vm((ff, d)), vm((ff, d))]
    act = vm((rows, d))
    kept = [
        ((part, d), BF16),
        ((rows, d), BF16),
        ((rows, 2 * qk), BF16),
        ((rows + 8, wide), F32),
        ((rows, wide), F32),
        ((heads, rows, LANES), F32),
        ((heads, PSI, LANES), BF16),
        ((rows, width), BF16),
        ((part, d), F32),
        ((rows, ff), BF16),
        ((rows, ff), BF16),
    ]
    keep_shapes = [shape(*k) for k in kept]
    gathered = shape((nz, rows, d))
    outs = (
        [shape((8, d), F32)]
        + [shape(w.shape) for w in own]
        + keep_shapes * 2
        + [shape((micro, rows, d)), gathered, gathered, shape((rows, d))]
    )
    scratch = (
        mats
        + mats
        + [
            act,
            act,
            act,
            vm((rows, 2 * qk)),
            vm((rows + 8, wide), F32),
            vm((2, 8, wide), F32),
            vm((rows, wide), F32),
            vm((rows, wide), F32),
            vm((heads, rows, LANES)),
            vm((heads, rows, LANES), F32),
            vm((2, heads, PSI_SENT, LANES)),
            vm((2, nz, heads, PSI_SENT, LANES)),
            vm((heads, PSI, LANES)),
            vm((rows, wide), F32),
            vm((rows, width)),
            vm((2, 2, rows, d)),
            vm((nh - 1, part, d)),
            vm((rows, ff)),
            vm((rows, ff)),
            vm((rows, ff)),
            vm((2, rows, d)),
            vm((part, d), F32),
            vm((8, d), F32),
            DMA((16,)),
            DMA((5,)),
            DMA((SAVED,)),
            DMA((10,)),
            DMA((10,)),
            DMA((2,)),
            DMA((2,)),
            DMA((2, nz)),
            DMA((2, nz)),
            DMA((2, 4, 2 * (nh - 1))),
            DMA((2, 4, 2 * (nh - 1))),
            DMA((2, 2, nz - 1, 2)),
            DMA((2, 2, nz - 1, 2)),
            DMA((2, 2, nz - 1, 2)),
            DMA((2, 2, nz - 1, 2)),
        ]
    )
    first = pl.pallas_call(
        functools.partial(fwd_kernel, dims),
        out_shape=outs,
        in_specs=[SM, ANY, ANY, VM, VM] + [ANY] * 8,
        out_specs=[ANY] * len(outs),
        scratch_shapes=scratch,
        compiler_params=params(0),
    )(lengths, inputs, out_grad, small_own, tables, *own)
    small_other, other = first[0], first[1:9]
    saved = first[9 : 9 + 2 * SAVED]
    section_out, gath_g1, gath_n2_0, n2_1 = first[9 + 2 * SAVED :]

    outs = (
        [shape((micro, rows, d)), shape((8, d), F32)]
        + [shape((block, g)) for g in groups]
        + [shape((block, ff), F32)] * 3
        + [gathered, gathered, gathered]
        + [shape((2, nz, block, g)) for g in groups]
        + [shape((2, 2, nz, block, g)) for g in groups]
        + [shape((block, ff))] * 3
    )
    out_specs = [ANY, VM] + [ANY] * (len(outs) - 2)
    scratch = (
        mats
        + [vm(*k) for k in kept]
        + [
            act,
            act,
            vm((nh - 1, part, d)),
            act,
            vm((part, d), F32),
            vm((rows, wide), F32),
            vm((rows, wide), F32),
            vm((heads, rows, LANES)),
            vm((heads, rows, LANES)),
            vm((2, heads, PSI_SENT, LANES)),
            vm((2, nz, heads, PSI_SENT, LANES)),
            vm((heads, PSI, LANES)),
            vm((rows, qk), F32),
            vm((rows, qk), F32),
            vm((rows + 8, wide), F32),
            vm((2, 8, wide), F32),
            vm((rows, 2 * qk + 2 * width)),
            vm((2, rows, d)),
            vm((2, 8, d), F32),
            vm((8, d), F32),
            vm((2, 8, d), F32),
            vm((nz - 1, 8, d), F32),
            vm((nh - 1, 8, d), F32),
        ]
        + [vm((block, ff), F32)] * 3
        + [vm((block, ff))] * 3
        + [act, act, vm((block, rows)), vm((block, rows))]
        + [vm((nz, block, g)) for g in groups]
        + [vm((3, block, g)) for g in groups]
        + [
            DMA((8,)),
            DMA((12,)),
            DMA((SAVED,)),
            DMA((2,)),
            DMA((2,)),
            DMA((2, nz)),
            DMA((2, nz)),
            DMA((2, 4, 2 * (nh - 1))),
            DMA((2, 4, 2 * (nh - 1))),
            DMA((2, 2, nz - 1, 2)),
            DMA((2, 2, nz - 1, 2)),
            DMA((3, 2, nz - 1, 2)),
            DMA((3, 2, nz - 1, 2)),
            DMA((3,)),
            DMA((3,)),
            DMA((2, nz)),
            DMA((2, 2, nz)),
            DMA((2, 2, 2, nz)),
            DMA((2, 2, 2, nz)),
            DMA((4,)),
            DMA((4,)),
            DMA((nz - 1,)),
            DMA((nz - 1,)),
            DMA((nh - 1,)),
            DMA((nh - 1,)),
        ]
    )
    second = pl.pallas_call(
        functools.partial(bwd_kernel, dims),
        out_shape=outs,
        in_specs=[SM, ANY, VM, VM, VM] + [ANY] * (16 + 2 * SAVED + 3),
        out_specs=out_specs,
        scratch_shapes=scratch,
        input_output_aliases={5 + 16 + 2 * SAVED + 1: 9},
        compiler_params=params(1),
    )(lengths, out_grad, small_own, small_other, tables, *own, *other, *saved, gath_g1, gath_n2_0, n2_1)
    input_grad, gains, att_early, att_late, g_gate, g_up, g_down = second[:7]
    far = second[-3:]
    finals = [
        shape((micro, rows, d)),
        shape((micro, rows, d)),
        shape((block, ff), F32),
        shape((block, ff), F32),
        shape((block, ff), F32),
        shape((qk, block), F32),
        shape((qk, block), F32),
        shape((block, width), F32),
        shape((block, width), F32),
        shape((width, block), F32),
    ]
    section_out, input_grad, g_gate, g_up, g_down, g_q, g_k, g_v, g_o, g_out = pl.pallas_call(
        functools.partial(final_kernel, qk, width),
        out_shape=finals,
        in_specs=[ANY] * 8 + [VM] * 2,
        out_specs=[ANY] * 5 + [VM] * 5,
        scratch_shapes=[vm((micro, rows, d))] * 2 + [vm((block, ff), F32)] * 3 + [vm((block, ff))] * 3 + [DMA((13,))],
        compiler_params=pltpu.CompilerParams(vmem_limit_bytes=VMEM_LIMIT),
    )(section_out, input_grad, g_gate, g_up, g_down, *far, att_early, att_late)
    return (
        section_out[None],
        input_grad[None],
        gains[0:1],
        gains[1:2],
        g_q.T[None],
        g_k.T[None],
        g_v[None],
        g_o[None],
        gains[None, 2 : 2 + KW, :width],
        g_out[None],
        g_gate[None],
        g_up[None],
        g_down.T[None],
    )


def solution(mesh):
    return jax.shard_map(
        functools.partial(shards, mesh.shape["seq"], mesh.shape["head"]),
        mesh=mesh,
        in_specs=(
            P(None, "seq", None),
            P(None, "seq", None),
            P(),
            P("section", None),
            P("section", None),
            P("section", None, "head"),
            P("section", None, "head"),
            P("section", None, "head"),
            P("section", None, "head"),
            P("section", None, "head"),
            P("section", "head", None),
            P("section", None, "head"),
            P("section", None, "head"),
            P("section", "head", None),
        ),
        out_specs=(
            P("section", None, "seq", None),
            P("section", None, "seq", None),
            P("section", None),
            P("section", None),
            P("section", "seq", "head"),
            P("section", "seq", "head"),
            P("section", "seq", "head"),
            P("section", "seq", "head"),
            P("section", None, "head"),
            P("section", "head", "seq"),
            P("section", "seq", "head"),
            P("section", "seq", "head"),
            P("section", "head", "seq"),
        ),
        check_vma=False,
    )
```

```python
import functools

import jax
import jax.numpy as jnp
import numpy as np
from jax import lax
from jax.experimental import pallas as pl
from jax.experimental.pallas import tpu as pltpu
from jax.sharding import PartitionSpec as P

HD = 112
FEAT = 16
KW = 3
EPS = 1e-05
LANES = 128
PSI = 256
PSI_SENT = 160
MESH = pl.DeviceIdType.MESH
F32 = jnp.float32
BF16 = jnp.bfloat16
VMEM_LIMIT = 63 << 20


def dot_nn(a, b):
    return lax.dot_general(a, b, (((1,), (0,)), ((), ())), preferred_element_type=F32)


def dot_nt(a, b):
    return lax.dot_general(a, b, (((1,), (1,)), ((), ())), preferred_element_type=F32)


def dot_tn(a, b):
    return lax.dot_general(a, b, (((0,), (0,)), ((), ())), preferred_element_type=F32)


def chunks(total, step, body):
    whole = total // step
    if whole > 1:

        def one(i, carry):
            body(pl.multiple_of(i * step, step), step)
            return carry

        lax.fori_loop(0, whole, one, 0)
    elif whole == 1:
        body(0, step)
    if total % step:
        body(whole * step, total % step)


def lift_tables(heads):
    first = np.zeros((heads * FEAT, heads * PSI), np.float32)
    second = np.zeros_like(first)
    second_key = np.zeros_like(first)
    for head in range(heads):
        row, col = head * FEAT, head * PSI
        for i in range(FEAT):
            first[row + i, col + 1 + i] = 1.0
        at = 1 + FEAT
        for i in range(FEAT):
            for j in range(i, FEAT):
                first[row + i, col + at] = 1.0
                second[row + j, col + at] = 1.0
                second_key[row + j, col + at] = 0.5 if i == j else 1.0
                at += 1
    return np.stack([first, second, second_key])


class Place:
    def __init__(self, lens, nz, nh, rows):
        self.sec, self.s, self.h = (lax.axis_index(a) for a in ("section", "seq", "head"))
        self.nz, self.nh, self.rows = nz, nh, rows
        self.l0 = lens[self.sec, 0]
        self.tot = self.l0 + lens[self.sec, 1]
        self.first = self.s * rows
        self.part = rows // nh
        self.mine = pl.ds(pl.multiple_of(self.h * self.part, self.part), self.part)

    def seg(self, pos):
        inside = (pos >= self.l0).astype(jnp.int32) + (pos >= self.tot).astype(jnp.int32)
        return jnp.where(pos >= 0, inside, -1)

    def pos(self, shift=0):
        return self.first + shift + lax.broadcasted_iota(jnp.int32, (self.rows, 1), 0)

    def same(self, shift):
        other = self.pos(shift)
        inside = other < self.nz * self.rows
        return (self.seg(other) == self.seg(self.pos())) & inside

    def allowed(self):
        shape = (self.rows, self.rows)
        row = lax.broadcasted_iota(jnp.int32, shape, 0)
        col = lax.broadcasted_iota(jnp.int32, shape, 1)
        return (col <= row) & (self.seg(self.first + col) == self.seg(self.first + row))

    def last_seg(self, block):
        return self.seg(block * self.rows + self.rows - 1)

    def prior_seg(self, block):
        return self.seg(block * self.rows - 1)

    def applies(self):
        return self.seg(self.pos()) == self.prior_seg(self.s)

    def tail(self):
        return self.seg(self.pos()) == self.last_seg(self.s)

    def peers(self):
        core = [(1 - self.sec, self.s, self.h)]
        seq = [(self.sec, (self.s + k) % self.nz, self.h) for k in range(1, self.nz)]
        head = [(self.sec, self.s, self.h ^ m) for m in range(1, self.nh)]
        return core, seq, head

    def barrier(self, core, seq, head):
        groups = self.peers()
        told = [d for use, g in zip((core, seq, head), groups) if use for d in g]
        sem = pltpu.get_barrier_semaphore()
        for device in told:
            pl.semaphore_signal(sem, 1, device_id=device, device_id_type=MESH)
        pl.semaphore_wait(sem, len(told))


def remote(src, dst, send, recv, device):
    return pltpu.make_async_remote_copy(
        src_ref=src, dst_ref=dst, send_sem=send, recv_sem=recv, device_id=device, device_id_type=MESH
    )


def half_cols(buf, half):
    size = buf.shape[-1] // 2
    return pl.ds(half * size, size)


def scatter_start(at, buf, got, send, recv, half):
    sent = []
    cols = half_cols(buf, half)
    for m in sorted(range(1, at.nh), reverse=True):
        peer = at.h ^ m
        rows = pl.ds(pl.multiple_of(peer * at.part, at.part), at.part)
        sem = half * (at.nh - 1) + m - 1
        copy = remote(
            buf.at[rows, cols], got.at[m - 1, :, cols], send.at[sem], recv.at[sem], (at.sec, at.s, peer)
        )
        copy.start()
        sent.append(copy)
    return sent


def scatter_sum(at, buf, got, sent):
    total = buf[at.mine].astype(F32)
    for copy in sent:
        copy.wait_recv()
    for m in range(1, at.nh):
        total = total + got[m - 1].astype(F32)
    return total


def gather_start(at, buf, send, recv):
    sent = []
    for m in sorted(range(1, at.nh), reverse=True):
        copy = remote(
            buf.at[at.mine], buf.at[at.mine], send.at[m - 1], recv.at[m - 1], (at.sec, at.s, at.h ^ m)
        )
        copy.start()
        sent.append(copy)
    return sent


def wait_recv(copies):
    for copy in copies:
        copy.wait_recv()


def wait_send(copies):
    for copy in copies:
        copy.wait_send()


def norm_rows(x, gain):
    return x * lax.rsqrt(jnp.mean(x * x, axis=-1, keepdims=True) + EPS) * gain


def norm_rows_back(x, gain, grad):
    inverse = lax.rsqrt(jnp.mean(x * x, axis=-1, keepdims=True) + EPS)
    unit = x * inverse
    scaled = grad * gain
    back = inverse * (scaled - unit * jnp.mean(scaled * unit, axis=-1, keepdims=True))
    return back, jnp.sum(grad * unit, axis=0, keepdims=True)


def lift_parts(low, tables, second, head):
    cols = slice(head * PSI, (head + 1) * PSI)
    lane = lax.broadcasted_iota(jnp.int32, (1, PSI), 1)
    one = dot_nn(low, tables[0, :, cols]) + (lane == 0).astype(F32)
    two = dot_nn(low, tables[second, :, cols]) + (lane <= FEAT).astype(F32)
    return one, two


def head_only(low, head):
    lane = lax.broadcasted_iota(jnp.int32, low.shape, 1)
    return jnp.where((lane >= head * FEAT) & (lane < (head + 1) * FEAT), low, jnp.zeros_like(low))


def convolve(at, u_s, taps, c_s, cx_s, heads):
    rows, width = at.rows, heads * HD
    out = taps[0:1, :width] * u_s[8 : 8 + rows, :width]
    for j in range(1, KW):
        shifted = u_s[8 - j : 8 - j + rows, :width]
        out = out + jnp.where(at.same(-j), shifted * taps[j : j + 1, :width], 0.0)
    c_s[0:rows, :width] = out
    lane = lax.broadcasted_iota(jnp.int32, (rows, LANES), 1)
    for head in range(heads):
        one = c_s[0:rows, head * HD : head * HD + LANES]
        cx_s[head] = jnp.where(lane < HD, one, jnp.where(lane == HD, 1.0, 0.0)).astype(BF16)


def order(at, i):
    left, right = at.s, at.nz - 1 - at.s
    both = 2 * jnp.minimum(left, right)
    near = i <= both
    dist = jnp.where(near, (i + 1) // 2, i - both // 2)
    leftward = jnp.where(near, i % 2 == 1, left > right)
    return jnp.where(leftward, at.s - dist, at.s + dist)


class Ring:
    def __init__(self, at, src, dst, send, recv, pair_send, pair_recv):
        self.at, self.src, self.dst, self.send, self.recv = at, src, dst, send, recv
        self.pair_send, self.pair_recv = pair_send, pair_recv

    def _view(self, c):
        at = self.at
        rows, cols = at.rows // 2, self.dst.shape[-1] // 2
        bit = lax.rem(at.h // (1 << c), 2)
        return pl.ds(pl.multiple_of(bit * rows, rows), rows), pl.ds(c * cols, cols)

    def _ways(self, k):
        at = self.at
        right = (at.s - k, at.s - k >= 0, at.s + 1 < at.nz, lax.rem(at.s + 1, at.nz))
        left = (at.s + k, at.s + k < at.nz, at.s > 0, lax.rem(at.s + at.nz - 1, at.nz))
        return right, left

    def _copies(self, way, k, block, to, first):
        at = self.at
        for c in range(2):
            rows, cols = self._view(c)
            src = self.src.at[rows, cols] if first else self.dst.at[block, rows, cols]
            yield remote(
                src, self.dst.at[block, rows, cols], self.send.at[way, k, c], self.recv.at[way, k, c], (at.sec, to, at.h)
            )

    def _pairs(self, way, k, block):
        at = self.at
        for c in range(2):
            rows, cols = self._view(c)
            view = self.dst.at[block, rows, cols]
            yield remote(view, view, self.pair_send.at[way, k, c], self.pair_recv.at[way, k, c], (at.sec, at.s, at.h ^ (1 << c)))

    def step(self, k):
        at = self.at
        first = isinstance(k, int) and k == 0
        for way, (block, there, onward, to) in enumerate(self._ways(k)):
            if not first:

                @pl.when(there)
                def _(way=way, block=block, to=to):
                    wait_recv(self._copies(way, k - 1, block, to, False))

            if not isinstance(k, int) or k < at.nz - 1:

                @pl.when(there & onward & (k < at.nz - 1))
                def _(way=way, block=block, to=to):
                    for copy in self._copies(way, k, block, to, first):
                        copy.start()

    def pair(self, k):
        for way, (block, there, _, _) in enumerate(self._ways(k + 1)):

            @pl.when(there)
            def _(way=way, block=block):
                for copy in self._pairs(way, k, block):
                    copy.start()

    def ready(self, k):
        for way, (block, there, _, _) in enumerate(self._ways(k + 1)):

            @pl.when(there)
            def _(way=way, block=block):
                wait_recv(self._pairs(way, k, block))

    def drain(self, line=True, pairs=True):
        def one(k, carry):
            for way, (_, there, onward, to) in enumerate(self._ways(k) if line else ()):

                @pl.when(there & onward)
                def _(way=way, to=to):
                    wait_send(self._copies(way, k, self.at.s, to, False))

            for way, (_, there, _, _) in enumerate(self._ways(k + 1) if pairs else ()):

                @pl.when(there)
                def _(way=way):
                    wait_send(self._pairs(way, k, self.at.s))

            return carry

        lax.fori_loop(0, self.at.nz - 1, one, 0)


def upward(begin, end, body):
    if end > begin:

        def one(k, carry):
            body(k)
            return carry

        lax.fori_loop(begin, end, one, 0)


class LineSum:
    def __init__(self, at, mine, peer, land, work, io, send, recv, peer_recv):
        self.at, self.mine, self.peer, self.land, self.work = at, mine, peer, land, work
        self.io, self.send, self.recv, self.peer_recv = io, send, recv, peer_recv

    def _hop(self, way, d):
        at = self.at
        to = lax.rem(at.s + (1 if way == 0 else at.nz - 1), at.nz)
        return remote(self.work.at[way], self.land.at[way, d], self.send.at[way, d], self.recv.at[way, d], (at.sec, to, at.h))

    def _load(self, src, slot):
        copy = pltpu.make_async_copy(src, self.work.at[slot], self.io)
        copy.start()
        copy.wait()

    def _add(self, slot, src):
        self._load(src, 2)
        self.work[slot] = (self.work[slot].astype(F32) + self.work[2].astype(F32)).astype(BF16)

    def _own(self, slot, d):
        at = self.at
        remote(self.mine.at[d], self.peer.at[d], self.peer_recv.at[d], self.peer_recv.at[d], (1 - at.sec, at.s, at.h)).wait_recv()
        self._load(self.peer.at[d], 2)
        self.work[slot] = (self.mine[d].astype(F32) + self.work[2].astype(F32)).astype(BF16)

    def slot(self, i):
        at = self.at
        for way in range(2):
            begun = i - at.s if way == 0 else i - (at.nz - 1 - at.s)
            d = at.nz - 1 - begun if way == 0 else begun
            earlier = at.s > 0 if way == 0 else at.s < at.nz - 1

            @pl.when((begun >= 0) & (i < at.nz - 1))
            def _(way=way, d=d, begun=begun, earlier=earlier):
                @pl.when(begun > 0)
                def _():
                    self._hop(way, d + 1 if way == 0 else d - 1).wait_send()

                self._own(way, d)

                @pl.when(earlier)
                def _():
                    self._hop(way, d).wait_recv()
                    self._add(way, self.land.at[way, d])

                self._hop(way, d).start()

    def last(self):
        at = self.at

        @pl.when(at.s < at.nz - 1)
        def _():
            self._hop(0, at.s + 1).wait_send()

        @pl.when(at.s > 0)
        def _():
            self._hop(1, at.s - 1).wait_send()

        self._own(0, at.s)

        @pl.when(at.s > 0)
        def _():
            self._hop(0, at.s).wait_recv()
            self._add(0, self.land.at[0, at.s])

        @pl.when(at.s < at.nz - 1)
        def _():
            self._hop(1, at.s).wait_recv()
            self._add(0, self.land.at[1, at.s])


def taker(refs):
    refs = list(refs)

    def take(n):
        out = refs[:n]
        del refs[:n]
        return out

    return take


def weight_slots(cat, out, gate, up, down, qk, width):
    at_row, views = 0, []
    for size in (qk, qk, width, width):
        views.append(cat.at[pl.ds(at_row, size)])
        at_row += size
    return views + [out, gate, up, down]


SAVED = 11


def fwd_kernel(dims, *refs):
    nz, nh, rows, heads = dims
    take = taker(refs)
    lens, inputs, out_grad, small_own, tables = take(5)
    own = take(8)
    small_other = take(1)[0]
    other = take(8)
    saved = [take(SAVED), take(SAVED)]
    x_out, gath_g1, gath_n2, n2_out = take(4)
    mats = [take(5), take(5)]
    (x_s, n1_s, n2_s, qk_s, u_s, edge_s, o_s, c_s, cx_s, yx_s, ss, sr, sin_s, g_s, gb_s, part_s, got_s, f_s, v_s, t_s, xo_s, h_s, sm_s) = take(23)
    w_sem, io_sem, save_sem, x_send, x_recv, e_send, e_recv, st_send, st_recv, head_send, head_recv = take(11)
    r_send, r_recv, p_send, p_recv = take(4)
    at = Place(lens, nz, nh, rows)
    d = x_s.shape[1]
    width, qk = heads * HD, heads * FEAT
    core = (1 - at.sec, at.s, at.h)
    slots = [weight_slots(*m, qk, width) for m in mats]

    x_copy = pltpu.make_async_copy(inputs.at[at.sec], x_s, io_sem.at[0])
    x_copy.start()

    def local(layer, i):
        return pltpu.make_async_copy(own[i].at[0], slots[layer][i], w_sem.at[i])

    def swap(layer, i):
        return remote(own[i].at[0], slots[layer][i], x_send.at[i], x_recv.at[i], core)

    def stash(layer, i):
        return pltpu.make_async_copy(slots[layer][i], other[i].at[0], w_sem.at[8 + i])

    for here in range(2):

        @pl.when(at.sec == here)
        def _(here=here):
            for i in (2, 0, 1, 3, 4, 5, 6, 7):
                local(here, i).start()

    at.barrier(True, True, True)
    small_swap = remote(small_own, small_other, x_send.at[8], x_recv.at[8], core)
    small_swap.start()
    for here in range(2):

        @pl.when(at.sec == here)
        def _(here=here):
            for i in (2, 0, 1, 3, 4, 5, 6, 7):
                swap(here, i).start()

    ring_g = Ring(at, out_grad.at[at.sec], gath_g1, r_send.at[0], r_recv.at[0], p_send.at[0], p_recv.at[0])
    ring_n = Ring(at, gath_n2.at[at.s], gath_n2, r_send.at[1], r_recv.at[1], p_send.at[1], p_recv.at[1])
    small_swap.wait_recv()
    small_copy = pltpu.make_async_copy(small_other, sm_s, io_sem.at[1])
    small_copy.start()
    small_copy.wait()

    def wait_weight(layer, i):
        @pl.when(at.sec == layer)
        def _():
            local(layer, i).wait()

        @pl.when(at.sec != layer)
        def _():
            swap(layer, i).wait_recv()
            stash(layer, i).start()

    allowed = at.allowed()
    applies, tail, prior = at.applies(), at.tail(), at.prior_seg(at.s)
    my_pos = at.first + at.h * at.part + lax.broadcasted_iota(jnp.int32, (at.part, 1), 0)
    my_valid = my_pos < at.tot

    def layer_forward(layer, x_s, hooks):
        cat, w_out, w_gate, w_up, w_down = mats[layer]
        small = jnp.where(at.sec == layer, small_own[...], sm_s[...])
        gain_attn, gain_ffn, taps = small[0:1], small[1:2], small[2 : 2 + KW]
        keep = []

        def save(src, i):
            copy = pltpu.make_async_copy(src, saved[layer][i], save_sem.at[i])
            copy.start()
            keep.append(copy)

        hooks["begin"]()
        n1_s[...] = norm_rows(x_s[...].astype(F32), gain_attn).astype(BF16)
        save(x_s.at[at.mine], 0)
        save(n1_s, 1)
        wait_weight(layer, 2)
        u_s[8 : 8 + rows, :width] = dot_nt(n1_s[...], cat[2 * qk : 2 * qk + width, :]).astype(BF16).astype(F32)
        edge = remote(
            u_s.at[pl.ds(rows, 8)], edge_s.at[layer], e_send.at[layer], e_recv.at[layer],
            (at.sec, lax.rem(at.s + 1, nz), at.h),
        )

        @pl.when(at.s + 1 < nz)
        def _():
            edge.start()

        wait_weight(layer, 0)
        wait_weight(layer, 1)
        low = dot_nt(n1_s[...], cat[0 : 2 * qk, :]).astype(BF16).astype(F32)
        qk_s[...] = (low * 0.5).astype(BF16)
        save(qk_s, 2)
        a_low, b_low = qk_s[:, 0:qk], qk_s[:, qk : 2 * qk]

        @pl.when(at.s > 0)
        def _():
            edge.wait_recv()

        u_s[0:8, :] = edge_s[layer]
        save(u_s, 3)
        convolve(at, u_s, taps, c_s, cx_s, heads)

        for head in range(heads):
            one, two = lift_parts(b_low, tables, 2, head)
            psi = jnp.where(tail, one * two, 0.0).astype(BF16)
            ss[layer, head] = dot_tn(psi, cx_s[head])[:PSI_SENT].astype(BF16)

        def state(k):
            return remote(
                ss.at[layer], sr.at[layer, at.s], st_send.at[layer, k - 1], st_recv.at[layer, at.s],
                (at.sec, lax.rem(at.s + k, nz), at.h),
            )

        for k in range(1, nz):

            @pl.when(at.s + k < nz)
            def _(k=k):
                state(k).start()

        wait_weight(layer, 3)
        o_s[:, :width] = dot_nt(n1_s[...], cat[2 * qk + width :, :])
        save(o_s, 4)
        for head in range(heads):
            e = dot_nt(a_low, head_only(b_low, head))
            kern = jnp.where(allowed, 1.0 + e + 0.5 * e * e, 0.0).astype(BF16)
            yx_s[head] = dot_nn(kern, cx_s[head])
        for j in range(nz - 1):

            @pl.when(j < at.s)
            def _(j=j):
                remote(ss.at[layer], sr.at[layer, j], st_send.at[layer, 0], st_recv.at[layer, j], core).wait_recv()

        hooks["states"]()
        sin_s[...] = jnp.zeros_like(sin_s)
        for head in range(heads):
            total = jnp.zeros((PSI_SENT, LANES), F32)
            for j in range(nz - 1):
                counts = (j < at.s) & (at.last_seg(j) == prior)
                total = total + jnp.where(counts, sr[layer, j, head].astype(F32), 0.0)
            sin_s[head, 0:PSI_SENT] = total.astype(BF16)
            one, two = lift_parts(a_low, tables, 1, head)
            psi = (one * two).astype(BF16)
            yx = yx_s[head] + jnp.where(applies, dot_nn(psi, sin_s[head]), 0.0)
            yx_s[head] = yx
            gate = o_s[:, head * HD : head * HD + LANES]
            y = yx / yx[:, HD : HD + 1]
            g_s[:, head * HD : head * HD + LANES] = y * (gate * jax.nn.sigmoid(gate))
        gb_s[...] = g_s[:, :width].astype(BF16)
        save(yx_s, 5)
        save(sin_s, 6)
        save(gb_s, 7)

        wait_weight(layer, 4)

        s1 = []
        for half in range(2):
            cols = half_cols(w_out, half)
            part_s[layer, 0, :, cols] = dot_nn(gb_s[...], w_out[:, cols]).astype(BF16)
            s1 += scatter_start(at, part_s.at[layer, 0], got_s, head_send.at[layer, 0], head_recv.at[layer, 0], half)
        hooks["rs1"]()
        hidden = x_s[at.mine].astype(F32) + scatter_sum(at, part_s.at[layer, 0], got_s, s1)
        h_s[...] = hidden
        n2_s[at.mine] = norm_rows(hidden, gain_ffn).astype(BF16)
        s2 = gather_start(at, n2_s, head_send.at[layer, 1], head_recv.at[layer, 1])
        save(h_s, 8)
        hooks["ag1"]()
        wait_recv(s2)
        hooks["n2"]()

        wait_weight(layer, 5)
        wait_weight(layer, 6)

        def up_chunk(at_row, size):
            cols = pl.ds(at_row, size)
            f = dot_nt(n2_s[...], w_gate[cols, :])
            v = dot_nt(n2_s[...], w_up[cols, :])
            f_s[:, cols] = f.astype(BF16)
            v_s[:, cols] = v.astype(BF16)
            t_s[:, cols] = (f * jax.nn.sigmoid(f) * v).astype(BF16)

        chunks(t_s.shape[1], 256, up_chunk)
        save(f_s, 9)
        save(v_s, 10)
        wait_weight(layer, 7)

        s3 = []
        for half in range(2):
            cols = half_cols(w_down, half)
            part_s[layer, 1, :, cols] = dot_nn(t_s[...], w_down[:, cols]).astype(BF16)
            s3 += scatter_start(at, part_s.at[layer, 1], got_s, head_send.at[layer, 2], head_recv.at[layer, 2], half)
        hooks["rs2"]()
        feed = scatter_sum(at, part_s.at[layer, 1], got_s, s3)
        xo_s[layer, at.mine] = jnp.where(my_valid, h_s[...] + feed, 0.0).astype(BF16)
        s4 = gather_start(at, xo_s.at[layer], head_send.at[layer, 3], head_recv.at[layer, 3])
        hooks["ag2"]()
        wait_recv(s4)
        for copy in keep:
            copy.wait()

        def finish():
            wait_send(s1 + s2 + s3 + s4)

            @pl.when(at.s + 1 < nz)
            def _():
                edge.wait_send()

            for k in range(1, nz):

                @pl.when(at.s + k < nz)
                def _(k=k):
                    state(k).wait_send()

        return finish

    def nothing():
        pass

    n2_copy = pltpu.make_async_copy(n2_s, gath_n2.at[at.s], io_sem.at[2])

    def f0_n2():
        n2_copy.start()
        ring_g.step(1)

    def f1_begin():
        n2_copy.wait()
        upward(3, nz, ring_g.step)
        upward(0, nz - 1, ring_g.pair)
        ring_n.step(0)

    def f1_n2():
        n2_last.start()
        ring_n.step(2)

    x_copy.wait()
    finish_0 = layer_forward(
        0, x_s, dict(begin=nothing, states=nothing, rs1=lambda: ring_g.step(0), ag1=nothing, n2=f0_n2, rs2=nothing, ag2=lambda: ring_g.step(2))
    )
    finish_0()

    def out_copy(layer):
        near = pltpu.make_async_copy(xo_s.at[layer], x_out.at[at.sec], io_sem.at[3])
        far = remote(xo_s.at[layer], x_out.at[at.sec], x_send.at[9], x_recv.at[9], core)
        return near, far

    def send_out(layer):
        near, far = out_copy(layer)

        @pl.when(at.sec == layer)
        def _():
            near.start()

        @pl.when(at.sec != layer)
        def _():
            far.start()

    send_out(0)
    n2_last = pltpu.make_async_copy(n2_s, n2_out, io_sem.at[4])
    finish_1 = layer_forward(
        1, xo_s.at[0], dict(begin=f1_begin, states=nothing, rs1=lambda: ring_n.step(1), ag1=nothing, n2=f1_n2, rs2=nothing, ag2=nothing)
    )
    send_out(1)
    finish_1()
    upward(0, nz - 1, ring_g.ready)
    upward(3, nz, ring_n.step)
    n2_last.wait()
    ring_g.drain()
    ring_n.drain(pairs=False)
    near, far = out_copy(0)
    near.wait()
    far.wait_send()
    far.wait_recv()
    small_swap.wait_send()
    for here in range(2):

        @pl.when(at.sec == here)
        def _(here=here):
            for i in range(8):
                swap(here, i).wait_send()
                stash(1 - here, i).wait()


def bwd_kernel(dims, *refs):
    nz, nh, rows, heads = dims
    take = taker(refs)
    lens, inputs_grad, small_own, small_other, tables = take(5)
    own = take(8)
    other = take(8)
    saved = [take(SAVED), take(SAVED)]
    gath_g1, _, n2_1 = take(3)
    ig_o, gains_o = take(2)
    att_o = take(2)
    ffn_o = take(3)
    gath_n2_1, gath_g0, gath_n2_0 = take(3)
    a_peer, a_land = take(2), take(2)
    wr_o = take(3)
    mats = take(5)
    keep_s = take(SAVED)
    (grad_s, t_s, part_s, got_s, dm_s, dh_s, dg_s, do_s, cx_s, dyx_s, ss, sr, st_s, da_s, db_s, dc_s, edge_s, dcat_s, ig_s) = take(19)
    gsum_s, gpeer_s, gtot_s, gz_s, gh_s = take(5)
    acc = take(3)
    wx_s = take(3)
    blk_n2, blk_g, n2t_s, gt_s = take(4)
    a_s, work_s = take(2), take(2)
    (w_sem, io_sem, keep_sem, e_send, e_recv, st_send, st_recv, head_send, head_recv, r_send, r_recv, p_send, p_recv) = take(13)
    (wx_send, wx_recv, ap_send, ap_recv, l_send, l_recv, x_send, x_recv, gz_send, gz_recv, gh_send, gh_recv) = take(12)
    x_s, n1_s, qk_s, u_s, o_s, yx_s, sin_s, gb_s, h_s, f_s, v_s = keep_s
    df_s, dv_s = f_s, v_s
    at = Place(lens, nz, nh, rows)
    cat, w_out, w_gate, w_up, w_down = mats
    d = n1_s.shape[1]
    width, qk = heads * HD, heads * FEAT
    block = d // nz
    core = (1 - at.sec, at.s, at.h)
    slots = weight_slots(*mats, qk, width)

    def weight_start(layer, i):
        @pl.when(at.sec == layer)
        def _():
            pltpu.make_async_copy(own[i].at[0], slots[i], w_sem.at[i]).start()

        @pl.when(at.sec != layer)
        def _():
            pltpu.make_async_copy(other[i].at[0], slots[i], w_sem.at[i]).start()

    def weight_wait(i):
        pltpu.make_async_copy(own[i].at[0], slots[i], w_sem.at[i]).wait()

    def keep_copy(layer, i):
        return pltpu.make_async_copy(saved[layer][i], keep_s[i], keep_sem.at[i])

    ring_n = Ring(at, n2_1, gath_n2_1, r_send.at[0], r_recv.at[0], p_send.at[0], p_recv.at[0])
    ring_g = Ring(at, ig_s.at[1], gath_g0, r_send.at[1], r_recv.at[1], p_send.at[1], p_recv.at[1])
    ring_0 = Ring(at, None, gath_n2_0, None, None, p_send.at[2], p_recv.at[2])
    line = [
        [
            LineSum(
                at, a_s[g], a_peer[g].at[layer], a_land[g].at[layer], work_s[g], io_sem.at[4],
                l_send.at[layer, g], l_recv.at[layer, g], ap_recv.at[layer, g],
            )
            for g in range(2)
        ]
        for layer in range(2)
    ]

    def turn_blocks(n2_ref, g_ref):
        for part in range(nz):

            @pl.when(at.s == part)
            def _(part=part):
                n2t_s[...] = n2_ref[:, part * block : (part + 1) * block].T
                gt_s[...] = g_ref[:, part * block : (part + 1) * block].T

    def own_piece(layer):
        copy = pltpu.make_async_copy(n2_1 if layer == 1 else gath_n2_0.at[at.s], blk_n2, io_sem.at[0])
        copy.start()
        copy.wait()
        turn_blocks(blk_n2, grad_s)

        def hidden(at_col, size):
            cols = pl.ds(at_col, size)
            acc[0][:, cols] = dot_nn(n2t_s[...], df_s[:, cols])
            acc[1][:, cols] = dot_nn(n2t_s[...], dv_s[:, cols])
            acc[2][:, cols] = dot_nn(gt_s[...], t_s[:, cols])

        chunks(w_gate.shape[0], 640, hidden)

    def piece(layer, i):
        which = order(at, i)
        n2_src = (gath_n2_1 if layer == 1 else gath_n2_0).at[which]
        g_src = (gath_g1 if layer == 1 else gath_g0).at[which]
        loads = [pltpu.make_async_copy(n2_src, blk_n2, io_sem.at[0]), pltpu.make_async_copy(g_src, blk_g, io_sem.at[1])]
        for copy in loads:
            copy.start()
        for copy in loads:
            copy.wait()
        pos = which * rows + lax.broadcasted_iota(jnp.int32, (rows, 1), 0)
        blk_g[...] = jnp.where(pos < at.tot, blk_g[...].astype(F32), 0.0).astype(BF16)
        turn_blocks(blk_n2, blk_g)

        def hidden(at_row, size):
            cols = pl.ds(at_row, size)
            f = dot_nt(blk_n2[...], w_gate[cols, :])
            v = dot_nt(blk_n2[...], w_up[cols, :])
            dt = dot_nt(blk_g[...], w_down[cols, :])
            sig = jax.nn.sigmoid(f)
            act = f * sig
            t = (act * v).astype(BF16)
            df = (dt * v * (sig + act * (1.0 - sig))).astype(BF16)
            dv = (dt * act).astype(BF16)
            acc[0][:, cols] += dot_nn(n2t_s[...], df)
            acc[1][:, cols] += dot_nn(n2t_s[...], dv)
            acc[2][:, cols] += dot_nn(gt_s[...], t)

        chunks(w_gate.shape[0], 640, hidden)

    def ffn_swap(i):
        return remote(wx_s[i], wr_o[i], wx_send.at[i], wx_recv.at[i], core)

    def ffn_own(i):
        return pltpu.make_async_copy(acc[i], ffn_o[i], io_sem.at[5 + i])

    def ffn_send(layer):
        @pl.when(at.sec != layer)
        def _():
            for i in range(3):
                wx_s[i][...] = acc[i][...].astype(BF16)
                ffn_swap(i).start()

        @pl.when(at.sec == layer)
        def _():
            for i in range(3):
                ffn_own(i).start()

    def ffn_done(layer):
        @pl.when(at.sec == layer)
        def _():
            for i in range(3):
                ffn_own(i).wait()

    def ig_copy(layer):
        near = pltpu.make_async_copy(ig_s.at[layer], ig_o.at[at.sec], io_sem.at[3])
        far = remote(ig_s.at[layer], ig_o.at[at.sec], x_send.at[0], x_recv.at[0], core)
        return near, far

    def ig_send(layer):
        near, far = ig_copy(layer)

        @pl.when(at.sec == layer)
        def _():
            near.start()

        @pl.when(at.sec != layer)
        def _():
            far.start()

    allowed = at.allowed()
    applies, tail, mine_last = at.applies(), at.tail(), at.last_seg(at.s)
    valid = at.pos() < at.tot
    lane = lax.broadcasted_iota(jnp.int32, (rows, LANES), 1)

    def line_core(layer, g):
        return g

    def peer_chunk(layer, g, i):
        return remote(a_s[g].at[i], a_peer[g].at[layer, i], ap_send.at[g, i], ap_recv.at[layer, g, i], core)

    def mixer_grads(layer, g):
        late = 2 * qk + width
        for i in range(nz):
            cols = slice(i * block, (i + 1) * block)
            if g == 0:
                a_s[0][i, :, 0:width] = dot_tn(n1_s[:, cols], dcat_s[:, late:]).astype(BF16)
                a_s[0][i, :, width:] = dot_tn(dm_s[:, cols], gb_s[...]).astype(BF16)
            else:
                a_s[1][i] = dot_tn(n1_s[:, cols], dcat_s[:, 0:late]).astype(BF16)

            @pl.when(at.sec != line_core(layer, g))
            def _(i=i):
                peer_chunk(layer, g, i).start()

    def mixer_sent(layer, g):
        for i in range(nz):

            @pl.when(at.sec != line_core(layer, g))
            def _(i=i):
                peer_chunk(layer, g, i).wait_send()

    def layer_backward(layer, hooks):
        small = jnp.where(at.sec == layer, small_own[...], small_other[...])
        gain_attn, gain_ffn, taps = small[0:1], small[1:2], small[2 : 2 + KW]
        hooks["begin"]()

        weight_wait(7)
        keep_copy(layer, 9).wait()
        keep_copy(layer, 10).wait()

        def down_chunk(at_row, size):
            cols = pl.ds(at_row, size)
            dt = dot_nt(grad_s[...], w_down[cols, :])
            f = f_s[:, cols].astype(F32)
            v = v_s[:, cols].astype(F32)
            sig = jax.nn.sigmoid(f)
            act = f * sig
            t_s[:, cols] = (act * v).astype(BF16)
            df_s[:, cols] = (dt * v * (sig + act * (1.0 - sig))).astype(BF16)
            dv_s[:, cols] = (dt * act).astype(BF16)

        chunks(df_s.shape[1], 256, down_chunk)
        weight_wait(5)
        weight_wait(6)

        s1 = []
        for half in range(2):
            cols = half_cols(w_up, half)
            part = dot_nn(df_s[...], w_gate[:, cols]) + dot_nn(dv_s[...], w_up[:, cols])
            part_s[:, cols] = part.astype(BF16)
            s1 += scatter_start(at, part_s, got_s, head_send.at[layer, 0], head_recv.at[layer, 0], half)
        hooks["rs1"]()
        keep_copy(layer, 3).wait()
        convolve(at, u_s, taps, do_s, cx_s, heads)
        keep_copy(layer, 8).wait()
        dn2 = scatter_sum(at, part_s, got_s, s1)
        back, gain_grad = norm_rows_back(h_s[...], gain_ffn, dn2)
        gsum_s[layer, 1:2, :] = gain_grad
        dh = grad_s[at.mine].astype(F32) + back
        dh_s[...] = dh
        dm_s[at.mine] = dh.astype(BF16)
        s2 = gather_start(at, dm_s, head_send.at[layer, 1], head_recv.at[layer, 1])
        for i in (0, 1, 2, 4, 5, 6, 7):
            keep_copy(layer, i).wait()
        for i in (4, 0, 1, 2, 3):
            weight_wait(i)
        a_low, b_low = qk_s[:, 0:qk], qk_s[:, qk : 2 * qk]
        hooks["ag1"]()
        wait_recv(s2)
        hooks["dm"]()

        def out_chunk(at_row, size):
            cols = pl.ds(at_row, size)
            dg_s[:, cols] = dot_nt(dm_s[...], w_out[cols, :])

        chunks(width, 256, out_chunk)
        for head in range(heads):
            cols = slice(head * HD, head * HD + LANES)
            gate, dg, yx = o_s[:, cols], dg_s[:, cols], yx_s[head]
            sig = jax.nn.sigmoid(gate)
            inverse = 1.0 / yx[:, HD : HD + 1]
            y = yx * inverse
            do_s[:, cols] = dg * y * sig * (1.0 + gate * (1.0 - sig))
            dy = jnp.where(lane < HD, dg * gate * sig, 0.0)
            dden = -jnp.sum(dy * y, axis=1, keepdims=True) * inverse
            dyx_s[head] = jnp.where(lane == HD, dden, dy * inverse).astype(BF16)
            one, two = lift_parts(a_low, tables, 1, head)
            psi = jnp.where(applies, one * two, 0.0).astype(BF16)
            ss[layer, head] = dot_tn(psi, dyx_s[head])[:PSI_SENT].astype(BF16)
        dcat_s[:, 2 * qk + width :] = do_s[:, :width].astype(BF16)

        def state(k):
            return remote(
                ss.at[layer], sr.at[layer, at.s], st_send.at[layer, k - 1], st_recv.at[layer, at.s],
                (at.sec, lax.rem(at.s + nz - k, nz), at.h),
            )

        for k in range(1, nz):

            @pl.when(at.s - k >= 0)
            def _(k=k):
                state(k).start()

        da_s[...] = jnp.zeros_like(da_s)
        db_s[...] = jnp.zeros_like(db_s)
        for head in range(heads):
            a_own, b_own = head_only(a_low, head), head_only(b_low, head)
            e = dot_nt(a_low, b_own)
            kern = jnp.where(allowed, 1.0 + e + 0.5 * e * e, 0.0).astype(BF16)
            dkern = dot_nt(dyx_s[head], cx_s[head])
            de = jnp.where(allowed, dkern * (1.0 + e), 0.0).astype(BF16)
            one, two = lift_parts(a_low, tables, 1, head)
            dpsi = jnp.where(applies, dot_nt(dyx_s[head], sin_s[head]), 0.0)
            pcols = slice(head * PSI, (head + 1) * PSI)
            da_s[...] += (
                dot_nn(de, b_own)
                + dot_nt((dpsi * two).astype(BF16), tables[0, :, pcols])
                + dot_nt((dpsi * one).astype(BF16), tables[1, :, pcols])
            )
            db_s[...] += dot_tn(de, a_own)
            yx_s[head] = dot_tn(kern, dyx_s[head])
        hooks["local"]()
        for j in range(1, nz):

            @pl.when(j > at.s)
            def _(j=j):
                remote(ss.at[layer], sr.at[layer, j], st_send.at[layer, 0], st_recv.at[layer, j], core).wait_recv()

        hooks["states"]()
        st_s[...] = jnp.zeros_like(st_s)
        for head in range(heads):
            total = jnp.zeros((PSI_SENT, LANES), F32)
            for j in range(1, nz):
                counts = (j > at.s) & (at.prior_seg(j) == mine_last)
                total = total + jnp.where(counts, sr[layer, j, head].astype(F32), 0.0)
            st_s[head, 0:PSI_SENT] = total.astype(BF16)
            one, two = lift_parts(b_low, tables, 2, head)
            psi = (one * two).astype(BF16)
            dpsi = jnp.where(tail, dot_nt(cx_s[head], st_s[head]), 0.0)
            pcols = slice(head * PSI, (head + 1) * PSI)
            db_s[...] += dot_nt((dpsi * two).astype(BF16), tables[0, :, pcols]) + dot_nt(
                (dpsi * one).astype(BF16), tables[2, :, pcols]
            )
            dc = yx_s[head] + jnp.where(tail, dot_nn(psi, st_s[head]), 0.0)
            dc_s[0:rows, head * HD : head * HD + LANES] = dc
        edge = remote(
            dc_s.at[pl.ds(0, 8)], edge_s.at[layer], e_send.at[layer], e_recv.at[layer],
            (at.sec, lax.rem(at.s + nz - 1, nz), at.h),
        )

        @pl.when(at.s > 0)
        def _():
            edge.start()

        dcat_s[:, 0:qk] = (da_s[...] * 0.5).astype(BF16)
        dcat_s[:, qk : 2 * qk] = (db_s[...] * 0.5).astype(BF16)
        gsum_s[layer, 2:8, :] = jnp.zeros((6, d), F32)
        for j in range(KW):
            product = dc_s[0:rows, :width] * u_s[8 - j : 8 - j + rows, :width]
            gsum_s[layer, 2 + j : 3 + j, :width] = jnp.sum(jnp.where(at.same(-j), product, 0.0), axis=0, keepdims=True)

        @pl.when(at.s + 1 < nz)
        def _():
            edge.wait_recv()

        dc_s[rows : rows + 8, :] = edge_s[layer]
        du = taps[0:1, :width] * dc_s[0:rows, :width]
        for j in range(1, KW):
            du = du + jnp.where(at.same(j), dc_s[j : j + rows, :width] * taps[j : j + 1, :width], 0.0)
        dcat_s[:, 2 * qk : 2 * qk + width] = du.astype(BF16)

        wait_send(s1)
        s3 = []
        for half in range(2):
            cols = half_cols(cat, half)
            part_s[:, cols] = dot_nn(dcat_s[...], cat[:, cols]).astype(BF16)
            s3 += scatter_start(at, part_s, got_s, head_send.at[layer, 2], head_recv.at[layer, 2], half)
        hooks["rs2"]()
        dn1 = scatter_sum(at, part_s, got_s, s3)
        back, gain_grad = norm_rows_back(x_s[...].astype(F32), gain_attn, dn1)
        gsum_s[layer, 0:1, :] = gain_grad
        ig_s[layer, at.mine] = (dh_s[...] + back).astype(BF16)
        s4 = gather_start(at, ig_s.at[layer], head_send.at[layer, 3], head_recv.at[layer, 3])
        hooks["ag2"]()
        wait_recv(s4)
        ig_send(layer)
        wait_send(s3)

        def finish():
            wait_send(s2 + s4)

            @pl.when(at.s > 0)
            def _():
                edge.wait_send()

            for k in range(1, nz):

                @pl.when(at.s - k >= 0)
                def _(k=k):
                    state(k).wait_send()

        return finish

    def owner(layer, what):
        @pl.when(at.sec == layer)
        def _():
            what()

    g_copy = pltpu.make_async_copy(inputs_grad.at[at.sec], grad_s, io_sem.at[2])
    g_copy.start()
    for i in (7, 5, 6, 4, 0, 1, 2, 3):
        weight_start(1, i)
    for i in (9, 10, 8, 3, 2, 4, 5, 6, 7, 1, 0):
        keep_copy(1, i).start()
    at.barrier(True, True, True)
    ring_n.step(0)
    g_copy.wait()
    grad_s[...] = jnp.where(valid, grad_s[...].astype(F32), 0.0).astype(BF16)

    def slot(layer, g, i):
        owner(line_core(layer, g), lambda: line[layer][g].slot(i))

    def far_sum(g):
        return remote(work_s[g].at[0], att_o[g], x_send.at[2 + g], x_recv.at[2 + g], core)

    def line_last(layer, g):
        def go():
            upward(3, nz - 1, line[layer][g].slot)
            line[layer][g].last()
            if line_core(layer, g) == layer:
                copy = pltpu.make_async_copy(work_s[g].at[0], att_o[g], io_sem.at[8])
                copy.start()
                copy.wait()
            else:
                far_sum(g).start()

        owner(line_core(layer, g), go)

    def pieces(layer, ring, begin, end):
        def one(k):
            ring.ready(k - 1)
            if layer == 0:
                ring_0.ready(k - 1)
            piece(layer, k)

        upward(begin, end, one)

    def spread(ring):
        upward(3, nz, ring.step)
        upward(1, nz - 1, ring.pair)

    def nothing():
        pass

    gain_swap = remote(gsum_s.at[1 - at.sec], gpeer_s, x_send.at[1], x_recv.at[1], core)

    def gain_seq(k):
        to = lax.rem(at.s + k, nz)
        return remote(gtot_s.at[0], gz_s.at[k - 1], gz_send.at[k - 1], gz_recv.at[k - 1], (at.sec, to, at.h))

    def b1_rs1():
        own_piece(1)
        ring_n.step(1)
        ring_n.pair(0)

    def b1_ag1():
        ring_n.step(2)
        pieces(1, ring_n, 1, 2)

    def b1_local():
        upward(0, nz - 1, ring_0.pair)
        mixer_grads(1, 0)

    def b1_rs2():
        mixer_grads(1, 1)
        slot(1, 0, 0)
        pieces(1, ring_n, 2, 3)

    def b1_ag2():
        for i in (4, 0, 1, 2, 3):
            weight_start(0, i)
        for i in (9, 10, 8, 3, 2, 4, 5, 6, 7, 1, 0):
            keep_copy(0, i).start()
        slot(1, 0, 1)
        pieces(1, ring_n, 3, nz)
        for i in (7, 5, 6):
            weight_start(0, i)
        ffn_send(1)

    finish_1 = layer_backward(
        1,
        dict(
            begin=nothing, rs1=b1_rs1, ag1=b1_ag1, dm=lambda: spread(ring_n), local=b1_local,
            states=nothing, rs2=b1_rs2, ag2=b1_ag2,
        ),
    )
    finish_1()
    grad_s[...] = jnp.where(valid, ig_s[1].astype(F32), 0.0).astype(BF16)

    def b0_begin():
        ring_g.step(0)
        slot(1, 0, 2)
        slot(1, 1, 0)

    def b0_rs1():
        ffn_done(1)
        own_piece(0)
        ring_g.step(1)
        ring_g.pair(0)
        slot(1, 1, 1)

    def b0_ag1():
        ring_g.step(2)
        pieces(0, ring_g, 1, 2)
        slot(1, 1, 2)

    def b0_local():
        line_last(1, 0)
        mixer_sent(1, 0)
        mixer_grads(0, 0)

    def b0_states():
        line_last(1, 1)

    def b0_rs2():
        mixer_sent(1, 1)
        mixer_grads(0, 1)
        owner(0, lambda: far_sum(0).wait_send())
        slot(0, 0, 0)
        pieces(0, ring_g, 2, 3)
        slot(0, 0, 1)
        slot(0, 1, 0)

    def b0_ag2():
        gain_swap.start()
        pieces(0, ring_g, 3, nz)
        ffn_send(0)
        slot(0, 0, 2)
        slot(0, 1, 1)
        gain_swap.wait_recv()
        gtot_s[0] = gsum_s[at.sec] + gpeer_s[...]
        for k in range(1, nz):
            gain_seq(k).start()

    finish_0 = layer_backward(
        0,
        dict(
            begin=b0_begin, rs1=b0_rs1, ag1=b0_ag1, dm=lambda: spread(ring_g), local=b0_local,
            states=b0_states, rs2=b0_rs2, ag2=b0_ag2,
        ),
    )

    slot(0, 1, 2)
    line_last(0, 0)
    for k in range(1, nz):
        gain_seq(k).wait_recv()
    total = gtot_s[0]
    for k in range(1, nz):
        total = total + gz_s[k - 1]
    gtot_s[1] = total

    def gain_head(m):
        return remote(gtot_s.at[1], gh_s.at[m - 1], gh_send.at[m - 1], gh_recv.at[m - 1], (at.sec, at.s, at.h ^ m))

    for m in range(1, nh):
        gain_head(m).start()
    line_last(0, 1)
    ffn_done(0)
    mixer_sent(0, 0)
    mixer_sent(0, 1)
    owner(1, lambda: far_sum(1).wait_send())
    owner(0, lambda: far_sum(1).wait_recv())
    owner(1, lambda: far_sum(0).wait_recv())
    for m in range(1, nh):
        gain_head(m).wait_recv()
    total = gtot_s[1, 0:2]
    for m in range(1, nh):
        total = total + gh_s[m - 1, 0:2]
    gains_o[...] = gtot_s[1]
    gains_o[0:2, :] = total

    finish_0()
    ring_n.drain()
    ring_g.drain()
    ring_0.drain(line=False)
    gain_swap.wait_send()
    for k in range(1, nz):
        gain_seq(k).wait_send()
    for m in range(1, nh):
        gain_head(m).wait_send()
    for i in range(3):
        ffn_swap(i).wait()
    near, far = ig_copy(0)
    near.wait()
    far.wait_send()
    far.wait_recv()


def final_kernel(qk, width, *refs):
    take = taker(refs)
    whole, far, (early, late), out, parts, held, held_far, (sems,) = take(5), take(3), take(2), take(5), take(5), take(5), take(3), take(1)
    loads = [pltpu.make_async_copy(a, b, sems.at[i]) for i, (a, b) in enumerate(zip(whole + far, held + held_far))]
    stores = [pltpu.make_async_copy(a, b, sems.at[8 + i]) for i, (a, b) in enumerate(zip(held, out))]
    for copy in loads:
        copy.start()
    g_q, g_k, g_v, g_o, g_out = parts
    turned = late[:, 0 : 2 * qk].astype(F32).T
    g_q[...] = turned[0:qk]
    g_k[...] = turned[qk : 2 * qk]
    g_v[...] = late[:, 2 * qk :].astype(F32)
    g_o[...] = early[:, 0:width].astype(F32)
    g_out[...] = early[:, width:].astype(F32).T
    for i in range(5):
        loads[i].wait()
        if i >= 2:
            loads[i + 3].wait()
            held[i][...] += held_far[i - 2][...].astype(F32)
        stores[i].start()
    for copy in stores:
        copy.wait()


def shape(dims, kind=BF16):
    return jax.ShapeDtypeStruct(tuple(dims), kind)


ANY = pl.BlockSpec(memory_space=pl.ANY)
VM = pl.BlockSpec(memory_space=pltpu.VMEM)
SM = pl.BlockSpec(memory_space=pltpu.SMEM)
DMA = pltpu.SemaphoreType.DMA


def params(number):
    return pltpu.CompilerParams(collective_id=number, has_side_effects=True, vmem_limit_bytes=VMEM_LIMIT)


def shards(nz, nh, inputs, out_grad, lengths, norm_attn, norm_ffn, w_query, w_key, w_value, w_output_gate, conv_kernel, w_out, w_gate, w_up, w_down):
    micro, rows, d = inputs.shape
    heads = w_query.shape[2] // FEAT
    width, qk, ff = w_value.shape[2], w_query.shape[2], w_gate.shape[2]
    part, block = rows // nh, d // nz
    dims = (nz, nh, rows, heads)
    wide = -(-((heads - 1) * HD + LANES) // LANES) * LANES
    groups = (2 * width, 2 * qk + width)
    tables = jnp.asarray(lift_tables(heads), BF16)
    turned = [jnp.swapaxes(w, 1, 2) for w in (w_query, w_key, w_value, w_output_gate)]
    own = (*turned, w_out, jnp.swapaxes(w_gate, 1, 2), jnp.swapaxes(w_up, 1, 2), w_down)
    small_own = jnp.concatenate(
        [norm_attn, norm_ffn, jnp.pad(conv_kernel[0], ((0, 0), (0, d - width))), jnp.zeros((3, d), F32)]
    )

    def vm(dims, kind=BF16):
        return pltpu.VMEM(tuple(dims), kind)

    mats = [vm((2 * qk + 2 * width, d)), vm((width, d)), vm((ff, d)), vm((ff, d)), vm((ff, d))]
    act = vm((rows, d))
    kept = [
        ((part, d), BF16),
        ((rows, d), BF16),
        ((rows, 2 * qk), BF16),
        ((rows + 8, wide), F32),
        ((rows, wide), F32),
        ((heads, rows, LANES), F32),
        ((heads, PSI, LANES), BF16),
        ((rows, width), BF16),
        ((part, d), F32),
        ((rows, ff), BF16),
        ((rows, ff), BF16),
    ]
    keep_shapes = [shape(*k) for k in kept]
    gathered = shape((nz, rows, d))
    outs = (
        [shape((8, d), F32)]
        + [shape(w.shape) for w in own]
        + keep_shapes * 2
        + [shape((micro, rows, d)), gathered, gathered, shape((rows, d))]
    )
    scratch = (
        mats
        + mats
        + [
            act,
            act,
            act,
            vm((rows, 2 * qk)),
            vm((rows + 8, wide), F32),
            vm((2, 8, wide), F32),
            vm((rows, wide), F32),
            vm((rows, wide), F32),
            vm((heads, rows, LANES)),
            vm((heads, rows, LANES), F32),
            vm((2, heads, PSI_SENT, LANES)),
            vm((2, nz, heads, PSI_SENT, LANES)),
            vm((heads, PSI, LANES)),
            vm((rows, wide), F32),
            vm((rows, width)),
            vm((2, 2, rows, d)),
            vm((nh - 1, part, d)),
            vm((rows, ff)),
            vm((rows, ff)),
            vm((rows, ff)),
            vm((2, rows, d)),
            vm((part, d), F32),
            vm((8, d), F32),
            DMA((16,)),
            DMA((5,)),
            DMA((SAVED,)),
            DMA((10,)),
            DMA((10,)),
            DMA((2,)),
            DMA((2,)),
            DMA((2, nz)),
            DMA((2, nz)),
            DMA((2, 4, 2 * (nh - 1))),
            DMA((2, 4, 2 * (nh - 1))),
            DMA((2, 2, nz - 1, 2)),
            DMA((2, 2, nz - 1, 2)),
            DMA((2, 2, nz - 1, 2)),
            DMA((2, 2, nz - 1, 2)),
        ]
    )
    first = pl.pallas_call(
        functools.partial(fwd_kernel, dims),
        out_shape=outs,
        in_specs=[SM, ANY, ANY, VM, VM] + [ANY] * 8,
        out_specs=[ANY] * len(outs),
        scratch_shapes=scratch,
        compiler_params=params(0),
    )(lengths, inputs, out_grad, small_own, tables, *own)
    small_other, other = first[0], first[1:9]
    saved = first[9 : 9 + 2 * SAVED]
    section_out, gath_g1, gath_n2_0, n2_1 = first[9 + 2 * SAVED :]

    outs = (
        [shape((micro, rows, d)), shape((8, d), F32)]
        + [shape((block, g)) for g in groups]
        + [shape((block, ff), F32)] * 3
        + [gathered, gathered, gathered]
        + [shape((2, nz, block, g)) for g in groups]
        + [shape((2, 2, nz, block, g)) for g in groups]
        + [shape((block, ff))] * 3
    )
    out_specs = [ANY, VM] + [ANY] * (len(outs) - 2)
    scratch = (
        mats
        + [vm(*k) for k in kept]
        + [
            act,
            vm((rows, ff)),
            act,
            vm((nh - 1, part, d)),
            act,
            vm((part, d), F32),
            vm((rows, wide), F32),
            vm((rows, wide), F32),
            vm((heads, rows, LANES)),
            vm((heads, rows, LANES)),
            vm((2, heads, PSI_SENT, LANES)),
            vm((2, nz, heads, PSI_SENT, LANES)),
            vm((heads, PSI, LANES)),
            vm((rows, qk), F32),
            vm((rows, qk), F32),
            vm((rows + 8, wide), F32),
            vm((2, 8, wide), F32),
            vm((rows, 2 * qk + 2 * width)),
            vm((2, rows, d)),
            vm((2, 8, d), F32),
            vm((8, d), F32),
            vm((2, 8, d), F32),
            vm((nz - 1, 8, d), F32),
            vm((nh - 1, 8, d), F32),
        ]
        + [vm((block, ff), F32)] * 3
        + [vm((block, ff))] * 3
        + [act, act, vm((block, rows)), vm((block, rows))]
        + [vm((nz, block, g)) for g in groups]
        + [vm((3, block, g)) for g in groups]
        + [
            DMA((8,)),
            DMA((12,)),
            DMA((SAVED,)),
            DMA((2,)),
            DMA((2,)),
            DMA((2, nz)),
            DMA((2, nz)),
            DMA((2, 4, 2 * (nh - 1))),
            DMA((2, 4, 2 * (nh - 1))),
            DMA((2, 2, nz - 1, 2)),
            DMA((2, 2, nz - 1, 2)),
            DMA((3, 2, nz - 1, 2)),
            DMA((3, 2, nz - 1, 2)),
            DMA((3,)),
            DMA((3,)),
            DMA((2, nz)),
            DMA((2, 2, nz)),
            DMA((2, 2, 2, nz)),
            DMA((2, 2, 2, nz)),
            DMA((4,)),
            DMA((4,)),
            DMA((nz - 1,)),
            DMA((nz - 1,)),
            DMA((nh - 1,)),
            DMA((nh - 1,)),
        ]
    )
    second = pl.pallas_call(
        functools.partial(bwd_kernel, dims),
        out_shape=outs,
        in_specs=[SM, ANY, VM, VM, VM] + [ANY] * (16 + 2 * SAVED + 3),
        out_specs=out_specs,
        scratch_shapes=scratch,
        input_output_aliases={5 + 16 + 2 * SAVED + 1: 9},
        compiler_params=params(1),
    )(lengths, out_grad, small_own, small_other, tables, *own, *other, *saved, gath_g1, gath_n2_0, n2_1)
    input_grad, gains, att_early, att_late, g_gate, g_up, g_down = second[:7]
    far = second[-3:]
    finals = [
        shape((micro, rows, d)),
        shape((micro, rows, d)),
        shape((block, ff), F32),
        shape((block, ff), F32),
        shape((block, ff), F32),
        shape((qk, block), F32),
        shape((qk, block), F32),
        shape((block, width), F32),
        shape((block, width), F32),
        shape((width, block), F32),
    ]
    section_out, input_grad, g_gate, g_up, g_down, g_q, g_k, g_v, g_o, g_out = pl.pallas_call(
        functools.partial(final_kernel, qk, width),
        out_shape=finals,
        in_specs=[ANY] * 8 + [VM] * 2,
        out_specs=[ANY] * 5 + [VM] * 5,
        scratch_shapes=[vm((micro, rows, d))] * 2 + [vm((block, ff), F32)] * 3 + [vm((block, ff))] * 3 + [DMA((13,))],
        compiler_params=pltpu.CompilerParams(vmem_limit_bytes=VMEM_LIMIT),
    )(section_out, input_grad, g_gate, g_up, g_down, *far, att_early, att_late)
    return (
        section_out[None],
        input_grad[None],
        gains[0:1],
        gains[1:2],
        g_q.T[None],
        g_k.T[None],
        g_v[None],
        g_o[None],
        gains[None, 2 : 2 + KW, :width],
        g_out[None],
        g_gate[None],
        g_up[None],
        g_down.T[None],
    )


def solution(mesh):
    return jax.shard_map(
        functools.partial(shards, mesh.shape["seq"], mesh.shape["head"]),
        mesh=mesh,
        in_specs=(
            P(None, "seq", None),
            P(None, "seq", None),
            P(),
            P("section", None),
            P("section", None),
            P("section", None, "head"),
            P("section", None, "head"),
            P("section", None, "head"),
            P("section", None, "head"),
            P("section", None, "head"),
            P("section", "head", None),
            P("section", None, "head"),
            P("section", None, "head"),
            P("section", "head", None),
        ),
        out_specs=(
            P("section", None, "seq", None),
            P("section", None, "seq", None),
            P("section", None),
            P("section", None),
            P("section", "seq", "head"),
            P("section", "seq", "head"),
            P("section", "seq", "head"),
            P("section", "seq", "head"),
            P("section", None, "head"),
            P("section", "head", "seq"),
            P("section", "seq", "head"),
            P("section", "seq", "head"),
            P("section", "head", "seq"),
        ),
        check_vma=False,
    )
```

```python
import functools

import jax
import jax.numpy as jnp
import numpy as np
from jax import lax
from jax.experimental import pallas as pl
from jax.experimental.pallas import tpu as pltpu
from jax.sharding import PartitionSpec as P

HD = 112
FEAT = 16
KW = 3
EPS = 1e-05
LANES = 128
PSI = 256
PSI_SENT = 160
MESH = pl.DeviceIdType.MESH
F32 = jnp.float32
BF16 = jnp.bfloat16
VMEM_LIMIT = 63 << 20


def dot_nn(a, b):
    return lax.dot_general(a, b, (((1,), (0,)), ((), ())), preferred_element_type=F32)


def dot_nt(a, b):
    return lax.dot_general(a, b, (((1,), (1,)), ((), ())), preferred_element_type=F32)


def dot_tn(a, b):
    return lax.dot_general(a, b, (((0,), (0,)), ((), ())), preferred_element_type=F32)


def chunks(total, step, body):
    whole = total // step
    if whole > 1:

        def one(i, carry):
            body(pl.multiple_of(i * step, step), step)
            return carry

        lax.fori_loop(0, whole, one, 0)
    elif whole == 1:
        body(0, step)
    if total % step:
        body(whole * step, total % step)


def lift_tables(heads):
    first = np.zeros((heads * FEAT, heads * PSI), np.float32)
    second = np.zeros_like(first)
    second_key = np.zeros_like(first)
    for head in range(heads):
        row, col = head * FEAT, head * PSI
        for i in range(FEAT):
            first[row + i, col + 1 + i] = 1.0
        at = 1 + FEAT
        for i in range(FEAT):
            for j in range(i, FEAT):
                first[row + i, col + at] = 1.0
                second[row + j, col + at] = 1.0
                second_key[row + j, col + at] = 0.5 if i == j else 1.0
                at += 1
    return np.stack([first, second, second_key])


class Place:
    def __init__(self, lens, nz, nh, rows):
        self.sec, self.s, self.h = (lax.axis_index(a) for a in ("section", "seq", "head"))
        self.nz, self.nh, self.rows = nz, nh, rows
        self.l0 = lens[self.sec, 0]
        self.tot = self.l0 + lens[self.sec, 1]
        self.first = self.s * rows
        self.part = rows // nh
        self.mine = pl.ds(pl.multiple_of(self.h * self.part, self.part), self.part)

    def seg(self, pos):
        inside = (pos >= self.l0).astype(jnp.int32) + (pos >= self.tot).astype(jnp.int32)
        return jnp.where(pos >= 0, inside, -1)

    def pos(self, shift=0):
        return self.first + shift + lax.broadcasted_iota(jnp.int32, (self.rows, 1), 0)

    def same(self, shift):
        other = self.pos(shift)
        inside = other < self.nz * self.rows
        return (self.seg(other) == self.seg(self.pos())) & inside

    def allowed(self):
        shape = (self.rows, self.rows)
        row = lax.broadcasted_iota(jnp.int32, shape, 0)
        col = lax.broadcasted_iota(jnp.int32, shape, 1)
        return (col <= row) & (self.seg(self.first + col) == self.seg(self.first + row))

    def last_seg(self, block):
        return self.seg(block * self.rows + self.rows - 1)

    def prior_seg(self, block):
        return self.seg(block * self.rows - 1)

    def applies(self):
        return self.seg(self.pos()) == self.prior_seg(self.s)

    def tail(self):
        return self.seg(self.pos()) == self.last_seg(self.s)

    def peers(self):
        core = [(1 - self.sec, self.s, self.h)]
        seq = [(self.sec, (self.s + k) % self.nz, self.h) for k in range(1, self.nz)]
        head = [(self.sec, self.s, self.h ^ m) for m in range(1, self.nh)]
        return core, seq, head

    def barrier(self, core, seq, head):
        groups = self.peers()
        told = [d for use, g in zip((core, seq, head), groups) if use for d in g]
        sem = pltpu.get_barrier_semaphore()
        for device in told:
            pl.semaphore_signal(sem, 1, device_id=device, device_id_type=MESH)
        pl.semaphore_wait(sem, len(told))


def remote(src, dst, send, recv, device):
    return pltpu.make_async_remote_copy(
        src_ref=src, dst_ref=dst, send_sem=send, recv_sem=recv, device_id=device, device_id_type=MESH
    )


def half_cols(buf, half):
    size = buf.shape[-1] // 2
    return pl.ds(half * size, size)


def scatter_start(at, buf, got, send, recv, half):
    sent = []
    cols = half_cols(buf, half)
    for m in sorted(range(1, at.nh), reverse=True):
        peer = at.h ^ m
        rows = pl.ds(pl.multiple_of(peer * at.part, at.part), at.part)
        sem = half * (at.nh - 1) + m - 1
        copy = remote(
            buf.at[rows, cols], got.at[m - 1, :, cols], send.at[sem], recv.at[sem], (at.sec, at.s, peer)
        )
        copy.start()
        sent.append(copy)
    return sent


def scatter_sum(at, buf, got, sent):
    total = buf[at.mine].astype(F32)
    for copy in sent:
        copy.wait_recv()
    for m in range(1, at.nh):
        total = total + got[m - 1].astype(F32)
    return total


def gather_start(at, buf, send, recv):
    sent = []
    for m in sorted(range(1, at.nh), reverse=True):
        copy = remote(
            buf.at[at.mine], buf.at[at.mine], send.at[m - 1], recv.at[m - 1], (at.sec, at.s, at.h ^ m)
        )
        copy.start()
        sent.append(copy)
    return sent


def wait_recv(copies):
    for copy in copies:
        copy.wait_recv()


def wait_send(copies):
    for copy in copies:
        copy.wait_send()


def norm_rows(x, gain):
    return x * lax.rsqrt(jnp.mean(x * x, axis=-1, keepdims=True) + EPS) * gain


def norm_rows_back(x, gain, grad):
    inverse = lax.rsqrt(jnp.mean(x * x, axis=-1, keepdims=True) + EPS)
    unit = x * inverse
    scaled = grad * gain
    back = inverse * (scaled - unit * jnp.mean(scaled * unit, axis=-1, keepdims=True))
    return back, jnp.sum(grad * unit, axis=0, keepdims=True)


def lift_parts(low, tables, second, head):
    cols = slice(head * PSI, (head + 1) * PSI)
    lane = lax.broadcasted_iota(jnp.int32, (1, PSI), 1)
    one = dot_nn(low, tables[0, :, cols]) + (lane == 0).astype(F32)
    two = dot_nn(low, tables[second, :, cols]) + (lane <= FEAT).astype(F32)
    return one, two


def head_only(low, head):
    lane = lax.broadcasted_iota(jnp.int32, low.shape, 1)
    return jnp.where((lane >= head * FEAT) & (lane < (head + 1) * FEAT), low, jnp.zeros_like(low))


def convolve(at, u_s, taps, c_s, cx_s, heads):
    rows, width = at.rows, heads * HD
    out = taps[0:1, :width] * u_s[8 : 8 + rows, :width]
    for j in range(1, KW):
        shifted = u_s[8 - j : 8 - j + rows, :width]
        out = out + jnp.where(at.same(-j), shifted * taps[j : j + 1, :width], 0.0)
    c_s[0:rows, :width] = out
    lane = lax.broadcasted_iota(jnp.int32, (rows, LANES), 1)
    for head in range(heads):
        one = c_s[0:rows, head * HD : head * HD + LANES]
        cx_s[head] = jnp.where(lane < HD, one, jnp.where(lane == HD, 1.0, 0.0)).astype(BF16)


def order(at, i):
    left, right = at.s, at.nz - 1 - at.s
    both = 2 * jnp.minimum(left, right)
    near = i <= both
    dist = jnp.where(near, (i + 1) // 2, i - both // 2)
    leftward = jnp.where(near, i % 2 == 1, left > right)
    return jnp.where(leftward, at.s - dist, at.s + dist)


class Ring:
    def __init__(self, at, src, dst, send, recv, pair_send, pair_recv):
        self.at, self.src, self.dst, self.send, self.recv = at, src, dst, send, recv
        self.pair_send, self.pair_recv = pair_send, pair_recv

    def _view(self, c):
        at = self.at
        rows, cols = at.rows // 2, self.dst.shape[-1] // 2
        bit = lax.rem(at.h // (1 << c), 2)
        return pl.ds(pl.multiple_of(bit * rows, rows), rows), pl.ds(c * cols, cols)

    def _ways(self, k):
        at = self.at
        right = (at.s - k, at.s - k >= 0, at.s + 1 < at.nz, lax.rem(at.s + 1, at.nz))
        left = (at.s + k, at.s + k < at.nz, at.s > 0, lax.rem(at.s + at.nz - 1, at.nz))
        return right, left

    def _copies(self, way, k, block, to, first):
        at = self.at
        for c in range(2):
            rows, cols = self._view(c)
            src = self.src.at[rows, cols] if first else self.dst.at[block, rows, cols]
            yield remote(
                src, self.dst.at[block, rows, cols], self.send.at[way, k, c], self.recv.at[way, k, c], (at.sec, to, at.h)
            )

    def _pairs(self, way, k, block):
        at = self.at
        for c in range(2):
            rows, cols = self._view(c)
            view = self.dst.at[block, rows, cols]
            yield remote(view, view, self.pair_send.at[way, k, c], self.pair_recv.at[way, k, c], (at.sec, at.s, at.h ^ (1 << c)))

    def step(self, k):
        at = self.at
        first = isinstance(k, int) and k == 0
        for way, (block, there, onward, to) in enumerate(self._ways(k)):
            if not first:

                @pl.when(there)
                def _(way=way, block=block, to=to):
                    wait_recv(self._copies(way, k - 1, block, to, False))

            if not isinstance(k, int) or k < at.nz - 1:

                @pl.when(there & onward & (k < at.nz - 1))
                def _(way=way, block=block, to=to):
                    for copy in self._copies(way, k, block, to, first):
                        copy.start()

    def pair(self, k):
        for way, (block, there, _, _) in enumerate(self._ways(k + 1)):

            @pl.when(there)
            def _(way=way, block=block):
                for copy in self._pairs(way, k, block):
                    copy.start()

    def ready(self, k):
        for way, (block, there, _, _) in enumerate(self._ways(k + 1)):

            @pl.when(there)
            def _(way=way, block=block):
                wait_recv(self._pairs(way, k, block))

    def drain(self, line=True, pairs=True):
        def one(k, carry):
            for way, (_, there, onward, to) in enumerate(self._ways(k) if line else ()):

                @pl.when(there & onward)
                def _(way=way, to=to):
                    wait_send(self._copies(way, k, self.at.s, to, False))

            for way, (_, there, _, _) in enumerate(self._ways(k + 1) if pairs else ()):

                @pl.when(there)
                def _(way=way):
                    wait_send(self._pairs(way, k, self.at.s))

            return carry

        lax.fori_loop(0, self.at.nz - 1, one, 0)


def upward(begin, end, body):
    if end > begin:

        def one(k, carry):
            body(k)
            return carry

        lax.fori_loop(begin, end, one, 0)


class LineSum:
    def __init__(self, at, mine, peer, land, held, io, send, recv, peer_recv):
        self.at, self.mine, self.peer, self.land, self.held = at, mine, peer, land, held
        self.io, self.send, self.recv, self.peer_recv = io, send, recv, peer_recv

    def _hop(self, way, d):
        at = self.at
        to = lax.rem(at.s + (1 if way == 0 else at.nz - 1), at.nz)
        return remote(self.mine.at[d], self.land.at[way, d], self.send.at[way, d], self.recv.at[way, d], (at.sec, to, at.h))

    def _add(self, way, d):
        self._hop(way, d).wait_recv()
        held = self.held.at[:, pl.ds(0, self.mine.shape[-1])]
        copy = pltpu.make_async_copy(self.land.at[way, d], held, self.io)
        copy.start()
        copy.wait()
        self.mine[d] += held[...]

    def slot(self, i):
        at = self.at
        if isinstance(i, int) and i == 0:
            for d in range(at.nz):
                peer = self.peer.at[d, :, pl.ds(0, self.mine.shape[-1])]
                remote(peer, peer, self.peer_recv.at[d], self.peer_recv.at[d], (1 - at.sec, at.s, at.h)).wait_recv()
                self.mine[d] += peer[...]
        for way in range(2):
            begun = i - at.s if way == 0 else i - (at.nz - 1 - at.s)
            d = at.nz - 1 - begun if way == 0 else begun
            earlier = at.s > 0 if way == 0 else at.s < at.nz - 1

            @pl.when((begun >= 0) & (i < at.nz - 1))
            def _(way=way, d=d, earlier=earlier):
                @pl.when(earlier)
                def _():
                    self._add(way, d)

                self._hop(way, d).start()

    def last(self):
        at = self.at
        for d in range(at.nz):
            for way, there in ((0, at.s < d), (1, at.s > d)):

                @pl.when(there)
                def _(way=way, d=d):
                    self._hop(way, d).wait_send()

        @pl.when(at.s > 0)
        def _():
            self._add(0, at.s)

        @pl.when(at.s < at.nz - 1)
        def _():
            self._add(1, at.s)


def taker(refs):
    refs = list(refs)

    def take(n):
        out = refs[:n]
        del refs[:n]
        return out

    return take


def weight_slots(cat, out, gate, up, down, qk, width):
    at_row, views = 0, []
    for size in (qk, qk, width, width):
        views.append(cat.at[pl.ds(at_row, size)])
        at_row += size
    return views + [out, gate, up, down]


SAVED = 11


def fwd_kernel(dims, *refs):
    nz, nh, rows, heads = dims
    take = taker(refs)
    lens, inputs, out_grad, small_own, tables = take(5)
    own = take(8)
    small_other = take(1)[0]
    other = take(8)
    saved = [take(SAVED), take(SAVED)]
    x_out, gath_g1, gath_n2, n2_out = take(4)
    mats = [take(5), take(5)]
    (x_s, n1_s, n2_s, qk_s, u_s, edge_s, o_s, c_s, cx_s, yx_s, ss, sr, sin_s, g_s, gb_s, part_s, got_s, f_s, v_s, t_s, xo_s, h_s, sm_s) = take(23)
    w_sem, io_sem, save_sem, x_send, x_recv, e_send, e_recv, st_send, st_recv, head_send, head_recv = take(11)
    r_send, r_recv, p_send, p_recv = take(4)
    at = Place(lens, nz, nh, rows)
    d = x_s.shape[1]
    width, qk = heads * HD, heads * FEAT
    core = (1 - at.sec, at.s, at.h)
    slots = [weight_slots(*m, qk, width) for m in mats]

    x_copy = pltpu.make_async_copy(inputs.at[at.sec], x_s, io_sem.at[0])
    x_copy.start()

    def local(layer, i):
        return pltpu.make_async_copy(own[i].at[0], slots[layer][i], w_sem.at[i])

    def swap(layer, i):
        return remote(own[i].at[0], slots[layer][i], x_send.at[i], x_recv.at[i], core)

    def stash(layer, i):
        return pltpu.make_async_copy(slots[layer][i], other[i].at[0], w_sem.at[8 + i])

    for here in range(2):

        @pl.when(at.sec == here)
        def _(here=here):
            for i in (2, 0, 1, 3, 4, 5, 6, 7):
                local(here, i).start()

    at.barrier(True, True, True)
    small_swap = remote(small_own, small_other, x_send.at[8], x_recv.at[8], core)
    small_swap.start()
    for here in range(2):

        @pl.when(at.sec == here)
        def _(here=here):
            for i in (2, 0, 1, 3, 4, 5, 6, 7):
                swap(here, i).start()

    ring_g = Ring(at, out_grad.at[at.sec], gath_g1, r_send.at[0], r_recv.at[0], p_send.at[0], p_recv.at[0])
    ring_n = Ring(at, gath_n2.at[at.s], gath_n2, r_send.at[1], r_recv.at[1], p_send.at[1], p_recv.at[1])
    small_swap.wait_recv()
    small_copy = pltpu.make_async_copy(small_other, sm_s, io_sem.at[1])
    small_copy.start()
    small_copy.wait()

    def wait_weight(layer, i):
        @pl.when(at.sec == layer)
        def _():
            local(layer, i).wait()

        @pl.when(at.sec != layer)
        def _():
            swap(layer, i).wait_recv()
            stash(layer, i).start()

    allowed = at.allowed()
    applies, tail, prior = at.applies(), at.tail(), at.prior_seg(at.s)
    my_pos = at.first + at.h * at.part + lax.broadcasted_iota(jnp.int32, (at.part, 1), 0)
    my_valid = my_pos < at.tot

    def layer_forward(layer, x_s, hooks):
        cat, w_out, w_gate, w_up, w_down = mats[layer]
        small = jnp.where(at.sec == layer, small_own[...], sm_s[...])
        gain_attn, gain_ffn, taps = small[0:1], small[1:2], small[2 : 2 + KW]
        keep = []

        def save(src, i):
            copy = pltpu.make_async_copy(src, saved[layer][i], save_sem.at[i])
            copy.start()
            keep.append(copy)

        hooks["begin"]()
        n1_s[...] = norm_rows(x_s[...].astype(F32), gain_attn).astype(BF16)
        save(x_s.at[at.mine], 0)
        save(n1_s, 1)
        wait_weight(layer, 2)
        u_s[8 : 8 + rows, :width] = dot_nt(n1_s[...], cat[2 * qk : 2 * qk + width, :]).astype(BF16).astype(F32)
        edge = remote(
            u_s.at[pl.ds(rows, 8)], edge_s.at[layer], e_send.at[layer], e_recv.at[layer],
            (at.sec, lax.rem(at.s + 1, nz), at.h),
        )

        @pl.when(at.s + 1 < nz)
        def _():
            edge.start()

        wait_weight(layer, 0)
        wait_weight(layer, 1)
        low = dot_nt(n1_s[...], cat[0 : 2 * qk, :]).astype(BF16).astype(F32)
        qk_s[...] = (low * 0.5).astype(BF16)
        save(qk_s, 2)
        a_low, b_low = qk_s[:, 0:qk], qk_s[:, qk : 2 * qk]

        @pl.when(at.s > 0)
        def _():
            edge.wait_recv()

        u_s[0:8, :] = edge_s[layer]
        save(u_s, 3)
        convolve(at, u_s, taps, c_s, cx_s, heads)

        for head in range(heads):
            one, two = lift_parts(b_low, tables, 2, head)
            psi = jnp.where(tail, one * two, 0.0).astype(BF16)
            ss[layer, head] = dot_tn(psi, cx_s[head])[:PSI_SENT].astype(BF16)

        def state(k):
            return remote(
                ss.at[layer], sr.at[layer, at.s], st_send.at[layer, k - 1], st_recv.at[layer, at.s],
                (at.sec, lax.rem(at.s + k, nz), at.h),
            )

        for k in range(1, nz):

            @pl.when(at.s + k < nz)
            def _(k=k):
                state(k).start()

        wait_weight(layer, 3)
        o_s[:, :width] = dot_nt(n1_s[...], cat[2 * qk + width :, :])
        save(o_s, 4)
        for head in range(heads):
            e = dot_nt(a_low, head_only(b_low, head))
            kern = jnp.where(allowed, 1.0 + e + 0.5 * e * e, 0.0).astype(BF16)
            yx_s[head] = dot_nn(kern, cx_s[head])
        for j in range(nz - 1):

            @pl.when(j < at.s)
            def _(j=j):
                remote(ss.at[layer], sr.at[layer, j], st_send.at[layer, 0], st_recv.at[layer, j], core).wait_recv()

        hooks["states"]()
        sin_s[...] = jnp.zeros_like(sin_s)
        for head in range(heads):
            total = jnp.zeros((PSI_SENT, LANES), F32)
            for j in range(nz - 1):
                counts = (j < at.s) & (at.last_seg(j) == prior)
                total = total + jnp.where(counts, sr[layer, j, head].astype(F32), 0.0)
            sin_s[head, 0:PSI_SENT] = total.astype(BF16)
            one, two = lift_parts(a_low, tables, 1, head)
            psi = (one * two).astype(BF16)
            yx = yx_s[head] + jnp.where(applies, dot_nn(psi, sin_s[head]), 0.0)
            yx_s[head] = yx
            gate = o_s[:, head * HD : head * HD + LANES]
            y = yx / yx[:, HD : HD + 1]
            g_s[:, head * HD : head * HD + LANES] = y * (gate * jax.nn.sigmoid(gate))
        gb_s[...] = g_s[:, :width].astype(BF16)
        save(yx_s, 5)
        save(sin_s, 6)
        save(gb_s, 7)

        wait_weight(layer, 4)

        s1 = []
        for half in range(2):
            cols = half_cols(w_out, half)
            part_s[layer, 0, :, cols] = dot_nn(gb_s[...], w_out[:, cols]).astype(BF16)
            s1 += scatter_start(at, part_s.at[layer, 0], got_s, head_send.at[layer, 0], head_recv.at[layer, 0], half)
        hooks["rs1"]()
        hidden = x_s[at.mine].astype(F32) + scatter_sum(at, part_s.at[layer, 0], got_s, s1)
        h_s[...] = hidden
        n2_s[at.mine] = norm_rows(hidden, gain_ffn).astype(BF16)
        s2 = gather_start(at, n2_s, head_send.at[layer, 1], head_recv.at[layer, 1])
        save(h_s, 8)
        hooks["ag1"]()
        wait_recv(s2)
        hooks["n2"]()

        wait_weight(layer, 5)
        wait_weight(layer, 6)

        def up_chunk(at_row, size):
            cols = pl.ds(at_row, size)
            f = dot_nt(n2_s[...], w_gate[cols, :])
            v = dot_nt(n2_s[...], w_up[cols, :])
            f_s[:, cols] = f.astype(BF16)
            v_s[:, cols] = v.astype(BF16)
            t_s[:, cols] = (f * jax.nn.sigmoid(f) * v).astype(BF16)

        chunks(t_s.shape[1], 256, up_chunk)
        save(f_s, 9)
        save(v_s, 10)
        wait_weight(layer, 7)

        s3 = []
        for half in range(2):
            cols = half_cols(w_down, half)
            part_s[layer, 1, :, cols] = dot_nn(t_s[...], w_down[:, cols]).astype(BF16)
            s3 += scatter_start(at, part_s.at[layer, 1], got_s, head_send.at[layer, 2], head_recv.at[layer, 2], half)
        hooks["rs2"]()
        feed = scatter_sum(at, part_s.at[layer, 1], got_s, s3)
        xo_s[layer, at.mine] = jnp.where(my_valid, h_s[...] + feed, 0.0).astype(BF16)
        s4 = gather_start(at, xo_s.at[layer], head_send.at[layer, 3], head_recv.at[layer, 3])
        hooks["ag2"]()
        wait_recv(s4)
        for copy in keep:
            copy.wait()

        def finish():
            wait_send(s1 + s2 + s3 + s4)

            @pl.when(at.s + 1 < nz)
            def _():
                edge.wait_send()

            for k in range(1, nz):

                @pl.when(at.s + k < nz)
                def _(k=k):
                    state(k).wait_send()

        return finish

    def nothing():
        pass

    n2_copy = pltpu.make_async_copy(n2_s, gath_n2.at[at.s], io_sem.at[2])

    def f0_n2():
        n2_copy.start()
        ring_g.step(1)

    def f1_begin():
        n2_copy.wait()
        upward(3, nz, ring_g.step)
        upward(0, nz - 1, ring_g.pair)
        ring_n.step(0)

    def f1_n2():
        n2_last.start()
        ring_n.step(2)

    x_copy.wait()
    finish_0 = layer_forward(
        0, x_s, dict(begin=nothing, states=nothing, rs1=lambda: ring_g.step(0), ag1=nothing, n2=f0_n2, rs2=nothing, ag2=lambda: ring_g.step(2))
    )
    finish_0()

    def out_copy(layer):
        near = pltpu.make_async_copy(xo_s.at[layer], x_out.at[at.sec], io_sem.at[3])
        far = remote(xo_s.at[layer], x_out.at[at.sec], x_send.at[9], x_recv.at[9], core)
        return near, far

    def send_out(layer):
        near, far = out_copy(layer)

        @pl.when(at.sec == layer)
        def _():
            near.start()

        @pl.when(at.sec != layer)
        def _():
            far.start()

    send_out(0)
    n2_last = pltpu.make_async_copy(n2_s, n2_out, io_sem.at[4])
    finish_1 = layer_forward(
        1, xo_s.at[0], dict(begin=f1_begin, states=nothing, rs1=lambda: ring_n.step(1), ag1=nothing, n2=f1_n2, rs2=nothing, ag2=nothing)
    )
    send_out(1)
    finish_1()
    upward(0, nz - 1, ring_g.ready)
    upward(3, nz, ring_n.step)
    n2_last.wait()
    ring_g.drain()
    ring_n.drain(pairs=False)
    near, far = out_copy(0)
    near.wait()
    far.wait_send()
    far.wait_recv()
    small_swap.wait_send()
    for here in range(2):

        @pl.when(at.sec == here)
        def _(here=here):
            for i in range(8):
                swap(here, i).wait_send()
                stash(1 - here, i).wait()


def bwd_kernel(dims, *refs):
    nz, nh, rows, heads = dims
    take = taker(refs)
    lens, inputs_grad, small_own, small_other, tables = take(5)
    own = take(8)
    other = take(8)
    saved = [take(SAVED), take(SAVED)]
    gath_g1, _, n2_1 = take(3)
    ig_o, gains_o = take(2)
    att_o = take(2)
    ffn_o = take(3)
    gath_n2_1, gath_g0, gath_n2_0 = take(3)
    a_land = take(2)
    wr_o = take(3)
    mats = take(5)
    keep_s = take(SAVED)
    (grad_s, t_s, part_s, got_s, dm_s, dh_s, dg_s, do_s, cx_s, dyx_s, ss, sr, st_s, da_s, db_s, dc_s, edge_s, dcat_s, ig_s) = take(19)
    gsum_s, gpeer_s, gtot_s, gz_s, gh_s = take(5)
    acc = take(3)
    wx_s = take(3)
    blk_n2, blk_g, n2t_s, gt_s = take(4)
    a_s = take(2)
    peer_s, held_s = take(2)
    (w_sem, io_sem, keep_sem, e_send, e_recv, st_send, st_recv, head_send, head_recv, r_send, r_recv, p_send, p_recv) = take(13)
    (wx_send, wx_recv, ap_send, ap_recv, l_send, l_recv, x_send, x_recv, gz_send, gz_recv, gh_send, gh_recv) = take(12)
    x_s, n1_s, qk_s, u_s, o_s, yx_s, sin_s, gb_s, h_s, f_s, v_s = keep_s
    df_s, dv_s = f_s, v_s
    at = Place(lens, nz, nh, rows)
    cat, w_out, w_gate, w_up, w_down = mats
    d = n1_s.shape[1]
    width, qk = heads * HD, heads * FEAT
    block = d // nz
    core = (1 - at.sec, at.s, at.h)
    slots = weight_slots(*mats, qk, width)

    def weight_start(layer, i):
        @pl.when(at.sec == layer)
        def _():
            pltpu.make_async_copy(own[i].at[0], slots[i], w_sem.at[i]).start()

        @pl.when(at.sec != layer)
        def _():
            pltpu.make_async_copy(other[i].at[0], slots[i], w_sem.at[i]).start()

    def weight_wait(i):
        pltpu.make_async_copy(own[i].at[0], slots[i], w_sem.at[i]).wait()

    def keep_copy(layer, i):
        return pltpu.make_async_copy(saved[layer][i], keep_s[i], keep_sem.at[i])

    ring_n = Ring(at, n2_1, gath_n2_1, r_send.at[0], r_recv.at[0], p_send.at[0], p_recv.at[0])
    ring_g = Ring(at, ig_s.at[1], gath_g0, r_send.at[1], r_recv.at[1], p_send.at[1], p_recv.at[1])
    ring_0 = Ring(at, None, gath_n2_0, None, None, p_send.at[2], p_recv.at[2])
    line = [
        [
            LineSum(
                at, a_s[g], peer_s, a_land[g].at[layer], held_s, io_sem.at[4],
                l_send.at[layer, g], l_recv.at[layer, g], ap_recv.at[layer, g],
            )
            for g in range(2)
        ]
        for layer in range(2)
    ]

    def turn_blocks(n2_ref, g_ref):
        for part in range(nz):

            @pl.when(at.s == part)
            def _(part=part):
                n2t_s[...] = n2_ref[:, part * block : (part + 1) * block].T
                gt_s[...] = g_ref[:, part * block : (part + 1) * block].T

    def own_piece(layer):
        copy = pltpu.make_async_copy(n2_1 if layer == 1 else gath_n2_0.at[at.s], blk_n2, io_sem.at[0])
        copy.start()
        copy.wait()
        turn_blocks(blk_n2, grad_s)

        def hidden(at_col, size):
            cols = pl.ds(at_col, size)
            acc[0][:, cols] = dot_nn(n2t_s[...], df_s[:, cols])
            acc[1][:, cols] = dot_nn(n2t_s[...], dv_s[:, cols])
            acc[2][:, cols] = dot_nn(gt_s[...], t_s[:, cols])

        chunks(w_gate.shape[0], 640, hidden)

    def piece(layer, i, between=None):
        which = order(at, i)
        n2_src = (gath_n2_1 if layer == 1 else gath_n2_0).at[which]
        g_src = (gath_g1 if layer == 1 else gath_g0).at[which]
        loads = [pltpu.make_async_copy(n2_src, blk_n2, io_sem.at[0]), pltpu.make_async_copy(g_src, blk_g, io_sem.at[1])]
        for copy in loads:
            copy.start()
        for copy in loads:
            copy.wait()
        pos = which * rows + lax.broadcasted_iota(jnp.int32, (rows, 1), 0)
        blk_g[...] = jnp.where(pos < at.tot, blk_g[...].astype(F32), 0.0).astype(BF16)
        turn_blocks(blk_n2, blk_g)

        def hidden(at_row, size):
            cols = pl.ds(at_row, size)
            f = dot_nt(blk_n2[...], w_gate[cols, :])
            v = dot_nt(blk_n2[...], w_up[cols, :])
            dt = dot_nt(blk_g[...], w_down[cols, :])
            sig = jax.nn.sigmoid(f)
            act = f * sig
            t = (act * v).astype(BF16)
            df = (dt * v * (sig + act * (1.0 - sig))).astype(BF16)
            dv = (dt * act).astype(BF16)
            acc[0][:, cols] += dot_nn(n2t_s[...], df)
            acc[1][:, cols] += dot_nn(n2t_s[...], dv)
            acc[2][:, cols] += dot_nn(gt_s[...], t)

        ff = w_gate.shape[0]
        if between is None:
            chunks(ff, 640, hidden)
        else:
            hidden(0, 640)
            between()
            hidden(640, ff - 640)

    def ffn_swap(i):
        return remote(wx_s[i], wr_o[i], wx_send.at[i], wx_recv.at[i], core)

    def ffn_own(i):
        return pltpu.make_async_copy(acc[i], ffn_o[i], io_sem.at[5 + i])

    def ffn_send(layer):
        @pl.when(at.sec != layer)
        def _():
            for i in range(3):
                wx_s[i][...] = acc[i][...].astype(BF16)
                ffn_swap(i).start()

        @pl.when(at.sec == layer)
        def _():
            for i in range(3):
                ffn_own(i).start()

    def ffn_done(layer):
        @pl.when(at.sec == layer)
        def _():
            for i in range(3):
                ffn_own(i).wait()

    def ig_copy(layer):
        near = pltpu.make_async_copy(ig_s.at[layer], ig_o.at[at.sec], io_sem.at[3])
        far = remote(ig_s.at[layer], ig_o.at[at.sec], x_send.at[0], x_recv.at[0], core)
        return near, far

    def ig_send(layer):
        near, far = ig_copy(layer)

        @pl.when(at.sec == layer)
        def _():
            near.start()

        @pl.when(at.sec != layer)
        def _():
            far.start()

    allowed = at.allowed()
    applies, tail, mine_last = at.applies(), at.tail(), at.last_seg(at.s)
    valid = at.pos() < at.tot
    lane = lax.broadcasted_iota(jnp.int32, (rows, LANES), 1)

    def line_core(layer, g):
        return g

    def peer_chunk(layer, g, i):
        there = peer_s.at[i, :, pl.ds(0, a_s[g].shape[-1])]
        return remote(a_s[g].at[i], there, ap_send.at[g, i], ap_recv.at[layer, g, i], core)

    def mixer_grads(layer, g):
        late = 2 * qk + width
        for i in range(nz):
            cols = slice(i * block, (i + 1) * block)
            if g == 0:
                a_s[0][i, :, 0:width] = dot_tn(n1_s[:, cols], dcat_s[:, late:]).astype(BF16)
                a_s[0][i, :, width:] = dot_tn(dm_s[:, cols], gb_s[...]).astype(BF16)
            else:
                a_s[1][i, :, 0:late] = dot_tn(n1_s[:, cols], dcat_s[:, 0:late]).astype(BF16)

            @pl.when(at.sec != line_core(layer, g))
            def _(i=i):
                peer_chunk(layer, g, i).start()

    def mixer_sent(layer, g):
        for i in range(nz):

            @pl.when(at.sec != line_core(layer, g))
            def _(i=i):
                peer_chunk(layer, g, i).wait_send()

    def layer_backward(layer, hooks):
        small = jnp.where(at.sec == layer, small_own[...], small_other[...])
        gain_attn, gain_ffn, taps = small[0:1], small[1:2], small[2 : 2 + KW]
        hooks["begin"]()

        weight_wait(7)
        keep_copy(layer, 9).wait()
        keep_copy(layer, 10).wait()

        def down_chunk(at_row, size):
            cols = pl.ds(at_row, size)
            dt = dot_nt(grad_s[...], w_down[cols, :])
            f = f_s[:, cols].astype(F32)
            v = v_s[:, cols].astype(F32)
            sig = jax.nn.sigmoid(f)
            act = f * sig
            t_s[:, cols] = (act * v).astype(BF16)
            df_s[:, cols] = (dt * v * (sig + act * (1.0 - sig))).astype(BF16)
            dv_s[:, cols] = (dt * act).astype(BF16)

        chunks(df_s.shape[1], 256, down_chunk)
        weight_wait(5)
        weight_wait(6)

        s1 = []
        for half in range(2):
            cols = half_cols(w_up, half)
            part = dot_nn(df_s[...], w_gate[:, cols]) + dot_nn(dv_s[...], w_up[:, cols])
            part_s[:, cols] = part.astype(BF16)
            s1 += scatter_start(at, part_s, got_s, head_send.at[layer, 0], head_recv.at[layer, 0], half)
        hooks["rs1"]()
        keep_copy(layer, 3).wait()
        convolve(at, u_s, taps, do_s, cx_s, heads)
        keep_copy(layer, 8).wait()
        dn2 = scatter_sum(at, part_s, got_s, s1)
        back, gain_grad = norm_rows_back(h_s[...], gain_ffn, dn2)
        gsum_s[layer, 1:2, :] = gain_grad
        dh = grad_s[at.mine].astype(F32) + back
        dh_s[...] = dh
        dm_s[at.mine] = dh.astype(BF16)
        s2 = gather_start(at, dm_s, head_send.at[layer, 1], head_recv.at[layer, 1])
        for i in (0, 1, 2, 4, 5, 6, 7):
            keep_copy(layer, i).wait()
        for i in (4, 0, 1, 2, 3):
            weight_wait(i)
        a_low, b_low = qk_s[:, 0:qk], qk_s[:, qk : 2 * qk]
        hooks["ag1"]()
        wait_recv(s2)
        hooks["dm"]()

        def out_chunk(at_row, size):
            cols = pl.ds(at_row, size)
            dg_s[:, cols] = dot_nt(dm_s[...], w_out[cols, :])

        chunks(width, 256, out_chunk)
        for head in range(heads):
            cols = slice(head * HD, head * HD + LANES)
            gate, dg, yx = o_s[:, cols], dg_s[:, cols], yx_s[head]
            sig = jax.nn.sigmoid(gate)
            inverse = 1.0 / yx[:, HD : HD + 1]
            y = yx * inverse
            do_s[:, cols] = dg * y * sig * (1.0 + gate * (1.0 - sig))
            dy = jnp.where(lane < HD, dg * gate * sig, 0.0)
            dden = -jnp.sum(dy * y, axis=1, keepdims=True) * inverse
            dyx_s[head] = jnp.where(lane == HD, dden, dy * inverse).astype(BF16)
            one, two = lift_parts(a_low, tables, 1, head)
            psi = jnp.where(applies, one * two, 0.0).astype(BF16)
            ss[layer, head] = dot_tn(psi, dyx_s[head])[:PSI_SENT].astype(BF16)
        dcat_s[:, 2 * qk + width :] = do_s[:, :width].astype(BF16)

        def state(k):
            return remote(
                ss.at[layer], sr.at[layer, at.s], st_send.at[layer, k - 1], st_recv.at[layer, at.s],
                (at.sec, lax.rem(at.s + nz - k, nz), at.h),
            )

        for k in range(1, nz):

            @pl.when(at.s - k >= 0)
            def _(k=k):
                state(k).start()

        da_s[...] = jnp.zeros_like(da_s)
        db_s[...] = jnp.zeros_like(db_s)
        for head in range(heads):
            a_own, b_own = head_only(a_low, head), head_only(b_low, head)
            e = dot_nt(a_low, b_own)
            kern = jnp.where(allowed, 1.0 + e + 0.5 * e * e, 0.0).astype(BF16)
            dkern = dot_nt(dyx_s[head], cx_s[head])
            de = jnp.where(allowed, dkern * (1.0 + e), 0.0).astype(BF16)
            one, two = lift_parts(a_low, tables, 1, head)
            dpsi = jnp.where(applies, dot_nt(dyx_s[head], sin_s[head]), 0.0)
            pcols = slice(head * PSI, (head + 1) * PSI)
            da_s[...] += (
                dot_nn(de, b_own)
                + dot_nt((dpsi * two).astype(BF16), tables[0, :, pcols])
                + dot_nt((dpsi * one).astype(BF16), tables[1, :, pcols])
            )
            db_s[...] += dot_tn(de, a_own)
            yx_s[head] = dot_tn(kern, dyx_s[head])
        hooks["local"]()
        for j in range(1, nz):

            @pl.when(j > at.s)
            def _(j=j):
                remote(ss.at[layer], sr.at[layer, j], st_send.at[layer, 0], st_recv.at[layer, j], core).wait_recv()

        hooks["states"]()
        st_s[...] = jnp.zeros_like(st_s)
        for head in range(heads):
            total = jnp.zeros((PSI_SENT, LANES), F32)
            for j in range(1, nz):
                counts = (j > at.s) & (at.prior_seg(j) == mine_last)
                total = total + jnp.where(counts, sr[layer, j, head].astype(F32), 0.0)
            st_s[head, 0:PSI_SENT] = total.astype(BF16)
            one, two = lift_parts(b_low, tables, 2, head)
            psi = (one * two).astype(BF16)
            dpsi = jnp.where(tail, dot_nt(cx_s[head], st_s[head]), 0.0)
            pcols = slice(head * PSI, (head + 1) * PSI)
            db_s[...] += dot_nt((dpsi * two).astype(BF16), tables[0, :, pcols]) + dot_nt(
                (dpsi * one).astype(BF16), tables[2, :, pcols]
            )
            dc = yx_s[head] + jnp.where(tail, dot_nn(psi, st_s[head]), 0.0)
            dc_s[0:rows, head * HD : head * HD + LANES] = dc
        edge = remote(
            dc_s.at[pl.ds(0, 8)], edge_s.at[layer], e_send.at[layer], e_recv.at[layer],
            (at.sec, lax.rem(at.s + nz - 1, nz), at.h),
        )

        @pl.when(at.s > 0)
        def _():
            edge.start()

        dcat_s[:, 0:qk] = (da_s[...] * 0.5).astype(BF16)
        dcat_s[:, qk : 2 * qk] = (db_s[...] * 0.5).astype(BF16)
        gsum_s[layer, 2:8, :] = jnp.zeros((6, d), F32)
        for j in range(KW):
            product = dc_s[0:rows, :width] * u_s[8 - j : 8 - j + rows, :width]
            gsum_s[layer, 2 + j : 3 + j, :width] = jnp.sum(jnp.where(at.same(-j), product, 0.0), axis=0, keepdims=True)

        @pl.when(at.s + 1 < nz)
        def _():
            edge.wait_recv()

        dc_s[rows : rows + 8, :] = edge_s[layer]
        du = taps[0:1, :width] * dc_s[0:rows, :width]
        for j in range(1, KW):
            du = du + jnp.where(at.same(j), dc_s[j : j + rows, :width] * taps[j : j + 1, :width], 0.0)
        dcat_s[:, 2 * qk : 2 * qk + width] = du.astype(BF16)

        wait_send(s1)
        s3 = []
        for half in range(2):
            cols = half_cols(cat, half)
            part_s[:, cols] = dot_nn(dcat_s[...], cat[:, cols]).astype(BF16)
            s3 += scatter_start(at, part_s, got_s, head_send.at[layer, 2], head_recv.at[layer, 2], half)
        hooks["rs2"]()
        dn1 = scatter_sum(at, part_s, got_s, s3)
        back, gain_grad = norm_rows_back(x_s[...].astype(F32), gain_attn, dn1)
        gsum_s[layer, 0:1, :] = gain_grad
        ig_s[layer, at.mine] = (dh_s[...] + back).astype(BF16)
        s4 = gather_start(at, ig_s.at[layer], head_send.at[layer, 3], head_recv.at[layer, 3])
        hooks["ag2"]()
        wait_recv(s4)
        ig_send(layer)
        wait_send(s3)

        def finish():
            wait_send(s2 + s4)

            @pl.when(at.s > 0)
            def _():
                edge.wait_send()

            for k in range(1, nz):

                @pl.when(at.s - k >= 0)
                def _(k=k):
                    state(k).wait_send()

        return finish

    def owner(layer, what):
        @pl.when(at.sec == layer)
        def _():
            what()

    g_copy = pltpu.make_async_copy(inputs_grad.at[at.sec], grad_s, io_sem.at[2])
    g_copy.start()
    for i in (7, 5, 6, 4, 0, 1, 2, 3):
        weight_start(1, i)
    for i in (9, 10, 8, 3, 2, 4, 5, 6, 7, 1, 0):
        keep_copy(1, i).start()
    at.barrier(True, True, True)
    ring_n.step(0)
    g_copy.wait()
    grad_s[...] = jnp.where(valid, grad_s[...].astype(F32), 0.0).astype(BF16)

    def slot(layer, g, i):
        owner(line_core(layer, g), lambda: line[layer][g].slot(i))

    def far_sum(g):
        return remote(a_s[g].at[at.s], att_o[g], x_send.at[2 + g], x_recv.at[2 + g], core)

    def line_last(layer, g):
        def go():
            upward(3, nz - 1, line[layer][g].slot)
            line[layer][g].last()
            if line_core(layer, g) == layer:
                copy = pltpu.make_async_copy(a_s[g].at[at.s], att_o[g], io_sem.at[8])
                copy.start()
                copy.wait()
            else:
                far_sum(g).start()

        owner(line_core(layer, g), go)

    def pieces(layer, ring, begin, end, between=None):
        def one(k):
            ring.ready(k - 1)
            if layer == 0:
                ring_0.ready(k - 1)
            piece(layer, k, between)

        if between is None:
            upward(begin, end, one)
        else:
            one(begin)
            upward(begin + 1, end, lambda k: late_piece(layer, ring, k))

    def late_piece(layer, ring, k):
        ring.ready(k - 1)
        if layer == 0:
            ring_0.ready(k - 1)
        piece(layer, k)

    def spread(ring):
        upward(3, nz, ring.step)
        upward(1, nz - 1, ring.pair)

    def nothing():
        pass

    gain_swap = remote(gsum_s.at[1 - at.sec], gpeer_s, x_send.at[1], x_recv.at[1], core)

    def gain_seq(k):
        to = lax.rem(at.s + k, nz)
        return remote(gtot_s.at[0], gz_s.at[k - 1], gz_send.at[k - 1], gz_recv.at[k - 1], (at.sec, to, at.h))

    def b1_rs1():
        own_piece(1)
        ring_n.step(1)
        ring_n.pair(0)

    def b1_ag1():
        ring_n.step(2)
        pieces(1, ring_n, 1, 2)

    def b1_local():
        upward(0, nz - 1, ring_0.pair)
        mixer_grads(1, 0)

    def b1_rs2():
        slot(1, 0, 0)
        mixer_grads(1, 1)
        pieces(1, ring_n, 2, 3)

    def b1_ag2():
        for i in (4, 0, 1, 2, 3):
            weight_start(0, i)
        for i in (9, 10, 8, 3, 2, 4, 5, 6, 7, 1, 0):
            keep_copy(0, i).start()
        slot(1, 0, 1)
        pieces(1, ring_n, 3, nz)
        for i in (7, 5, 6):
            weight_start(0, i)
        ffn_send(1)

    finish_1 = layer_backward(
        1,
        dict(
            begin=nothing, rs1=b1_rs1, ag1=b1_ag1, dm=lambda: spread(ring_n), local=b1_local,
            states=nothing, rs2=b1_rs2, ag2=b1_ag2,
        ),
    )
    finish_1()
    grad_s[...] = jnp.where(valid, ig_s[1].astype(F32), 0.0).astype(BF16)

    def b0_begin():
        ring_g.step(0)
        slot(1, 0, 2)
        slot(1, 1, 0)

    def b0_rs1():
        ffn_done(1)
        own_piece(0)
        ring_g.step(1)
        ring_g.pair(0)
        slot(1, 1, 1)

    def b0_ag1():
        ring_g.step(2)
        pieces(0, ring_g, 1, 2)
        slot(1, 1, 2)
        line_last(1, 0)

    def b0_local():
        owner(0, lambda: far_sum(0).wait_send())
        mixer_sent(1, 0)
        mixer_grads(0, 0)

    def b0_states():
        line_last(1, 1)

    def b0_rs2():
        slot(0, 0, 0)
        mixer_sent(1, 1)
        mixer_grads(0, 1)
        pieces(0, ring_g, 2, 3, lambda: slot(0, 1, 0))
        slot(0, 0, 1)

    def b0_ag2():
        gain_swap.start()

        def between():
            slot(0, 1, 1)
            slot(0, 0, 2)

        pieces(0, ring_g, 3, nz, between)
        ffn_send(0)
        slot(0, 1, 2)
        gain_swap.wait_recv()
        gtot_s[0] = gsum_s[at.sec] + gpeer_s[...]
        for k in range(1, nz):
            gain_seq(k).start()

    finish_0 = layer_backward(
        0,
        dict(
            begin=b0_begin, rs1=b0_rs1, ag1=b0_ag1, dm=lambda: spread(ring_g), local=b0_local,
            states=b0_states, rs2=b0_rs2, ag2=b0_ag2,
        ),
    )

    line_last(0, 0)
    for k in range(1, nz):
        gain_seq(k).wait_recv()
    total = gtot_s[0]
    for k in range(1, nz):
        total = total + gz_s[k - 1]
    gtot_s[1] = total

    def gain_head(m):
        return remote(gtot_s.at[1], gh_s.at[m - 1], gh_send.at[m - 1], gh_recv.at[m - 1], (at.sec, at.s, at.h ^ m))

    for m in range(1, nh):
        gain_head(m).start()
    line_last(0, 1)
    ffn_done(0)
    mixer_sent(0, 0)
    mixer_sent(0, 1)
    owner(1, lambda: far_sum(1).wait_send())
    owner(0, lambda: far_sum(1).wait_recv())
    owner(1, lambda: far_sum(0).wait_recv())
    for m in range(1, nh):
        gain_head(m).wait_recv()
    total = gtot_s[1, 0:2]
    for m in range(1, nh):
        total = total + gh_s[m - 1, 0:2]
    gains_o[...] = gtot_s[1]
    gains_o[0:2, :] = total

    finish_0()
    ring_n.drain()
    ring_g.drain()
    ring_0.drain(line=False)
    gain_swap.wait_send()
    for k in range(1, nz):
        gain_seq(k).wait_send()
    for m in range(1, nh):
        gain_head(m).wait_send()
    for i in range(3):
        ffn_swap(i).wait()
    near, far = ig_copy(0)
    near.wait()
    far.wait_send()
    far.wait_recv()


def final_kernel(qk, width, *refs):
    take = taker(refs)
    whole, far, (early, late, gains), out, parts = take(5), take(3), take(3), take(5), take(8)
    held, held_far, (sems,) = take(5), take(3), take(1)
    loads = [pltpu.make_async_copy(a, b, sems.at[i]) for i, (a, b) in enumerate(zip(whole + far, held + held_far))]
    stores = [pltpu.make_async_copy(a, b, sems.at[8 + i]) for i, (a, b) in enumerate(zip(held, out))]
    for copy in loads:
        copy.start()
    g_q, g_k, g_v, g_o, g_out, g_attn, g_ffn, g_conv = parts
    g_attn[...] = gains[0:1]
    g_ffn[...] = gains[1:2]
    g_conv[...] = gains[2 : 2 + KW, 0:width]
    turned = late[:, 0 : 2 * qk].astype(F32).T
    g_q[...] = turned[0:qk]
    g_k[...] = turned[qk : 2 * qk]
    g_v[...] = late[:, 2 * qk : 2 * qk + width].astype(F32)
    g_o[...] = early[:, 0:width].astype(F32)
    g_out[...] = early[:, width:].astype(F32).T
    for i in range(5):
        loads[i].wait()
        if i >= 2:
            loads[i + 3].wait()
            held[i][...] += held_far[i - 2][...].astype(F32)
        stores[i].start()
    for copy in stores:
        copy.wait()


def shape(dims, kind=BF16):
    return jax.ShapeDtypeStruct(tuple(dims), kind)


ANY = pl.BlockSpec(memory_space=pl.ANY)
VM = pl.BlockSpec(memory_space=pltpu.VMEM)
SM = pl.BlockSpec(memory_space=pltpu.SMEM)
DMA = pltpu.SemaphoreType.DMA


def params(number):
    return pltpu.CompilerParams(collective_id=number, has_side_effects=True, vmem_limit_bytes=VMEM_LIMIT)


def shards(nz, nh, inputs, out_grad, lengths, norm_attn, norm_ffn, w_query, w_key, w_value, w_output_gate, conv_kernel, w_out, w_gate, w_up, w_down):
    micro, rows, d = inputs.shape
    heads = w_query.shape[2] // FEAT
    width, qk, ff = w_value.shape[2], w_query.shape[2], w_gate.shape[2]
    part, block = rows // nh, d // nz
    dims = (nz, nh, rows, heads)
    wide = -(-((heads - 1) * HD + LANES) // LANES) * LANES
    groups = (2 * width, -(-(2 * qk + width) // LANES) * LANES)
    tables = jnp.asarray(lift_tables(heads), BF16)
    turned = [jnp.swapaxes(w, 1, 2) for w in (w_query, w_key, w_value, w_output_gate)]
    own = (*turned, w_out, jnp.swapaxes(w_gate, 1, 2), jnp.swapaxes(w_up, 1, 2), w_down)
    small_own = jnp.concatenate(
        [norm_attn, norm_ffn, jnp.pad(conv_kernel[0], ((0, 0), (0, d - width))), jnp.zeros((3, d), F32)]
    )

    def vm(dims, kind=BF16):
        return pltpu.VMEM(tuple(dims), kind)

    mats = [vm((2 * qk + 2 * width, d)), vm((width, d)), vm((ff, d)), vm((ff, d)), vm((ff, d))]
    act = vm((rows, d))
    kept = [
        ((part, d), BF16),
        ((rows, d), BF16),
        ((rows, 2 * qk), BF16),
        ((rows + 8, wide), F32),
        ((rows, wide), F32),
        ((heads, rows, LANES), F32),
        ((heads, PSI, LANES), BF16),
        ((rows, width), BF16),
        ((part, d), F32),
        ((rows, ff), BF16),
        ((rows, ff), BF16),
    ]
    keep_shapes = [shape(*k) for k in kept]
    gathered = shape((nz, rows, d))
    outs = (
        [shape((8, d), F32)]
        + [shape(w.shape) for w in own]
        + keep_shapes * 2
        + [shape((micro, rows, d)), gathered, gathered, shape((rows, d))]
    )
    scratch = (
        mats
        + mats
        + [
            act,
            act,
            act,
            vm((rows, 2 * qk)),
            vm((rows + 8, wide), F32),
            vm((2, 8, wide), F32),
            vm((rows, wide), F32),
            vm((rows, wide), F32),
            vm((heads, rows, LANES)),
            vm((heads, rows, LANES), F32),
            vm((2, heads, PSI_SENT, LANES)),
            vm((2, nz, heads, PSI_SENT, LANES)),
            vm((heads, PSI, LANES)),
            vm((rows, wide), F32),
            vm((rows, width)),
            vm((2, 2, rows, d)),
            vm((nh - 1, part, d)),
            vm((rows, ff)),
            vm((rows, ff)),
            vm((rows, ff)),
            vm((2, rows, d)),
            vm((part, d), F32),
            vm((8, d), F32),
            DMA((16,)),
            DMA((5,)),
            DMA((SAVED,)),
            DMA((10,)),
            DMA((10,)),
            DMA((2,)),
            DMA((2,)),
            DMA((2, nz)),
            DMA((2, nz)),
            DMA((2, 4, 2 * (nh - 1))),
            DMA((2, 4, 2 * (nh - 1))),
            DMA((2, 2, nz - 1, 2)),
            DMA((2, 2, nz - 1, 2)),
            DMA((2, 2, nz - 1, 2)),
            DMA((2, 2, nz - 1, 2)),
        ]
    )
    first = pl.pallas_call(
        functools.partial(fwd_kernel, dims),
        out_shape=outs,
        in_specs=[SM, ANY, ANY, VM, VM] + [ANY] * 8,
        out_specs=[ANY] * len(outs),
        scratch_shapes=scratch,
        compiler_params=params(0),
    )(lengths, inputs, out_grad, small_own, tables, *own)
    small_other, other = first[0], first[1:9]
    saved = first[9 : 9 + 2 * SAVED]
    section_out, gath_g1, gath_n2_0, n2_1 = first[9 + 2 * SAVED :]

    outs = (
        [shape((micro, rows, d)), shape((8, d), F32)]
        + [shape((block, g)) for g in groups]
        + [shape((block, ff), F32)] * 3
        + [gathered, gathered, gathered]
        + [shape((2, 2, nz, block, g)) for g in groups]
        + [shape((block, ff))] * 3
    )
    out_specs = [ANY, VM] + [ANY] * (len(outs) - 2)
    scratch = (
        mats
        + [vm(*k) for k in kept]
        + [
            act,
            vm((rows, ff)),
            act,
            vm((nh - 1, part, d)),
            act,
            vm((part, d), F32),
            vm((rows, wide), F32),
            vm((rows, wide), F32),
            vm((heads, rows, LANES)),
            vm((heads, rows, LANES)),
            vm((2, heads, PSI_SENT, LANES)),
            vm((2, nz, heads, PSI_SENT, LANES)),
            vm((heads, PSI, LANES)),
            vm((rows, qk), F32),
            vm((rows, qk), F32),
            vm((rows + 8, wide), F32),
            vm((2, 8, wide), F32),
            vm((rows, 2 * qk + 2 * width)),
            vm((2, rows, d)),
            vm((2, 8, d), F32),
            vm((8, d), F32),
            vm((2, 8, d), F32),
            vm((nz - 1, 8, d), F32),
            vm((nh - 1, 8, d), F32),
        ]
        + [vm((block, ff), F32)] * 3
        + [vm((block, ff))] * 3
        + [act, act, vm((block, rows)), vm((block, rows))]
        + [vm((nz, block, g)) for g in groups]
        + [vm((nz, block, max(groups))), vm((block, max(groups)))]
        + [
            DMA((8,)),
            DMA((12,)),
            DMA((SAVED,)),
            DMA((2,)),
            DMA((2,)),
            DMA((2, nz)),
            DMA((2, nz)),
            DMA((2, 4, 2 * (nh - 1))),
            DMA((2, 4, 2 * (nh - 1))),
            DMA((2, 2, nz - 1, 2)),
            DMA((2, 2, nz - 1, 2)),
            DMA((3, 2, nz - 1, 2)),
            DMA((3, 2, nz - 1, 2)),
            DMA((3,)),
            DMA((3,)),
            DMA((2, nz)),
            DMA((2, 2, nz)),
            DMA((2, 2, 2, nz)),
            DMA((2, 2, 2, nz)),
            DMA((4,)),
            DMA((4,)),
            DMA((nz - 1,)),
            DMA((nz - 1,)),
            DMA((nh - 1,)),
            DMA((nh - 1,)),
        ]
    )
    second = pl.pallas_call(
        functools.partial(bwd_kernel, dims),
        out_shape=outs,
        in_specs=[SM, ANY, VM, VM, VM] + [ANY] * (16 + 2 * SAVED + 3),
        out_specs=out_specs,
        scratch_shapes=scratch,
        input_output_aliases={5 + 16 + 2 * SAVED + 1: 9},
        compiler_params=params(1),
    )(lengths, out_grad, small_own, small_other, tables, *own, *other, *saved, gath_g1, gath_n2_0, n2_1)
    input_grad, gains, att_early, att_late, g_gate, g_up, g_down = second[:7]
    far = second[-3:]
    finals = [
        shape((micro, rows, d)),
        shape((micro, rows, d)),
        shape((block, ff), F32),
        shape((block, ff), F32),
        shape((block, ff), F32),
        shape((qk, block), F32),
        shape((qk, block), F32),
        shape((block, width), F32),
        shape((block, width), F32),
        shape((width, block), F32),
        shape((1, d), F32),
        shape((1, d), F32),
        shape((KW, width), F32),
    ]
    section_out, input_grad, g_gate, g_up, g_down, g_q, g_k, g_v, g_o, g_out, g_attn, g_ffn, g_conv = pl.pallas_call(
        functools.partial(final_kernel, qk, width),
        out_shape=finals,
        in_specs=[ANY] * 8 + [VM] * 3,
        out_specs=[ANY] * 5 + [VM] * 8,
        scratch_shapes=[vm((micro, rows, d))] * 2 + [vm((block, ff), F32)] * 3 + [vm((block, ff))] * 3 + [DMA((13,))],
        compiler_params=pltpu.CompilerParams(vmem_limit_bytes=VMEM_LIMIT),
    )(section_out, input_grad, g_gate, g_up, g_down, *far, att_early, att_late, gains)
    return (
        section_out[None],
        input_grad[None],
        g_attn,
        g_ffn,
        g_q.T[None],
        g_k.T[None],
        g_v[None],
        g_o[None],
        g_conv[None],
        g_out[None],
        g_gate[None],
        g_up[None],
        g_down.T[None],
    )


def solution(mesh):
    return jax.shard_map(
        functools.partial(shards, mesh.shape["seq"], mesh.shape["head"]),
        mesh=mesh,
        in_specs=(
            P(None, "seq", None),
            P(None, "seq", None),
            P(),
            P("section", None),
            P("section", None),
            P("section", None, "head"),
            P("section", None, "head"),
            P("section", None, "head"),
            P("section", None, "head"),
            P("section", None, "head"),
            P("section", "head", None),
            P("section", None, "head"),
            P("section", None, "head"),
            P("section", "head", None),
        ),
        out_specs=(
            P("section", None, "seq", None),
            P("section", None, "seq", None),
            P("section", None),
            P("section", None),
            P("section", "seq", "head"),
            P("section", "seq", "head"),
            P("section", "seq", "head"),
            P("section", "seq", "head"),
            P("section", None, "head"),
            P("section", "head", "seq"),
            P("section", "seq", "head"),
            P("section", "seq", "head"),
            P("section", "head", "seq"),
        ),
        check_vma=False,
    )
```

```python
import functools

import jax
import jax.numpy as jnp
import numpy as np
from jax import lax
from jax.experimental import pallas as pl
from jax.experimental.pallas import tpu as pltpu
from jax.sharding import PartitionSpec as P

HD = 112
FEAT = 16
KW = 3
EPS = 1e-05
LANES = 128
PSI = 256
PSI_SENT = 160
MESH = pl.DeviceIdType.MESH
F32 = jnp.float32
BF16 = jnp.bfloat16
VMEM_LIMIT = 63 << 20


def dot_nn(a, b):
    return lax.dot_general(a, b, (((1,), (0,)), ((), ())), preferred_element_type=F32)


def dot_nt(a, b):
    return lax.dot_general(a, b, (((1,), (1,)), ((), ())), preferred_element_type=F32)


def dot_tn(a, b):
    return lax.dot_general(a, b, (((0,), (0,)), ((), ())), preferred_element_type=F32)


def chunks(total, step, body):
    whole = total // step
    if whole > 1:

        def one(i, carry):
            body(pl.multiple_of(i * step, step), step)
            return carry

        lax.fori_loop(0, whole, one, 0)
    elif whole == 1:
        body(0, step)
    if total % step:
        body(whole * step, total % step)


def lift_tables(heads):
    first = np.zeros((heads * FEAT, heads * PSI), np.float32)
    second = np.zeros_like(first)
    second_key = np.zeros_like(first)
    for head in range(heads):
        row, col = head * FEAT, head * PSI
        for i in range(FEAT):
            first[row + i, col + 1 + i] = 1.0
        at = 1 + FEAT
        for i in range(FEAT):
            for j in range(i, FEAT):
                first[row + i, col + at] = 1.0
                second[row + j, col + at] = 1.0
                second_key[row + j, col + at] = 0.5 if i == j else 1.0
                at += 1
    return np.stack([first, second, second_key])


class Place:
    def __init__(self, lens, nz, nh, rows):
        self.sec, self.s, self.h = (lax.axis_index(a) for a in ("section", "seq", "head"))
        self.nz, self.nh, self.rows = nz, nh, rows
        self.l0 = lens[self.sec, 0]
        self.tot = self.l0 + lens[self.sec, 1]
        self.first = self.s * rows
        self.part = rows // nh
        self.mine = pl.ds(pl.multiple_of(self.h * self.part, self.part), self.part)

    def seg(self, pos):
        inside = (pos >= self.l0).astype(jnp.int32) + (pos >= self.tot).astype(jnp.int32)
        return jnp.where(pos >= 0, inside, -1)

    def pos(self, shift=0):
        return self.first + shift + lax.broadcasted_iota(jnp.int32, (self.rows, 1), 0)

    def same(self, shift):
        other = self.pos(shift)
        inside = other < self.nz * self.rows
        return (self.seg(other) == self.seg(self.pos())) & inside

    def allowed(self):
        shape = (self.rows, self.rows)
        row = lax.broadcasted_iota(jnp.int32, shape, 0)
        col = lax.broadcasted_iota(jnp.int32, shape, 1)
        return (col <= row) & (self.seg(self.first + col) == self.seg(self.first + row))

    def last_seg(self, block):
        return self.seg(block * self.rows + self.rows - 1)

    def prior_seg(self, block):
        return self.seg(block * self.rows - 1)

    def applies(self):
        return self.seg(self.pos()) == self.prior_seg(self.s)

    def tail(self):
        return self.seg(self.pos()) == self.last_seg(self.s)

    def peers(self):
        core = [(1 - self.sec, self.s, self.h)]
        seq = [(self.sec, (self.s + k) % self.nz, self.h) for k in range(1, self.nz)]
        head = [(self.sec, self.s, self.h ^ m) for m in range(1, self.nh)]
        return core, seq, head

    def barrier(self, core, seq, head):
        groups = self.peers()
        told = [d for use, g in zip((core, seq, head), groups) if use for d in g]
        sem = pltpu.get_barrier_semaphore()
        for device in told:
            pl.semaphore_signal(sem, 1, device_id=device, device_id_type=MESH)
        pl.semaphore_wait(sem, len(told))


def remote(src, dst, send, recv, device):
    return pltpu.make_async_remote_copy(
        src_ref=src, dst_ref=dst, send_sem=send, recv_sem=recv, device_id=device, device_id_type=MESH
    )


def half_cols(buf, half):
    size = buf.shape[-1] // 2
    return pl.ds(half * size, size)


def scatter_start(at, buf, got, send, recv, half):
    sent = []
    cols = half_cols(buf, half)
    for m in sorted(range(1, at.nh), reverse=True):
        peer = at.h ^ m
        rows = pl.ds(pl.multiple_of(peer * at.part, at.part), at.part)
        sem = half * (at.nh - 1) + m - 1
        copy = remote(
            buf.at[rows, cols], got.at[m - 1, :, cols], send.at[sem], recv.at[sem], (at.sec, at.s, peer)
        )
        copy.start()
        sent.append(copy)
    return sent


def scatter_sum(at, buf, got, sent):
    total = buf[at.mine].astype(F32)
    for copy in sent:
        copy.wait_recv()
    for m in range(1, at.nh):
        total = total + got[m - 1].astype(F32)
    return total


def gather_start(at, buf, send, recv):
    sent = []
    for m in sorted(range(1, at.nh), reverse=True):
        copy = remote(
            buf.at[at.mine], buf.at[at.mine], send.at[m - 1], recv.at[m - 1], (at.sec, at.s, at.h ^ m)
        )
        copy.start()
        sent.append(copy)
    return sent


def wait_recv(copies):
    for copy in copies:
        copy.wait_recv()


def wait_send(copies):
    for copy in copies:
        copy.wait_send()


def norm_rows(x, gain):
    return x * lax.rsqrt(jnp.mean(x * x, axis=-1, keepdims=True) + EPS) * gain


def norm_rows_back(x, gain, grad):
    inverse = lax.rsqrt(jnp.mean(x * x, axis=-1, keepdims=True) + EPS)
    unit = x * inverse
    scaled = grad * gain
    back = inverse * (scaled - unit * jnp.mean(scaled * unit, axis=-1, keepdims=True))
    return back, jnp.sum(grad * unit, axis=0, keepdims=True)


def lift_parts(low, tables, second, head):
    cols = slice(head * PSI, (head + 1) * PSI)
    lane = lax.broadcasted_iota(jnp.int32, (1, PSI), 1)
    one = dot_nn(low, tables[0, :, cols]) + (lane == 0).astype(F32)
    two = dot_nn(low, tables[second, :, cols]) + (lane <= FEAT).astype(F32)
    return one, two


def head_only(low, head):
    lane = lax.broadcasted_iota(jnp.int32, low.shape, 1)
    return jnp.where((lane >= head * FEAT) & (lane < (head + 1) * FEAT), low, jnp.zeros_like(low))


def convolve(at, u_s, taps, c_s, cx_s, heads):
    rows, width = at.rows, heads * HD
    out = taps[0:1, :width] * u_s[8 : 8 + rows, :width]
    for j in range(1, KW):
        shifted = u_s[8 - j : 8 - j + rows, :width]
        out = out + jnp.where(at.same(-j), shifted * taps[j : j + 1, :width], 0.0)
    c_s[0:rows, :width] = out
    lane = lax.broadcasted_iota(jnp.int32, (rows, LANES), 1)
    for head in range(heads):
        one = c_s[0:rows, head * HD : head * HD + LANES]
        cx_s[head] = jnp.where(lane < HD, one, jnp.where(lane == HD, 1.0, 0.0)).astype(BF16)


def order(at, i):
    left, right = at.s, at.nz - 1 - at.s
    both = 2 * jnp.minimum(left, right)
    near = i <= both
    dist = jnp.where(near, (i + 1) // 2, i - both // 2)
    leftward = jnp.where(near, i % 2 == 1, left > right)
    return jnp.where(leftward, at.s - dist, at.s + dist)


class Ring:
    def __init__(self, at, src, dst, send, recv, pair_send, pair_recv):
        self.at, self.src, self.dst, self.send, self.recv = at, src, dst, send, recv
        self.pair_send, self.pair_recv = pair_send, pair_recv

    def _view(self, c):
        at = self.at
        rows, cols = at.rows // 2, self.dst.shape[-1] // 2
        bit = lax.rem(at.h // (1 << c), 2)
        return pl.ds(pl.multiple_of(bit * rows, rows), rows), pl.ds(c * cols, cols)

    def _ways(self, k):
        at = self.at
        right = (at.s - k, at.s - k >= 0, at.s + 1 < at.nz, lax.rem(at.s + 1, at.nz))
        left = (at.s + k, at.s + k < at.nz, at.s > 0, lax.rem(at.s + at.nz - 1, at.nz))
        return right, left

    def _copies(self, way, k, block, to, first):
        at = self.at
        for c in range(2):
            rows, cols = self._view(c)
            src = self.src.at[rows, cols] if first else self.dst.at[block, rows, cols]
            yield remote(
                src, self.dst.at[block, rows, cols], self.send.at[way, k, c], self.recv.at[way, k, c], (at.sec, to, at.h)
            )

    def _pairs(self, way, k, block):
        at = self.at
        for c in range(2):
            rows, cols = self._view(c)
            view = self.dst.at[block, rows, cols]
            yield remote(view, view, self.pair_send.at[way, k, c], self.pair_recv.at[way, k, c], (at.sec, at.s, at.h ^ (1 << c)))

    def step(self, k):
        at = self.at
        first = isinstance(k, int) and k == 0
        for way, (block, there, onward, to) in enumerate(self._ways(k)):
            if not first:

                @pl.when(there)
                def _(way=way, block=block, to=to):
                    wait_recv(self._copies(way, k - 1, block, to, False))

            if not isinstance(k, int) or k < at.nz - 1:

                @pl.when(there & onward & (k < at.nz - 1))
                def _(way=way, block=block, to=to):
                    for copy in self._copies(way, k, block, to, first):
                        copy.start()

    def pair(self, k):
        for way, (block, there, _, _) in enumerate(self._ways(k + 1)):

            @pl.when(there)
            def _(way=way, block=block):
                for copy in self._pairs(way, k, block):
                    copy.start()

    def ready(self, k):
        for way, (block, there, _, _) in enumerate(self._ways(k + 1)):

            @pl.when(there)
            def _(way=way, block=block):
                wait_recv(self._pairs(way, k, block))

    def drain(self, line=True, pairs=True):
        def one(k, carry):
            for way, (_, there, onward, to) in enumerate(self._ways(k) if line else ()):

                @pl.when(there & onward)
                def _(way=way, to=to):
                    wait_send(self._copies(way, k, self.at.s, to, False))

            for way, (_, there, _, _) in enumerate(self._ways(k + 1) if pairs else ()):

                @pl.when(there)
                def _(way=way):
                    wait_send(self._pairs(way, k, self.at.s))

            return carry

        lax.fori_loop(0, self.at.nz - 1, one, 0)


def upward(begin, end, body):
    if end > begin:

        def one(k, carry):
            body(k)
            return carry

        lax.fori_loop(begin, end, one, 0)


class LineSum:
    def __init__(self, at, mine, peer, land, held, io, send, recv, peer_recv):
        self.at, self.mine, self.peer, self.land, self.held = at, mine, peer, land, held
        self.io, self.send, self.recv, self.peer_recv = io, send, recv, peer_recv

    def _hop(self, way, d):
        at = self.at
        to = lax.rem(at.s + (1 if way == 0 else at.nz - 1), at.nz)
        return remote(self.mine.at[d], self.land.at[way, d], self.send.at[way, d], self.recv.at[way, d], (at.sec, to, at.h))

    def _add(self, way, d):
        self._hop(way, d).wait_recv()
        held = self.held.at[:, pl.ds(0, self.mine.shape[-1])]
        copy = pltpu.make_async_copy(self.land.at[way, d], held, self.io)
        copy.start()
        copy.wait()
        self.mine[d] += held[...]

    def slot(self, i):
        at = self.at
        if isinstance(i, int) and i == 0:
            for d in range(at.nz):
                peer = self.peer.at[d, :, pl.ds(0, self.mine.shape[-1])]
                remote(peer, peer, self.peer_recv.at[d], self.peer_recv.at[d], (1 - at.sec, at.s, at.h)).wait_recv()
                self.mine[d] += peer[...]
        for way in range(2):
            begun = i - at.s if way == 0 else i - (at.nz - 1 - at.s)
            d = at.nz - 1 - begun if way == 0 else begun
            earlier = at.s > 0 if way == 0 else at.s < at.nz - 1

            @pl.when((begun >= 0) & (i < at.nz - 1))
            def _(way=way, d=d, earlier=earlier):
                @pl.when(earlier)
                def _():
                    self._add(way, d)

                self._hop(way, d).start()

    def last(self):
        at = self.at
        for d in range(at.nz):
            for way, there in ((0, at.s < d), (1, at.s > d)):

                @pl.when(there)
                def _(way=way, d=d):
                    self._hop(way, d).wait_send()

        @pl.when(at.s > 0)
        def _():
            self._add(0, at.s)

        @pl.when(at.s < at.nz - 1)
        def _():
            self._add(1, at.s)


def taker(refs):
    refs = list(refs)

    def take(n):
        out = refs[:n]
        del refs[:n]
        return out

    return take


def weight_slots(cat, out, gate, up, down, qk, width):
    at_row, views = 0, []
    for size in (qk, qk, width, width):
        views.append(cat.at[pl.ds(at_row, size)])
        at_row += size
    return views + [out, gate, up, down]


SAVED = 11


def fwd_kernel(dims, *refs):
    nz, nh, rows, heads = dims
    take = taker(refs)
    lens, inputs, out_grad, small_own, tables = take(5)
    own = take(8)
    small_other = take(1)[0]
    other = take(8)
    saved = [take(SAVED), take(SAVED)]
    x_out, gath_g1, gath_n2, n2_out = take(4)
    mats = [take(5), take(5)]
    (x_s, n1_s, n2_s, qk_s, u_s, edge_s, o_s, c_s, cx_s, yx_s, ss, sr, sin_s, g_s, gb_s, part_s, got_s, f_s, v_s, t_s, xo_s, h_s, sm_s) = take(23)
    w_sem, io_sem, save_sem, x_send, x_recv, e_send, e_recv, st_send, st_recv, head_send, head_recv = take(11)
    r_send, r_recv, p_send, p_recv = take(4)
    at = Place(lens, nz, nh, rows)
    d = x_s.shape[1]
    width, qk = heads * HD, heads * FEAT
    core = (1 - at.sec, at.s, at.h)
    slots = [weight_slots(*m, qk, width) for m in mats]

    x_copy = pltpu.make_async_copy(inputs.at[at.sec], x_s, io_sem.at[0])
    x_copy.start()

    def local(layer, i):
        return pltpu.make_async_copy(own[i].at[0], slots[layer][i], w_sem.at[i])

    def swap(layer, i):
        return remote(own[i].at[0], slots[layer][i], x_send.at[i], x_recv.at[i], core)

    def stash(layer, i):
        return pltpu.make_async_copy(slots[layer][i], other[i].at[0], w_sem.at[8 + i])

    for here in range(2):

        @pl.when(at.sec == here)
        def _(here=here):
            for i in (2, 0, 1, 3, 4, 5, 6, 7):
                local(here, i).start()

    at.barrier(True, True, True)
    small_swap = remote(small_own, small_other, x_send.at[8], x_recv.at[8], core)
    small_swap.start()
    for here in range(2):

        @pl.when(at.sec == here)
        def _(here=here):
            for i in (2, 0, 1, 3, 4, 5, 6, 7):
                swap(here, i).start()

    ring_g = Ring(at, out_grad.at[at.sec], gath_g1, r_send.at[0], r_recv.at[0], p_send.at[0], p_recv.at[0])
    ring_n = Ring(at, gath_n2.at[at.s], gath_n2, r_send.at[1], r_recv.at[1], p_send.at[1], p_recv.at[1])
    small_swap.wait_recv()
    small_copy = pltpu.make_async_copy(small_other, sm_s, io_sem.at[1])
    small_copy.start()
    small_copy.wait()

    def wait_weight(layer, i):
        @pl.when(at.sec == layer)
        def _():
            local(layer, i).wait()

        @pl.when(at.sec != layer)
        def _():
            swap(layer, i).wait_recv()
            stash(layer, i).start()

    allowed = at.allowed()
    applies, tail, prior = at.applies(), at.tail(), at.prior_seg(at.s)
    my_pos = at.first + at.h * at.part + lax.broadcasted_iota(jnp.int32, (at.part, 1), 0)
    my_valid = my_pos < at.tot

    def layer_forward(layer, x_s, hooks):
        cat, w_out, w_gate, w_up, w_down = mats[layer]
        small = jnp.where(at.sec == layer, small_own[...], sm_s[...])
        gain_attn, gain_ffn, taps = small[0:1], small[1:2], small[2 : 2 + KW]
        keep = []

        def save(src, i):
            copy = pltpu.make_async_copy(src, saved[layer][i], save_sem.at[i])
            copy.start()
            keep.append(copy)

        hooks["begin"]()
        n1_s[...] = norm_rows(x_s[...].astype(F32), gain_attn).astype(BF16)
        save(x_s.at[at.mine], 0)
        save(n1_s, 1)
        wait_weight(layer, 2)
        u_s[8 : 8 + rows, :width] = dot_nt(n1_s[...], cat[2 * qk : 2 * qk + width, :]).astype(BF16).astype(F32)
        edge = remote(
            u_s.at[pl.ds(rows, 8)], edge_s.at[layer], e_send.at[layer], e_recv.at[layer],
            (at.sec, lax.rem(at.s + 1, nz), at.h),
        )

        @pl.when(at.s + 1 < nz)
        def _():
            edge.start()

        wait_weight(layer, 0)
        wait_weight(layer, 1)
        low = dot_nt(n1_s[...], cat[0 : 2 * qk, :]).astype(BF16).astype(F32)
        qk_s[...] = (low * 0.5).astype(BF16)
        save(qk_s, 2)
        a_low, b_low = qk_s[:, 0:qk], qk_s[:, qk : 2 * qk]

        @pl.when(at.s > 0)
        def _():
            edge.wait_recv()

        u_s[0:8, :] = edge_s[layer]
        save(u_s, 3)
        convolve(at, u_s, taps, c_s, cx_s, heads)

        for head in range(heads):
            one, two = lift_parts(b_low, tables, 2, head)
            psi = jnp.where(tail, one * two, 0.0).astype(BF16)
            ss[layer, head] = dot_tn(psi, cx_s[head])[:PSI_SENT].astype(BF16)

        def state(k):
            return remote(
                ss.at[layer], sr.at[layer, at.s], st_send.at[layer, k - 1], st_recv.at[layer, at.s],
                (at.sec, lax.rem(at.s + k, nz), at.h),
            )

        for k in range(1, nz):

            @pl.when(at.s + k < nz)
            def _(k=k):
                state(k).start()

        wait_weight(layer, 3)
        o_s[:, :width] = dot_nt(n1_s[...], cat[2 * qk + width :, :])
        save(o_s, 4)
        for head in range(heads):
            e = dot_nt(a_low, head_only(b_low, head))
            kern = jnp.where(allowed, 1.0 + e + 0.5 * e * e, 0.0).astype(BF16)
            yx_s[head] = dot_nn(kern, cx_s[head])
        for j in range(nz - 1):

            @pl.when(j < at.s)
            def _(j=j):
                remote(ss.at[layer], sr.at[layer, j], st_send.at[layer, 0], st_recv.at[layer, j], core).wait_recv()

        hooks["states"]()
        sin_s[...] = jnp.zeros_like(sin_s)
        for head in range(heads):
            total = jnp.zeros((PSI_SENT, LANES), F32)
            for j in range(nz - 1):
                counts = (j < at.s) & (at.last_seg(j) == prior)
                total = total + jnp.where(counts, sr[layer, j, head].astype(F32), 0.0)
            sin_s[head, 0:PSI_SENT] = total.astype(BF16)
            one, two = lift_parts(a_low, tables, 1, head)
            psi = (one * two).astype(BF16)
            yx = yx_s[head] + jnp.where(applies, dot_nn(psi, sin_s[head]), 0.0)
            yx_s[head] = yx
            gate = o_s[:, head * HD : head * HD + LANES]
            y = yx / yx[:, HD : HD + 1]
            g_s[:, head * HD : head * HD + LANES] = y * (gate * jax.nn.sigmoid(gate))
        gb_s[...] = g_s[:, :width].astype(BF16)
        save(yx_s, 5)
        save(sin_s, 6)
        save(gb_s, 7)

        wait_weight(layer, 4)

        s1 = []
        for half in range(2):
            cols = half_cols(w_out, half)
            part_s[layer, 0, :, cols] = dot_nn(gb_s[...], w_out[:, cols]).astype(BF16)
            s1 += scatter_start(at, part_s.at[layer, 0], got_s, head_send.at[layer, 0], head_recv.at[layer, 0], half)
        hooks["rs1"]()
        hidden = x_s[at.mine].astype(F32) + scatter_sum(at, part_s.at[layer, 0], got_s, s1)
        h_s[...] = hidden
        n2_s[at.mine] = norm_rows(hidden, gain_ffn).astype(BF16)
        s2 = gather_start(at, n2_s, head_send.at[layer, 1], head_recv.at[layer, 1])
        save(h_s, 8)
        hooks["ag1"]()
        wait_recv(s2)
        hooks["n2"]()

        wait_weight(layer, 5)
        wait_weight(layer, 6)

        def up_chunk(at_row, size):
            cols = pl.ds(at_row, size)
            f = dot_nt(n2_s[...], w_gate[cols, :])
            v = dot_nt(n2_s[...], w_up[cols, :])
            f_s[:, cols] = f.astype(BF16)
            v_s[:, cols] = v.astype(BF16)
            t_s[:, cols] = (f * jax.nn.sigmoid(f) * v).astype(BF16)

        chunks(t_s.shape[1], 256, up_chunk)
        save(f_s, 9)
        save(v_s, 10)
        wait_weight(layer, 7)

        s3 = []
        for half in range(2):
            cols = half_cols(w_down, half)
            part_s[layer, 1, :, cols] = dot_nn(t_s[...], w_down[:, cols]).astype(BF16)
            s3 += scatter_start(at, part_s.at[layer, 1], got_s, head_send.at[layer, 2], head_recv.at[layer, 2], half)
        hooks["rs2"]()
        feed = scatter_sum(at, part_s.at[layer, 1], got_s, s3)
        xo_s[layer, at.mine] = jnp.where(my_valid, h_s[...] + feed, 0.0).astype(BF16)
        s4 = gather_start(at, xo_s.at[layer], head_send.at[layer, 3], head_recv.at[layer, 3])
        hooks["ag2"]()
        wait_recv(s4)
        for copy in keep:
            copy.wait()

        def finish():
            wait_send(s1 + s2 + s3 + s4)

            @pl.when(at.s + 1 < nz)
            def _():
                edge.wait_send()

            for k in range(1, nz):

                @pl.when(at.s + k < nz)
                def _(k=k):
                    state(k).wait_send()

        return finish

    def nothing():
        pass

    n2_copy = pltpu.make_async_copy(n2_s, gath_n2.at[at.s], io_sem.at[2])

    def f0_n2():
        n2_copy.start()
        ring_g.step(1)

    def f1_begin():
        n2_copy.wait()
        upward(3, nz, ring_g.step)
        upward(0, nz - 1, ring_g.pair)
        ring_n.step(0)

    def f1_n2():
        n2_last.start()
        ring_n.step(2)

    x_copy.wait()
    finish_0 = layer_forward(
        0, x_s, dict(begin=nothing, states=nothing, rs1=lambda: ring_g.step(0), ag1=nothing, n2=f0_n2, rs2=nothing, ag2=lambda: ring_g.step(2))
    )
    finish_0()

    def out_copy(layer):
        near = pltpu.make_async_copy(xo_s.at[layer], x_out.at[at.sec], io_sem.at[3])
        far = remote(xo_s.at[layer], x_out.at[at.sec], x_send.at[9], x_recv.at[9], core)
        return near, far

    def send_out(layer):
        near, far = out_copy(layer)

        @pl.when(at.sec == layer)
        def _():
            near.start()

        @pl.when(at.sec != layer)
        def _():
            far.start()

    send_out(0)
    n2_last = pltpu.make_async_copy(n2_s, n2_out, io_sem.at[4])
    finish_1 = layer_forward(
        1, xo_s.at[0], dict(begin=f1_begin, states=nothing, rs1=lambda: ring_n.step(1), ag1=nothing, n2=f1_n2, rs2=nothing, ag2=nothing)
    )
    send_out(1)
    finish_1()
    upward(0, nz - 1, ring_g.ready)
    upward(3, nz, ring_n.step)
    n2_last.wait()
    ring_g.drain()
    ring_n.drain(pairs=False)
    near, far = out_copy(0)
    near.wait()
    far.wait_send()
    far.wait_recv()
    small_swap.wait_send()
    for here in range(2):

        @pl.when(at.sec == here)
        def _(here=here):
            for i in range(8):
                swap(here, i).wait_send()
                stash(1 - here, i).wait()


def bwd_kernel(dims, *refs):
    nz, nh, rows, heads = dims
    take = taker(refs)
    lens, inputs_grad, small_own, small_other, tables = take(5)
    own = take(8)
    other = take(8)
    saved = [take(SAVED), take(SAVED)]
    gath_g1, _, n2_1 = take(3)
    ig_o, gains_o = take(2)
    att_o = take(2)
    ffn_o = take(3)
    gath_n2_1, gath_g0, gath_n2_0 = take(3)
    a_land = take(2)
    wr_o = take(3)
    mats = take(5)
    keep_s = take(SAVED)
    (grad_s, t_s, part_s, got_s, dm_s, dh_s, dg_s, do_s, cx_s, dyx_s, ss, sr, st_s, da_s, db_s, dc_s, edge_s, dcat_s, ig_s) = take(19)
    gsum_s, gpeer_s, gtot_s, gz_s, gh_s = take(5)
    acc = take(3)
    wx_s = take(3)
    blk_n2, blk_g, n2t_s, gt_s = take(4)
    a_s = take(2)
    peer_s, held_s = take(2)
    (w_sem, io_sem, keep_sem, e_send, e_recv, st_send, st_recv, head_send, head_recv, r_send, r_recv, p_send, p_recv) = take(13)
    (wx_send, wx_recv, ap_send, ap_recv, l_send, l_recv, x_send, x_recv, gz_send, gz_recv, gh_send, gh_recv) = take(12)
    x_s, n1_s, qk_s, u_s, o_s, yx_s, sin_s, gb_s, h_s, f_s, v_s = keep_s
    df_s, dv_s = f_s, v_s
    at = Place(lens, nz, nh, rows)
    cat, w_out, w_gate, w_up, w_down = mats
    d = n1_s.shape[1]
    width, qk = heads * HD, heads * FEAT
    block = d // nz
    core = (1 - at.sec, at.s, at.h)
    slots = weight_slots(*mats, qk, width)

    def weight_start(layer, i):
        @pl.when(at.sec == layer)
        def _():
            pltpu.make_async_copy(own[i].at[0], slots[i], w_sem.at[i]).start()

        @pl.when(at.sec != layer)
        def _():
            pltpu.make_async_copy(other[i].at[0], slots[i], w_sem.at[i]).start()

    def weight_wait(i):
        pltpu.make_async_copy(own[i].at[0], slots[i], w_sem.at[i]).wait()

    def keep_copy(layer, i):
        return pltpu.make_async_copy(saved[layer][i], keep_s[i], keep_sem.at[i])

    ring_n = Ring(at, n2_1, gath_n2_1, r_send.at[0], r_recv.at[0], p_send.at[0], p_recv.at[0])
    ring_g = Ring(at, ig_s.at[1], gath_g0, r_send.at[1], r_recv.at[1], p_send.at[1], p_recv.at[1])
    ring_0 = Ring(at, None, gath_n2_0, None, None, p_send.at[2], p_recv.at[2])
    line = [
        [
            LineSum(
                at, a_s[g], peer_s, a_land[g].at[layer], held_s, io_sem.at[4],
                l_send.at[layer, g], l_recv.at[layer, g], ap_recv.at[layer, g],
            )
            for g in range(2)
        ]
        for layer in range(2)
    ]

    def turn_blocks(n2_ref, g_ref):
        for part in range(nz):

            @pl.when(at.s == part)
            def _(part=part):
                n2t_s[...] = n2_ref[:, part * block : (part + 1) * block].T
                gt_s[...] = g_ref[:, part * block : (part + 1) * block].T

    def own_fetch(layer):
        return pltpu.make_async_copy(n2_1 if layer == 1 else gath_n2_0.at[at.s], blk_n2, io_sem.at[0])

    def own_piece(layer):
        own_fetch(layer).wait()
        turn_blocks(blk_n2, grad_s)

        def hidden(at_col, size):
            cols = pl.ds(at_col, size)
            acc[0][:, cols] = dot_nn(n2t_s[...], df_s[:, cols])
            acc[1][:, cols] = dot_nn(n2t_s[...], dv_s[:, cols])
            acc[2][:, cols] = dot_nn(gt_s[...], t_s[:, cols])

        chunks(w_gate.shape[0], 640, hidden)

    def fetch(layer, i):
        which = order(at, i)
        n2_src = (gath_n2_1 if layer == 1 else gath_n2_0).at[which]
        g_src = (gath_g1 if layer == 1 else gath_g0).at[which]
        return pltpu.make_async_copy(n2_src, blk_n2, io_sem.at[0]), pltpu.make_async_copy(g_src, blk_g, io_sem.at[1])

    def prefetch(layer, ring, k):
        ring.ready(k - 1)
        if layer == 0:
            ring_0.ready(k - 1)
        for copy in fetch(layer, k):
            copy.start()

    def piece(layer, i, between=None):
        which = order(at, i)
        for copy in fetch(layer, i):
            copy.wait()
        pos = which * rows + lax.broadcasted_iota(jnp.int32, (rows, 1), 0)
        blk_g[...] = jnp.where(pos < at.tot, blk_g[...].astype(F32), 0.0).astype(BF16)
        turn_blocks(blk_n2, blk_g)

        def hidden(at_row, size):
            cols = pl.ds(at_row, size)
            f = dot_nt(blk_n2[...], w_gate[cols, :])
            v = dot_nt(blk_n2[...], w_up[cols, :])
            dt = dot_nt(blk_g[...], w_down[cols, :])
            sig = jax.nn.sigmoid(f)
            act = f * sig
            t = (act * v).astype(BF16)
            df = (dt * v * (sig + act * (1.0 - sig))).astype(BF16)
            dv = (dt * act).astype(BF16)
            acc[0][:, cols] += dot_nn(n2t_s[...], df)
            acc[1][:, cols] += dot_nn(n2t_s[...], dv)
            acc[2][:, cols] += dot_nn(gt_s[...], t)

        ff = w_gate.shape[0]
        if between is None:
            chunks(ff, 640, hidden)
        else:
            hidden(0, 640)
            between()
            hidden(640, ff - 640)

    def ffn_swap(i):
        return remote(wx_s[i], wr_o[i], wx_send.at[i], wx_recv.at[i], core)

    def ffn_own(i):
        return pltpu.make_async_copy(acc[i], ffn_o[i], io_sem.at[5 + i])

    def ffn_send(layer):
        @pl.when(at.sec != layer)
        def _():
            for i in range(3):
                wx_s[i][...] = acc[i][...].astype(BF16)
                ffn_swap(i).start()

        @pl.when(at.sec == layer)
        def _():
            for i in range(3):
                ffn_own(i).start()

    def ffn_done(layer):
        @pl.when(at.sec == layer)
        def _():
            for i in range(3):
                ffn_own(i).wait()

    def ig_copy(layer):
        near = pltpu.make_async_copy(ig_s.at[layer], ig_o.at[at.sec], io_sem.at[3])
        far = remote(ig_s.at[layer], ig_o.at[at.sec], x_send.at[0], x_recv.at[0], core)
        return near, far

    def ig_send(layer):
        near, far = ig_copy(layer)

        @pl.when(at.sec == layer)
        def _():
            near.start()

        @pl.when(at.sec != layer)
        def _():
            far.start()

    allowed = at.allowed()
    applies, tail, mine_last = at.applies(), at.tail(), at.last_seg(at.s)
    valid = at.pos() < at.tot
    lane = lax.broadcasted_iota(jnp.int32, (rows, LANES), 1)

    def line_core(layer, g):
        return g

    def peer_chunk(layer, g, i):
        there = peer_s.at[i, :, pl.ds(0, a_s[g].shape[-1])]
        return remote(a_s[g].at[i], there, ap_send.at[g, i], ap_recv.at[layer, g, i], core)

    def mixer_grads(layer, g):
        late = 2 * qk + width
        for i in range(nz):
            cols = slice(i * block, (i + 1) * block)
            if g == 0:
                a_s[0][i, :, 0:width] = dot_tn(n1_s[:, cols], dcat_s[:, late:]).astype(BF16)
                a_s[0][i, :, width:] = dot_tn(dm_s[:, cols], gb_s[...]).astype(BF16)
            else:
                a_s[1][i, :, 0:late] = dot_tn(n1_s[:, cols], dcat_s[:, 0:late]).astype(BF16)

            @pl.when(at.sec != line_core(layer, g))
            def _(i=i):
                peer_chunk(layer, g, i).start()

    def mixer_sent(layer, g):
        for i in range(nz):

            @pl.when(at.sec != line_core(layer, g))
            def _(i=i):
                peer_chunk(layer, g, i).wait_send()

    def layer_backward(layer, hooks):
        small = jnp.where(at.sec == layer, small_own[...], small_other[...])
        gain_attn, gain_ffn, taps = small[0:1], small[1:2], small[2 : 2 + KW]
        hooks["begin"]()

        weight_wait(7)
        keep_copy(layer, 9).wait()
        keep_copy(layer, 10).wait()

        def down_chunk(at_row, size):
            cols = pl.ds(at_row, size)
            dt = dot_nt(grad_s[...], w_down[cols, :])
            f = f_s[:, cols].astype(F32)
            v = v_s[:, cols].astype(F32)
            sig = jax.nn.sigmoid(f)
            act = f * sig
            t_s[:, cols] = (act * v).astype(BF16)
            df_s[:, cols] = (dt * v * (sig + act * (1.0 - sig))).astype(BF16)
            dv_s[:, cols] = (dt * act).astype(BF16)

        chunks(df_s.shape[1], 256, down_chunk)
        weight_wait(5)
        weight_wait(6)

        s1 = []
        for half in range(2):
            cols = half_cols(w_up, half)
            part = dot_nn(df_s[...], w_gate[:, cols]) + dot_nn(dv_s[...], w_up[:, cols])
            part_s[:, cols] = part.astype(BF16)
            s1 += scatter_start(at, part_s, got_s, head_send.at[layer, 0], head_recv.at[layer, 0], half)
        hooks["rs1"]()
        keep_copy(layer, 3).wait()
        convolve(at, u_s, taps, do_s, cx_s, heads)
        keep_copy(layer, 8).wait()
        dn2 = scatter_sum(at, part_s, got_s, s1)
        back, gain_grad = norm_rows_back(h_s[...], gain_ffn, dn2)
        gsum_s[layer, 1:2, :] = gain_grad
        dh = grad_s[at.mine].astype(F32) + back
        dh_s[...] = dh
        dm_s[at.mine] = dh.astype(BF16)
        s2 = gather_start(at, dm_s, head_send.at[layer, 1], head_recv.at[layer, 1])
        for i in (0, 1, 2, 4, 5, 6, 7):
            keep_copy(layer, i).wait()
        for i in (4, 0, 1, 2, 3):
            weight_wait(i)
        a_low, b_low = qk_s[:, 0:qk], qk_s[:, qk : 2 * qk]
        hooks["ag1"]()
        wait_recv(s2)
        hooks["dm"]()

        def out_chunk(at_row, size):
            cols = pl.ds(at_row, size)
            dg_s[:, cols] = dot_nt(dm_s[...], w_out[cols, :])

        chunks(width, 256, out_chunk)
        for head in range(heads):
            cols = slice(head * HD, head * HD + LANES)
            gate, dg, yx = o_s[:, cols], dg_s[:, cols], yx_s[head]
            sig = jax.nn.sigmoid(gate)
            inverse = 1.0 / yx[:, HD : HD + 1]
            y = yx * inverse
            do_s[:, cols] = dg * y * sig * (1.0 + gate * (1.0 - sig))
            dy = jnp.where(lane < HD, dg * gate * sig, 0.0)
            dden = -jnp.sum(dy * y, axis=1, keepdims=True) * inverse
            dyx_s[head] = jnp.where(lane == HD, dden, dy * inverse).astype(BF16)
            one, two = lift_parts(a_low, tables, 1, head)
            psi = jnp.where(applies, one * two, 0.0).astype(BF16)
            ss[layer, head] = dot_tn(psi, dyx_s[head])[:PSI_SENT].astype(BF16)
        dcat_s[:, 2 * qk + width :] = do_s[:, :width].astype(BF16)

        def state(k):
            return remote(
                ss.at[layer], sr.at[layer, at.s], st_send.at[layer, k - 1], st_recv.at[layer, at.s],
                (at.sec, lax.rem(at.s + nz - k, nz), at.h),
            )

        for k in range(1, nz):

            @pl.when(at.s - k >= 0)
            def _(k=k):
                state(k).start()

        hooks["sent"]()
        da_s[...] = jnp.zeros_like(da_s)
        db_s[...] = jnp.zeros_like(db_s)
        for head in range(heads):
            a_own, b_own = head_only(a_low, head), head_only(b_low, head)
            e = dot_nt(a_low, b_own)
            kern = jnp.where(allowed, 1.0 + e + 0.5 * e * e, 0.0).astype(BF16)
            dkern = dot_nt(dyx_s[head], cx_s[head])
            de = jnp.where(allowed, dkern * (1.0 + e), 0.0).astype(BF16)
            one, two = lift_parts(a_low, tables, 1, head)
            dpsi = jnp.where(applies, dot_nt(dyx_s[head], sin_s[head]), 0.0)
            pcols = slice(head * PSI, (head + 1) * PSI)
            da_s[...] += (
                dot_nn(de, b_own)
                + dot_nt((dpsi * two).astype(BF16), tables[0, :, pcols])
                + dot_nt((dpsi * one).astype(BF16), tables[1, :, pcols])
            )
            db_s[...] += dot_tn(de, a_own)
            yx_s[head] = dot_tn(kern, dyx_s[head])
        hooks["local"]()
        for j in range(1, nz):

            @pl.when(j > at.s)
            def _(j=j):
                remote(ss.at[layer], sr.at[layer, j], st_send.at[layer, 0], st_recv.at[layer, j], core).wait_recv()

        hooks["states"]()
        st_s[...] = jnp.zeros_like(st_s)
        for head in range(heads):
            total = jnp.zeros((PSI_SENT, LANES), F32)
            for j in range(1, nz):
                counts = (j > at.s) & (at.prior_seg(j) == mine_last)
                total = total + jnp.where(counts, sr[layer, j, head].astype(F32), 0.0)
            st_s[head, 0:PSI_SENT] = total.astype(BF16)
            one, two = lift_parts(b_low, tables, 2, head)
            psi = (one * two).astype(BF16)
            dpsi = jnp.where(tail, dot_nt(cx_s[head], st_s[head]), 0.0)
            pcols = slice(head * PSI, (head + 1) * PSI)
            db_s[...] += dot_nt((dpsi * two).astype(BF16), tables[0, :, pcols]) + dot_nt(
                (dpsi * one).astype(BF16), tables[2, :, pcols]
            )
            dc = yx_s[head] + jnp.where(tail, dot_nn(psi, st_s[head]), 0.0)
            dc_s[0:rows, head * HD : head * HD + LANES] = dc
        edge = remote(
            dc_s.at[pl.ds(0, 8)], edge_s.at[layer], e_send.at[layer], e_recv.at[layer],
            (at.sec, lax.rem(at.s + nz - 1, nz), at.h),
        )

        @pl.when(at.s > 0)
        def _():
            edge.start()

        dcat_s[:, 0:qk] = (da_s[...] * 0.5).astype(BF16)
        dcat_s[:, qk : 2 * qk] = (db_s[...] * 0.5).astype(BF16)
        gsum_s[layer, 2:8, :] = jnp.zeros((6, d), F32)
        for j in range(KW):
            product = dc_s[0:rows, :width] * u_s[8 - j : 8 - j + rows, :width]
            gsum_s[layer, 2 + j : 3 + j, :width] = jnp.sum(jnp.where(at.same(-j), product, 0.0), axis=0, keepdims=True)

        @pl.when(at.s + 1 < nz)
        def _():
            edge.wait_recv()

        dc_s[rows : rows + 8, :] = edge_s[layer]
        du = taps[0:1, :width] * dc_s[0:rows, :width]
        for j in range(1, KW):
            du = du + jnp.where(at.same(j), dc_s[j : j + rows, :width] * taps[j : j + 1, :width], 0.0)
        dcat_s[:, 2 * qk : 2 * qk + width] = du.astype(BF16)

        wait_send(s1)
        s3 = []
        for half in range(2):
            cols = half_cols(cat, half)
            part_s[:, cols] = dot_nn(dcat_s[...], cat[:, cols]).astype(BF16)
            s3 += scatter_start(at, part_s, got_s, head_send.at[layer, 2], head_recv.at[layer, 2], half)
        hooks["rs2"]()
        dn1 = scatter_sum(at, part_s, got_s, s3)
        back, gain_grad = norm_rows_back(x_s[...].astype(F32), gain_attn, dn1)
        gsum_s[layer, 0:1, :] = gain_grad
        ig_s[layer, at.mine] = (dh_s[...] + back).astype(BF16)
        s4 = gather_start(at, ig_s.at[layer], head_send.at[layer, 3], head_recv.at[layer, 3])
        hooks["ag2"]()
        wait_recv(s4)
        ig_send(layer)
        wait_send(s3)

        def finish():
            wait_send(s2 + s4)

            @pl.when(at.s > 0)
            def _():
                edge.wait_send()

            for k in range(1, nz):

                @pl.when(at.s - k >= 0)
                def _(k=k):
                    state(k).wait_send()

        return finish

    def owner(layer, what):
        @pl.when(at.sec == layer)
        def _():
            what()

    g_copy = pltpu.make_async_copy(inputs_grad.at[at.sec], grad_s, io_sem.at[2])
    g_copy.start()
    for i in (7, 5, 6, 4, 0, 1, 2, 3):
        weight_start(1, i)
    for i in (9, 10, 8, 3, 2, 4, 5, 6, 7, 1, 0):
        keep_copy(1, i).start()
    own_fetch(1).start()
    at.barrier(True, True, True)
    ring_n.step(0)
    g_copy.wait()
    grad_s[...] = jnp.where(valid, grad_s[...].astype(F32), 0.0).astype(BF16)

    def slot(layer, g, i):
        owner(line_core(layer, g), lambda: line[layer][g].slot(i))

    def far_sum(g):
        return remote(a_s[g].at[at.s], att_o[g], x_send.at[2 + g], x_recv.at[2 + g], core)

    def line_last(layer, g):
        def go():
            upward(3, nz - 1, line[layer][g].slot)
            line[layer][g].last()
            if line_core(layer, g) == layer:
                copy = pltpu.make_async_copy(a_s[g].at[at.s], att_o[g], io_sem.at[8])
                copy.start()
                copy.wait()
            else:
                far_sum(g).start()

        owner(line_core(layer, g), go)

    def pieces(layer, ring, begin, end, between=None):
        piece(layer, begin, between)

        def one(k):
            prefetch(layer, ring, k)
            piece(layer, k)

        upward(begin + 1, end, one)

    def spread(ring):
        upward(3, nz, ring.step)
        upward(1, nz - 1, ring.pair)

    def nothing():
        pass

    gain_swap = remote(gsum_s.at[1 - at.sec], gpeer_s, x_send.at[1], x_recv.at[1], core)

    def gain_seq(k):
        to = lax.rem(at.s + k, nz)
        return remote(gtot_s.at[0], gz_s.at[k - 1], gz_send.at[k - 1], gz_recv.at[k - 1], (at.sec, to, at.h))

    def b1_rs1():
        own_piece(1)
        ring_n.step(1)
        ring_n.pair(0)

    def b1_ag1():
        ring_n.step(2)
        prefetch(1, ring_n, 1)
        pieces(1, ring_n, 1, 2)

    def b1_sent():
        upward(0, nz - 1, ring_0.pair)
        mixer_grads(1, 0)

    def b1_rs2():
        slot(1, 0, 1)
        mixer_grads(1, 1)
        pieces(1, ring_n, 2, 3)
        prefetch(1, ring_n, 3)
        slot(1, 0, 2)

    def b1_ag2():
        for i in (4, 0, 1, 2, 3):
            weight_start(0, i)
        for i in (9, 10, 8, 3, 2, 4, 5, 6, 7, 1, 0):
            keep_copy(0, i).start()
        pieces(1, ring_n, 3, nz, lambda: slot(1, 1, 0))
        for i in (7, 5, 6):
            weight_start(0, i)
        own_fetch(0).start()
        ffn_send(1)

    finish_1 = layer_backward(
        1,
        dict(
            begin=nothing, rs1=b1_rs1, ag1=b1_ag1, dm=lambda: spread(ring_n), sent=b1_sent, local=lambda: slot(1, 0, 0),
            states=lambda: prefetch(1, ring_n, 2), rs2=b1_rs2, ag2=b1_ag2,
        ),
    )
    finish_1()
    grad_s[...] = jnp.where(valid, ig_s[1].astype(F32), 0.0).astype(BF16)

    def b0_begin():
        ring_g.step(0)
        slot(1, 1, 1)

    def b0_rs1():
        ffn_done(1)
        own_piece(0)
        ring_g.step(1)
        ring_g.pair(0)
        line_last(1, 0)
        slot(1, 1, 2)

    def b0_ag1():
        ring_g.step(2)
        prefetch(0, ring_g, 1)
        pieces(0, ring_g, 1, 2)
        line_last(1, 1)

    def b0_sent():
        owner(0, lambda: far_sum(0).wait_send())
        mixer_sent(1, 0)
        mixer_grads(0, 0)

    def b0_rs2():
        slot(0, 0, 1)
        mixer_sent(1, 1)
        mixer_grads(0, 1)
        pieces(0, ring_g, 2, 3, lambda: slot(0, 1, 0))
        prefetch(0, ring_g, 3)
        slot(0, 0, 2)

    def b0_ag2():
        gain_swap.start()
        pieces(0, ring_g, 3, nz, lambda: slot(0, 1, 1))
        ffn_send(0)
        slot(0, 1, 2)
        line_last(0, 0)
        gain_swap.wait_recv()
        gtot_s[0] = gsum_s[at.sec] + gpeer_s[...]
        for k in range(1, nz):
            gain_seq(k).start()

    finish_0 = layer_backward(
        0,
        dict(
            begin=b0_begin, rs1=b0_rs1, ag1=b0_ag1, dm=lambda: spread(ring_g), sent=b0_sent, local=lambda: slot(0, 0, 0),
            states=lambda: prefetch(0, ring_g, 2), rs2=b0_rs2, ag2=b0_ag2,
        ),
    )

    for k in range(1, nz):
        gain_seq(k).wait_recv()
    total = gtot_s[0]
    for k in range(1, nz):
        total = total + gz_s[k - 1]
    gtot_s[1] = total

    def gain_head(m):
        return remote(gtot_s.at[1], gh_s.at[m - 1], gh_send.at[m - 1], gh_recv.at[m - 1], (at.sec, at.s, at.h ^ m))

    for m in range(1, nh):
        gain_head(m).start()
    line_last(0, 1)
    ffn_done(0)
    mixer_sent(0, 0)
    mixer_sent(0, 1)
    owner(1, lambda: far_sum(1).wait_send())
    owner(0, lambda: far_sum(1).wait_recv())
    owner(1, lambda: far_sum(0).wait_recv())
    for m in range(1, nh):
        gain_head(m).wait_recv()
    total = gtot_s[1, 0:2]
    for m in range(1, nh):
        total = total + gh_s[m - 1, 0:2]
    gains_o[...] = gtot_s[1]
    gains_o[0:2, :] = total

    finish_0()
    ring_n.drain()
    ring_g.drain()
    ring_0.drain(line=False)
    gain_swap.wait_send()
    for k in range(1, nz):
        gain_seq(k).wait_send()
    for m in range(1, nh):
        gain_head(m).wait_send()
    for i in range(3):
        ffn_swap(i).wait()
    near, far = ig_copy(0)
    near.wait()
    far.wait_send()
    far.wait_recv()


def final_kernel(qk, width, *refs):
    take = taker(refs)
    whole, far, (early, late, gains), out, parts = take(5), take(3), take(3), take(5), take(8)
    held, held_far, (sems,) = take(5), take(3), take(1)
    loads = [pltpu.make_async_copy(a, b, sems.at[i]) for i, (a, b) in enumerate(zip(whole + far, held + held_far))]
    stores = [pltpu.make_async_copy(a, b, sems.at[8 + i]) for i, (a, b) in enumerate(zip(held, out))]
    for copy in loads:
        copy.start()
    g_q, g_k, g_v, g_o, g_out, g_attn, g_ffn, g_conv = parts
    g_attn[...] = gains[0:1]
    g_ffn[...] = gains[1:2]
    g_conv[...] = gains[2 : 2 + KW, 0:width]
    turned = late[:, 0 : 2 * qk].astype(F32).T
    g_q[...] = turned[0:qk]
    g_k[...] = turned[qk : 2 * qk]
    g_v[...] = late[:, 2 * qk : 2 * qk + width].astype(F32)
    g_o[...] = early[:, 0:width].astype(F32)
    g_out[...] = early[:, width:].astype(F32).T
    for i in range(5):
        loads[i].wait()
        if i >= 2:
            loads[i + 3].wait()
            held[i][...] += held_far[i - 2][...].astype(F32)
        stores[i].start()
    for copy in stores:
        copy.wait()


def shape(dims, kind=BF16):
    return jax.ShapeDtypeStruct(tuple(dims), kind)


ANY = pl.BlockSpec(memory_space=pl.ANY)
VM = pl.BlockSpec(memory_space=pltpu.VMEM)
SM = pl.BlockSpec(memory_space=pltpu.SMEM)
DMA = pltpu.SemaphoreType.DMA


def params(number):
    return pltpu.CompilerParams(collective_id=number, has_side_effects=True, vmem_limit_bytes=VMEM_LIMIT)


def shards(nz, nh, inputs, out_grad, lengths, norm_attn, norm_ffn, w_query, w_key, w_value, w_output_gate, conv_kernel, w_out, w_gate, w_up, w_down):
    micro, rows, d = inputs.shape
    heads = w_query.shape[2] // FEAT
    width, qk, ff = w_value.shape[2], w_query.shape[2], w_gate.shape[2]
    part, block = rows // nh, d // nz
    dims = (nz, nh, rows, heads)
    wide = -(-((heads - 1) * HD + LANES) // LANES) * LANES
    groups = (2 * width, -(-(2 * qk + width) // LANES) * LANES)
    tables = jnp.asarray(lift_tables(heads), BF16)
    turned = [jnp.swapaxes(w, 1, 2) for w in (w_query, w_key, w_value, w_output_gate)]
    own = (*turned, w_out, jnp.swapaxes(w_gate, 1, 2), jnp.swapaxes(w_up, 1, 2), w_down)
    small_own = jnp.concatenate(
        [norm_attn, norm_ffn, jnp.pad(conv_kernel[0], ((0, 0), (0, d - width))), jnp.zeros((3, d), F32)]
    )

    def vm(dims, kind=BF16):
        return pltpu.VMEM(tuple(dims), kind)

    mats = [vm((2 * qk + 2 * width, d)), vm((width, d)), vm((ff, d)), vm((ff, d)), vm((ff, d))]
    act = vm((rows, d))
    kept = [
        ((part, d), BF16),
        ((rows, d), BF16),
        ((rows, 2 * qk), BF16),
        ((rows + 8, wide), F32),
        ((rows, wide), F32),
        ((heads, rows, LANES), F32),
        ((heads, PSI, LANES), BF16),
        ((rows, width), BF16),
        ((part, d), F32),
        ((rows, ff), BF16),
        ((rows, ff), BF16),
    ]
    keep_shapes = [shape(*k) for k in kept]
    gathered = shape((nz, rows, d))
    outs = (
        [shape((8, d), F32)]
        + [shape(w.shape) for w in own]
        + keep_shapes * 2
        + [shape((micro, rows, d)), gathered, gathered, shape((rows, d))]
    )
    scratch = (
        mats
        + mats
        + [
            act,
            act,
            act,
            vm((rows, 2 * qk)),
            vm((rows + 8, wide), F32),
            vm((2, 8, wide), F32),
            vm((rows, wide), F32),
            vm((rows, wide), F32),
            vm((heads, rows, LANES)),
            vm((heads, rows, LANES), F32),
            vm((2, heads, PSI_SENT, LANES)),
            vm((2, nz, heads, PSI_SENT, LANES)),
            vm((heads, PSI, LANES)),
            vm((rows, wide), F32),
            vm((rows, width)),
            vm((2, 2, rows, d)),
            vm((nh - 1, part, d)),
            vm((rows, ff)),
            vm((rows, ff)),
            vm((rows, ff)),
            vm((2, rows, d)),
            vm((part, d), F32),
            vm((8, d), F32),
            DMA((16,)),
            DMA((5,)),
            DMA((SAVED,)),
            DMA((10,)),
            DMA((10,)),
            DMA((2,)),
            DMA((2,)),
            DMA((2, nz)),
            DMA((2, nz)),
            DMA((2, 4, 2 * (nh - 1))),
            DMA((2, 4, 2 * (nh - 1))),
            DMA((2, 2, nz - 1, 2)),
            DMA((2, 2, nz - 1, 2)),
            DMA((2, 2, nz - 1, 2)),
            DMA((2, 2, nz - 1, 2)),
        ]
    )
    first = pl.pallas_call(
        functools.partial(fwd_kernel, dims),
        out_shape=outs,
        in_specs=[SM, ANY, ANY, VM, VM] + [ANY] * 8,
        out_specs=[ANY] * len(outs),
        scratch_shapes=scratch,
        compiler_params=params(0),
    )(lengths, inputs, out_grad, small_own, tables, *own)
    small_other, other = first[0], first[1:9]
    saved = first[9 : 9 + 2 * SAVED]
    section_out, gath_g1, gath_n2_0, n2_1 = first[9 + 2 * SAVED :]

    outs = (
        [shape((micro, rows, d)), shape((8, d), F32)]
        + [shape((block, g)) for g in groups]
        + [shape((block, ff), F32)] * 3
        + [gathered, gathered, gathered]
        + [shape((2, 2, nz, block, g)) for g in groups]
        + [shape((block, ff))] * 3
    )
    out_specs = [ANY, VM] + [ANY] * (len(outs) - 2)
    scratch = (
        mats
        + [vm(*k) for k in kept]
        + [
            act,
            vm((rows, ff)),
            act,
            vm((nh - 1, part, d)),
            act,
            vm((part, d), F32),
            vm((rows, wide), F32),
            vm((rows, wide), F32),
            vm((heads, rows, LANES)),
            vm((heads, rows, LANES)),
            vm((2, heads, PSI_SENT, LANES)),
            vm((2, nz, heads, PSI_SENT, LANES)),
            vm((heads, PSI, LANES)),
            vm((rows, qk), F32),
            vm((rows, qk), F32),
            vm((rows + 8, wide), F32),
            vm((2, 8, wide), F32),
            vm((rows, 2 * qk + 2 * width)),
            vm((2, rows, d)),
            vm((2, 8, d), F32),
            vm((8, d), F32),
            vm((2, 8, d), F32),
            vm((nz - 1, 8, d), F32),
            vm((nh - 1, 8, d), F32),
        ]
        + [vm((block, ff), F32)] * 3
        + [vm((block, ff))] * 3
        + [act, act, vm((block, rows)), vm((block, rows))]
        + [vm((nz, block, g)) for g in groups]
        + [vm((nz, block, max(groups))), vm((block, max(groups)))]
        + [
            DMA((8,)),
            DMA((12,)),
            DMA((SAVED,)),
            DMA((2,)),
            DMA((2,)),
            DMA((2, nz)),
            DMA((2, nz)),
            DMA((2, 4, 2 * (nh - 1))),
            DMA((2, 4, 2 * (nh - 1))),
            DMA((2, 2, nz - 1, 2)),
            DMA((2, 2, nz - 1, 2)),
            DMA((3, 2, nz - 1, 2)),
            DMA((3, 2, nz - 1, 2)),
            DMA((3,)),
            DMA((3,)),
            DMA((2, nz)),
            DMA((2, 2, nz)),
            DMA((2, 2, 2, nz)),
            DMA((2, 2, 2, nz)),
            DMA((4,)),
            DMA((4,)),
            DMA((nz - 1,)),
            DMA((nz - 1,)),
            DMA((nh - 1,)),
            DMA((nh - 1,)),
        ]
    )
    second = pl.pallas_call(
        functools.partial(bwd_kernel, dims),
        out_shape=outs,
        in_specs=[SM, ANY, VM, VM, VM] + [ANY] * (16 + 2 * SAVED + 3),
        out_specs=out_specs,
        scratch_shapes=scratch,
        input_output_aliases={5 + 16 + 2 * SAVED + 1: 9},
        compiler_params=params(1),
    )(lengths, out_grad, small_own, small_other, tables, *own, *other, *saved, gath_g1, gath_n2_0, n2_1)
    input_grad, gains, att_early, att_late, g_gate, g_up, g_down = second[:7]
    far = second[-3:]
    finals = [
        shape((micro, rows, d)),
        shape((micro, rows, d)),
        shape((block, ff), F32),
        shape((block, ff), F32),
        shape((block, ff), F32),
        shape((qk, block), F32),
        shape((qk, block), F32),
        shape((block, width), F32),
        shape((block, width), F32),
        shape((width, block), F32),
        shape((1, d), F32),
        shape((1, d), F32),
        shape((KW, width), F32),
    ]
    section_out, input_grad, g_gate, g_up, g_down, g_q, g_k, g_v, g_o, g_out, g_attn, g_ffn, g_conv = pl.pallas_call(
        functools.partial(final_kernel, qk, width),
        out_shape=finals,
        in_specs=[ANY] * 8 + [VM] * 3,
        out_specs=[ANY] * 5 + [VM] * 8,
        scratch_shapes=[vm((micro, rows, d))] * 2 + [vm((block, ff), F32)] * 3 + [vm((block, ff))] * 3 + [DMA((13,))],
        compiler_params=pltpu.CompilerParams(vmem_limit_bytes=VMEM_LIMIT),
    )(section_out, input_grad, g_gate, g_up, g_down, *far, att_early, att_late, gains)
    return (
        section_out[None],
        input_grad[None],
        g_attn,
        g_ffn,
        g_q.T[None],
        g_k.T[None],
        g_v[None],
        g_o[None],
        g_conv[None],
        g_out[None],
        g_gate[None],
        g_up[None],
        g_down.T[None],
    )


def solution(mesh):
    return jax.shard_map(
        functools.partial(shards, mesh.shape["seq"], mesh.shape["head"]),
        mesh=mesh,
        in_specs=(
            P(None, "seq", None),
            P(None, "seq", None),
            P(),
            P("section", None),
            P("section", None),
            P("section", None, "head"),
            P("section", None, "head"),
            P("section", None, "head"),
            P("section", None, "head"),
            P("section", None, "head"),
            P("section", "head", None),
            P("section", None, "head"),
            P("section", None, "head"),
            P("section", "head", None),
        ),
        out_specs=(
            P("section", None, "seq", None),
            P("section", None, "seq", None),
            P("section", None),
            P("section", None),
            P("section", "seq", "head"),
            P("section", "seq", "head"),
            P("section", "seq", "head"),
            P("section", "seq", "head"),
            P("section", None, "head"),
            P("section", "head", "seq"),
            P("section", "seq", "head"),
            P("section", "seq", "head"),
            P("section", "head", "seq"),
        ),
        check_vma=False,
    )
```

```python
import functools

import jax
import jax.numpy as jnp
import numpy as np
from jax import lax
from jax.experimental import pallas as pl
from jax.experimental.pallas import tpu as pltpu
from jax.sharding import PartitionSpec as P

HD = 112
FEAT = 16
KW = 3
EPS = 1e-05
LANES = 128
PSI = 256
PSI_SENT = 160
MESH = pl.DeviceIdType.MESH
F32 = jnp.float32
BF16 = jnp.bfloat16
VMEM_LIMIT = 63 << 20


def dot_nn(a, b):
    return lax.dot_general(a, b, (((1,), (0,)), ((), ())), preferred_element_type=F32)


def dot_nt(a, b):
    return lax.dot_general(a, b, (((1,), (1,)), ((), ())), preferred_element_type=F32)


def dot_tn(a, b):
    return lax.dot_general(a, b, (((0,), (0,)), ((), ())), preferred_element_type=F32)


def chunks(total, step, body):
    whole = total // step
    if whole > 1:

        def one(i, carry):
            body(pl.multiple_of(i * step, step), step)
            return carry

        lax.fori_loop(0, whole, one, 0)
    elif whole == 1:
        body(0, step)
    if total % step:
        body(whole * step, total % step)


def lift_tables(heads):
    first = np.zeros((heads * FEAT, heads * PSI), np.float32)
    second = np.zeros_like(first)
    second_key = np.zeros_like(first)
    for head in range(heads):
        row, col = head * FEAT, head * PSI
        for i in range(FEAT):
            first[row + i, col + 1 + i] = 1.0
        at = 1 + FEAT
        for i in range(FEAT):
            for j in range(i, FEAT):
                first[row + i, col + at] = 1.0
                second[row + j, col + at] = 1.0
                second_key[row + j, col + at] = 0.5 if i == j else 1.0
                at += 1
    return np.stack([first, second, second_key])


class Place:
    def __init__(self, lens, nz, nh, rows):
        self.sec, self.s, self.h = (lax.axis_index(a) for a in ("section", "seq", "head"))
        self.nz, self.nh, self.rows = nz, nh, rows
        self.l0 = lens[self.sec, 0]
        self.tot = self.l0 + lens[self.sec, 1]
        self.first = self.s * rows
        self.part = rows // nh
        self.mine = pl.ds(pl.multiple_of(self.h * self.part, self.part), self.part)

    def seg(self, pos):
        inside = (pos >= self.l0).astype(jnp.int32) + (pos >= self.tot).astype(jnp.int32)
        return jnp.where(pos >= 0, inside, -1)

    def pos(self, shift=0):
        return self.first + shift + lax.broadcasted_iota(jnp.int32, (self.rows, 1), 0)

    def same(self, shift):
        other = self.pos(shift)
        inside = other < self.nz * self.rows
        return (self.seg(other) == self.seg(self.pos())) & inside

    def allowed(self):
        shape = (self.rows, self.rows)
        row = lax.broadcasted_iota(jnp.int32, shape, 0)
        col = lax.broadcasted_iota(jnp.int32, shape, 1)
        return (col <= row) & (self.seg(self.first + col) == self.seg(self.first + row))

    def last_seg(self, block):
        return self.seg(block * self.rows + self.rows - 1)

    def prior_seg(self, block):
        return self.seg(block * self.rows - 1)

    def applies(self):
        return self.seg(self.pos()) == self.prior_seg(self.s)

    def tail(self):
        return self.seg(self.pos()) == self.last_seg(self.s)

    def peers(self):
        core = [(1 - self.sec, self.s, self.h)]
        seq = [(self.sec, (self.s + k) % self.nz, self.h) for k in range(1, self.nz)]
        head = [(self.sec, self.s, self.h ^ m) for m in range(1, self.nh)]
        return core, seq, head

    def barrier(self, core, seq, head):
        groups = self.peers()
        told = [d for use, g in zip((core, seq, head), groups) if use for d in g]
        sem = pltpu.get_barrier_semaphore()
        for device in told:
            pl.semaphore_signal(sem, 1, device_id=device, device_id_type=MESH)
        pl.semaphore_wait(sem, len(told))


def remote(src, dst, send, recv, device):
    return pltpu.make_async_remote_copy(
        src_ref=src, dst_ref=dst, send_sem=send, recv_sem=recv, device_id=device, device_id_type=MESH
    )


def half_cols(buf, half):
    size = buf.shape[-1] // 2
    return pl.ds(half * size, size)


def scatter_start(at, buf, got, send, recv, half):
    sent = []
    cols = half_cols(buf, half)
    for m in sorted(range(1, at.nh), reverse=True):
        peer = at.h ^ m
        rows = pl.ds(pl.multiple_of(peer * at.part, at.part), at.part)
        sem = half * (at.nh - 1) + m - 1
        copy = remote(
            buf.at[rows, cols], got.at[m - 1, :, cols], send.at[sem], recv.at[sem], (at.sec, at.s, peer)
        )
        copy.start()
        sent.append(copy)
    return sent


def scatter_sum(at, buf, got, sent):
    total = buf[at.mine].astype(F32)
    for copy in sent:
        copy.wait_recv()
    for m in range(1, at.nh):
        total = total + got[m - 1].astype(F32)
    return total


def gather_start(at, buf, send, recv):
    sent = []
    for m in sorted(range(1, at.nh), reverse=True):
        copy = remote(
            buf.at[at.mine], buf.at[at.mine], send.at[m - 1], recv.at[m - 1], (at.sec, at.s, at.h ^ m)
        )
        copy.start()
        sent.append(copy)
    return sent


def wait_recv(copies):
    for copy in copies:
        copy.wait_recv()


def wait_send(copies):
    for copy in copies:
        copy.wait_send()


def norm_rows(x, gain):
    return x * lax.rsqrt(jnp.mean(x * x, axis=-1, keepdims=True) + EPS) * gain


def norm_rows_back(x, gain, grad):
    inverse = lax.rsqrt(jnp.mean(x * x, axis=-1, keepdims=True) + EPS)
    unit = x * inverse
    scaled = grad * gain
    back = inverse * (scaled - unit * jnp.mean(scaled * unit, axis=-1, keepdims=True))
    return back, jnp.sum(grad * unit, axis=0, keepdims=True)


def lift_parts(low, tables, second, head):
    cols = slice(head * PSI, (head + 1) * PSI)
    lane = lax.broadcasted_iota(jnp.int32, (1, PSI), 1)
    one = dot_nn(low, tables[0, :, cols]) + (lane == 0).astype(F32)
    two = dot_nn(low, tables[second, :, cols]) + (lane <= FEAT).astype(F32)
    return one, two


def head_only(low, head):
    lane = lax.broadcasted_iota(jnp.int32, low.shape, 1)
    return jnp.where((lane >= head * FEAT) & (lane < (head + 1) * FEAT), low, jnp.zeros_like(low))


def convolve(at, u_s, taps, c_s, cx_s, heads):
    rows, width = at.rows, heads * HD
    out = taps[0:1, :width] * u_s[8 : 8 + rows, :width]
    for j in range(1, KW):
        shifted = u_s[8 - j : 8 - j + rows, :width]
        out = out + jnp.where(at.same(-j), shifted * taps[j : j + 1, :width], 0.0)
    c_s[0:rows, :width] = out
    lane = lax.broadcasted_iota(jnp.int32, (rows, LANES), 1)
    for head in range(heads):
        one = c_s[0:rows, head * HD : head * HD + LANES]
        cx_s[head] = jnp.where(lane < HD, one, jnp.where(lane == HD, 1.0, 0.0)).astype(BF16)


def order(at, i):
    left, right = at.s, at.nz - 1 - at.s
    both = 2 * jnp.minimum(left, right)
    near = i <= both
    dist = jnp.where(near, (i + 1) // 2, i - both // 2)
    leftward = jnp.where(near, i % 2 == 1, left > right)
    return jnp.where(leftward, at.s - dist, at.s + dist)


class Ring:
    def __init__(self, at, src, dst, send, recv, pair_send, pair_recv):
        self.at, self.src, self.dst, self.send, self.recv = at, src, dst, send, recv
        self.pair_send, self.pair_recv = pair_send, pair_recv

    def _view(self, c):
        at = self.at
        rows, cols = at.rows // 2, self.dst.shape[-1] // 2
        bit = lax.rem(at.h // (1 << c), 2)
        return pl.ds(pl.multiple_of(bit * rows, rows), rows), pl.ds(c * cols, cols)

    def _ways(self, k):
        at = self.at
        right = (at.s - k, at.s - k >= 0, at.s + 1 < at.nz, lax.rem(at.s + 1, at.nz))
        left = (at.s + k, at.s + k < at.nz, at.s > 0, lax.rem(at.s + at.nz - 1, at.nz))
        return right, left

    def _copies(self, way, k, block, to, first):
        at = self.at
        for c in range(2):
            rows, cols = self._view(c)
            src = self.src.at[rows, cols] if first else self.dst.at[block, rows, cols]
            yield remote(
                src, self.dst.at[block, rows, cols], self.send.at[way, k, c], self.recv.at[way, k, c], (at.sec, to, at.h)
            )

    def _pairs(self, way, k, block):
        at = self.at
        for c in range(2):
            rows, cols = self._view(c)
            view = self.dst.at[block, rows, cols]
            yield remote(view, view, self.pair_send.at[way, k, c], self.pair_recv.at[way, k, c], (at.sec, at.s, at.h ^ (1 << c)))

    def step(self, k):
        at = self.at
        first = isinstance(k, int) and k == 0
        for way, (block, there, onward, to) in enumerate(self._ways(k)):
            if not first:

                @pl.when(there)
                def _(way=way, block=block, to=to):
                    wait_recv(self._copies(way, k - 1, block, to, False))

            if not isinstance(k, int) or k < at.nz - 1:

                @pl.when(there & onward & (k < at.nz - 1))
                def _(way=way, block=block, to=to):
                    for copy in self._copies(way, k, block, to, first):
                        copy.start()

    def pair(self, k):
        for way, (block, there, _, _) in enumerate(self._ways(k + 1)):

            @pl.when(there)
            def _(way=way, block=block):
                for copy in self._pairs(way, k, block):
                    copy.start()

    def ready(self, k):
        for way, (block, there, _, _) in enumerate(self._ways(k + 1)):

            @pl.when(there)
            def _(way=way, block=block):
                wait_recv(self._pairs(way, k, block))

    def drain(self, line=True, pairs=True):
        def one(k, carry):
            for way, (_, there, onward, to) in enumerate(self._ways(k) if line else ()):

                @pl.when(there & onward)
                def _(way=way, to=to):
                    wait_send(self._copies(way, k, self.at.s, to, False))

            for way, (_, there, _, _) in enumerate(self._ways(k + 1) if pairs else ()):

                @pl.when(there)
                def _(way=way):
                    wait_send(self._pairs(way, k, self.at.s))

            return carry

        lax.fori_loop(0, self.at.nz - 1, one, 0)


def upward(begin, end, body):
    if end > begin:

        def one(k, carry):
            body(k)
            return carry

        lax.fori_loop(begin, end, one, 0)


class LineSum:
    def __init__(self, at, mine, peer, land, held, io, send, recv, peer_recv):
        self.at, self.mine, self.peer, self.land, self.held = at, mine, peer, land, held
        self.io, self.send, self.recv, self.peer_recv = io, send, recv, peer_recv

    def _hop(self, way, d):
        at = self.at
        to = lax.rem(at.s + (1 if way == 0 else at.nz - 1), at.nz)
        return remote(self.mine.at[d], self.land.at[way, d], self.send.at[way, d], self.recv.at[way, d], (at.sec, to, at.h))

    def _add(self, way, d):
        self._hop(way, d).wait_recv()
        held = self.held.at[:, pl.ds(0, self.mine.shape[-1])]
        copy = pltpu.make_async_copy(self.land.at[way, d], held, self.io)
        copy.start()
        copy.wait()
        self.mine[d] += held[...]

    def slot(self, i):
        at = self.at
        if isinstance(i, int) and i == 0:
            for d in range(at.nz):
                peer = self.peer.at[d, :, pl.ds(0, self.mine.shape[-1])]
                remote(peer, peer, self.peer_recv.at[d], self.peer_recv.at[d], (1 - at.sec, at.s, at.h)).wait_recv()
                self.mine[d] += peer[...]
        for way in range(2):
            begun = i - at.s if way == 0 else i - (at.nz - 1 - at.s)
            d = at.nz - 1 - begun if way == 0 else begun
            earlier = at.s > 0 if way == 0 else at.s < at.nz - 1

            @pl.when((begun >= 0) & (i < at.nz - 1))
            def _(way=way, d=d, earlier=earlier):
                @pl.when(earlier)
                def _():
                    self._add(way, d)

                self._hop(way, d).start()

    def last(self):
        at = self.at
        for d in range(at.nz):
            for way, there in ((0, at.s < d), (1, at.s > d)):

                @pl.when(there)
                def _(way=way, d=d):
                    self._hop(way, d).wait_send()

        @pl.when(at.s > 0)
        def _():
            self._add(0, at.s)

        @pl.when(at.s < at.nz - 1)
        def _():
            self._add(1, at.s)


def taker(refs):
    refs = list(refs)

    def take(n):
        out = refs[:n]
        del refs[:n]
        return out

    return take


def weight_slots(cat, out, gate, up, down, qk, width):
    at_row, views = 0, []
    for size in (qk, qk, width, width):
        views.append(cat.at[pl.ds(at_row, size)])
        at_row += size
    return views + [out, gate, up, down]


SAVED = 11


def fwd_kernel(dims, *refs):
    nz, nh, rows, heads = dims
    take = taker(refs)
    lens, inputs, out_grad, small_own, tables = take(5)
    own = take(8)
    small_other = take(1)[0]
    other = take(8)
    saved = [take(SAVED), take(SAVED)]
    x_out, gath_g1, gath_n2, n2_out = take(4)
    mats = [take(5), take(5)]
    (x_s, n1_s, n2_s, qk_s, u_s, edge_s, o_s, c_s, cx_s, yx_s, ss, sr, sin_s, g_s, gb_s, part_s, got_s, f_s, v_s, t_s, xo_s, h_s, sm_s) = take(23)
    w_sem, io_sem, save_sem, x_send, x_recv, e_send, e_recv, st_send, st_recv, head_send, head_recv = take(11)
    r_send, r_recv, p_send, p_recv = take(4)
    at = Place(lens, nz, nh, rows)
    d = x_s.shape[1]
    width, qk = heads * HD, heads * FEAT
    core = (1 - at.sec, at.s, at.h)
    slots = [weight_slots(*m, qk, width) for m in mats]

    x_copy = pltpu.make_async_copy(inputs.at[at.sec], x_s, io_sem.at[0])
    x_copy.start()

    def local(layer, i):
        return pltpu.make_async_copy(own[i].at[0], slots[layer][i], w_sem.at[i])

    def swap(layer, i):
        return remote(own[i].at[0], slots[layer][i], x_send.at[i], x_recv.at[i], core)

    def stash(layer, i):
        return pltpu.make_async_copy(slots[layer][i], other[i].at[0], w_sem.at[8 + i])

    for here in range(2):

        @pl.when(at.sec == here)
        def _(here=here):
            for i in (2, 0, 1, 3, 4, 5, 6, 7):
                local(here, i).start()

    at.barrier(True, True, True)
    small_swap = remote(small_own, small_other, x_send.at[8], x_recv.at[8], core)
    small_swap.start()
    for here in range(2):

        @pl.when(at.sec == here)
        def _(here=here):
            for i in (2, 0, 1, 3, 4, 5, 6, 7):
                swap(here, i).start()

    ring_g = Ring(at, out_grad.at[at.sec], gath_g1, r_send.at[0], r_recv.at[0], p_send.at[0], p_recv.at[0])
    ring_n = Ring(at, gath_n2.at[at.s], gath_n2, r_send.at[1], r_recv.at[1], p_send.at[1], p_recv.at[1])
    small_swap.wait_recv()
    small_copy = pltpu.make_async_copy(small_other, sm_s, io_sem.at[1])
    small_copy.start()
    small_copy.wait()

    def arrived(layer, i):
        @pl.when(at.sec != layer)
        def _():
            swap(layer, i).wait_recv()
            stash(layer, i).start()

    def wait_weight(layer, i):
        @pl.when(at.sec == layer)
        def _():
            local(layer, i).wait()

        if layer == 1:
            arrived(layer, i)

    allowed = at.allowed()
    applies, tail, prior = at.applies(), at.tail(), at.prior_seg(at.s)
    my_pos = at.first + at.h * at.part + lax.broadcasted_iota(jnp.int32, (at.part, 1), 0)
    my_valid = my_pos < at.tot

    def layer_forward(layer, x_s, hooks):
        cat, w_out, w_gate, w_up, w_down = mats[layer]
        small = jnp.where(at.sec == layer, small_own[...], sm_s[...])
        gain_attn, gain_ffn, taps = small[0:1], small[1:2], small[2 : 2 + KW]
        keep = []

        def save(src, i):
            copy = pltpu.make_async_copy(src, saved[layer][i], save_sem.at[i])
            copy.start()
            keep.append(copy)

        hooks["begin"]()
        n1_s[...] = norm_rows(x_s[...].astype(F32), gain_attn).astype(BF16)
        save(x_s.at[at.mine], 0)
        save(n1_s, 1)
        wait_weight(layer, 2)
        u_s[8 : 8 + rows, :width] = dot_nt(n1_s[...], cat[2 * qk : 2 * qk + width, :]).astype(BF16).astype(F32)
        edge = remote(
            u_s.at[pl.ds(rows, 8)], edge_s.at[layer], e_send.at[layer], e_recv.at[layer],
            (at.sec, lax.rem(at.s + 1, nz), at.h),
        )

        @pl.when(at.s + 1 < nz)
        def _():
            edge.start()

        wait_weight(layer, 0)
        wait_weight(layer, 1)
        low = dot_nt(n1_s[...], cat[0 : 2 * qk, :]).astype(BF16).astype(F32)
        qk_s[...] = (low * 0.5).astype(BF16)
        save(qk_s, 2)
        a_low, b_low = qk_s[:, 0:qk], qk_s[:, qk : 2 * qk]

        @pl.when(at.s > 0)
        def _():
            edge.wait_recv()

        u_s[0:8, :] = edge_s[layer]
        save(u_s, 3)
        convolve(at, u_s, taps, c_s, cx_s, heads)

        for head in range(heads):
            one, two = lift_parts(b_low, tables, 2, head)
            psi = jnp.where(tail, one * two, 0.0).astype(BF16)
            ss[layer, head] = dot_tn(psi, cx_s[head])[:PSI_SENT].astype(BF16)

        def state(k):
            return remote(
                ss.at[layer], sr.at[layer, at.s], st_send.at[layer, k - 1], st_recv.at[layer, at.s],
                (at.sec, lax.rem(at.s + k, nz), at.h),
            )

        for k in range(1, nz):

            @pl.when(at.s + k < nz)
            def _(k=k):
                state(k).start()

        wait_weight(layer, 3)
        o_s[:, :width] = dot_nt(n1_s[...], cat[2 * qk + width :, :])
        save(o_s, 4)
        for head in range(heads):
            e = dot_nt(a_low, head_only(b_low, head))
            kern = jnp.where(allowed, 1.0 + e + 0.5 * e * e, 0.0).astype(BF16)
            yx_s[head] = dot_nn(kern, cx_s[head])
        for j in range(nz - 1):

            @pl.when(j < at.s)
            def _(j=j):
                remote(ss.at[layer], sr.at[layer, j], st_send.at[layer, 0], st_recv.at[layer, j], core).wait_recv()

        hooks["states"]()
        sin_s[...] = jnp.zeros_like(sin_s)
        for head in range(heads):
            total = jnp.zeros((PSI_SENT, LANES), F32)
            for j in range(nz - 1):
                counts = (j < at.s) & (at.last_seg(j) == prior)
                total = total + jnp.where(counts, sr[layer, j, head].astype(F32), 0.0)
            sin_s[head, 0:PSI_SENT] = total.astype(BF16)
            one, two = lift_parts(a_low, tables, 1, head)
            psi = (one * two).astype(BF16)
            yx = yx_s[head] + jnp.where(applies, dot_nn(psi, sin_s[head]), 0.0)
            yx_s[head] = yx
            gate = o_s[:, head * HD : head * HD + LANES]
            y = yx / yx[:, HD : HD + 1]
            g_s[:, head * HD : head * HD + LANES] = y * (gate * jax.nn.sigmoid(gate))
        gb_s[...] = g_s[:, :width].astype(BF16)
        save(yx_s, 5)
        save(sin_s, 6)
        save(gb_s, 7)

        wait_weight(layer, 4)

        s1 = []
        for half in range(2):
            cols = half_cols(w_out, half)
            part_s[layer, 0, :, cols] = dot_nn(gb_s[...], w_out[:, cols]).astype(BF16)
            s1 += scatter_start(at, part_s.at[layer, 0], got_s, head_send.at[layer, 0], head_recv.at[layer, 0], half)
        hooks["rs1"]()
        hidden = x_s[at.mine].astype(F32) + scatter_sum(at, part_s.at[layer, 0], got_s, s1)
        h_s[...] = hidden
        n2_s[at.mine] = norm_rows(hidden, gain_ffn).astype(BF16)
        s2 = gather_start(at, n2_s, head_send.at[layer, 1], head_recv.at[layer, 1])
        save(h_s, 8)
        hooks["ag1"]()
        wait_recv(s2)
        hooks["n2"]()

        wait_weight(layer, 5)
        wait_weight(layer, 6)

        def up_chunk(at_row, size):
            cols = pl.ds(at_row, size)
            f = dot_nt(n2_s[...], w_gate[cols, :])
            v = dot_nt(n2_s[...], w_up[cols, :])
            f_s[:, cols] = f.astype(BF16)
            v_s[:, cols] = v.astype(BF16)
            t_s[:, cols] = (f * jax.nn.sigmoid(f) * v).astype(BF16)

        chunks(t_s.shape[1], 256, up_chunk)
        save(f_s, 9)
        save(v_s, 10)
        wait_weight(layer, 7)

        s3 = []
        for half in range(2):
            cols = half_cols(w_down, half)
            part_s[layer, 1, :, cols] = dot_nn(t_s[...], w_down[:, cols]).astype(BF16)
            s3 += scatter_start(at, part_s.at[layer, 1], got_s, head_send.at[layer, 2], head_recv.at[layer, 2], half)
        hooks["rs2"]()
        feed = scatter_sum(at, part_s.at[layer, 1], got_s, s3)
        xo_s[layer, at.mine] = jnp.where(my_valid, h_s[...] + feed, 0.0).astype(BF16)
        s4 = gather_start(at, xo_s.at[layer], head_send.at[layer, 3], head_recv.at[layer, 3])
        hooks["ag2"]()
        wait_recv(s4)
        for copy in keep:
            copy.wait()

        def finish():
            wait_send(s1 + s2 + s3 + s4)

            @pl.when(at.s + 1 < nz)
            def _():
                edge.wait_send()

            for k in range(1, nz):

                @pl.when(at.s + k < nz)
                def _(k=k):
                    state(k).wait_send()

        return finish

    def nothing():
        pass

    n2_copy = pltpu.make_async_copy(n2_s, gath_n2.at[at.s], io_sem.at[2])

    def f0_n2():
        n2_copy.start()
        ring_g.step(1)

    def f1_begin():
        n2_copy.wait()
        upward(3, nz, ring_g.step)
        upward(0, nz - 1, ring_g.pair)
        ring_n.step(0)

    def f1_n2():
        n2_last.start()
        ring_n.step(2)

    for i in (2, 0, 1, 3, 4, 5, 6, 7):
        arrived(0, i)
    x_copy.wait()
    finish_0 = layer_forward(
        0, x_s, dict(begin=nothing, states=nothing, rs1=lambda: ring_g.step(0), ag1=nothing, n2=f0_n2, rs2=nothing, ag2=lambda: ring_g.step(2))
    )
    finish_0()

    def out_copy(layer):
        near = pltpu.make_async_copy(xo_s.at[layer], x_out.at[at.sec], io_sem.at[3])
        far = remote(xo_s.at[layer], x_out.at[at.sec], x_send.at[9], x_recv.at[9], core)
        return near, far

    def send_out(layer):
        near, far = out_copy(layer)

        @pl.when(at.sec == layer)
        def _():
            near.start()

        @pl.when(at.sec != layer)
        def _():
            far.start()

    send_out(0)
    n2_last = pltpu.make_async_copy(n2_s, n2_out, io_sem.at[4])
    finish_1 = layer_forward(
        1, xo_s.at[0], dict(begin=f1_begin, states=nothing, rs1=lambda: ring_n.step(1), ag1=nothing, n2=f1_n2, rs2=nothing, ag2=nothing)
    )
    send_out(1)
    finish_1()
    upward(0, nz - 1, ring_g.ready)
    upward(3, nz, ring_n.step)
    n2_last.wait()
    ring_g.drain()
    ring_n.drain(pairs=False)
    near, far = out_copy(0)
    near.wait()
    far.wait_send()
    far.wait_recv()
    small_swap.wait_send()
    for here in range(2):

        @pl.when(at.sec == here)
        def _(here=here):
            for i in range(8):
                swap(here, i).wait_send()
                stash(1 - here, i).wait()


def bwd_kernel(dims, *refs):
    nz, nh, rows, heads = dims
    take = taker(refs)
    lens, inputs_grad, small_own, small_other, tables = take(5)
    own = take(8)
    other = take(8)
    saved = [take(SAVED), take(SAVED)]
    gath_g1, _, n2_1 = take(3)
    ig_o, gains_o = take(2)
    att_o = take(2)
    ffn_o = take(3)
    gath_n2_1, gath_g0, gath_n2_0 = take(3)
    a_land = take(2)
    wr_o = take(3)
    mats = take(5)
    keep_s = take(SAVED)
    (grad_s, t_s, part_s, got_s, dm_s, dh_s, dg_s, do_s, cx_s, dyx_s, ss, sr, st_s, da_s, db_s, dc_s, edge_s, dcat_s, ig_s) = take(19)
    gsum_s, gpeer_s, gtot_s, gz_s, gh_s = take(5)
    acc = take(3)
    wx_s = take(3)
    blk_n2, blk_g, n2t_s, gt_s = take(4)
    a_s = take(2)
    peer_s, held_s = take(2)
    (w_sem, io_sem, keep_sem, e_send, e_recv, st_send, st_recv, head_send, head_recv, r_send, r_recv, p_send, p_recv) = take(13)
    (wx_send, wx_recv, ap_send, ap_recv, l_send, l_recv, x_send, x_recv, gz_send, gz_recv, gh_send, gh_recv) = take(12)
    x_s, n1_s, qk_s, u_s, o_s, yx_s, sin_s, gb_s, h_s, f_s, v_s = keep_s
    df_s, dv_s = f_s, v_s
    at = Place(lens, nz, nh, rows)
    cat, w_out, w_gate, w_up, w_down = mats
    d = n1_s.shape[1]
    width, qk = heads * HD, heads * FEAT
    block = d // nz
    core = (1 - at.sec, at.s, at.h)
    slots = weight_slots(*mats, qk, width)

    def weight_start(layer, i):
        @pl.when(at.sec == layer)
        def _():
            pltpu.make_async_copy(own[i].at[0], slots[i], w_sem.at[i]).start()

        @pl.when(at.sec != layer)
        def _():
            pltpu.make_async_copy(other[i].at[0], slots[i], w_sem.at[i]).start()

    def weight_wait(i):
        pltpu.make_async_copy(own[i].at[0], slots[i], w_sem.at[i]).wait()

    def keep_copy(layer, i):
        return pltpu.make_async_copy(saved[layer][i], keep_s[i], keep_sem.at[i])

    ring_n = Ring(at, n2_1, gath_n2_1, r_send.at[0], r_recv.at[0], p_send.at[0], p_recv.at[0])
    ring_g = Ring(at, ig_s.at[1], gath_g0, r_send.at[1], r_recv.at[1], p_send.at[1], p_recv.at[1])
    ring_0 = Ring(at, None, gath_n2_0, None, None, p_send.at[2], p_recv.at[2])
    line = [
        [
            LineSum(
                at, a_s[g], peer_s, a_land[g].at[layer], held_s, io_sem.at[4],
                l_send.at[layer, g], l_recv.at[layer, g], ap_recv.at[layer, g],
            )
            for g in range(2)
        ]
        for layer in range(2)
    ]

    def turn_blocks(n2_ref, g_ref):
        for part in range(nz):

            @pl.when(at.s == part)
            def _(part=part):
                n2t_s[...] = n2_ref[:, part * block : (part + 1) * block].T
                gt_s[...] = g_ref[:, part * block : (part + 1) * block].T

    def own_fetch(layer):
        return pltpu.make_async_copy(n2_1 if layer == 1 else gath_n2_0.at[at.s], blk_n2, io_sem.at[0])

    def own_piece(layer):
        own_fetch(layer).wait()
        turn_blocks(blk_n2, grad_s)

        def hidden(at_col, size):
            cols = pl.ds(at_col, size)
            acc[0][:, cols] = dot_nn(n2t_s[...], df_s[:, cols])
            acc[1][:, cols] = dot_nn(n2t_s[...], dv_s[:, cols])
            acc[2][:, cols] = dot_nn(gt_s[...], t_s[:, cols])

        chunks(w_gate.shape[0], 640, hidden)

    def fetch(layer, i):
        which = order(at, i)
        n2_src = (gath_n2_1 if layer == 1 else gath_n2_0).at[which]
        g_src = (gath_g1 if layer == 1 else gath_g0).at[which]
        return pltpu.make_async_copy(n2_src, blk_n2, io_sem.at[0]), pltpu.make_async_copy(g_src, blk_g, io_sem.at[1])

    def prefetch(layer, ring, k):
        ring.ready(k - 1)
        if layer == 0:
            ring_0.ready(k - 1)
        for copy in fetch(layer, k):
            copy.start()

    def piece(layer, i, between=None):
        which = order(at, i)
        for copy in fetch(layer, i):
            copy.wait()
        pos = which * rows + lax.broadcasted_iota(jnp.int32, (rows, 1), 0)
        blk_g[...] = jnp.where(pos < at.tot, blk_g[...].astype(F32), 0.0).astype(BF16)
        turn_blocks(blk_n2, blk_g)

        def hidden(at_row, size):
            cols = pl.ds(at_row, size)
            f = dot_nt(blk_n2[...], w_gate[cols, :])
            v = dot_nt(blk_n2[...], w_up[cols, :])
            dt = dot_nt(blk_g[...], w_down[cols, :])
            sig = jax.nn.sigmoid(f)
            act = f * sig
            t = (act * v).astype(BF16)
            df = (dt * v * (sig + act * (1.0 - sig))).astype(BF16)
            dv = (dt * act).astype(BF16)
            acc[0][:, cols] += dot_nn(n2t_s[...], df)
            acc[1][:, cols] += dot_nn(n2t_s[...], dv)
            acc[2][:, cols] += dot_nn(gt_s[...], t)

        ff = w_gate.shape[0]
        if between is None:
            chunks(ff, 640, hidden)
        else:
            hidden(0, 640)
            between()
            hidden(640, ff - 640)

    def ffn_swap(i):
        return remote(wx_s[i], wr_o[i], wx_send.at[i], wx_recv.at[i], core)

    def ffn_own(i):
        return pltpu.make_async_copy(acc[i], ffn_o[i], io_sem.at[5 + i])

    def ffn_send(layer):
        @pl.when(at.sec != layer)
        def _():
            for i in range(3):
                wx_s[i][...] = acc[i][...].astype(BF16)
                ffn_swap(i).start()

        @pl.when(at.sec == layer)
        def _():
            for i in range(3):
                ffn_own(i).start()

    def ffn_done(layer):
        @pl.when(at.sec == layer)
        def _():
            for i in range(3):
                ffn_own(i).wait()

    def ig_copy(layer):
        near = pltpu.make_async_copy(ig_s.at[layer], ig_o.at[at.sec], io_sem.at[3])
        far = remote(ig_s.at[layer], ig_o.at[at.sec], x_send.at[0], x_recv.at[0], core)
        return near, far

    def ig_send(layer):
        near, far = ig_copy(layer)

        @pl.when(at.sec == layer)
        def _():
            near.start()

        @pl.when(at.sec != layer)
        def _():
            far.start()

    allowed = at.allowed()
    applies, tail, mine_last = at.applies(), at.tail(), at.last_seg(at.s)
    valid = at.pos() < at.tot
    lane = lax.broadcasted_iota(jnp.int32, (rows, LANES), 1)

    def line_core(layer, g):
        return g

    def peer_chunk(layer, g, i):
        there = peer_s.at[i, :, pl.ds(0, a_s[g].shape[-1])]
        return remote(a_s[g].at[i], there, ap_send.at[g, i], ap_recv.at[layer, g, i], core)

    def mixer_grads(layer, g):
        late = 2 * qk + width
        for i in range(nz):
            cols = slice(i * block, (i + 1) * block)
            if g == 0:
                a_s[0][i, :, 0:width] = dot_tn(n1_s[:, cols], dcat_s[:, late:]).astype(BF16)
                a_s[0][i, :, width:] = dot_tn(dm_s[:, cols], gb_s[...]).astype(BF16)
            else:
                a_s[1][i, :, 0:late] = dot_tn(n1_s[:, cols], dcat_s[:, 0:late]).astype(BF16)

            @pl.when(at.sec != line_core(layer, g))
            def _(i=i):
                peer_chunk(layer, g, i).start()

    def mixer_sent(layer, g):
        for i in range(nz):

            @pl.when(at.sec != line_core(layer, g))
            def _(i=i):
                peer_chunk(layer, g, i).wait_send()

    def layer_backward(layer, hooks):
        small = jnp.where(at.sec == layer, small_own[...], small_other[...])
        gain_attn, gain_ffn, taps = small[0:1], small[1:2], small[2 : 2 + KW]
        hooks["begin"]()

        weight_wait(7)
        keep_copy(layer, 9).wait()
        keep_copy(layer, 10).wait()

        def down_chunk(at_row, size):
            cols = pl.ds(at_row, size)
            dt = dot_nt(grad_s[...], w_down[cols, :])
            f = f_s[:, cols].astype(F32)
            v = v_s[:, cols].astype(F32)
            sig = jax.nn.sigmoid(f)
            act = f * sig
            t_s[:, cols] = (act * v).astype(BF16)
            df_s[:, cols] = (dt * v * (sig + act * (1.0 - sig))).astype(BF16)
            dv_s[:, cols] = (dt * act).astype(BF16)

        chunks(df_s.shape[1], 256, down_chunk)
        weight_wait(5)
        weight_wait(6)
        hooks["loads"]()

        s1 = []
        for half in range(2):
            cols = half_cols(w_up, half)
            part = dot_nn(df_s[...], w_gate[:, cols]) + dot_nn(dv_s[...], w_up[:, cols])
            part_s[:, cols] = part.astype(BF16)
            s1 += scatter_start(at, part_s, got_s, head_send.at[layer, 0], head_recv.at[layer, 0], half)
        hooks["rs1"]()
        keep_copy(layer, 3).wait()
        convolve(at, u_s, taps, do_s, cx_s, heads)
        keep_copy(layer, 8).wait()
        dn2 = scatter_sum(at, part_s, got_s, s1)
        back, gain_grad = norm_rows_back(h_s[...], gain_ffn, dn2)
        gsum_s[layer, 1:2, :] = gain_grad
        dh = grad_s[at.mine].astype(F32) + back
        dh_s[...] = dh
        dm_s[at.mine] = dh.astype(BF16)
        s2 = gather_start(at, dm_s, head_send.at[layer, 1], head_recv.at[layer, 1])
        for i in (0, 1, 2, 4, 5, 6, 7):
            keep_copy(layer, i).wait()
        for i in (4, 0, 1, 2, 3):
            weight_wait(i)
        a_low, b_low = qk_s[:, 0:qk], qk_s[:, qk : 2 * qk]
        hooks["ag1"]()
        wait_recv(s2)
        hooks["dm"]()

        def out_chunk(at_row, size):
            cols = pl.ds(at_row, size)
            dg_s[:, cols] = dot_nt(dm_s[...], w_out[cols, :])

        chunks(width, 256, out_chunk)
        for head in range(heads):
            cols = slice(head * HD, head * HD + LANES)
            gate, dg, yx = o_s[:, cols], dg_s[:, cols], yx_s[head]
            sig = jax.nn.sigmoid(gate)
            inverse = 1.0 / yx[:, HD : HD + 1]
            y = yx * inverse
            do_s[:, cols] = dg * y * sig * (1.0 + gate * (1.0 - sig))
            dy = jnp.where(lane < HD, dg * gate * sig, 0.0)
            dden = -jnp.sum(dy * y, axis=1, keepdims=True) * inverse
            dyx_s[head] = jnp.where(lane == HD, dden, dy * inverse).astype(BF16)
            one, two = lift_parts(a_low, tables, 1, head)
            psi = jnp.where(applies, one * two, 0.0).astype(BF16)
            ss[layer, head] = dot_tn(psi, dyx_s[head])[:PSI_SENT].astype(BF16)
        dcat_s[:, 2 * qk + width :] = do_s[:, :width].astype(BF16)

        def state(k):
            return remote(
                ss.at[layer], sr.at[layer, at.s], st_send.at[layer, k - 1], st_recv.at[layer, at.s],
                (at.sec, lax.rem(at.s + nz - k, nz), at.h),
            )

        for k in range(1, nz):

            @pl.when(at.s - k >= 0)
            def _(k=k):
                state(k).start()

        hooks["sent"]()
        da_s[...] = jnp.zeros_like(da_s)
        db_s[...] = jnp.zeros_like(db_s)
        for head in range(heads):
            a_own, b_own = head_only(a_low, head), head_only(b_low, head)
            e = dot_nt(a_low, b_own)
            kern = jnp.where(allowed, 1.0 + e + 0.5 * e * e, 0.0).astype(BF16)
            dkern = dot_nt(dyx_s[head], cx_s[head])
            de = jnp.where(allowed, dkern * (1.0 + e), 0.0).astype(BF16)
            one, two = lift_parts(a_low, tables, 1, head)
            dpsi = jnp.where(applies, dot_nt(dyx_s[head], sin_s[head]), 0.0)
            pcols = slice(head * PSI, (head + 1) * PSI)
            da_s[...] += (
                dot_nn(de, b_own)
                + dot_nt((dpsi * two).astype(BF16), tables[0, :, pcols])
                + dot_nt((dpsi * one).astype(BF16), tables[1, :, pcols])
            )
            db_s[...] += dot_tn(de, a_own)
            yx_s[head] = dot_tn(kern, dyx_s[head])
        hooks["local"]()
        for j in range(1, nz):

            @pl.when(j > at.s)
            def _(j=j):
                remote(ss.at[layer], sr.at[layer, j], st_send.at[layer, 0], st_recv.at[layer, j], core).wait_recv()

        hooks["states"]()
        st_s[...] = jnp.zeros_like(st_s)
        for head in range(heads):
            total = jnp.zeros((PSI_SENT, LANES), F32)
            for j in range(1, nz):
                counts = (j > at.s) & (at.prior_seg(j) == mine_last)
                total = total + jnp.where(counts, sr[layer, j, head].astype(F32), 0.0)
            st_s[head, 0:PSI_SENT] = total.astype(BF16)
            one, two = lift_parts(b_low, tables, 2, head)
            psi = (one * two).astype(BF16)
            dpsi = jnp.where(tail, dot_nt(cx_s[head], st_s[head]), 0.0)
            pcols = slice(head * PSI, (head + 1) * PSI)
            db_s[...] += dot_nt((dpsi * two).astype(BF16), tables[0, :, pcols]) + dot_nt(
                (dpsi * one).astype(BF16), tables[2, :, pcols]
            )
            dc = yx_s[head] + jnp.where(tail, dot_nn(psi, st_s[head]), 0.0)
            dc_s[0:rows, head * HD : head * HD + LANES] = dc
        edge = remote(
            dc_s.at[pl.ds(0, 8)], edge_s.at[layer], e_send.at[layer], e_recv.at[layer],
            (at.sec, lax.rem(at.s + nz - 1, nz), at.h),
        )

        @pl.when(at.s > 0)
        def _():
            edge.start()

        dcat_s[:, 0:qk] = (da_s[...] * 0.5).astype(BF16)
        dcat_s[:, qk : 2 * qk] = (db_s[...] * 0.5).astype(BF16)
        gsum_s[layer, 2:8, :] = jnp.zeros((6, d), F32)
        for j in range(KW):
            product = dc_s[0:rows, :width] * u_s[8 - j : 8 - j + rows, :width]
            gsum_s[layer, 2 + j : 3 + j, :width] = jnp.sum(jnp.where(at.same(-j), product, 0.0), axis=0, keepdims=True)

        @pl.when(at.s + 1 < nz)
        def _():
            edge.wait_recv()

        dc_s[rows : rows + 8, :] = edge_s[layer]
        du = taps[0:1, :width] * dc_s[0:rows, :width]
        for j in range(1, KW):
            du = du + jnp.where(at.same(j), dc_s[j : j + rows, :width] * taps[j : j + 1, :width], 0.0)
        dcat_s[:, 2 * qk : 2 * qk + width] = du.astype(BF16)

        wait_send(s1)
        s3 = []
        for half in range(2):
            cols = half_cols(cat, half)
            part_s[:, cols] = dot_nn(dcat_s[...], cat[:, cols]).astype(BF16)
            s3 += scatter_start(at, part_s, got_s, head_send.at[layer, 2], head_recv.at[layer, 2], half)
        hooks["rs2"]()
        dn1 = scatter_sum(at, part_s, got_s, s3)
        back, gain_grad = norm_rows_back(x_s[...].astype(F32), gain_attn, dn1)
        gsum_s[layer, 0:1, :] = gain_grad
        ig_s[layer, at.mine] = (dh_s[...] + back).astype(BF16)
        s4 = gather_start(at, ig_s.at[layer], head_send.at[layer, 3], head_recv.at[layer, 3])
        hooks["ag2"]()
        wait_recv(s4)
        ig_send(layer)
        wait_send(s3)

        def finish():
            wait_send(s2 + s4)

            @pl.when(at.s > 0)
            def _():
                edge.wait_send()

            for k in range(1, nz):

                @pl.when(at.s - k >= 0)
                def _(k=k):
                    state(k).wait_send()

        return finish

    def owner(layer, what):
        @pl.when(at.sec == layer)
        def _():
            what()

    g_copy = pltpu.make_async_copy(inputs_grad.at[at.sec], grad_s, io_sem.at[2])
    g_copy.start()
    weight_start(1, 7)
    for i in (9, 10):
        keep_copy(1, i).start()
    at.barrier(True, True, True)
    ring_n.step(0)
    for i in (5, 6):
        weight_start(1, i)
    g_copy.wait()
    grad_s[...] = jnp.where(valid, grad_s[...].astype(F32), 0.0).astype(BF16)

    def slot(layer, g, i):
        owner(line_core(layer, g), lambda: line[layer][g].slot(i))

    def far_sum(g):
        return remote(a_s[g].at[at.s], att_o[g], x_send.at[2 + g], x_recv.at[2 + g], core)

    def line_last(layer, g):
        def go():
            upward(3, nz - 1, line[layer][g].slot)
            line[layer][g].last()
            if line_core(layer, g) == layer:
                copy = pltpu.make_async_copy(a_s[g].at[at.s], att_o[g], io_sem.at[8])
                copy.start()
                copy.wait()
            else:
                far_sum(g).start()

        owner(line_core(layer, g), go)

    def pieces(layer, ring, begin, end, between=None):
        piece(layer, begin, between)

        def one(k):
            prefetch(layer, ring, k)
            piece(layer, k)

        upward(begin + 1, end, one)

    def spread(ring):
        upward(3, nz, ring.step)
        upward(1, nz - 1, ring.pair)

    def nothing():
        pass

    gain_swap = remote(gsum_s.at[1 - at.sec], gpeer_s, x_send.at[1], x_recv.at[1], core)

    def gain_seq(k):
        to = lax.rem(at.s + k, nz)
        return remote(gtot_s.at[0], gz_s.at[k - 1], gz_send.at[k - 1], gz_recv.at[k - 1], (at.sec, to, at.h))

    def b1_loads():
        own_fetch(1).start()
        for i in (8, 3, 2, 4, 5, 6, 7, 1, 0):
            keep_copy(1, i).start()
        for i in (4, 0, 1, 2, 3):
            weight_start(1, i)

    def b1_rs1():
        own_piece(1)
        ring_n.step(1)
        ring_n.pair(0)

    def b1_ag1():
        ring_n.step(2)
        prefetch(1, ring_n, 1)
        pieces(1, ring_n, 1, 2)

    def b1_sent():
        upward(0, nz - 1, ring_0.pair)
        mixer_grads(1, 0)

    def b1_rs2():
        slot(1, 0, 1)
        mixer_grads(1, 1)
        pieces(1, ring_n, 2, 3)
        prefetch(1, ring_n, 3)
        slot(1, 0, 2)

    def b1_ag2():
        for i in (4, 0, 1, 2, 3):
            weight_start(0, i)
        for i in (9, 10, 8, 3, 2, 4, 5, 6, 7, 1, 0):
            keep_copy(0, i).start()
        pieces(1, ring_n, 3, nz, lambda: slot(1, 1, 0))
        weight_start(0, 7)
        ffn_send(1)
        for i in (5, 6):
            weight_start(0, i)
        own_fetch(0).start()

    finish_1 = layer_backward(
        1,
        dict(
            begin=nothing, loads=b1_loads, rs1=b1_rs1, ag1=b1_ag1, dm=lambda: spread(ring_n), sent=b1_sent, local=lambda: slot(1, 0, 0),
            states=lambda: prefetch(1, ring_n, 2), rs2=b1_rs2, ag2=b1_ag2,
        ),
    )
    finish_1()
    grad_s[...] = jnp.where(valid, ig_s[1].astype(F32), 0.0).astype(BF16)

    def b0_begin():
        ring_g.step(0)
        slot(1, 1, 1)

    def b0_rs1():
        ffn_done(1)
        own_piece(0)
        ring_g.step(1)
        ring_g.pair(0)
        line_last(1, 0)
        slot(1, 1, 2)

    def b0_ag1():
        ring_g.step(2)
        prefetch(0, ring_g, 1)
        pieces(0, ring_g, 1, 2)
        line_last(1, 1)

    def b0_sent():
        owner(0, lambda: far_sum(0).wait_send())
        mixer_sent(1, 0)
        mixer_grads(0, 0)

    def b0_rs2():
        slot(0, 0, 1)
        mixer_sent(1, 1)
        mixer_grads(0, 1)
        pieces(0, ring_g, 2, 3, lambda: slot(0, 1, 0))
        prefetch(0, ring_g, 3)
        slot(0, 0, 2)

    def b0_ag2():
        gain_swap.start()
        pieces(0, ring_g, 3, nz, lambda: slot(0, 1, 1))
        ffn_send(0)
        slot(0, 1, 2)
        line_last(0, 0)
        gain_swap.wait_recv()
        gtot_s[0] = gsum_s[at.sec] + gpeer_s[...]
        for k in range(1, nz):
            gain_seq(k).start()

    finish_0 = layer_backward(
        0,
        dict(
            begin=b0_begin, loads=nothing, rs1=b0_rs1, ag1=b0_ag1, dm=lambda: spread(ring_g), sent=b0_sent, local=lambda: slot(0, 0, 0),
            states=lambda: prefetch(0, ring_g, 2), rs2=b0_rs2, ag2=b0_ag2,
        ),
    )

    for k in range(1, nz):
        gain_seq(k).wait_recv()
    total = gtot_s[0]
    for k in range(1, nz):
        total = total + gz_s[k - 1]
    gtot_s[1] = total

    def gain_head(m):
        return remote(gtot_s.at[1], gh_s.at[m - 1], gh_send.at[m - 1], gh_recv.at[m - 1], (at.sec, at.s, at.h ^ m))

    for m in range(1, nh):
        gain_head(m).start()
    line_last(0, 1)
    ffn_done(0)
    mixer_sent(0, 0)
    mixer_sent(0, 1)
    owner(1, lambda: far_sum(1).wait_send())
    owner(0, lambda: far_sum(1).wait_recv())
    owner(1, lambda: far_sum(0).wait_recv())
    for m in range(1, nh):
        gain_head(m).wait_recv()
    total = gtot_s[1, 0:2]
    for m in range(1, nh):
        total = total + gh_s[m - 1, 0:2]
    gains_o[...] = gtot_s[1]
    gains_o[0:2, :] = total

    finish_0()
    ring_n.drain()
    ring_g.drain()
    ring_0.drain(line=False)
    gain_swap.wait_send()
    for k in range(1, nz):
        gain_seq(k).wait_send()
    for m in range(1, nh):
        gain_head(m).wait_send()
    for i in range(3):
        ffn_swap(i).wait()
    near, far = ig_copy(0)
    near.wait()
    far.wait_send()
    far.wait_recv()


def final_kernel(qk, width, *refs):
    take = taker(refs)
    whole, far, (early, late, gains), out, parts = take(5), take(3), take(3), take(5), take(8)
    held, held_far, (sems,) = take(5), take(3), take(1)
    loads = [pltpu.make_async_copy(a, b, sems.at[i]) for i, (a, b) in enumerate(zip(whole + far, held + held_far))]
    stores = [pltpu.make_async_copy(a, b, sems.at[8 + i]) for i, (a, b) in enumerate(zip(held, out))]
    for copy in loads:
        copy.start()
    g_q, g_k, g_v, g_o, g_out, g_attn, g_ffn, g_conv = parts
    g_attn[...] = gains[0:1]
    g_ffn[...] = gains[1:2]
    g_conv[...] = gains[2 : 2 + KW, 0:width]
    turned = late[:, 0 : 2 * qk].astype(F32).T
    g_q[...] = turned[0:qk]
    g_k[...] = turned[qk : 2 * qk]
    g_v[...] = late[:, 2 * qk : 2 * qk + width].astype(F32)
    g_o[...] = early[:, 0:width].astype(F32)
    g_out[...] = early[:, width:].astype(F32).T
    for i in range(5):
        loads[i].wait()
        if i >= 2:
            loads[i + 3].wait()
            held[i][...] += held_far[i - 2][...].astype(F32)
        stores[i].start()
    for copy in stores:
        copy.wait()


def shape(dims, kind=BF16):
    return jax.ShapeDtypeStruct(tuple(dims), kind)


ANY = pl.BlockSpec(memory_space=pl.ANY)
VM = pl.BlockSpec(memory_space=pltpu.VMEM)
SM = pl.BlockSpec(memory_space=pltpu.SMEM)
DMA = pltpu.SemaphoreType.DMA


def params(number):
    return pltpu.CompilerParams(collective_id=number, has_side_effects=True, vmem_limit_bytes=VMEM_LIMIT)


def shards(nz, nh, inputs, out_grad, lengths, norm_attn, norm_ffn, w_query, w_key, w_value, w_output_gate, conv_kernel, w_out, w_gate, w_up, w_down):
    micro, rows, d = inputs.shape
    heads = w_query.shape[2] // FEAT
    width, qk, ff = w_value.shape[2], w_query.shape[2], w_gate.shape[2]
    part, block = rows // nh, d // nz
    dims = (nz, nh, rows, heads)
    wide = -(-((heads - 1) * HD + LANES) // LANES) * LANES
    groups = (2 * width, -(-(2 * qk + width) // LANES) * LANES)
    tables = jnp.asarray(lift_tables(heads), BF16)
    turned = [jnp.swapaxes(w, 1, 2) for w in (w_query, w_key, w_value, w_output_gate)]
    own = (*turned, w_out, jnp.swapaxes(w_gate, 1, 2), jnp.swapaxes(w_up, 1, 2), w_down)
    small_own = jnp.concatenate(
        [norm_attn, norm_ffn, jnp.pad(conv_kernel[0], ((0, 0), (0, d - width))), jnp.zeros((3, d), F32)]
    )

    def vm(dims, kind=BF16):
        return pltpu.VMEM(tuple(dims), kind)

    mats = [vm((2 * qk + 2 * width, d)), vm((width, d)), vm((ff, d)), vm((ff, d)), vm((ff, d))]
    act = vm((rows, d))
    kept = [
        ((part, d), BF16),
        ((rows, d), BF16),
        ((rows, 2 * qk), BF16),
        ((rows + 8, wide), F32),
        ((rows, wide), F32),
        ((heads, rows, LANES), F32),
        ((heads, PSI, LANES), BF16),
        ((rows, width), BF16),
        ((part, d), F32),
        ((rows, ff), BF16),
        ((rows, ff), BF16),
    ]
    keep_shapes = [shape(*k) for k in kept]
    gathered = shape((nz, rows, d))
    outs = (
        [shape((8, d), F32)]
        + [shape(w.shape) for w in own]
        + keep_shapes * 2
        + [shape((micro, rows, d)), gathered, gathered, shape((rows, d))]
    )
    scratch = (
        mats
        + mats
        + [
            act,
            act,
            act,
            vm((rows, 2 * qk)),
            vm((rows + 8, wide), F32),
            vm((2, 8, wide), F32),
            vm((rows, wide), F32),
            vm((rows, wide), F32),
            vm((heads, rows, LANES)),
            vm((heads, rows, LANES), F32),
            vm((2, heads, PSI_SENT, LANES)),
            vm((2, nz, heads, PSI_SENT, LANES)),
            vm((heads, PSI, LANES)),
            vm((rows, wide), F32),
            vm((rows, width)),
            vm((2, 2, rows, d)),
            vm((nh - 1, part, d)),
            vm((rows, ff)),
            vm((rows, ff)),
            vm((rows, ff)),
            vm((2, rows, d)),
            vm((part, d), F32),
            vm((8, d), F32),
            DMA((16,)),
            DMA((5,)),
            DMA((SAVED,)),
            DMA((10,)),
            DMA((10,)),
            DMA((2,)),
            DMA((2,)),
            DMA((2, nz)),
            DMA((2, nz)),
            DMA((2, 4, 2 * (nh - 1))),
            DMA((2, 4, 2 * (nh - 1))),
            DMA((2, 2, nz - 1, 2)),
            DMA((2, 2, nz - 1, 2)),
            DMA((2, 2, nz - 1, 2)),
            DMA((2, 2, nz - 1, 2)),
        ]
    )
    first = pl.pallas_call(
        functools.partial(fwd_kernel, dims),
        out_shape=outs,
        in_specs=[SM, ANY, ANY, VM, VM] + [ANY] * 8,
        out_specs=[ANY] * len(outs),
        scratch_shapes=scratch,
        compiler_params=params(0),
    )(lengths, inputs, out_grad, small_own, tables, *own)
    small_other, other = first[0], first[1:9]
    saved = first[9 : 9 + 2 * SAVED]
    section_out, gath_g1, gath_n2_0, n2_1 = first[9 + 2 * SAVED :]

    outs = (
        [shape((micro, rows, d)), shape((8, d), F32)]
        + [shape((block, g)) for g in groups]
        + [shape((block, ff), F32)] * 3
        + [gathered, gathered, gathered]
        + [shape((2, 2, nz, block, g)) for g in groups]
        + [shape((block, ff))] * 3
    )
    out_specs = [ANY, VM] + [ANY] * (len(outs) - 2)
    scratch = (
        mats
        + [vm(*k) for k in kept]
        + [
            act,
            vm((rows, ff)),
            act,
            vm((nh - 1, part, d)),
            act,
            vm((part, d), F32),
            vm((rows, wide), F32),
            vm((rows, wide), F32),
            vm((heads, rows, LANES)),
            vm((heads, rows, LANES)),
            vm((2, heads, PSI_SENT, LANES)),
            vm((2, nz, heads, PSI_SENT, LANES)),
            vm((heads, PSI, LANES)),
            vm((rows, qk), F32),
            vm((rows, qk), F32),
            vm((rows + 8, wide), F32),
            vm((2, 8, wide), F32),
            vm((rows, 2 * qk + 2 * width)),
            vm((2, rows, d)),
            vm((2, 8, d), F32),
            vm((8, d), F32),
            vm((2, 8, d), F32),
            vm((nz - 1, 8, d), F32),
            vm((nh - 1, 8, d), F32),
        ]
        + [vm((block, ff), F32)] * 3
        + [vm((block, ff))] * 3
        + [act, act, vm((block, rows)), vm((block, rows))]
        + [vm((nz, block, g)) for g in groups]
        + [vm((nz, block, max(groups))), vm((block, max(groups)))]
        + [
            DMA((8,)),
            DMA((12,)),
            DMA((SAVED,)),
            DMA((2,)),
            DMA((2,)),
            DMA((2, nz)),
            DMA((2, nz)),
            DMA((2, 4, 2 * (nh - 1))),
            DMA((2, 4, 2 * (nh - 1))),
            DMA((2, 2, nz - 1, 2)),
            DMA((2, 2, nz - 1, 2)),
            DMA((3, 2, nz - 1, 2)),
            DMA((3, 2, nz - 1, 2)),
            DMA((3,)),
            DMA((3,)),
            DMA((2, nz)),
            DMA((2, 2, nz)),
            DMA((2, 2, 2, nz)),
            DMA((2, 2, 2, nz)),
            DMA((4,)),
            DMA((4,)),
            DMA((nz - 1,)),
            DMA((nz - 1,)),
            DMA((nh - 1,)),
            DMA((nh - 1,)),
        ]
    )
    second = pl.pallas_call(
        functools.partial(bwd_kernel, dims),
        out_shape=outs,
        in_specs=[SM, ANY, VM, VM, VM] + [ANY] * (16 + 2 * SAVED + 3),
        out_specs=out_specs,
        scratch_shapes=scratch,
        input_output_aliases={5 + 16 + 2 * SAVED + 1: 9},
        compiler_params=params(1),
    )(lengths, out_grad, small_own, small_other, tables, *own, *other, *saved, gath_g1, gath_n2_0, n2_1)
    input_grad, gains, att_early, att_late, g_gate, g_up, g_down = second[:7]
    far = second[-3:]
    finals = [
        shape((micro, rows, d)),
        shape((micro, rows, d)),
        shape((block, ff), F32),
        shape((block, ff), F32),
        shape((block, ff), F32),
        shape((qk, block), F32),
        shape((qk, block), F32),
        shape((block, width), F32),
        shape((block, width), F32),
        shape((width, block), F32),
        shape((1, d), F32),
        shape((1, d), F32),
        shape((KW, width), F32),
    ]
    section_out, input_grad, g_gate, g_up, g_down, g_q, g_k, g_v, g_o, g_out, g_attn, g_ffn, g_conv = pl.pallas_call(
        functools.partial(final_kernel, qk, width),
        out_shape=finals,
        in_specs=[ANY] * 8 + [VM] * 3,
        out_specs=[ANY] * 5 + [VM] * 8,
        scratch_shapes=[vm((micro, rows, d))] * 2 + [vm((block, ff), F32)] * 3 + [vm((block, ff))] * 3 + [DMA((13,))],
        compiler_params=pltpu.CompilerParams(vmem_limit_bytes=VMEM_LIMIT),
    )(section_out, input_grad, g_gate, g_up, g_down, *far, att_early, att_late, gains)
    return (
        section_out[None],
        input_grad[None],
        g_attn,
        g_ffn,
        g_q.T[None],
        g_k.T[None],
        g_v[None],
        g_o[None],
        g_conv[None],
        g_out[None],
        g_gate[None],
        g_up[None],
        g_down.T[None],
    )


def solution(mesh):
    return jax.shard_map(
        functools.partial(shards, mesh.shape["seq"], mesh.shape["head"]),
        mesh=mesh,
        in_specs=(
            P(None, "seq", None),
            P(None, "seq", None),
            P(),
            P("section", None),
            P("section", None),
            P("section", None, "head"),
            P("section", None, "head"),
            P("section", None, "head"),
            P("section", None, "head"),
            P("section", None, "head"),
            P("section", "head", None),
            P("section", None, "head"),
            P("section", None, "head"),
            P("section", "head", None),
        ),
        out_specs=(
            P("section", None, "seq", None),
            P("section", None, "seq", None),
            P("section", None),
            P("section", None),
            P("section", "seq", "head"),
            P("section", "seq", "head"),
            P("section", "seq", "head"),
            P("section", "seq", "head"),
            P("section", None, "head"),
            P("section", "head", "seq"),
            P("section", "seq", "head"),
            P("section", "seq", "head"),
            P("section", "head", "seq"),
        ),
        check_vma=False,
    )
```
